32 devices in a mesh: dp: 4 (over z), tx: 4 (over y, core), ty: 2 (over x).
Axes of the slice: x: 2, y: 2, z: 4, core: 2. Of those that a mesh axis runs over, the one named last changes fastest.
Arguments:
- tokens: bfloat16 [8192, 2048], P(('dp', 'tx'), 'ty'), may hold values from -6 to 6
- seg_ids: int32 [8, 1024], P(('dp', 'ty')), may hold values from 0 to 3, as said below
- w_query: bfloat16 [2048, 2048], P('ty', 'tx'), may hold values from -0.125 to 0.125
- w_key: bfloat16 [2048, 1024], P('ty', 'tx'), may hold values from -0.125 to 0.125
- w_value: bfloat16 [2048, 1024], P('ty', 'tx'), may hold values from -0.125 to 0.125
- w_out: bfloat16 [2048, 2048], P('tx', 'ty'), may hold values from -1 to 1
- w_gate: bfloat16 [2048, 6144], P('ty', 'tx'), may hold values from -0.125 to 0.125
- w_up: bfloat16 [2048, 6144], P('ty', 'tx'), may hold values from -0.125 to 0.125
- w_down: bfloat16 [6144, 2048], P('tx', 'ty'), may hold values from -0.078125 to 0.078125
- attn_gain: float32 [2048], P('ty'), may hold values from 0.5 to 1.5
- mlp_gain: float32 [2048], P('ty'), may hold values from 0.5 to 1.5
- query_gain: float32 [128], replicated, may hold values from 1 to 2
- key_gain: float32 [128], replicated, may hold values from 1 to 2
- cotangent: bfloat16 [8192, 2048], P(('dp', 'tx'), 'ty'), may hold values from -6 to 6
Outputs:
- output: bfloat16 [8192, 2048], P(('dp', 'tx'), 'ty')
- input_grad: bfloat16 [8192, 2048], P(('dp', 'tx'), 'ty')
- query_weight_grad: float32 [2048, 2048], P(('ty', 'dp'), 'tx')
- key_weight_grad: float32 [2048, 1024], P(('ty', 'dp'), 'tx')
- value_weight_grad: float32 [2048, 1024], P(('ty', 'dp'), 'tx')
- out_weight_grad: float32 [2048, 2048], P('tx', ('ty', 'dp'))
- gate_weight_grad: float32 [2048, 6144], P(('ty', 'dp'), 'tx')
- up_weight_grad: float32 [2048, 6144], P(('ty', 'dp'), 'tx')
- down_weight_grad: float32 [6144, 2048], P('tx', ('ty', 'dp'))
- attn_gain_grad: float32 [2048], replicated
- mlp_gain_grad: float32 [2048], replicated
- query_gain_grad: float32 [128], replicated
- key_gain_grad: float32 [128], replicated
The draws below stay inside these ranges and needn't reach their ends.
Inputs may be any that keep to these rules, and one draw needn't show every extreme that they name: `seg_ids`: document numbers never fall along a sequence and every one of 0 to 3 occurs; each document has 102 to 512 tokens, and in every sequence one document has exactly 512.
All inputs are finite; a program needn't handle non-finite values.
Results may differ from the reference program's by a relative error of at most 0.023.
Values may be sent and summed in bfloat16 or wider, within the bound.
A program may use at most 256 MiB of HBM per device.

```python
import math
import jax
import jax.numpy as jnp
from jax import lax

D = 2048
HEADS = 16
KV_HEADS = 8
HEAD_DIM = 128
FF = 6144
LEN = 1024
DOCS = 4
DOC_MOST = 512
DOC_LEAST = 102
SEQS = 8
TOKENS = 8192


def draw_seg_ids(key, part):
    key = jax.random.fold_in(key, 7)
    place_key, cut_key = jax.random.split(key)
    spare = LEN - DOC_MOST - (DOCS - 1) * DOC_LEAST
    place = jax.random.randint(place_key, (SEQS, 1), 0, DOCS)
    cuts = jnp.sort(jax.random.randint(cut_key, (SEQS, DOCS - 2), 0, spare + 1), axis=1)
    bounds = jnp.concatenate([jnp.zeros((SEQS, 1), jnp.int32), cuts.astype(jnp.int32), jnp.full((SEQS, 1), spare, jnp.int32)], axis=1)
    others = bounds[:, 1:] - bounds[:, :-1] + DOC_LEAST
    slot = jnp.arange(DOCS, dtype=jnp.int32)[None, :]
    pick = jnp.clip(jnp.where(slot > place, slot - 1, slot), 0, DOCS - 2)
    taken = jnp.take_along_axis(others, pick, axis=1)
    lengths = jnp.where(slot == place, DOC_MOST, taken).astype(jnp.int32)
    ends = jnp.cumsum(lengths, axis=1)
    where = jnp.arange(LEN, dtype=jnp.int32)[None, :, None]
    seg = jnp.sum((where >= ends[:, None, :-1]).astype(jnp.int32), axis=2)
    return seg.astype(jnp.int32)


def shard_levels(rng, extent, pieces, low, top_value):
    loudness, own = 1.0, jax.random.fold_in(rng, 6)
    for dim, blocks in pieces:
        steps = jnp.exp(jax.random.uniform(jax.random.fold_in(own, dim), (blocks,), jnp.float32, low / len(pieces), top_value / len(pieces)))
        loudness = loudness * jnp.repeat(steps, extent[dim] // blocks).reshape([-1 if axis == dim else 1 for axis in range(len(extent))])
    return loudness


def normal_values(rng, dims, deviation, most, shards=(), kind=jnp.bfloat16):
    array = jax.random.normal(rng, dims, jnp.float32) * deviation
    if len(shards) > 0:
        array = shard_levels(rng, dims, shards, -0.22, 0.18) * array
    return jnp.clip(array, min=-most, max=most).astype(kind)


def setup_inputs(seed: int = 0) -> dict:
    key_list = jax.random.split(jax.random.key(seed), 15)
    tokens = normal_values(key_list[0], (TOKENS, D), 1.0, 6.0, ((0, 16), (1, 2)))
    seg_ids = draw_seg_ids(jax.random.fold_in(key_list[14], 71), 0)
    w_query = normal_values(key_list[2], (D, HEADS * HEAD_DIM), D ** -0.5, 0.125, ((0, 2), (1, 4)))
    w_key = normal_values(key_list[3], (D, KV_HEADS * HEAD_DIM), D ** -0.5, 0.125, ((0, 2), (1, 4)))
    w_value = normal_values(key_list[4], (D, KV_HEADS * HEAD_DIM), D ** -0.5, 0.125, ((0, 2), (1, 4)))
    w_out = normal_values(key_list[5], (HEADS * HEAD_DIM, D), (HEAD_DIM // 4) ** -0.5, 1.0, ((0, 4), (1, 2)))
    w_gate = normal_values(key_list[6], (D, FF), D ** -0.5, 0.125, ((0, 2), (1, 4)))
    w_up = normal_values(key_list[7], (D, FF), D ** -0.5, 0.125, ((0, 2), (1, 4)))
    w_down = normal_values(key_list[8], (FF, D), FF ** -0.5, 0.078125, ((0, 4), (1, 2)))
    attn_gain = jnp.clip(1.0 + 0.1 * jax.random.normal(key_list[9], (D,), jnp.float32), 0.5, 1.5)
    mlp_gain = jnp.clip(1.0 + 0.1 * jax.random.normal(key_list[10], (D,), jnp.float32), 0.5, 1.5)
    query_gain = jnp.clip(jnp.exp(jax.random.uniform(key_list[11], (HEAD_DIM,), jnp.float32, math.log(1.0), math.log(2.0))), 1.0, 2.0)
    key_gain = jnp.clip(jnp.exp(jax.random.uniform(key_list[12], (HEAD_DIM,), jnp.float32, math.log(1.0), math.log(2.0))), 1.0, 2.0)
    cotangent = normal_values(key_list[13], (TOKENS, D), 1.0, 6.0, ((0, 16), (1, 2)))
    return dict(tokens=tokens, seg_ids=seg_ids, w_query=w_query, w_key=w_key, w_value=w_value, w_out=w_out, w_gate=w_gate, w_up=w_up, w_down=w_down, attn_gain=attn_gain, mlp_gain=mlp_gain, query_gain=query_gain, key_gain=key_gain, cotangent=cotangent)


EPS = 1e-06
THETA = 1000000.0
NEG = -1e+30

@jax.custom_vjp
def low(v):
    return lax.optimization_barrier(v.astype(jnp.bfloat16)).astype(jnp.float32)

@jax.custom_vjp
def low_back(v):
    return v

def low_keep(v):
    return (low(v), None)

def low_pass(kept, grad):
    return (grad,)

def back_keep(v):
    return (v, None)

def back_low(kept, grad):
    return (low(grad),)
low.defvjp(low_keep, low_pass)
low_back.defvjp(back_keep, back_low)

def exact(left, right):
    return jnp.dot(left, right, precision=lax.Precision.HIGHEST)

def rms(value, gain):
    return value * lax.rsqrt(lax.optimization_barrier(jnp.mean(value * value, axis=-1, keepdims=True)) + EPS) * gain

def doc_positions(seg):
    count = seg.shape[-1]
    index = jnp.arange(count, dtype=jnp.int32)
    edge = jnp.concatenate([jnp.ones((1,), dtype=jnp.bool_), seg[1:] != seg[:-1]])
    first = lax.cummax(jnp.where(edge, index, jnp.zeros_like(index)), axis=0)
    return (index - first).astype(jnp.int32)

def rotary(positions, depth):
    half = depth // 2
    freq = THETA ** (-jnp.arange(half, dtype=jnp.float32) * 2.0 / depth)
    angle = positions.astype(jnp.float32)[..., None] * freq
    return (jnp.cos(angle), jnp.sin(angle))

def turn(value, gain, cosine, sine):
    normed = rms(value, gain)
    half = value.shape[-1] // 2
    first = normed[..., :half]
    second = normed[..., half:]
    return jnp.concatenate([first * cosine - second * sine, second * cosine + first * sine], axis=-1)

def attend(query, keys, values, seg):
    length = seg.shape[0]
    kv_heads = keys.shape[1]
    groups = query.shape[1] // kv_heads
    scale = query.shape[-1] ** (-0.5)
    index = jnp.arange(length, dtype=jnp.int32)
    mask = (seg[None, :] == seg[:, None]) & (index[None, :] <= index[:, None])
    query = query.reshape(length, kv_heads, groups, -1).transpose(1, 2, 0, 3)
    keys = keys.transpose(1, 0, 2)
    values = values.transpose(1, 0, 2)

    def one_head(operands):
        head_query, head_keys, head_values = operands
        scores = jnp.einsum('gld,md->glm', head_query, head_keys, precision=lax.Precision.HIGHEST)
        scores = low_back(scores * scale)
        scores = jnp.where(mask[None], scores, NEG)
        top = lax.optimization_barrier(jnp.max(scores, axis=-1, keepdims=True))
        weights = jnp.exp(scores - top)
        probs = low(weights / lax.optimization_barrier(jnp.sum(weights, axis=-1, keepdims=True)))
        return jnp.einsum('glm,md->lgd', probs, head_values, precision=lax.Precision.HIGHEST)
    mixed = lax.map(jax.checkpoint(one_head), (query, keys, values))
    return mixed.transpose(1, 0, 2, 3).reshape(length, -1)

def layer(rows, seg, w_query, w_key, w_value, w_out, w_gate, w_up, w_down, attn_gain, mlp_gain, query_gain, key_gain):
    length = rows.shape[0]
    depth = query_gain.shape[0]
    normed = low(rms(rows, attn_gain))
    query_proj = low_back(exact(normed, w_query)).reshape(length, -1, depth)
    key_proj = low_back(exact(normed, w_key)).reshape(length, -1, depth)
    values = low(low_back(exact(normed, w_value))).reshape(length, -1, depth)
    cosine, sine = rotary(doc_positions(seg), depth)
    cosine = cosine[:, None, :]
    sine = sine[:, None, :]
    query = low(turn(query_proj, query_gain, cosine, sine))
    keys = low(turn(key_proj, key_gain, cosine, sine))
    attended = low(low_back(attend(query, keys, values, seg)))
    residual = rows + low_back(exact(attended, w_out))
    second = low(rms(residual, mlp_gain))
    gate = low_back(exact(second, w_gate))
    upper = low_back(exact(second, w_up))
    hidden = low(jax.nn.silu(gate) * upper)
    return residual + exact(hidden, w_down)

def reference(tokens, seg_ids, w_query, w_key, w_value, w_out, w_gate, w_up, w_down, attn_gain, mlp_gain, query_gain, key_gain, cotangent):
    seqs = seg_ids.shape[0]
    length = seg_ids.shape[1]
    floats = [item.astype(jnp.float32) for item in (tokens, w_query, w_key, w_value, w_out, w_gate, w_up, w_down, attn_gain, mlp_gain, query_gain, key_gain)]

    def forward(rows_all, *weights):

        def one_sequence(operands):
            rows, seg = operands
            return layer(rows, seg, *weights)
        shaped = rows_all.reshape(seqs, length, -1)
        result = lax.map(jax.checkpoint(one_sequence), (shaped, seg_ids))
        return result.reshape(rows_all.shape)
    output, pull = jax.vjp(forward, *floats)
    grads = pull(cotangent.astype(jnp.float32))
    return (output.astype(jnp.bfloat16), grads[0].astype(jnp.bfloat16), grads[1], grads[2], grads[3], grads[4], grads[5], grads[6], grads[7], grads[8], grads[9], grads[10], grads[11])
```

```python
import jax
import jax.numpy as jnp
from jax import lax
from jax.experimental import pallas as pl
from jax.experimental.pallas import tpu as pltpu
from jax.sharding import PartitionSpec as P

EPS = 1e-06
THETA = 1000000.0
NEG = -1e30
F32 = jnp.float32
B16 = jnp.bfloat16
MESH = pl.DeviceIdType.MESH


def width_sum(value):
    return lax.psum(value, "ty")


def token_gather(rows):
    return lax.all_gather(rows, "tx", axis=0, tiled=True)


def branch_gather(rows):
    return lax.all_gather(rows, "ty", axis=0, tiled=True)


def width_reduce(whole, apply):
    return lax.psum_scatter(apply(whole), "ty", scatter_dimension=0, tiled=True)


def head_reduce(whole, apply):
    return lax.psum_scatter(
        apply(whole).astype(jnp.bfloat16), "tx", scatter_dimension=0, tiled=True
    ).astype(jnp.float32)


def forward_with(weight):
    return lambda rows: jnp.dot(rows, weight, preferred_element_type=F32)


def backward_with(weight):
    return lambda rows: lax.dot_general(
        rows, weight, (((1,), (1,)), ((), ())), preferred_element_type=F32
    )


def weight_grad(left, right):
    return lax.dot_general(left, right, (((0,), (0,)), ((), ())), preferred_element_type=F32)


def norm_scale(rows):
    width = rows.shape[1] * lax.axis_size("ty")
    return lax.rsqrt(width_sum(jnp.sum(rows * rows, axis=1)) / width + EPS)


def norm_back(rows, scale, gain, upstream):
    width = rows.shape[1] * lax.axis_size("ty")
    inner = width_sum(jnp.sum(upstream * gain * rows, axis=1))
    back = scale[:, None] * gain * upstream - rows * (scale**3 * inner / width)[:, None]
    gain_part = jnp.sum(upstream * rows * scale[:, None], axis=0)
    return (back, gain_part)


def widen(part):
    whole = jnp.zeros((part.shape[0] * lax.axis_size("ty"),), F32)
    return lax.dynamic_update_slice_in_dim(whole, part, lax.axis_index("ty") * part.shape[0], 0)


def doc_positions(seg):
    count = seg.shape[-1]
    index = jnp.arange(count, dtype=jnp.int32)
    edge = jnp.concatenate([jnp.ones((1,), dtype=jnp.bool_), seg[1:] != seg[:-1]])
    first = lax.cummax(jnp.where(edge, index, jnp.zeros_like(index)), axis=0)
    return index - first


def rotary(positions, depth):
    half = depth // 2
    freq = THETA ** (-jnp.arange(half, dtype=F32) * 2.0 / depth)
    angle = positions.astype(F32)[..., None] * freq
    return (jnp.cos(angle), jnp.sin(angle))


def turn(value, gain, cosine, sine):
    normed = value * lax.rsqrt(jnp.mean(value * value, axis=-1, keepdims=True) + EPS) * gain
    half = value.shape[-1] // 2
    first = normed[..., :half]
    second = normed[..., half:]
    return jnp.concatenate(
        [first * cosine - second * sine, second * cosine + first * sine], axis=-1
    )


def block_scores(part, seq_keys, seq_ids, start, scale):
    block = part.shape[0]
    length = seq_ids.shape[0]
    index = jnp.arange(length, dtype=jnp.int32)
    rows = start + jnp.arange(block, dtype=jnp.int32)
    row_ids = lax.dynamic_slice_in_dim(seq_ids, start, block, 0)
    mask = (seq_ids[None, :] == row_ids[:, None]) & (index[None, :] <= rows[:, None])
    scores = jnp.einsum("qkgd,mkd->kgqm", part, seq_keys, preferred_element_type=F32) * scale
    return jnp.where(mask[None, None], scores, NEG)


def attend_forward(query, keys, values, seg, block):
    seqs, length, heads, depth = query.shape
    kv_heads = keys.shape[2]
    groups = heads // kv_heads
    scale = depth ** (-0.5)
    count = length // block
    starts = jnp.arange(count, dtype=jnp.int32) * block

    def one_sequence(operands):
        seq_query, seq_keys, seq_values, seq_ids = operands
        blocks = seq_query.reshape(count, block, kv_heads, groups, depth)

        def one_block(inputs):
            part, start = inputs
            scores = block_scores(part, seq_keys, seq_ids, start, scale)
            top = jnp.max(scores, axis=-1)
            weights = jnp.exp(scores - top[..., None])
            total = jnp.sum(weights, axis=-1)
            probs = (weights / total[..., None]).astype(B16)
            mixed = jnp.einsum("kgqm,mkd->qkgd", probs, seq_values, preferred_element_type=F32)
            return (mixed, top + jnp.log(total))

        mixed, logs = lax.map(one_block, (blocks, starts))
        return (mixed.reshape(length, heads * depth), logs)

    return lax.map(one_sequence, (query, keys, values, seg))


def attend_backward(query, keys, values, seg, logs, grad_out, block):
    seqs, length, heads, depth = query.shape
    kv_heads = keys.shape[2]
    groups = heads // kv_heads
    scale = depth ** (-0.5)
    count = length // block
    starts = jnp.arange(count, dtype=jnp.int32) * block

    def one_sequence(operands):
        seq_query, seq_keys, seq_values, seq_ids, seq_logs, seq_grad = operands
        blocks = seq_query.reshape(count, block, kv_heads, groups, depth)
        grads = seq_grad.reshape(count, block, kv_heads, groups, depth)

        def one_block(carry, inputs):
            key_acc, value_acc = carry
            part, grad_part, log_part, start = inputs
            scores = block_scores(part, seq_keys, seq_ids, start, scale)
            probs = jnp.exp(scores - log_part[..., None])
            value_acc = value_acc + jnp.einsum(
                "kgqm,qkgd->mkd", probs.astype(B16), grad_part, preferred_element_type=F32
            )
            prob_grad = jnp.einsum(
                "qkgd,mkd->kgqm", grad_part, seq_values, preferred_element_type=F32
            )
            delta = jnp.sum(probs * prob_grad, axis=-1, keepdims=True)
            score_grad = (probs * (prob_grad - delta)).astype(B16)
            query_grad = (
                jnp.einsum("kgqm,mkd->qkgd", score_grad, seq_keys, preferred_element_type=F32)
                * scale
            )
            key_acc = (
                key_acc
                + jnp.einsum("kgqm,qkgd->mkd", score_grad, part, preferred_element_type=F32) * scale
            )
            return ((key_acc, value_acc), query_grad)

        zeros = jnp.zeros((length, kv_heads, depth), F32)
        (key_grad, value_grad), query_grad = lax.scan(
            one_block, (zeros, zeros), (blocks, grads, seq_logs, starts)
        )
        return (query_grad.reshape(length, heads, depth), key_grad, value_grad)

    return lax.map(one_sequence, (query, keys, values, seg, logs, grad_out))


def general_device(
    tokens,
    seg_ids,
    w_query,
    w_key,
    w_value,
    w_out,
    w_gate,
    w_up,
    w_down,
    attn_gain,
    mlp_gain,
    query_gain,
    key_gain,
    cotangent,
):
    seqs, length = seg_ids.shape
    depth = query_gain.shape[0]
    query_width = w_query.shape[1]
    key_width = w_key.shape[1]
    units = w_gate.shape[1]
    block = min(512, length)
    inputs = tokens.astype(F32)
    first_scale = norm_scale(inputs)
    first_normed = (inputs * first_scale[:, None] * attn_gain).astype(B16)
    first_whole = token_gather(first_normed)
    w_project = jnp.concatenate([w_query, w_key, w_value], axis=1)
    projected = width_reduce(first_whole, forward_with(w_project))
    query_proj = projected[:, :query_width].reshape(seqs, length, -1, depth)
    key_proj = projected[:, query_width : query_width + key_width].reshape(seqs, length, -1, depth)
    values = projected[:, query_width + key_width :].astype(B16).reshape(seqs, length, -1, depth)
    positions = jax.vmap(doc_positions)(seg_ids)
    cosine, sine = rotary(positions, depth)
    cosine = cosine[:, :, None, :]
    sine = sine[:, :, None, :]
    query = turn(query_proj, query_gain, cosine, sine).astype(B16)
    keys = turn(key_proj, key_gain, cosine, sine).astype(B16)
    mixed, logs = attend_forward(query, keys, values, seg_ids, block)
    attended = mixed.reshape(seqs * length, -1).astype(B16)
    attended_whole = branch_gather(attended)
    residual = inputs + head_reduce(attended_whole, forward_with(w_out))
    second_scale = norm_scale(residual)
    second_normed = (residual * second_scale[:, None] * mlp_gain).astype(B16)
    second_whole = token_gather(second_normed)
    w_both = jnp.concatenate([w_gate, w_up], axis=1)
    gate_up = width_reduce(second_whole, forward_with(w_both))
    gate = gate_up[:, :units]
    upper = gate_up[:, units:]
    hidden = (jax.nn.silu(gate) * upper).astype(B16)
    hidden_whole = branch_gather(hidden)
    output = residual + head_reduce(hidden_whole, forward_with(w_down))
    grad_whole = token_gather(cotangent)
    hidden_grad = width_reduce(grad_whole, backward_with(w_down))
    down_grad = weight_grad(hidden_whole, grad_whole)
    gate_grad, up_grad = jax.vjp(lambda left, right: jax.nn.silu(left) * right, gate, upper)[1](
        hidden_grad
    )
    unit_grads = jnp.concatenate([gate_grad, up_grad], axis=1).astype(B16)
    unit_whole = branch_gather(unit_grads)
    second_grad = head_reduce(unit_whole, backward_with(w_both))
    both_grad = weight_grad(second_whole, unit_whole)
    gate_weight = both_grad[:, :units]
    up_weight = both_grad[:, units:]
    resid_norm_grad, mlp_gain_part = norm_back(residual, second_scale, mlp_gain, second_grad)
    residual_grad = cotangent.astype(F32) + resid_norm_grad
    residual_whole = token_gather(residual_grad.astype(B16))
    mixed_grad = width_reduce(residual_whole, backward_with(w_out)).astype(B16)
    out_grad = weight_grad(attended_whole, residual_whole)
    query_grad, key_grad, value_grad = attend_backward(
        query, keys, values, seg_ids, logs, mixed_grad.reshape(seqs, length, -1), block
    )
    query_proj_grad, query_gain_grad = jax.vjp(
        lambda value, gain: turn(value, gain, cosine, sine), query_proj, query_gain
    )[1](query_grad)
    key_proj_grad, key_gain_grad = jax.vjp(
        lambda value, gain: turn(value, gain, cosine, sine), key_proj, key_gain
    )[1](key_grad)
    rows = seqs * length
    proj_grad = jnp.concatenate(
        [
            query_proj_grad.reshape(rows, -1),
            key_proj_grad.reshape(rows, -1),
            value_grad.reshape(rows, -1),
        ],
        axis=1,
    ).astype(B16)
    proj_whole = branch_gather(proj_grad)
    first_grad = head_reduce(proj_whole, backward_with(w_project))
    project_grad = weight_grad(first_whole, proj_whole)
    query_weight = project_grad[:, :query_width]
    key_weight = project_grad[:, query_width : query_width + key_width]
    value_weight = project_grad[:, query_width + key_width :]
    input_norm_grad, attn_gain_part = norm_back(inputs, first_scale, attn_gain, first_grad)
    input_grad = (residual_grad + input_norm_grad).astype(B16)
    attn_total, mlp_total, query_total, key_total = lax.psum(
        (widen(attn_gain_part), widen(mlp_gain_part), query_gain_grad, key_gain_grad),
        ("dp", "tx", "ty"),
    )
    query_share, key_share, value_share, gate_share, up_share = (
        lax.psum_scatter(
            query_weight.astype(jnp.bfloat16), "dp", scatter_dimension=0, tiled=True
        ).astype(jnp.float32),
        lax.psum_scatter(
            key_weight.astype(jnp.bfloat16), "dp", scatter_dimension=0, tiled=True
        ).astype(jnp.float32),
        lax.psum_scatter(
            value_weight.astype(jnp.bfloat16), "dp", scatter_dimension=0, tiled=True
        ).astype(jnp.float32),
        lax.psum_scatter(
            gate_weight.astype(jnp.bfloat16), "dp", scatter_dimension=0, tiled=True
        ).astype(jnp.float32),
        lax.psum_scatter(
            up_weight.astype(jnp.bfloat16), "dp", scatter_dimension=0, tiled=True
        ).astype(jnp.float32),
    )
    out_share, down_share = (
        lax.psum_scatter(
            out_grad.astype(jnp.bfloat16), "dp", scatter_dimension=1, tiled=True
        ).astype(jnp.float32),
        lax.psum_scatter(
            down_grad.astype(jnp.bfloat16), "dp", scatter_dimension=1, tiled=True
        ).astype(jnp.float32),
    )
    return (
        output.astype(B16),
        input_grad,
        query_share,
        key_share,
        value_share,
        out_share,
        gate_share,
        up_share,
        down_share,
        attn_total,
        mlp_total,
        query_total,
        key_total,
    )


PARTS = 2


def fits(mesh):
    return mesh.shape["tx"] == 4 and mesh.shape["ty"] == 2 and mesh.shape["dp"] == 4


def swap_x(value):
    return lax.ppermute(value, "ty", [(0, 1), (1, 0)])


def swap_y(value):
    return lax.ppermute(value, "tx", [(i, i ^ 2) for i in range(4)])


def swap_core(value):
    return lax.ppermute(value, "tx", [(i, i ^ 1) for i in range(4)])


def after(value, *waits):
    return lax.optimization_barrier((value,) + waits)[0]


def plane_gather(block, part):
    beside = swap_x(block)
    across = swap_y(block)
    corner = swap_y(beside) if part % 2 == 0 else swap_x(across)
    mine = [block, across, swap_core(block), swap_core(across)]
    theirs = [beside, corner, swap_core(beside), swap_core(corner)]
    return jnp.concatenate(mine, axis=0), jnp.concatenate(theirs, axis=0)


def plane_reduce(rows, apply_mine, apply_theirs, part):
    count = rows.shape[0] // 2
    other = rows[count:]
    own = rows[:count]
    from_mine = swap_core(apply_mine(other).astype(B16))
    from_theirs = swap_core(apply_theirs(other).astype(B16))
    mine = (apply_mine(own) + from_mine.astype(F32)).astype(B16)
    theirs = (apply_theirs(own) + from_theirs.astype(F32)).astype(B16)
    step = count // 2
    own_mine, far_mine = mine[:step], mine[step:]
    own_theirs, far_theirs = theirs[:step], theirs[step:]
    if part % 2 == 0:
        far_mine = (far_mine.astype(F32) + swap_x(far_theirs).astype(F32)).astype(B16)
    else:
        own_theirs = (own_theirs.astype(F32) + swap_y(far_theirs).astype(F32)).astype(B16)
    return own_mine.astype(F32) + swap_x(own_theirs).astype(F32) + swap_y(far_mine).astype(F32)


def line_reduce(share):
    place = lax.axis_index("dp")
    count = lax.axis_size("dp")
    up = None
    down = None
    for step in range(1, count):
        rise = share(lax.rem(place - step + count, count)).astype(F32)
        fall = share(lax.rem(place + step, count)).astype(F32)
        if up is not None:
            rise = rise + up.astype(F32)
            fall = fall + down.astype(F32)
        up = lax.ppermute(rise.astype(B16), "dp", [(i, i + 1) for i in range(step)])
        down = lax.ppermute(
            fall.astype(B16), "dp", [(i, i - 1) for i in range(count - step, count)]
        )
    return share(place).astype(F32) + up.astype(F32) + down.astype(F32)


def row_share(grad):
    size = grad.shape[0] // lax.axis_size("dp")
    return lambda place: lax.dynamic_slice_in_dim(grad, place * size, size, 0)


def column_share(grad):
    size = grad.shape[1] // lax.axis_size("dp")
    return lambda place: lax.dynamic_slice_in_dim(grad, place * size, size, 1)


def in_order(mine, theirs, axis):
    first = lax.axis_index("ty") == 0
    return jnp.concatenate(
        [jnp.where(first, mine, theirs), jnp.where(first, theirs, mine)], axis=axis
    )


def half_of(weight, place, axis):
    size = weight.shape[axis] // 2
    return lax.dynamic_slice_in_dim(weight, place * size, size, axis)


def spin(value, cosine, sine):
    return value * cosine + pltpu.roll(value, value.shape[1] // 2, 1) * sine


def spin_back(value, cosine, sine):
    return value * cosine + pltpu.roll(value * sine, value.shape[1] // 2, 1)


def head_scale(value):
    return lax.rsqrt(jnp.mean(value * value, axis=1, keepdims=True) + EPS)


def window(first, block, most):
    return max(0, first - most), first + block


def kept(first, block, low, high, starts):
    shape = (block, high - low)
    column = low + lax.broadcasted_iota(jnp.int32, shape, 1)
    row = first + lax.broadcasted_iota(jnp.int32, shape, 0)
    return (column >= starts) & (column <= row)


def rows_dot(left, right):
    return lax.dot_general(left, right, (((1,), (1,)), ((), ())), preferred_element_type=F32)


def attend_kernel(parts, heads, depth, block, most, core_ref, *refs):
    projected = refs[:parts]
    starts_ref, cosine_ref, sine_ref, query_gain_ref, key_gain_ref = refs[parts : parts + 5]
    refs = refs[parts + 5 :]
    mixed = refs[:parts]
    query_ref, key_ref, value_ref, log_ref = refs[parts:]
    core = core_ref[0]
    rows = projected[0].shape[2]
    length = query_ref.shape[1]
    scale = depth ** (-0.5)
    for half in range(2):
        place = jnp.bitwise_xor(core, half)
        for part in range(parts):
            at = half * (length // 2) + part * rows
            cosine = cosine_ref[0, at : at + rows, :]
            sine = sine_ref[0, at : at + rows, :]
            whole = projected[part][place, 0]
            for head in range(heads):
                value = whole[:, head * depth : (head + 1) * depth]
                normed = value * head_scale(value) * query_gain_ref[...]
                query_ref[0, at : at + rows, head * depth : (head + 1) * depth] = spin(
                    normed, cosine, sine
                ).astype(B16)
            value = whole[:, heads * depth : (heads + 1) * depth]
            normed = value * head_scale(value) * key_gain_ref[...]
            key_ref[0, at : at + rows, :] = spin(normed, cosine, sine).astype(B16)
            value_ref[0, at : at + rows, :] = whole[:, (heads + 1) * depth :].astype(B16)
    for first in range(0, length, block):
        low, high = window(first, block, most)
        mask = kept(first, block, low, high, starts_ref[0, first : first + block, :])
        half, left = divmod(first, length // 2)
        part, inner = divmod(left, rows)
        for head in range(heads):
            query = query_ref[0, first : first + block, head * depth : (head + 1) * depth]
            scores = rows_dot(query, key_ref[0, low:high, :]) * scale
            scores = jnp.where(mask, scores, NEG)
            top = jnp.max(scores, axis=1, keepdims=True)
            weights = jnp.exp(scores - top)
            total = jnp.sum(weights, axis=1, keepdims=True)
            probs = (weights * (1.0 / total)).astype(B16)
            out = jnp.dot(probs, value_ref[0, low:high, :], preferred_element_type=F32)
            mixed[part][
                jnp.bitwise_xor(core, half),
                0,
                inner : inner + block,
                head * depth : (head + 1) * depth,
            ] = out.astype(B16)
            log_ref[0, head, first : first + block, :] = top + jnp.log(total)


def attend_back_kernel(parts, heads, depth, block, most, core_ref, *refs):
    projected = refs[:parts]
    upstream = refs[parts : 2 * parts]
    refs = refs[2 * parts :]
    starts_ref, cosine_ref, sine_ref, query_gain_ref, key_gain_ref = refs[:5]
    query_ref, key_ref, value_ref, log_ref = refs[5:9]
    refs = refs[9:]
    result = refs[:parts]
    gain_ref, query_acc, key_acc, value_acc = refs[parts:]
    core = core_ref[0]
    rows = projected[0].shape[2]
    length = query_ref.shape[1]
    scale = depth ** (-0.5)
    key_acc[...] = jnp.zeros_like(key_acc)
    value_acc[...] = jnp.zeros_like(value_acc)
    for first in range(0, length, block):
        low, high = window(first, block, most)
        mask = kept(first, block, low, high, starts_ref[0, first : first + block, :])
        half, left = divmod(first, length // 2)
        part, inner = divmod(left, rows)
        keys = key_ref[0, low:high, :]
        values = value_ref[0, low:high, :]
        for head in range(heads):
            lanes = slice(head * depth, (head + 1) * depth)
            query = query_ref[0, first : first + block, lanes]
            grad = upstream[part][jnp.bitwise_xor(core, half), 0, inner : inner + block, lanes]
            scores = rows_dot(query, keys) * scale - log_ref[0, head, first : first + block, :]
            probs = jnp.where(mask, jnp.exp(jnp.where(mask, scores, 0.0)), 0.0)
            prob_grad = rows_dot(grad, values)
            delta = jnp.sum(probs * prob_grad, axis=1, keepdims=True)
            score_grad = (probs * (prob_grad - delta)).astype(B16)
            query_acc[first : first + block, lanes] = (
                jnp.dot(score_grad, keys, preferred_element_type=F32) * scale
            )
            key_acc[low:high, :] += weight_grad(score_grad, query) * scale
            value_acc[low:high, :] += weight_grad(probs.astype(B16), grad)
    query_total = jnp.zeros((1, depth), F32)
    key_total = jnp.zeros((1, depth), F32)
    for half in range(2):
        place = jnp.bitwise_xor(core, half)
        for part in range(parts):
            at = half * (length // 2) + part * rows
            cosine = cosine_ref[0, at : at + rows, :]
            sine = sine_ref[0, at : at + rows, :]
            for head in range(heads + 1):
                lanes = slice(head * depth, (head + 1) * depth)
                value = projected[part][place, 0, :, lanes]
                if head < heads:
                    grad = query_acc[at : at + rows, lanes]
                    gain = query_gain_ref[...]
                else:
                    grad = key_acc[at : at + rows, :]
                    gain = key_gain_ref[...]
                grad = spin_back(grad, cosine, sine)
                scaled = value * head_scale(value)
                share = jnp.sum(grad * scaled, axis=0, keepdims=True)
                if head < heads:
                    query_total += share
                else:
                    key_total += share
                inner = jnp.mean(gain * grad * scaled, axis=1, keepdims=True)
                back = head_scale(value) * (gain * grad - scaled * inner)
                result[part][place, 0, :, lanes] = back.astype(B16)
            result[part][place, 0, :, (heads + 1) * depth :] = value_acc[
                at : at + rows, :
            ].astype(B16)
    gain_ref[0, 0:1, :] = query_total
    gain_ref[0, 1:2, :] = key_total


def by_sequence(shape):
    return pl.BlockSpec((1,) + shape[1:], lambda i, core: (i,) + (0,) * (len(shape) - 1))


def by_block(shape):
    return pl.BlockSpec((shape[0], 1) + shape[2:], lambda i, core: (0, i, 0, 0))


def fixed(shape):
    return pl.BlockSpec(shape, lambda i, core: (0,) * len(shape))


def attend_sizes(projected, cosine, depth):
    parts = len(projected)
    heads = projected[0].shape[3] // depth - 2
    rows = projected[0].shape[2]
    length = cosine.shape[1]
    return parts, heads, rows, length, min(rows, 256)


def attend(projected, core, starts, cosine, sine, query_gain, key_gain, most):
    depth = query_gain.shape[1]
    parts, heads, rows, length, block = attend_sizes(projected, cosine, depth)
    common = (starts, cosine, sine)
    outs = [jax.ShapeDtypeStruct((2, 2, rows, heads * depth), B16)] * parts + [
        jax.ShapeDtypeStruct((2, length, heads * depth), B16),
        jax.ShapeDtypeStruct((2, length, depth), B16),
        jax.ShapeDtypeStruct((2, length, depth), B16),
        jax.ShapeDtypeStruct((2, heads, length, 1), F32),
    ]
    made = pl.pallas_call(
        lambda *refs: attend_kernel(parts, heads, depth, block, most, *refs),
        out_shape=outs,
        grid_spec=pltpu.PrefetchScalarGridSpec(
            num_scalar_prefetch=1,
            grid=(2,),
            in_specs=[by_block(item.shape) for item in projected]
            + [by_sequence(item.shape) for item in common]
            + [fixed(query_gain.shape)] * 2,
            out_specs=[by_block(item.shape) for item in outs[:parts]]
            + [by_sequence(item.shape) for item in outs[parts:]],
        ),
        compiler_params=pltpu.CompilerParams(vmem_limit_bytes=48 * 1024 * 1024),
        cost_estimate=pl.CostEstimate(
            flops=8 * length * length * depth * heads // 2 * 2,
            bytes_accessed=16 * 1024 * 1024,
            transcendentals=2 * heads * length * length // 2,
        ),
    )(core, *projected, *common, query_gain, key_gain)
    return made[:parts], made[parts:]


def attend_back(projected, upstream, saved, core, starts, cosine, sine, query_gain, key_gain, most):
    depth = query_gain.shape[1]
    parts, heads, rows, length, block = attend_sizes(projected, cosine, depth)
    common = (starts, cosine, sine)
    outs = [jax.ShapeDtypeStruct((2, 2, rows, (heads + 2) * depth), B16)] * parts + [
        jax.ShapeDtypeStruct((2, 8, depth), F32)
    ]
    made = pl.pallas_call(
        lambda *refs: attend_back_kernel(parts, heads, depth, block, most, *refs),
        out_shape=outs,
        grid_spec=pltpu.PrefetchScalarGridSpec(
            num_scalar_prefetch=1,
            grid=(2,),
            in_specs=[by_block(item.shape) for item in projected]
            + [by_block(item.shape) for item in upstream]
            + [by_sequence(item.shape) for item in common]
            + [fixed(query_gain.shape)] * 2
            + [by_sequence(item.shape) for item in saved],
            out_specs=[by_block(item.shape) for item in outs[:parts]]
            + [by_sequence(item.shape) for item in outs[parts:]],
            scratch_shapes=[
                pltpu.VMEM((length, heads * depth), F32),
                pltpu.VMEM((length, depth), F32),
                pltpu.VMEM((length, depth), F32),
            ],
        ),
        compiler_params=pltpu.CompilerParams(vmem_limit_bytes=48 * 1024 * 1024),
        cost_estimate=pl.CostEstimate(
            flops=20 * length * length * depth * heads // 2 * 2,
            bytes_accessed=20 * 1024 * 1024,
            transcendentals=2 * heads * length * length // 2,
        ),
    )(core, *projected, *upstream, *common, query_gain, key_gain, *saved)
    return made[:parts], made[parts]


def neighbours():
    spot = lax.axis_index("tx")
    core = lax.rem(spot, 2)
    return (
        {"ty": 1 - lax.axis_index("ty")},
        {"tx": lax.rem(spot + 2, 4)},
        {"tx": spot + 1 - 2 * core},
    )


def greet(targets):
    barrier = pltpu.get_barrier_semaphore()
    for target in targets:
        pl.semaphore_signal(barrier, inc=1, device_id=target, device_id_type=MESH)
    pl.semaphore_wait(barrier, len(targets))


class Wires:
    def __init__(self, send_sems, recv_sems):
        self.send_sems = send_sems
        self.recv_sems = recv_sems

    def copy(self, kind, chunk, source, target, device):
        return pltpu.make_async_remote_copy(
            src_ref=source,
            dst_ref=target,
            send_sem=self.send_sems.at[kind, chunk],
            recv_sem=self.recv_sems.at[kind, chunk],
            device_id=device,
            device_id_type=MESH,
        )


CHUNK = 256
SIBLING, CORNER, FINAL_X, FINAL_Y = 0, 1, 2, 3
REDUCE_KINDS = 4
OUT_X, OUT_Y, OUT_CORNER, CORE_OWN, CORE_X, CORE_Y, CORE_CORNER = range(7)
GATHER_KINDS = 7


def lanes(chunk, half, width):
    return pl.ds(pl.multiple_of(half * width + chunk * CHUNK, CHUNK), CHUNK)


class Gather:
    def __init__(self, wires, base, whole, own, local_sem):
        self.wires, self.base, self.whole, self.own, self.local_sem = (
            wires,
            base,
            whole,
            own,
            local_sem,
        )
        self.width = whole.shape[2] // 2
        self.count = self.width // CHUNK

    def place(self, block, chunk, half):
        return self.whole.at[block, :, lanes(chunk, half, self.width)]

    def copy(self, name, chunk):
        side, across, core = neighbours()
        at = self.place
        own = self.own.at[chunk]
        if name == "local":
            return pltpu.make_async_copy(own, at(0, chunk, 0), self.local_sem.at[chunk])
        kind, source, target, device = {
            "x": (OUT_X, own, at(0, chunk, 1), side),
            "y": (OUT_Y, own, at(1, chunk, 0), across),
            "core": (CORE_OWN, own, at(2, chunk, 0), core),
            "even": (OUT_CORNER, at(0, chunk, 1), at(1, chunk, 1), across),
            "odd": (OUT_CORNER, at(1, chunk, 0), at(1, chunk, 1), side),
            "core_x": (CORE_X, at(0, chunk, 1), at(2, chunk, 1), core),
            "core_y": (CORE_Y, at(1, chunk, 0), at(3, chunk, 0), core),
            "core_corner": (CORE_CORNER, at(1, chunk, 1), at(3, chunk, 1), core),
        }[name]
        return self.wires.copy(self.base + kind, chunk, source, target, device)

    def send(self, chunk):
        for name in ("x", "y", "core", "local"):
            self.copy(name, chunk).start()

    def finish(self):
        @pl.loop(0, self.count)
        def _(chunk):
            even = lax.rem(chunk, 2) == 0
            self.copy("x", chunk).wait_recv()

            @pl.when(even)
            def _():
                self.copy("even", chunk).start()

            self.copy("core_x", chunk).start()
            self.copy("y", chunk).wait_recv()

            @pl.when(jnp.logical_not(even))
            def _():
                self.copy("odd", chunk).start()

            self.copy("core_y", chunk).start()

        @pl.loop(0, self.count)
        def _(chunk):
            self.copy("even", chunk).wait_recv()
            self.copy("core_corner", chunk).start()

        @pl.loop(0, self.count)
        def _(chunk):
            for name in ("core", "core_x", "core_y", "core_corner"):
                self.copy(name, chunk).wait_recv()
            for name in ("x", "y", "core", "even", "core_x", "core_y", "core_corner"):
                self.copy(name, chunk).wait_send()
            self.copy("local", chunk).wait()


def reduce_stage(wires, rows_ref, weight_ref, transposed, bufs):
    sibling_send, sibling_recv, kept_ref, send, corner_recv, x_recv, y_recv = bufs
    side, across, core = neighbours()
    rows, depth = rows_ref.shape[1:]
    width = (weight_ref.shape[0] if transposed else weight_ref.shape[1]) // 2
    count = width // CHUNK

    def product(block, chunk, half):
        left = rows_ref[block : block + 2].reshape(2 * rows, depth)
        at = lanes(chunk, half, width)
        if transposed:
            return rows_dot(left, weight_ref[at, :])
        return jnp.dot(left, weight_ref[:, at], preferred_element_type=F32)

    def sibling(chunk):
        return wires.copy(SIBLING, chunk, sibling_send.at[chunk], sibling_recv.at[chunk], core)

    def corner(chunk, device):
        return wires.copy(CORNER, chunk, send.at[2, chunk], corner_recv.at[chunk], device)

    def final_x(chunk):
        return wires.copy(FINAL_X, chunk, send.at[0, chunk], x_recv.at[chunk], side)

    def final_y(chunk):
        return wires.copy(FINAL_Y, chunk, send.at[1, chunk], y_recv.at[chunk], across)

    @pl.loop(0, count)
    def _(chunk):
        @pl.loop(0, 2)
        def _(half):
            sibling_send[chunk, half] = product(2, chunk, half).astype(B16)

        sibling(chunk).start()

    @pl.loop(0, count)
    def _(chunk):
        even = lax.rem(chunk, 2) == 0
        sibling(chunk).wait_recv()

        @pl.loop(0, 2)
        def _(half):
            total = product(0, chunk, half) + sibling_recv[chunk, half].astype(F32)

            @pl.when(half == 1)
            def _():
                send[0, chunk] = total[:rows].astype(B16)
                send[2, chunk] = total[rows:].astype(B16)

            @pl.when(half == 0)
            def _():
                kept_ref[chunk] = total[:rows]
                send[1, chunk] = total[rows:].astype(B16)

        @pl.when(even)
        def _():
            corner(chunk, side).start()
            final_x(chunk).start()

        @pl.when(jnp.logical_not(even))
        def _():
            corner(chunk, across).start()
            final_y(chunk).start()

    @pl.loop(0, count)
    def _(chunk):
        even = lax.rem(chunk, 2) == 0
        corner(chunk, side).wait_recv()

        @pl.when(even)
        def _():
            send[1, chunk] = (send[1, chunk].astype(F32) + corner_recv[chunk].astype(F32)).astype(
                B16
            )
            final_y(chunk).start()

        @pl.when(jnp.logical_not(even))
        def _():
            send[0, chunk] = (send[0, chunk].astype(F32) + corner_recv[chunk].astype(F32)).astype(
                B16
            )
            final_x(chunk).start()

    def total(chunk):
        final_x(chunk).wait_recv()
        final_y(chunk).wait_recv()
        return kept_ref[chunk] + x_recv[chunk].astype(F32) + y_recv[chunk].astype(F32)

    def finish():
        @pl.loop(0, count)
        def _(chunk):
            sibling(chunk).wait_send()
            corner(chunk, side).wait_send()
            final_x(chunk).wait_send()
            final_y(chunk).wait_send()

    return total, finish


def reduce_scratch(rows, width):
    count = width // CHUNK
    return [
        pltpu.VMEM((count, 2, 2 * rows, CHUNK), B16),
        pltpu.VMEM((count, 2, 2 * rows, CHUNK), B16),
        pltpu.VMEM((count, rows, CHUNK), F32),
        pltpu.VMEM((3, count, rows, CHUNK), B16),
        pltpu.VMEM((count, rows, CHUNK), B16),
        pltpu.VMEM((count, rows, CHUNK), B16),
        pltpu.VMEM((count, rows, CHUNK), B16),
    ]


def wire_scratch(kinds, count):
    return [pltpu.SemaphoreType.DMA((kinds, count))] * 2


IN_VMEM = pl.BlockSpec(memory_space=pltpu.VMEM)
IN_ANY = pl.BlockSpec(memory_space=pl.ANY)
VMEM_MOST = 58 * 1024 * 1024


def remote_params(number):
    return pltpu.CompilerParams(
        collective_id=number, has_side_effects=True, vmem_limit_bytes=VMEM_MOST
    )


def gather_kernel(block_ref, whole_ref, own, send_sems, recv_sems, local_sem):
    count = own.shape[0]
    for chunk in range(count):
        own[chunk] = block_ref[:, chunk * CHUNK : (chunk + 1) * CHUNK]
    greet(neighbours())
    gather = Gather(Wires(send_sems, recv_sems), 0, whole_ref, own, local_sem)

    @pl.loop(0, count)
    def _(chunk):
        gather.send(chunk)

    gather.finish()


def gather_call(block, number):
    rows, width = block.shape
    count = width // CHUNK
    return pl.pallas_call(
        gather_kernel,
        out_shape=jax.ShapeDtypeStruct((4, rows, 2 * width), B16),
        in_specs=[IN_VMEM],
        out_specs=IN_ANY,
        scratch_shapes=[pltpu.VMEM((count, rows, CHUNK), B16)]
        + wire_scratch(GATHER_KINDS, count)
        + [pltpu.SemaphoreType.DMA((count,))],
        compiler_params=remote_params(number),
        cost_estimate=pl.CostEstimate(
            flops=0, bytes_accessed=16 * rows * width * 2, transcendentals=0
        ),
    )(block)


def branch_kernel(
    rows_ref, weight_ref, input_ref, residual_ref, whole_ref, *scratch
):
    bufs = scratch[:7]
    own, send_sems, recv_sems, local_sem = scratch[7:]
    width = input_ref.shape[1]
    greet(neighbours())
    wires = Wires(send_sems, recv_sems)
    total, finish = reduce_stage(wires, rows_ref, weight_ref, False, bufs)
    gather = Gather(wires, REDUCE_KINDS, whole_ref, own, local_sem)

    @pl.loop(0, width // CHUNK)
    def _(chunk):
        at = lanes(chunk, 0, width)
        residual = input_ref[:, at].astype(F32) + total(chunk)
        residual_ref[:, at] = residual
        own[chunk] = residual.astype(B16)
        gather.send(chunk)

    gather.finish()
    finish()


def branch_call(rows, weight, inputs, number):
    count = inputs.shape[1] // CHUNK
    height, width = inputs.shape
    return pl.pallas_call(
        branch_kernel,
        out_shape=(
            jax.ShapeDtypeStruct((height, width), F32),
            jax.ShapeDtypeStruct((4, height, 2 * width), B16),
        ),
        in_specs=[IN_VMEM] * 3,
        out_specs=(IN_VMEM, IN_ANY),
        scratch_shapes=reduce_scratch(height, width)
        + [pltpu.VMEM((count, height, CHUNK), B16)]
        + wire_scratch(REDUCE_KINDS + GATHER_KINDS, count)
        + [pltpu.SemaphoreType.DMA((count,))],
        compiler_params=remote_params(number),
        cost_estimate=pl.CostEstimate(
            flops=2 * 4 * height * rows.shape[2] * 2 * width,
            bytes_accessed=32 * height * width * 2,
            transcendentals=0,
        ),
    )(rows, weight, inputs)


def share_stats(wires, base, stats_ref, recv):
    side, across, core = neighbours()
    first = wires.copy(base, 0, stats_ref.at[2:4], recv.at[0:2], core)
    first.start()
    first.wait()
    stats_ref[0:2] = stats_ref[0:2] + recv[0:2]
    second = wires.copy(base, 1, stats_ref.at[1:2], recv.at[2:3], across)
    second.start()
    second.wait()
    stats_ref[0:1] = stats_ref[0:1] + recv[2:3]
    third = wires.copy(base, 2, stats_ref.at[0:1], recv.at[3:4], side)
    third.start()
    third.wait()
    stats_ref[0:1] = stats_ref[0:1] + recv[3:4]


def stand(row):
    return jnp.transpose(jnp.broadcast_to(row, (row.shape[1], row.shape[1])))


def pull_kernel(
    gathers,
    rows_ref,
    weight_ref,
    stats_in_ref,
    scale_ref,
    value_ref,
    gain_ref,
    base_ref,
    *refs,
):
    if gathers:
        result_ref, gain_grad_ref, whole_ref = refs[:3]
        scratch = refs[3:]
    else:
        result_ref, gain_grad_ref = refs[:2]
        scratch = refs[2:]
    bufs = scratch[:7]
    stats_ref, stats_recv, column_ref, send_sems, recv_sems = scratch[7:12]
    rows, width = value_ref.shape
    stats_ref[...] = stats_in_ref[...]
    greet(neighbours())
    wires = Wires(send_sems, recv_sems)
    total, finish = reduce_stage(wires, rows_ref, weight_ref, True, bufs)
    share_stats(wires, REDUCE_KINDS, stats_ref, stats_recv)
    for part in range(rows // 128):
        at = slice(part * 128, (part + 1) * 128)
        scale = stand(scale_ref[part : part + 1, :])
        column_ref[0, at, :] = scale
        column_ref[1, at, :] = (
            stand(stats_ref[0, part : part + 1, :]) * scale * scale / (2 * width)
        )
    if gathers:
        own, local_sem = scratch[12:]
        gather = Gather(wires, REDUCE_KINDS + 1, whole_ref, own, local_sem)

    @pl.loop(0, width // CHUNK)
    def _(chunk):
        at = lanes(chunk, 0, width)
        upstream = total(chunk)
        value = value_ref[:, at].astype(F32)
        scale = column_ref[0, :, 0:1]
        pulled = base_ref[:, at].astype(F32) + (
            scale * gain_ref[:, at] * upstream - value * column_ref[1, :, 0:1]
        )
        gain_grad_ref[:, at] = jnp.sum(upstream * value * scale, axis=0, keepdims=True)
        result_ref[:, at] = pulled.astype(result_ref.dtype)
        if gathers:
            own[chunk] = pulled.astype(B16)
            gather.send(chunk)

    if gathers:
        gather.finish()
    finish()


def pull_call(rows, weight, stats, scale, value, gain, base, gathers, kind, number):
    height, width = value.shape
    count = width // CHUNK
    outs = [
        jax.ShapeDtypeStruct((height, width), kind),
        jax.ShapeDtypeStruct((1, width), F32),
    ]
    scratch = reduce_scratch(height, width) + [
        pltpu.VMEM((4, 8, 128), F32),
        pltpu.VMEM((4, 8, 128), F32),
        pltpu.VMEM((2, height, 128), F32),
    ]
    specs = [IN_VMEM] * 2
    if gathers:
        outs.append(jax.ShapeDtypeStruct((4, height, 2 * width), B16))
        specs.append(IN_ANY)
        scratch += wire_scratch(REDUCE_KINDS + 1 + GATHER_KINDS, count)
        scratch += [
            pltpu.VMEM((count, height, CHUNK), B16),
            pltpu.SemaphoreType.DMA((count,)),
        ]
    else:
        scratch += wire_scratch(REDUCE_KINDS + 1, count)
    return pl.pallas_call(
        lambda *refs: pull_kernel(gathers, *refs),
        out_shape=tuple(outs),
        in_specs=[IN_VMEM] * 7,
        out_specs=tuple(specs),
        scratch_shapes=scratch,
        compiler_params=remote_params(number),
        cost_estimate=pl.CostEstimate(
            flops=2 * 4 * height * rows.shape[2] * 2 * width,
            bytes_accessed=32 * height * width * 2,
            transcendentals=0,
        ),
    )(rows, weight, stats, scale, value, gain, base)


def sum_kernel(rows_ref, weight_ref, base_ref, result_ref, *scratch):
    bufs = scratch[:7]
    width = base_ref.shape[1]
    greet(neighbours())
    total, finish = reduce_stage(Wires(*scratch[7:]), rows_ref, weight_ref, False, bufs)

    @pl.loop(0, width // CHUNK)
    def _(chunk):
        at = lanes(chunk, 0, width)
        result_ref[:, at] = (base_ref[:, at] + total(chunk)).astype(B16)

    finish()


def sum_call(rows, weight, base, number):
    height, width = base.shape
    count = width // CHUNK
    return pl.pallas_call(
        sum_kernel,
        out_shape=jax.ShapeDtypeStruct((height, width), B16),
        in_specs=[IN_VMEM] * 3,
        out_specs=IN_VMEM,
        scratch_shapes=reduce_scratch(height, width) + wire_scratch(REDUCE_KINDS, count),
        compiler_params=remote_params(number),
        cost_estimate=pl.CostEstimate(
            flops=2 * 4 * height * rows.shape[2] * 2 * width,
            bytes_accessed=16 * height * width * 2,
            transcendentals=0,
        ),
    )(rows, weight, base)


def whole_norm(whole, gain):
    value = whole.reshape(-1, whole.shape[2]).astype(F32)
    scale = lax.rsqrt(jnp.mean(value * value, axis=1) + EPS)
    return (value * scale[:, None] * gain).astype(B16), scale


def as_rows(value):
    return value.reshape(-1, 128)


def as_stats(value):
    return jnp.pad(value.reshape(4, -1, 128), ((0, 0), (0, 8 - value.shape[0] // 512), (0, 0)))


def row_shares(grad):
    size = grad.shape[0] // (2 * lax.axis_size("dp"))
    parts = grad.reshape(2, -1, grad.shape[1])
    return lambda place: lax.dynamic_slice_in_dim(parts, place * size, size, 1)


def column_shares(grad):
    width = grad.shape[1] // 2
    size = width // lax.axis_size("dp")
    return lambda place: jnp.stack(
        [
            lax.dynamic_slice_in_dim(grad, place * size, size, 1),
            lax.dynamic_slice_in_dim(grad, width + place * size, size, 1),
        ]
    )


def meet(shares, axis):
    return in_order(shares[0], swap_x(shares[1].astype(B16)).astype(F32), axis)


def plane_device(
    tokens,
    seg_ids,
    w_query,
    w_key,
    w_value,
    w_out,
    w_gate,
    w_up,
    w_down,
    attn_gain,
    mlp_gain,
    query_gain,
    key_gain,
    cotangent,
):
    place = lax.axis_index("ty")
    spot = lax.axis_index("tx")
    core = lax.rem(spot, 2)
    depth = query_gain.shape[0]
    length = seg_ids.shape[1]
    most = length // 2
    rows, width = tokens.shape
    head_width = w_query.shape[1] // 2
    kv_width = w_key.shape[1] // 2
    units = w_gate.shape[1] // 2

    def columns(weights, which):
        return jnp.concatenate([half_of(item, which, 1) for item in weights], axis=1)

    def full(mine, theirs, axis):
        return jnp.concatenate([mine, swap_x(theirs)], axis=axis)

    w_project = full(
        columns([w_query, w_key, w_value], place),
        columns([w_query, w_key, w_value], 1 - place),
        0,
    )
    gains = jnp.stack([attn_gain, mlp_gain])
    gains = jnp.concatenate([gains, swap_x(gains)], axis=1)
    seg_theirs = swap_x(seg_ids)
    token_whole = gather_call(tokens, 0)
    w_branch = full(half_of(w_out, place, 0), half_of(w_out, 1 - place, 0), 1)
    w_both = full(columns([w_gate, w_up], place), columns([w_gate, w_up], 1 - place), 0)
    w_back = full(half_of(w_down, place, 0), half_of(w_down, 1 - place, 0), 1)
    grad_whole = gather_call(cotangent, 1).reshape(4 * rows, 2 * width)

    seg_all = in_order(seg_ids, seg_theirs, 0)
    seg_all = jnp.where(lax.div(spot, 2) == 0, seg_all, seg_all[::-1])
    index = jnp.arange(length, dtype=jnp.int32)[None]
    edge = jnp.concatenate(
        [jnp.ones((2, 1), dtype=jnp.bool_), seg_all[:, 1:] != seg_all[:, :-1]], axis=1
    )
    starts = lax.cummax(jnp.where(edge, index, 0), axis=1)
    cosine, sine = rotary(index - starts, depth)
    cosine = jnp.concatenate([cosine, cosine], axis=-1)
    sine = jnp.concatenate([-sine, sine], axis=-1)
    starts = starts[:, :, None]
    core_arg = core.reshape(1).astype(jnp.int32)
    fixed_args = (core_arg, starts, cosine, sine, query_gain[None], key_gain[None], most)

    first, first_scale = whole_norm(token_whole, gains[0])
    projected = forward_with(w_project)(first)
    blocks = [projected.reshape(2, 2, rows, -1)]
    mixed, saved = attend(blocks, *fixed_args)
    attended = mixed[0].reshape(4 * rows, head_width)
    residual, residual_whole = branch_call(
        attended.reshape(4, rows, head_width), w_branch, tokens, 2
    )
    second, second_scale = whole_norm(residual_whole, gains[1])
    gate_up = forward_with(w_both)(second)
    gate = gate_up[:, :units]
    upper = gate_up[:, units:]
    sigma = jax.nn.sigmoid(gate)
    hidden = (gate * sigma * upper).astype(B16)
    hidden_grad = backward_with(w_back)(grad_whole)
    gate_grad = hidden_grad * upper * (sigma * (1.0 + gate * (1.0 - sigma)))
    up_grad = hidden_grad * (gate * sigma)
    unit_grads = jnp.concatenate([gate_grad, up_grad], axis=1).astype(B16)
    unit_stats = jnp.sum(unit_grads.astype(F32) * gate_up, axis=1)
    down_sums = line_reduce(column_shares(weight_grad(hidden, grad_whole).astype(B16)))
    residual_grad, mlp_gain_part, branch_whole = pull_call(
        unit_grads.reshape(4, rows, 2 * units),
        w_both,
        as_stats(unit_stats),
        as_rows(second_scale[:rows]),
        residual,
        mlp_gain[None],
        cotangent,
        True,
        F32,
        3,
    )
    both_sums = line_reduce(row_shares(weight_grad(second, unit_grads).astype(B16)))
    branch_whole = branch_whole.reshape(4 * rows, 2 * width)
    upstream = [
        backward_with(w_branch)(branch_whole).astype(B16).reshape(2, 2, rows, head_width)
    ]
    out_sums = line_reduce(column_shares(weight_grad(attended, branch_whole).astype(B16)))
    output = sum_call(hidden.reshape(4, rows, units), w_back, residual, 4)
    proj_grads, gain_parts = attend_back(blocks, upstream, saved, *fixed_args)
    proj_grads = proj_grads[0].reshape(4 * rows, -1)
    proj_stats = jnp.sum(proj_grads.astype(F32) * projected, axis=1)
    input_grad, attn_gain_part = pull_call(
        proj_grads.reshape(4, rows, -1),
        w_project,
        as_stats(proj_stats),
        as_rows(first_scale[:rows]),
        tokens,
        attn_gain[None],
        residual_grad,
        False,
        B16,
        5,
    )
    project_sums = line_reduce(row_shares(weight_grad(first, proj_grads).astype(B16)))

    down_share = meet(down_sums, 0)
    out_share = meet(out_sums, 0)
    both_theirs = swap_x(both_sums[1].astype(B16)).astype(F32)
    project_theirs = swap_x(project_sums[1].astype(B16)).astype(F32)
    ends = (0, head_width, head_width + kv_width, head_width + 2 * kv_width)
    query_share, key_share, value_share = (
        in_order(project_sums[0][:, low:high], project_theirs[:, low:high], 1)
        for low, high in zip(ends[:-1], ends[1:])
    )
    gate_share, up_share = (
        in_order(both_sums[0][:, low:high], both_theirs[:, low:high], 1)
        for low, high in ((0, units), (units, 2 * units))
    )
    gain_sums = jnp.sum(gain_parts, axis=0)
    attn_total, mlp_total, query_total, key_total = lax.psum(
        (widen(attn_gain_part[0]), widen(mlp_gain_part[0]), gain_sums[0], gain_sums[1]),
        ("dp", "tx", "ty"),
    )
    return (
        output,
        input_grad,
        query_share,
        key_share,
        value_share,
        out_share,
        gate_share,
        up_share,
        down_share,
        attn_total,
        mlp_total,
        query_total,
        key_total,
    )


def solution(mesh):
    placed = (
        P(("dp", "tx"), "ty"),
        P(("dp", "ty"), None),
        P("ty", "tx"),
        P("ty", "tx"),
        P("ty", "tx"),
        P("tx", "ty"),
        P("ty", "tx"),
        P("ty", "tx"),
        P("tx", "ty"),
        P("ty"),
        P("ty"),
        P(),
        P(),
        P(("dp", "tx"), "ty"),
    )
    return jax.shard_map(
        plane_device if fits(mesh) else general_device,
        mesh=mesh,
        in_specs=placed,
        out_specs=(
            P(("dp", "tx"), "ty"),
            P(("dp", "tx"), "ty"),
            P(("ty", "dp"), "tx"),
            P(("ty", "dp"), "tx"),
            P(("ty", "dp"), "tx"),
            P("tx", ("ty", "dp")),
            P(("ty", "dp"), "tx"),
            P(("ty", "dp"), "tx"),
            P("tx", ("ty", "dp")),
            P(),
            P(),
            P(),
            P(),
        ),
        check_vma=False,
    )
```

```python
import jax
import jax.numpy as jnp
from jax import lax
from jax.experimental import pallas as pl
from jax.experimental.pallas import tpu as pltpu
from jax.sharding import PartitionSpec as P

EPS = 1e-06
THETA = 1000000.0
NEG = -1e30
F32 = jnp.float32
B16 = jnp.bfloat16
MESH = pl.DeviceIdType.MESH


def width_sum(value):
    return lax.psum(value, "ty")


def token_gather(rows):
    return lax.all_gather(rows, "tx", axis=0, tiled=True)


def branch_gather(rows):
    return lax.all_gather(rows, "ty", axis=0, tiled=True)


def width_reduce(whole, apply):
    return lax.psum_scatter(apply(whole), "ty", scatter_dimension=0, tiled=True)


def head_reduce(whole, apply):
    return lax.psum_scatter(
        apply(whole).astype(jnp.bfloat16), "tx", scatter_dimension=0, tiled=True
    ).astype(jnp.float32)


def forward_with(weight):
    return lambda rows: jnp.dot(rows, weight, preferred_element_type=F32)


def backward_with(weight):
    return lambda rows: lax.dot_general(
        rows, weight, (((1,), (1,)), ((), ())), preferred_element_type=F32
    )


def weight_grad(left, right):
    return lax.dot_general(left, right, (((0,), (0,)), ((), ())), preferred_element_type=F32)


def norm_scale(rows):
    width = rows.shape[1] * lax.axis_size("ty")
    return lax.rsqrt(width_sum(jnp.sum(rows * rows, axis=1)) / width + EPS)


def norm_back(rows, scale, gain, upstream):
    width = rows.shape[1] * lax.axis_size("ty")
    inner = width_sum(jnp.sum(upstream * gain * rows, axis=1))
    back = scale[:, None] * gain * upstream - rows * (scale**3 * inner / width)[:, None]
    gain_part = jnp.sum(upstream * rows * scale[:, None], axis=0)
    return (back, gain_part)


def widen(part):
    whole = jnp.zeros((part.shape[0] * lax.axis_size("ty"),), F32)
    return lax.dynamic_update_slice_in_dim(whole, part, lax.axis_index("ty") * part.shape[0], 0)


def doc_positions(seg):
    count = seg.shape[-1]
    index = jnp.arange(count, dtype=jnp.int32)
    edge = jnp.concatenate([jnp.ones((1,), dtype=jnp.bool_), seg[1:] != seg[:-1]])
    first = lax.cummax(jnp.where(edge, index, jnp.zeros_like(index)), axis=0)
    return index - first


def rotary(positions, depth):
    half = depth // 2
    freq = THETA ** (-jnp.arange(half, dtype=F32) * 2.0 / depth)
    angle = positions.astype(F32)[..., None] * freq
    return (jnp.cos(angle), jnp.sin(angle))


def turn(value, gain, cosine, sine):
    normed = value * lax.rsqrt(jnp.mean(value * value, axis=-1, keepdims=True) + EPS) * gain
    half = value.shape[-1] // 2
    first = normed[..., :half]
    second = normed[..., half:]
    return jnp.concatenate(
        [first * cosine - second * sine, second * cosine + first * sine], axis=-1
    )


def block_scores(part, seq_keys, seq_ids, start, scale):
    block = part.shape[0]
    length = seq_ids.shape[0]
    index = jnp.arange(length, dtype=jnp.int32)
    rows = start + jnp.arange(block, dtype=jnp.int32)
    row_ids = lax.dynamic_slice_in_dim(seq_ids, start, block, 0)
    mask = (seq_ids[None, :] == row_ids[:, None]) & (index[None, :] <= rows[:, None])
    scores = jnp.einsum("qkgd,mkd->kgqm", part, seq_keys, preferred_element_type=F32) * scale
    return jnp.where(mask[None, None], scores, NEG)


def attend_forward(query, keys, values, seg, block):
    seqs, length, heads, depth = query.shape
    kv_heads = keys.shape[2]
    groups = heads // kv_heads
    scale = depth ** (-0.5)
    count = length // block
    starts = jnp.arange(count, dtype=jnp.int32) * block

    def one_sequence(operands):
        seq_query, seq_keys, seq_values, seq_ids = operands
        blocks = seq_query.reshape(count, block, kv_heads, groups, depth)

        def one_block(inputs):
            part, start = inputs
            scores = block_scores(part, seq_keys, seq_ids, start, scale)
            top = jnp.max(scores, axis=-1)
            weights = jnp.exp(scores - top[..., None])
            total = jnp.sum(weights, axis=-1)
            probs = (weights / total[..., None]).astype(B16)
            mixed = jnp.einsum("kgqm,mkd->qkgd", probs, seq_values, preferred_element_type=F32)
            return (mixed, top + jnp.log(total))

        mixed, logs = lax.map(one_block, (blocks, starts))
        return (mixed.reshape(length, heads * depth), logs)

    return lax.map(one_sequence, (query, keys, values, seg))


def attend_backward(query, keys, values, seg, logs, grad_out, block):
    seqs, length, heads, depth = query.shape
    kv_heads = keys.shape[2]
    groups = heads // kv_heads
    scale = depth ** (-0.5)
    count = length // block
    starts = jnp.arange(count, dtype=jnp.int32) * block

    def one_sequence(operands):
        seq_query, seq_keys, seq_values, seq_ids, seq_logs, seq_grad = operands
        blocks = seq_query.reshape(count, block, kv_heads, groups, depth)
        grads = seq_grad.reshape(count, block, kv_heads, groups, depth)

        def one_block(carry, inputs):
            key_acc, value_acc = carry
            part, grad_part, log_part, start = inputs
            scores = block_scores(part, seq_keys, seq_ids, start, scale)
            probs = jnp.exp(scores - log_part[..., None])
            value_acc = value_acc + jnp.einsum(
                "kgqm,qkgd->mkd", probs.astype(B16), grad_part, preferred_element_type=F32
            )
            prob_grad = jnp.einsum(
                "qkgd,mkd->kgqm", grad_part, seq_values, preferred_element_type=F32
            )
            delta = jnp.sum(probs * prob_grad, axis=-1, keepdims=True)
            score_grad = (probs * (prob_grad - delta)).astype(B16)
            query_grad = (
                jnp.einsum("kgqm,mkd->qkgd", score_grad, seq_keys, preferred_element_type=F32)
                * scale
            )
            key_acc = (
                key_acc
                + jnp.einsum("kgqm,qkgd->mkd", score_grad, part, preferred_element_type=F32) * scale
            )
            return ((key_acc, value_acc), query_grad)

        zeros = jnp.zeros((length, kv_heads, depth), F32)
        (key_grad, value_grad), query_grad = lax.scan(
            one_block, (zeros, zeros), (blocks, grads, seq_logs, starts)
        )
        return (query_grad.reshape(length, heads, depth), key_grad, value_grad)

    return lax.map(one_sequence, (query, keys, values, seg, logs, grad_out))


def general_device(
    tokens,
    seg_ids,
    w_query,
    w_key,
    w_value,
    w_out,
    w_gate,
    w_up,
    w_down,
    attn_gain,
    mlp_gain,
    query_gain,
    key_gain,
    cotangent,
):
    seqs, length = seg_ids.shape
    depth = query_gain.shape[0]
    query_width = w_query.shape[1]
    key_width = w_key.shape[1]
    units = w_gate.shape[1]
    block = min(512, length)
    inputs = tokens.astype(F32)
    first_scale = norm_scale(inputs)
    first_normed = (inputs * first_scale[:, None] * attn_gain).astype(B16)
    first_whole = token_gather(first_normed)
    w_project = jnp.concatenate([w_query, w_key, w_value], axis=1)
    projected = width_reduce(first_whole, forward_with(w_project))
    query_proj = projected[:, :query_width].reshape(seqs, length, -1, depth)
    key_proj = projected[:, query_width : query_width + key_width].reshape(seqs, length, -1, depth)
    values = projected[:, query_width + key_width :].astype(B16).reshape(seqs, length, -1, depth)
    positions = jax.vmap(doc_positions)(seg_ids)
    cosine, sine = rotary(positions, depth)
    cosine = cosine[:, :, None, :]
    sine = sine[:, :, None, :]
    query = turn(query_proj, query_gain, cosine, sine).astype(B16)
    keys = turn(key_proj, key_gain, cosine, sine).astype(B16)
    mixed, logs = attend_forward(query, keys, values, seg_ids, block)
    attended = mixed.reshape(seqs * length, -1).astype(B16)
    attended_whole = branch_gather(attended)
    residual = inputs + head_reduce(attended_whole, forward_with(w_out))
    second_scale = norm_scale(residual)
    second_normed = (residual * second_scale[:, None] * mlp_gain).astype(B16)
    second_whole = token_gather(second_normed)
    w_both = jnp.concatenate([w_gate, w_up], axis=1)
    gate_up = width_reduce(second_whole, forward_with(w_both))
    gate = gate_up[:, :units]
    upper = gate_up[:, units:]
    hidden = (jax.nn.silu(gate) * upper).astype(B16)
    hidden_whole = branch_gather(hidden)
    output = residual + head_reduce(hidden_whole, forward_with(w_down))
    grad_whole = token_gather(cotangent)
    hidden_grad = width_reduce(grad_whole, backward_with(w_down))
    down_grad = weight_grad(hidden_whole, grad_whole)
    gate_grad, up_grad = jax.vjp(lambda left, right: jax.nn.silu(left) * right, gate, upper)[1](
        hidden_grad
    )
    unit_grads = jnp.concatenate([gate_grad, up_grad], axis=1).astype(B16)
    unit_whole = branch_gather(unit_grads)
    second_grad = head_reduce(unit_whole, backward_with(w_both))
    both_grad = weight_grad(second_whole, unit_whole)
    gate_weight = both_grad[:, :units]
    up_weight = both_grad[:, units:]
    resid_norm_grad, mlp_gain_part = norm_back(residual, second_scale, mlp_gain, second_grad)
    residual_grad = cotangent.astype(F32) + resid_norm_grad
    residual_whole = token_gather(residual_grad.astype(B16))
    mixed_grad = width_reduce(residual_whole, backward_with(w_out)).astype(B16)
    out_grad = weight_grad(attended_whole, residual_whole)
    query_grad, key_grad, value_grad = attend_backward(
        query, keys, values, seg_ids, logs, mixed_grad.reshape(seqs, length, -1), block
    )
    query_proj_grad, query_gain_grad = jax.vjp(
        lambda value, gain: turn(value, gain, cosine, sine), query_proj, query_gain
    )[1](query_grad)
    key_proj_grad, key_gain_grad = jax.vjp(
        lambda value, gain: turn(value, gain, cosine, sine), key_proj, key_gain
    )[1](key_grad)
    rows = seqs * length
    proj_grad = jnp.concatenate(
        [
            query_proj_grad.reshape(rows, -1),
            key_proj_grad.reshape(rows, -1),
            value_grad.reshape(rows, -1),
        ],
        axis=1,
    ).astype(B16)
    proj_whole = branch_gather(proj_grad)
    first_grad = head_reduce(proj_whole, backward_with(w_project))
    project_grad = weight_grad(first_whole, proj_whole)
    query_weight = project_grad[:, :query_width]
    key_weight = project_grad[:, query_width : query_width + key_width]
    value_weight = project_grad[:, query_width + key_width :]
    input_norm_grad, attn_gain_part = norm_back(inputs, first_scale, attn_gain, first_grad)
    input_grad = (residual_grad + input_norm_grad).astype(B16)
    attn_total, mlp_total, query_total, key_total = lax.psum(
        (widen(attn_gain_part), widen(mlp_gain_part), query_gain_grad, key_gain_grad),
        ("dp", "tx", "ty"),
    )
    query_share, key_share, value_share, gate_share, up_share = (
        lax.psum_scatter(
            query_weight.astype(jnp.bfloat16), "dp", scatter_dimension=0, tiled=True
        ).astype(jnp.float32),
        lax.psum_scatter(
            key_weight.astype(jnp.bfloat16), "dp", scatter_dimension=0, tiled=True
        ).astype(jnp.float32),
        lax.psum_scatter(
            value_weight.astype(jnp.bfloat16), "dp", scatter_dimension=0, tiled=True
        ).astype(jnp.float32),
        lax.psum_scatter(
            gate_weight.astype(jnp.bfloat16), "dp", scatter_dimension=0, tiled=True
        ).astype(jnp.float32),
        lax.psum_scatter(
            up_weight.astype(jnp.bfloat16), "dp", scatter_dimension=0, tiled=True
        ).astype(jnp.float32),
    )
    out_share, down_share = (
        lax.psum_scatter(
            out_grad.astype(jnp.bfloat16), "dp", scatter_dimension=1, tiled=True
        ).astype(jnp.float32),
        lax.psum_scatter(
            down_grad.astype(jnp.bfloat16), "dp", scatter_dimension=1, tiled=True
        ).astype(jnp.float32),
    )
    return (
        output.astype(B16),
        input_grad,
        query_share,
        key_share,
        value_share,
        out_share,
        gate_share,
        up_share,
        down_share,
        attn_total,
        mlp_total,
        query_total,
        key_total,
    )


def fits(mesh):
    return mesh.shape["tx"] == 4 and mesh.shape["ty"] == 2 and mesh.shape["dp"] == 4


def swap_x(value):
    return lax.ppermute(value, "ty", [(0, 1), (1, 0)])


def in_order(mine, theirs, axis):
    first = lax.axis_index("ty") == 0
    return jnp.concatenate(
        [jnp.where(first, mine, theirs), jnp.where(first, theirs, mine)], axis=axis
    )


def spin(value, cosine, sine):
    return value * cosine + pltpu.roll(value, value.shape[1] // 2, 1) * sine


def spin_back(value, cosine, sine):
    return value * cosine + pltpu.roll(value * sine, value.shape[1] // 2, 1)


def head_scale(value):
    return lax.rsqrt(jnp.mean(value * value, axis=1, keepdims=True) + EPS)


def window(first, block, most):
    return max(0, first - most), first + block


def kept(first, block, low, high, starts):
    shape = (block, high - low)
    column = low + lax.broadcasted_iota(jnp.int32, shape, 1)
    row = first + lax.broadcasted_iota(jnp.int32, shape, 0)
    return (column >= starts) & (column <= row)


def rows_dot(left, right):
    return lax.dot_general(left, right, (((1,), (1,)), ((), ())), preferred_element_type=F32)


def stand(row):
    return jnp.transpose(jnp.broadcast_to(row, (row.shape[1], row.shape[1])))


def lie(column):
    return jnp.transpose(jnp.broadcast_to(column, (column.shape[0], column.shape[0])))[0:1]


def put_stats(stats_ref, tile, column):
    stats_ref[tile, 0:1, :] = lie(column[:128])
    stats_ref[tile, 1:2, :] = lie(column[128:])


BLOCK = 256


def attend_sequence(core, seq, most, projected, fixed_refs, mixed, saved_refs):
    starts_ref, cosine_ref, sine_ref, query_gain_ref, key_gain_ref = fixed_refs
    query_ref, key_ref, value_ref, log_ref = saved_refs
    rows = projected.shape[1]
    length = query_ref.shape[1]
    depth = key_ref.shape[2]
    heads = query_ref.shape[2] // depth
    scale = depth ** (-0.5)
    for half in range(2):
        place = 2 * lax.rem(core + half, 2) + seq
        for at in range(half * rows, (half + 1) * rows, BLOCK):
            inner = at - half * rows
            cosine = cosine_ref[seq, at : at + BLOCK, :]
            sine = sine_ref[seq, at : at + BLOCK, :]
            for head in range(heads + 2):
                lane = slice(head * depth, (head + 1) * depth)
                value = projected[place, inner : inner + BLOCK, lane]
                if head < heads:
                    normed = value * head_scale(value) * query_gain_ref[...]
                    query_ref[seq, at : at + BLOCK, lane] = spin(normed, cosine, sine).astype(B16)
                elif head == heads:
                    normed = value * head_scale(value) * key_gain_ref[...]
                    key_ref[seq, at : at + BLOCK, :] = spin(normed, cosine, sine).astype(B16)
                else:
                    value_ref[seq, at : at + BLOCK, :] = value.astype(B16)
    for first in range(0, length, BLOCK):
        low, high = window(first, BLOCK, most)
        mask = kept(first, BLOCK, low, high, starts_ref[seq, first : first + BLOCK, :])
        half, inner = divmod(first, rows)
        place = 2 * lax.rem(core + half, 2) + seq
        for head in range(heads):
            lane = slice(head * depth, (head + 1) * depth)
            query = query_ref[seq, first : first + BLOCK, lane]
            scores = rows_dot(query, key_ref[seq, low:high, :]) * scale
            scores = jnp.where(mask, scores, NEG)
            top = jnp.max(scores, axis=1, keepdims=True)
            weights = jnp.exp(scores - top)
            total = jnp.sum(weights, axis=1, keepdims=True)
            probs = (weights * (1.0 / total)).astype(B16)
            out = jnp.dot(probs, value_ref[seq, low:high, :], preferred_element_type=F32)
            mixed[place, inner : inner + BLOCK, lane] = out.astype(B16)
            log_ref[seq, head, first : first + BLOCK, :] = top + jnp.log(total)


def attend_sequence_back(
    core, seq, most, projected, upstream, fixed_refs, saved_refs, result, stats, gains, accs
):
    starts_ref, cosine_ref, sine_ref, query_gain_ref, key_gain_ref = fixed_refs
    query_ref, key_ref, value_ref, log_ref = saved_refs
    query_acc, key_acc, value_acc = accs
    rows = projected.shape[1]
    length = query_ref.shape[1]
    depth = key_ref.shape[2]
    heads = query_ref.shape[2] // depth
    scale = depth ** (-0.5)
    key_acc[...] = jnp.zeros_like(key_acc)
    value_acc[...] = jnp.zeros_like(value_acc)
    for first in range(0, length, BLOCK):
        low, high = window(first, BLOCK, most)
        mask = kept(first, BLOCK, low, high, starts_ref[seq, first : first + BLOCK, :])
        half, inner = divmod(first, rows)
        place = 2 * lax.rem(core + half, 2) + seq
        keys = key_ref[seq, low:high, :]
        values = value_ref[seq, low:high, :]
        for head in range(heads):
            lane = slice(head * depth, (head + 1) * depth)
            query = query_ref[seq, first : first + BLOCK, lane]
            grad = upstream[place, inner : inner + BLOCK, lane]
            scores = rows_dot(query, keys) * scale - log_ref[seq, head, first : first + BLOCK, :]
            probs = jnp.exp(jnp.where(mask, scores, NEG))
            prob_grad = rows_dot(grad, values)
            delta = jnp.sum(probs * prob_grad, axis=1, keepdims=True)
            score_grad = (probs * (prob_grad - delta)).astype(B16)
            query_acc[first : first + BLOCK, lane] = (
                jnp.dot(score_grad, keys, preferred_element_type=F32) * scale
            )
            key_acc[low:high, :] += weight_grad(score_grad, query) * scale
            value_acc[low:high, :] += weight_grad(probs.astype(B16), grad)
    query_total = jnp.zeros((1, depth), F32)
    key_total = jnp.zeros((1, depth), F32)
    for half in range(2):
        block = 2 * lax.rem(core + half, 2) + seq
        for at in range(half * rows, (half + 1) * rows, BLOCK):
            inner = at - half * rows
            cosine = cosine_ref[seq, at : at + BLOCK, :]
            sine = sine_ref[seq, at : at + BLOCK, :]
            total = jnp.zeros((BLOCK, 1), F32)
            for head in range(heads + 2):
                lane = slice(head * depth, (head + 1) * depth)
                value = projected[block, inner : inner + BLOCK, lane]
                if head == heads + 1:
                    back = value_acc[at : at + BLOCK, :].astype(B16)
                else:
                    if head < heads:
                        grad = query_acc[at : at + BLOCK, lane]
                        gain = query_gain_ref[...]
                    else:
                        grad = key_acc[at : at + BLOCK, :]
                        gain = key_gain_ref[...]
                    grad = spin_back(grad, cosine, sine)
                    rate = head_scale(value)
                    scaled = value * rate
                    share = jnp.sum(grad * scaled, axis=0, keepdims=True)
                    if head < heads:
                        query_total += share
                    else:
                        key_total += share
                    middle = jnp.mean(gain * grad * scaled, axis=1, keepdims=True)
                    back = (rate * (gain * grad - scaled * middle)).astype(B16)
                result[block, inner : inner + BLOCK, lane] = back
                total += jnp.sum(back.astype(F32) * value, axis=1, keepdims=True)
            put_stats(stats, 2 * block + inner // BLOCK, total)
    gains[seq, 0:1, :] = query_total
    gains[seq, 1:2, :] = key_total


def neighbours():
    spot = lax.axis_index("tx")
    core = lax.rem(spot, 2)
    return (
        {"ty": 1 - lax.axis_index("ty")},
        {"tx": lax.rem(spot + 2, 4)},
        {"tx": spot + 1 - 2 * core},
    )


def planes():
    plane = lax.axis_index("dp")
    return {"dp": plane + 1 - 2 * lax.rem(plane, 2)}, {"dp": lax.rem(plane + 2, 4)}


def greet(targets):
    barrier = pltpu.get_barrier_semaphore()
    for target in targets:
        pl.semaphore_signal(barrier, inc=1, device_id=target, device_id_type=MESH)
    pl.semaphore_wait(barrier, len(targets))


class Wires:
    def __init__(self, send_sems, recv_sems):
        self.send_sems = send_sems
        self.recv_sems = recv_sems

    def copy(self, kind, chunk, source, target, device):
        return pltpu.make_async_remote_copy(
            src_ref=source,
            dst_ref=target,
            send_sem=self.send_sems.at[kind, chunk],
            recv_sem=self.recv_sems.at[kind, chunk],
            device_id=device,
            device_id_type=MESH,
        )


CHUNK = 256
SIBLING, CORNER, FINAL_X, FINAL_Y = 0, 1, 2, 3
REDUCE_KINDS = 4
OUT_X, OUT_Y, OUT_CORNER, CORE_OWN, CORE_X, CORE_Y, CORE_CORNER = range(7)
GATHER_KINDS = 7
SHARE_X, SHARE_Z = 0, 1
SHARE_KINDS = 2


def lanes(chunk, half, width):
    return pl.ds(pl.multiple_of(half * width + chunk * CHUNK, CHUNK), CHUNK)


class Gather:
    def __init__(self, wires, base, whole, own, local_sem):
        self.wires, self.base, self.whole, self.own, self.local_sem = (
            wires,
            base,
            whole,
            own,
            local_sem,
        )
        self.width = whole.shape[2] // 2
        self.count = self.width // CHUNK

    def place(self, block, chunk, half):
        return self.whole.at[block, :, lanes(chunk, half, self.width)]

    def copy(self, name, chunk):
        side, across, core = neighbours()
        at = self.place
        own = self.own.at[chunk]
        if name == "local":
            return pltpu.make_async_copy(own, at(0, chunk, 0), self.local_sem.at[chunk])
        kind, source, target, device = {
            "x": (OUT_X, own, at(0, chunk, 1), side),
            "y": (OUT_Y, own, at(1, chunk, 0), across),
            "core": (CORE_OWN, own, at(2, chunk, 0), core),
            "even": (OUT_CORNER, at(0, chunk, 1), at(1, chunk, 1), across),
            "odd": (OUT_CORNER, at(1, chunk, 0), at(1, chunk, 1), side),
            "core_x": (CORE_X, at(0, chunk, 1), at(2, chunk, 1), core),
            "core_y": (CORE_Y, at(1, chunk, 0), at(3, chunk, 0), core),
            "core_corner": (CORE_CORNER, at(1, chunk, 1), at(3, chunk, 1), core),
        }[name]
        return self.wires.copy(self.base + kind, chunk, source, target, device)

    def send(self, chunk):
        for name in ("x", "y", "core", "local"):
            self.copy(name, chunk).start()

    def relay(self):
        @pl.loop(0, self.count)
        def _(chunk):
            even = lax.rem(chunk, 2) == 0
            self.copy("x", chunk).wait_recv()

            @pl.when(even)
            def _():
                self.copy("even", chunk).start()

            self.copy("core_x", chunk).start()
            self.copy("y", chunk).wait_recv()

            @pl.when(jnp.logical_not(even))
            def _():
                self.copy("odd", chunk).start()

            self.copy("core_y", chunk).start()

    def close(self):
        @pl.loop(0, self.count)
        def _(chunk):
            self.copy("even", chunk).wait_recv()
            self.copy("core_corner", chunk).start()

        @pl.loop(0, self.count)
        def _(chunk):
            for name in ("core", "core_x", "core_y", "core_corner"):
                self.copy(name, chunk).wait_recv()
            for name in ("x", "y", "core", "even", "core_x", "core_y", "core_corner"):
                self.copy(name, chunk).wait_send()
            self.copy("local", chunk).wait()


class Share:
    def __init__(self, wires, base, sources, whole, by_rows, local_sems):
        self.wires, self.base, self.sources, self.whole, self.by_rows, self.local_sems = (
            wires,
            base,
            sources,
            whole,
            by_rows,
            local_sems,
        )
        self.size = (whole.shape[0] // 2 if by_rows else whole.shape[0]) // 4

    def quarter(self, plane):
        start = plane * self.size
        if self.by_rows:
            rows = pl.ds(pl.multiple_of(self.whole.shape[0] // 2 + start, self.size), self.size)
            return self.whole.at[rows]
        width = self.whole.shape[1] // 2
        return self.whole.at[pl.ds(pl.multiple_of(start, self.size), self.size), width:]

    def cross(self, index):
        side, _, _ = neighbours()
        plane = lax.axis_index("dp")
        other = 1 - lax.axis_index("ty")
        source = self.sources[index]
        if self.by_rows:
            rows = pl.ds(pl.multiple_of(plane * self.size, self.size), self.size)
            columns = source.shape[1] // 2
            part = source.at[rows, pl.ds(pl.multiple_of(other * columns, columns), columns)]
            offset = sum(item.shape[1] // 2 for item in self.sources[:index])
            target = self.quarter(plane).at[:, offset : offset + columns]
        else:
            start = pl.multiple_of(other * (source.shape[0] // 2) + plane * self.size, self.size)
            part = source.at[pl.ds(start, self.size)]
            target = self.quarter(plane)
        return self.wires.copy(self.base + SHARE_X, index, part, target, side)

    def local(self, index):
        mine = lax.axis_index("ty")
        source = self.sources[index]
        if self.by_rows:
            columns = source.shape[1] // 2
            offset = sum(item.shape[1] // 2 for item in self.sources[:index])
            part = source.at[:, pl.ds(pl.multiple_of(mine * columns, columns), columns)]
            target = self.whole.at[: self.whole.shape[0] // 2, offset : offset + columns]
        else:
            half = source.shape[0] // 2
            part = source.at[pl.ds(pl.multiple_of(mine * half, half), half)]
            target = self.whole.at[:, : self.whole.shape[1] // 2]
        return pltpu.make_async_copy(part, target, self.local_sems.at[index])

    def over(self, index):
        near, far = planes()
        plane = lax.axis_index("dp")
        owner = lax.rem(plane + 2, 4) if index == 2 else plane
        place = self.quarter(owner)
        return self.wires.copy(
            self.base + SHARE_Z, index, place, place, far if index == 0 else near
        )

    def start(self):
        for index in range(len(self.sources)):
            self.cross(index).start()
            self.local(index).start()

    def middle(self):
        for index in range(len(self.sources)):
            self.cross(index).wait_recv()
        self.over(0).start()
        self.over(1).start()

    def late(self):
        self.over(0).wait_recv()
        self.over(2).start()

    def close(self):
        self.over(1).wait_recv()
        self.over(2).wait_recv()
        for index in range(3):
            self.over(index).wait_send()
        for index in range(len(self.sources)):
            self.cross(index).wait_send()
            self.local(index).wait()


FOLD_NEAR, FOLD_FAR, FOLD_X = 0, 1, 2
FOLD_KINDS = 3


class Fold:
    def __init__(self, wires, base, tiles, bufs, mine, theirs):
        self.wires, self.base, self.tiles, self.mine, self.theirs = (
            wires,
            base,
            tiles,
            mine,
            theirs,
        )
        self.near_recv, self.far_recv = bufs
        plane = lax.axis_index("dp")
        self.low = lax.rem(plane, 2)
        self.high = lax.div(plane, 2)

    def index(self, half, high, low):
        return half * 4 + 2 * high + low

    def near(self, half, high):
        source = self.tiles.at[self.index(half, high, 1 - self.low)]
        slot = 2 * half + high
        return self.wires.copy(
            self.base + FOLD_NEAR, slot, source, self.near_recv.at[slot], planes()[0]
        )

    def far(self, half):
        source = self.tiles.at[self.index(half, 1 - self.high, self.low)]
        return self.wires.copy(
            self.base + FOLD_FAR, half, source, self.far_recv.at[half], planes()[1]
        )

    def cross(self):
        source = self.tiles.at[self.index(1, self.high, self.low)]
        return self.wires.copy(self.base + FOLD_X, 0, source, self.theirs, neighbours()[0])

    def start(self):
        for half in range(2):
            for high in range(2):
                self.near(half, high).start()

    def add(self, half, high):
        self.near(half, high).wait_recv()
        at = self.index(half, high, self.low)
        came = self.near_recv[2 * half + high].astype(F32)
        self.tiles[at] = (self.tiles[at].astype(F32) + came).astype(B16)

    def middle(self):
        @pl.loop(0, 2)
        def _(turn):
            half = 1 - turn
            self.add(half, 1 - self.high)
            self.far(half).start()

        @pl.loop(0, 2)
        def _(half):
            self.add(half, self.high)

    def late(self):
        at = self.index(1, self.high, self.low)
        self.far(1).wait_recv()
        self.tiles[at] = (self.tiles[at].astype(F32) + self.far_recv[1].astype(F32)).astype(B16)
        self.cross().start()
        self.far(0).wait_recv()
        at = self.index(0, self.high, self.low)
        self.mine[...] = self.tiles[at].astype(F32) + self.far_recv[0].astype(F32)

    def close(self):
        self.cross().wait_recv()
        for half in range(2):
            for high in range(2):
                self.near(half, high).wait_send()
            self.far(half).wait_send()
        self.cross().wait_send()


def fold_scratch(rows, columns):
    return [pltpu.VMEM((4, rows, columns), B16), pltpu.VMEM((2, rows, columns), B16)]


def turn_tile(step):
    low = lax.rem(lax.axis_index("dp"), 2)
    kept_now = lax.div(step, 4)
    low = kept_now * low + (1 - kept_now) * (1 - low)
    return lax.div(lax.rem(step, 4), 2) * 4 + 2 * lax.rem(step, 2) + low


class Reduce:
    def __init__(self, wires, rows_ref, weight_ref, transposed, bufs):
        self.wires, self.rows_ref, self.weight_ref, self.transposed = (
            wires,
            rows_ref,
            weight_ref,
            transposed,
        )
        (
            self.sibling_send,
            self.sibling_recv,
            self.kept_ref,
            self.out,
            self.corner_recv,
            self.x_recv,
            self.y_recv,
        ) = bufs
        self.rows = rows_ref.shape[1]
        self.width = (weight_ref.shape[0] if transposed else weight_ref.shape[1]) // 2
        self.count = self.width // CHUNK

    def product(self, block, chunk, half):
        left = self.rows_ref[block : block + 2].reshape(2 * self.rows, self.rows_ref.shape[2])
        at = lanes(chunk, half, self.width)
        if self.transposed:
            return rows_dot(left, self.weight_ref[at, :])
        return jnp.dot(left, self.weight_ref[:, at], preferred_element_type=F32)

    def sibling(self, chunk):
        return self.wires.copy(
            SIBLING,
            chunk,
            self.sibling_send.at[chunk],
            self.sibling_recv.at[chunk],
            neighbours()[2],
        )

    def corner(self, chunk, device):
        return self.wires.copy(
            CORNER, chunk, self.out.at[2, chunk], self.corner_recv.at[chunk], device
        )

    def final_x(self, chunk):
        return self.wires.copy(
            FINAL_X, chunk, self.out.at[0, chunk], self.x_recv.at[chunk], neighbours()[0]
        )

    def final_y(self, chunk):
        return self.wires.copy(
            FINAL_Y, chunk, self.out.at[1, chunk], self.y_recv.at[chunk], neighbours()[1]
        )

    def start(self):
        @pl.loop(0, self.count)
        def _(chunk):
            @pl.loop(0, 2)
            def _(half):
                self.sibling_send[chunk, half] = self.product(2, chunk, half).astype(B16)

            self.sibling(chunk).start()

        rows = self.rows

        @pl.loop(0, self.count)
        def _(chunk):
            even = lax.rem(chunk, 2) == 0
            self.sibling(chunk).wait_recv()

            @pl.loop(0, 2)
            def _(half):
                total = self.product(0, chunk, half) + self.sibling_recv[chunk, half].astype(F32)

                @pl.when(half == 1)
                def _():
                    self.out[0, chunk] = total[:rows].astype(B16)
                    self.out[2, chunk] = total[rows:].astype(B16)

                @pl.when(half == 0)
                def _():
                    self.kept_ref[chunk] = total[:rows]
                    self.out[1, chunk] = total[rows:].astype(B16)

            side, across, _ = neighbours()

            @pl.when(even)
            def _():
                self.corner(chunk, side).start()
                self.final_x(chunk).start()

            @pl.when(jnp.logical_not(even))
            def _():
                self.corner(chunk, across).start()
                self.final_y(chunk).start()

    def middle(self):
        @pl.loop(0, self.count)
        def _(chunk):
            even = lax.rem(chunk, 2) == 0
            self.corner(chunk, neighbours()[0]).wait_recv()
            came = self.corner_recv[chunk].astype(F32)

            @pl.when(even)
            def _():
                self.out[1, chunk] = (self.out[1, chunk].astype(F32) + came).astype(B16)
                self.final_y(chunk).start()

            @pl.when(jnp.logical_not(even))
            def _():
                self.out[0, chunk] = (self.out[0, chunk].astype(F32) + came).astype(B16)
                self.final_x(chunk).start()

    def total(self, chunk):
        self.final_x(chunk).wait_recv()
        self.final_y(chunk).wait_recv()
        return (
            self.kept_ref[chunk] + self.x_recv[chunk].astype(F32) + self.y_recv[chunk].astype(F32)
        )

    def close(self):
        @pl.loop(0, self.count)
        def _(chunk):
            self.sibling(chunk).wait_send()
            self.corner(chunk, neighbours()[0]).wait_send()
            self.final_x(chunk).wait_send()
            self.final_y(chunk).wait_send()


def reduce_scratch(rows, width):
    count = width // CHUNK
    return [
        pltpu.VMEM((count, 2, 2 * rows, CHUNK), B16),
        pltpu.VMEM((count, 2, 2 * rows, CHUNK), B16),
        pltpu.VMEM((count, rows, CHUNK), F32),
        pltpu.VMEM((3, count, rows, CHUNK), B16),
        pltpu.VMEM((count, rows, CHUNK), B16),
        pltpu.VMEM((count, rows, CHUNK), B16),
        pltpu.VMEM((count, rows, CHUNK), B16),
    ]


def gather_scratch(rows, width):
    count = width // CHUNK
    return [pltpu.VMEM((count, rows, CHUNK), B16), pltpu.SemaphoreType.DMA((count,))]


def wire_scratch(kinds, count):
    return [pltpu.SemaphoreType.DMA((kinds, count))] * 2


IN_VMEM = pl.BlockSpec(memory_space=pltpu.VMEM)
IN_ANY = pl.BlockSpec(memory_space=pl.ANY)
VMEM_MOST = 60 * 1024 * 1024


def remote_params(number):
    return pltpu.CompilerParams(
        collective_id=number, has_side_effects=True, vmem_limit_bytes=VMEM_MOST
    )


def cost(flops, size):
    return pl.CostEstimate(flops=flops, bytes_accessed=size, transcendentals=0)


def shape(dims, kind=B16):
    return jax.ShapeDtypeStruct(dims, kind)


def cut(own, block_ref):
    for chunk in range(own.shape[0]):
        own[chunk] = block_ref[:, chunk * CHUNK : (chunk + 1) * CHUNK]


def open_kernel(
    tokens_ref, query_ref, key_ref, value_ref, out_ref, whole_ref, project_ref, branch_ref, *scratch
):
    own, gather_sem, send_sems, recv_sems, project_sem, branch_sem = scratch
    cut(own, tokens_ref)
    greet(neighbours() + planes())
    wires = Wires(send_sems, recv_sems)
    gather = Gather(wires, 0, whole_ref, own, gather_sem)
    shares = [
        Share(wires, GATHER_KINDS, (query_ref, key_ref, value_ref), project_ref, True, project_sem),
        Share(wires, GATHER_KINDS + SHARE_KINDS, (out_ref,), branch_ref, False, branch_sem),
    ]
    shares[0].start()

    @pl.loop(0, gather.count)
    def _(chunk):
        gather.send(chunk)

    shares[1].start()
    shares[0].middle()
    gather.relay()
    shares[1].middle()
    shares[0].late()
    shares[1].late()
    gather.close()
    shares[0].close()
    shares[1].close()


def open_call(tokens, w_query, w_key, w_value, w_out, number):
    rows, width = tokens.shape
    columns = (w_query.shape[1] + w_key.shape[1] + w_value.shape[1]) // 2
    return pl.pallas_call(
        open_kernel,
        out_shape=(
            shape((4, rows, 2 * width)),
            shape((2 * width, columns)),
            shape((w_out.shape[0] // 2, 2 * width)),
        ),
        in_specs=[IN_VMEM] + [IN_ANY] * 4,
        out_specs=(IN_ANY,) * 3,
        scratch_shapes=gather_scratch(rows, width)
        + wire_scratch(GATHER_KINDS + 2 * SHARE_KINDS, width // CHUNK)
        + [pltpu.SemaphoreType.DMA((3,)), pltpu.SemaphoreType.DMA((1,))],
        compiler_params=remote_params(number),
        cost_estimate=cost(0, 32 * rows * width),
    )(tokens, w_query, w_key, w_value, w_out)


def front_kernel(
    most,
    whole_ref,
    project_ref,
    gain_ref,
    starts_ref,
    cosine_ref,
    sine_ref,
    query_gain_ref,
    key_gain_ref,
    grad_ref,
    down_ref,
    first_ref,
    scale_ref,
    projected_ref,
    mixed_ref,
    query_ref,
    key_ref,
    value_ref,
    log_ref,
    grad_whole_ref,
    back_ref,
    *scratch,
):
    own, gather_sem, send_sems, recv_sems, back_sem = scratch
    core = lax.rem(lax.axis_index("tx"), 2)
    cut(own, grad_ref)
    greet(neighbours() + planes())
    wires = Wires(send_sems, recv_sems)
    gather = Gather(wires, 0, grad_whole_ref, own, gather_sem)
    back = Share(wires, GATHER_KINDS, (down_ref,), back_ref, False, back_sem)

    @pl.loop(0, gather.count)
    def _(chunk):
        gather.send(chunk)

    back.start()
    rows = whole_ref.shape[1]

    @pl.loop(0, 4 * rows // BLOCK)
    def _(tile):
        block = lax.div(tile, rows // BLOCK)
        at = pl.ds(pl.multiple_of(lax.rem(tile, rows // BLOCK) * BLOCK, BLOCK), BLOCK)
        value = whole_ref[block, at, :].astype(F32)
        scale = lax.rsqrt(jnp.mean(value * value, axis=1, keepdims=True) + EPS)
        first = (value * scale * gain_ref[...]).astype(B16)
        first_ref[block, at, :] = first
        projected_ref[block, at, :] = jnp.dot(
            first, project_ref[...], preferred_element_type=F32
        )

        @pl.when(block == 0)
        def _():
            scale_ref[at, :] = jnp.broadcast_to(scale, (BLOCK, 128))

    gather.relay()
    back.middle()
    fixed_refs = (starts_ref, cosine_ref, sine_ref, query_gain_ref, key_gain_ref)
    saved_refs = (query_ref, key_ref, value_ref, log_ref)

    @pl.loop(0, 2)
    def _(seq):
        attend_sequence(core, seq, most, projected_ref, fixed_refs, mixed_ref, saved_refs)

        @pl.when(seq == 0)
        def _():
            back.late()

    gather.close()
    back.close()


def front_call(whole, w_project, gain, fixed_args, most, cotangent, w_down, number):
    starts, cosine, sine, query_gain, key_gain = fixed_args
    rows, width = cotangent.shape
    length = cosine.shape[1]
    depth = query_gain.shape[1]
    columns = w_project.shape[1]
    heads = columns // depth - 2
    outs = (
        shape((4, rows, 2 * width)),
        shape((rows, 128), F32),
        shape((4, rows, columns), F32),
        shape((4, rows, heads * depth)),
        shape((2, length, heads * depth)),
        shape((2, length, depth)),
        shape((2, length, depth)),
        shape((2, heads, length, 1), F32),
        shape((4, rows, 2 * width)),
        shape((w_down.shape[0] // 2, 2 * width)),
    )
    return pl.pallas_call(
        lambda *refs: front_kernel(most, *refs),
        out_shape=outs,
        in_specs=[IN_VMEM] * 9 + [IN_ANY],
        out_specs=[IN_VMEM] * 8 + [IN_ANY] * 2,
        scratch_shapes=gather_scratch(rows, width)
        + wire_scratch(GATHER_KINDS + SHARE_KINDS, width // CHUNK)
        + [pltpu.SemaphoreType.DMA((1,))],
        compiler_params=remote_params(number),
        cost_estimate=cost(16 * rows * width * columns, 64 * rows * width),
    )(whole, w_project, gain, *fixed_args, cotangent, w_down)


def branch_kernel(
    rows_ref,
    weight_ref,
    input_ref,
    gate_ref,
    up_ref,
    residual_ref,
    whole_ref,
    both_ref,
    *scratch,
):
    bufs = scratch[:7]
    own, gather_sem, send_sems, recv_sems, both_sem = scratch[7:]
    width = input_ref.shape[1]
    greet(neighbours() + planes())
    wires = Wires(send_sems, recv_sems)
    reduce = Reduce(wires, rows_ref, weight_ref, False, bufs)
    gather = Gather(wires, REDUCE_KINDS, whole_ref, own, gather_sem)
    both = Share(
        wires, REDUCE_KINDS + GATHER_KINDS, (gate_ref, up_ref), both_ref, True, both_sem
    )
    both.start()
    reduce.start()
    both.middle()
    reduce.middle()

    @pl.loop(0, width // CHUNK)
    def _(chunk):
        at = lanes(chunk, 0, width)
        residual = input_ref[:, at].astype(F32) + reduce.total(chunk)
        residual_ref[:, at] = residual
        own[chunk] = residual.astype(B16)
        gather.send(chunk)

    both.late()
    gather.relay()
    gather.close()
    both.close()
    reduce.close()


def branch_call(rows, weight, inputs, w_gate, w_up, number):
    height, width = inputs.shape
    count = width // CHUNK
    return pl.pallas_call(
        branch_kernel,
        out_shape=(
            shape((height, width), F32),
            shape((4, height, 2 * width)),
            shape((2 * width, w_gate.shape[1])),
        ),
        in_specs=[IN_VMEM] * 3 + [IN_ANY] * 2,
        out_specs=(IN_VMEM, IN_ANY, IN_ANY),
        scratch_shapes=reduce_scratch(height, width)
        + gather_scratch(height, width)
        + wire_scratch(REDUCE_KINDS + GATHER_KINDS + SHARE_KINDS, count)
        + [pltpu.SemaphoreType.DMA((2,))],
        compiler_params=remote_params(number),
        cost_estimate=cost(16 * height * rows.shape[2] * width, 64 * height * width),
    )(rows, weight, inputs, w_gate, w_up)


def units_kernel(
    whole_ref, grad_ref, both_ref, back_ref, gain_ref, second_ref, hidden_ref, unit_ref, scale_ref, stats_ref
):
    units = hidden_ref.shape[1]
    value = whole_ref[...].astype(F32)
    scale = lax.rsqrt(jnp.mean(value * value, axis=1, keepdims=True) + EPS)
    second = (value * scale * gain_ref[...]).astype(B16)
    second_ref[...] = second
    scale_ref[...] = jnp.broadcast_to(scale, scale_ref.shape)
    total = jnp.zeros((value.shape[0], 1), F32)
    for low in range(0, units, CHUNK):
        at = slice(low, low + CHUNK)
        beside = slice(units + low, units + low + CHUNK)
        gate = jnp.dot(second, both_ref[:, at], preferred_element_type=F32)
        upper = jnp.dot(second, both_ref[:, beside], preferred_element_type=F32)
        hidden_grad = rows_dot(grad_ref[...], back_ref[at, :])
        sigma = jax.nn.sigmoid(gate)
        passed = gate * sigma
        hidden_ref[:, at] = (passed * upper).astype(B16)
        gate_grad = (hidden_grad * upper * (sigma + passed * (1.0 - sigma))).astype(B16)
        up_grad = (hidden_grad * passed).astype(B16)
        unit_ref[:, at] = gate_grad
        unit_ref[:, beside] = up_grad
        total += jnp.sum(
            gate_grad.astype(F32) * gate + up_grad.astype(F32) * upper, axis=1, keepdims=True
        )
    stats_ref[...] = jnp.zeros_like(stats_ref)
    put_stats(stats_ref, 0, total)


def units_call(whole, grad, w_both, w_back, gain):
    tokens, width = whole.shape
    units = w_back.shape[0]
    tiles = tokens // BLOCK

    def tile(columns):
        return pl.BlockSpec((BLOCK, columns), lambda i: (i, 0))

    def all_of(item):
        return pl.BlockSpec(item.shape, lambda i: (0, 0))

    return pl.pallas_call(
        units_kernel,
        out_shape=(
            shape((tokens, width)),
            shape((tokens, units)),
            shape((tokens, 2 * units)),
            shape((tokens, 128), F32),
            shape((tiles, 8, 128), F32),
        ),
        grid=(tiles,),
        in_specs=[tile(width), tile(width), all_of(w_both), all_of(w_back), all_of(gain)],
        out_specs=(
            tile(width),
            tile(units),
            tile(2 * units),
            tile(128),
            pl.BlockSpec((1, 8, 128), lambda i: (i, 0, 0)),
        ),
        compiler_params=pltpu.CompilerParams(vmem_limit_bytes=VMEM_MOST),
        cost_estimate=cost(6 * tokens * width * units, 20 * tokens * width // 2),
    )(whole, grad, w_both, w_back, gain)


def share_stats(wires, base, stats_ref, recv):
    side, across, core = neighbours()
    first = wires.copy(base, 0, stats_ref.at[4:8], recv.at[0:4], core)
    first.start()
    first.wait()
    stats_ref[0:4] = stats_ref[0:4] + recv[0:4]
    second = wires.copy(base, 1, stats_ref.at[2:4], recv.at[4:6], across)
    second.start()
    second.wait()
    stats_ref[0:2] = stats_ref[0:2] + recv[4:6]
    third = wires.copy(base, 2, stats_ref.at[0:2], recv.at[6:8], side)
    third.start()
    third.wait()
    stats_ref[0:2] = stats_ref[0:2] + recv[6:8]


def pull_columns(stats_ref, scale_ref, column_ref, width):
    for part in range(scale_ref.shape[0] // 128):
        at = slice(part * 128, (part + 1) * 128)
        scale = scale_ref[at, :]
        column_ref[at, :] = (
            stand(stats_ref[part // 2, part % 2 : part % 2 + 1, :]) * scale * scale / (2 * width)
        )


def pulled(reduce, chunk, refs, column_ref):
    scale_ref, value_ref, gain_ref, base_ref = refs
    at = lanes(chunk, 0, value_ref.shape[1])
    upstream = reduce.total(chunk)
    value = value_ref[:, at].astype(F32)
    scale = scale_ref[:, 0:1]
    back = scale * gain_ref[:, at] * upstream - value * column_ref[:, 0:1]
    return at, base_ref[:, at].astype(F32) + back, upstream * value * scale


def tile_columns(tile):
    return pl.ds(pl.multiple_of(tile * BLOCK, BLOCK), BLOCK)


def middle_kernel(
    rows_ref,
    weight_ref,
    stats_in_ref,
    scale_ref,
    value_ref,
    gain_ref,
    base_ref,
    down_in_ref,
    second_ref,
    result_ref,
    gain_grad_ref,
    whole_ref,
    down_mine_ref,
    down_theirs_ref,
    gate_mine_ref,
    gate_theirs_ref,
    up_ref,
    *scratch,
):
    bufs = scratch[:7]
    stats_ref, stats_recv, column_ref, send_sems, recv_sems, own, gather_sem = scratch[7:14]
    down_ref, gate_ref, stream, stream_sem, down_sem = scratch[14:19]
    down_bufs, gate_bufs = scratch[19:21], scratch[21:23]
    rows, width = value_ref.shape
    units = up_ref.shape[2]
    load = pltpu.make_async_copy(down_in_ref, down_ref, down_sem)
    load.start()

    def fetch(step):
        return pltpu.make_async_copy(
            second_ref.at[:, :, tile_columns(turn_tile(step))],
            stream.at[lax.rem(step, 2)],
            stream_sem.at[lax.rem(step, 2)],
        )

    fetch(0).start()
    stats_ref[...] = stats_in_ref[...]
    greet(neighbours() + planes())
    wires = Wires(send_sems, recv_sems)
    base = REDUCE_KINDS + 1 + GATHER_KINDS
    down = Fold(wires, base, down_ref, down_bufs, down_mine_ref, down_theirs_ref)
    gate = Fold(wires, base + FOLD_KINDS, gate_ref, gate_bufs, gate_mine_ref, gate_theirs_ref)
    load.wait()
    down.start()
    reduce = Reduce(wires, rows_ref, weight_ref, True, bufs)
    reduce.start()
    share_stats(wires, REDUCE_KINDS, stats_ref, stats_recv)
    pull_columns(stats_ref, scale_ref, column_ref, width)

    def make(step):
        @pl.when(step < 7)
        def _():
            fetch(step + 1).start()

        fetch(step).wait()
        left = stream[lax.rem(step, 2)].reshape(4 * rows, BLOCK)
        tile = turn_tile(step)
        flat = rows_ref[...].reshape(4 * rows, 2 * units)
        gate_ref[tile] = weight_grad(left, flat[:, :units]).astype(B16)
        up_ref[tile] = weight_grad(left, flat[:, units:]).astype(B16)

    @pl.loop(0, 4)
    def _(step):
        make(step)
        gate.near(lax.div(step, 2), lax.rem(step, 2)).start()

    reduce.middle()

    @pl.loop(4, 8)
    def _(step):
        make(step)

    down.middle()
    gather = Gather(wires, REDUCE_KINDS + 1, whole_ref, own, gather_sem)

    @pl.loop(0, width // CHUNK)
    def _(chunk):
        at, result, share = pulled(
            reduce, chunk, (scale_ref, value_ref, gain_ref, base_ref), column_ref
        )
        result_ref[:, at] = result
        own[chunk] = result.astype(B16)
        gather.send(chunk)
        gain_grad_ref[:, at] = jnp.sum(share, axis=0, keepdims=True)

    down.late()
    gather.relay()
    gate.middle()
    gather.close()
    gate.late()
    down.close()
    gate.close()
    reduce.close()


def middle_call(rows, weight, stats, scale, value, gain, base, down, second, number):
    height, width = value.shape
    count = width // CHUNK
    units = down.shape[2]
    quarter = down.shape[1]
    return pl.pallas_call(
        middle_kernel,
        out_shape=(
            shape((height, width), F32),
            shape((1, width), F32),
            shape((4, height, 2 * width)),
            shape((quarter, units), F32),
            shape((quarter, units)),
            shape((quarter, units), F32),
            shape((quarter, units)),
            shape((8, quarter, units)),
        ),
        in_specs=[IN_VMEM] * 7 + [IN_ANY] * 2,
        out_specs=(IN_VMEM, IN_VMEM, IN_ANY) + (IN_VMEM, IN_ANY) * 2 + (IN_VMEM,),
        scratch_shapes=reduce_scratch(height, width)
        + [
            pltpu.VMEM((8, 8, 128), F32),
            pltpu.VMEM((8, 8, 128), F32),
            pltpu.VMEM((height, 128), F32),
        ]
        + wire_scratch(REDUCE_KINDS + 1 + GATHER_KINDS + 2 * FOLD_KINDS, count)
        + gather_scratch(height, width)
        + [
            pltpu.VMEM((8, quarter, units), B16),
            pltpu.VMEM((8, quarter, units), B16),
            pltpu.VMEM((2, 4, height, BLOCK), B16),
            pltpu.SemaphoreType.DMA((2,)),
            pltpu.SemaphoreType.DMA,
        ]
        + fold_scratch(quarter, units) * 2,
        compiler_params=remote_params(number),
        cost_estimate=cost(48 * height * units * width, 64 * height * width),
    )(rows, weight, stats, scale, value, gain, base, down, second)


def last_kernel(
    rows_ref,
    weight_ref,
    stats_in_ref,
    scale_ref,
    value_ref,
    gain_ref,
    base_ref,
    extra_ref,
    out_in_ref,
    first_ref,
    result_ref,
    totals_ref,
    out_mine_ref,
    out_theirs_ref,
    project_mine_ref,
    project_theirs_ref,
    *scratch,
):
    bufs = scratch[:7]
    stats_ref, stats_recv, column_ref, send_sems, recv_sems = scratch[7:12]
    out_ref, project_ref, whole, sums_ref, sums_recv, load_sem = scratch[12:18]
    out_bufs, project_bufs = scratch[18:20], scratch[20:22]
    rows, width = value_ref.shape
    loads = [
        pltpu.make_async_copy(out_in_ref, out_ref, load_sem.at[0]),
        pltpu.make_async_copy(first_ref, whole, load_sem.at[1]),
    ]
    for load in loads:
        load.start()
    stats_ref[...] = stats_in_ref[...]
    sums_ref[...] = jnp.zeros_like(sums_ref)
    greet(neighbours() + planes())
    wires = Wires(send_sems, recv_sems)
    base = REDUCE_KINDS + 1
    out = Fold(wires, base, out_ref, out_bufs, out_mine_ref, out_theirs_ref)
    project = Fold(
        wires, base + FOLD_KINDS, project_ref, project_bufs, project_mine_ref, project_theirs_ref
    )
    reduce = Reduce(wires, rows_ref, weight_ref, True, bufs)
    reduce.start()
    for load in loads:
        load.wait()

    def make(step):
        tile = turn_tile(step)
        left = whole[:, :, tile_columns(tile)].reshape(4 * rows, BLOCK)
        grad = weight_grad(left, rows_ref[...].reshape(4 * rows, rows_ref.shape[2]))
        project_ref[tile] = grad.astype(B16)
        share = jnp.sum(
            grad * weight_ref[tile_columns(tile), :].astype(F32), axis=1, keepdims=True
        )
        sums_ref[tile, 0:1, :] = lie(share[:128])
        sums_ref[tile, 1:2, :] = lie(share[128:])

    @pl.loop(0, 4)
    def _(step):
        make(step)
        project.near(lax.div(step, 2), lax.rem(step, 2)).start()

    out.start()
    share_stats(wires, REDUCE_KINDS, stats_ref, stats_recv)
    pull_columns(stats_ref, scale_ref, column_ref, width)
    reduce.middle()

    @pl.loop(4, 8)
    def _(step):
        make(step)

    sums_ref[8] = extra_ref[0]
    sums_ref[9] = extra_ref[1]
    side, across, core = neighbours()
    near, far = planes()
    for hop, device in enumerate((core, across, near, far)):
        move = wires.copy(base + 2 * FOLD_KINDS, hop, sums_ref, sums_recv.at[hop], device)
        move.start()
        move.wait()
        sums_ref[...] = sums_ref[...] + sums_recv[hop]

    @pl.loop(0, width // CHUNK)
    def _(chunk):
        at, result, _ = pulled(
            reduce, chunk, (scale_ref, value_ref, gain_ref, base_ref), column_ref
        )
        result_ref[:, at] = result.astype(B16)

    project.middle()
    out.middle()
    move = wires.copy(base + 2 * FOLD_KINDS + 1, 0, sums_ref, sums_recv.at[4], side)
    move.start()
    project.late()
    out.late()
    move.wait()
    totals_ref[0:4] = sums_ref[0:4] + sums_recv[4, 4:8]
    totals_ref[4:8] = sums_ref[4:8] + sums_recv[4, 0:4]
    totals_ref[8] = sums_ref[8]
    totals_ref[9] = sums_recv[4, 8]
    totals_ref[10] = sums_ref[9] + sums_recv[4, 9]
    project.close()
    out.close()
    reduce.close()


def last_call(rows, weight, stats, scale, value, gain, base, extra, out, first, number):
    height, width = value.shape
    count = width // CHUNK
    quarter, branch = out.shape[1:]
    columns = rows.shape[2]
    return pl.pallas_call(
        last_kernel,
        out_shape=(
            shape((height, width)),
            shape((11, 8, 128), F32),
            shape((quarter, branch), F32),
            shape((quarter, branch)),
            shape((quarter, columns), F32),
            shape((quarter, columns)),
        ),
        in_specs=[IN_VMEM] * 8 + [IN_ANY] * 2,
        out_specs=(IN_VMEM, IN_VMEM) + (IN_VMEM, IN_ANY) * 2,
        scratch_shapes=reduce_scratch(height, width)
        + [
            pltpu.VMEM((8, 8, 128), F32),
            pltpu.VMEM((8, 8, 128), F32),
            pltpu.VMEM((height, 128), F32),
        ]
        + wire_scratch(REDUCE_KINDS + 1 + 2 * FOLD_KINDS + 2, count)
        + [
            pltpu.VMEM((8, quarter, branch), B16),
            pltpu.VMEM((8, quarter, columns), B16),
            pltpu.VMEM((4, height, 2 * width), B16),
            pltpu.VMEM((10, 8, 128), F32),
            pltpu.VMEM((5, 10, 8, 128), F32),
            pltpu.SemaphoreType.DMA((2,)),
        ]
        + fold_scratch(quarter, branch)
        + fold_scratch(quarter, columns),
        compiler_params=remote_params(number),
        cost_estimate=cost(32 * height * columns * width, 64 * height * width),
    )(rows, weight, stats, scale, value, gain, base, extra, out, first)


def back_kernel(
    most,
    upstream,
    hidden_ref,
    down_ref,
    residual_ref,
    starts_ref,
    cosine_ref,
    sine_ref,
    query_gain_ref,
    key_gain_ref,
    projected_ref,
    query_ref,
    key_ref,
    value_ref,
    log_ref,
    up_in_ref,
    output_ref,
    result_ref,
    stats_ref,
    gains_ref,
    up_mine_ref,
    up_theirs_ref,
    *scratch,
):
    bufs = scratch[:7]
    query_acc, key_acc, value_acc, send_sems, recv_sems, up_ref, up_sem = scratch[7:14]
    width = residual_ref.shape[1]
    core = lax.rem(lax.axis_index("tx"), 2)
    load = pltpu.make_async_copy(up_in_ref, up_ref, up_sem)
    load.start()
    greet(neighbours() + planes())
    wires = Wires(send_sems, recv_sems)
    up = Fold(wires, REDUCE_KINDS, up_ref, scratch[14:16], up_mine_ref, up_theirs_ref)
    load.wait()
    up.start()
    reduce = Reduce(wires, hidden_ref, down_ref, False, bufs)
    reduce.start()
    stats_ref[...] = jnp.zeros_like(stats_ref)
    fixed_refs = (starts_ref, cosine_ref, sine_ref, query_gain_ref, key_gain_ref)
    saved_refs = (query_ref, key_ref, value_ref, log_ref)

    @pl.loop(0, 2)
    def _(seq):
        attend_sequence_back(
            core,
            seq,
            most,
            projected_ref,
            upstream,
            fixed_refs,
            saved_refs,
            result_ref,
            stats_ref,
            gains_ref,
            (query_acc, key_acc, value_acc),
        )

        @pl.when(seq == 0)
        def _():
            reduce.middle()

    up.middle()

    @pl.loop(0, width // CHUNK)
    def _(chunk):
        at = lanes(chunk, 0, width)
        output_ref[:, at] = (residual_ref[:, at] + reduce.total(chunk)).astype(B16)

    up.late()
    up.close()
    reduce.close()


def back_call(upstream, hidden, w_back, residual, fixed_args, projected, saved, up, most, number):
    height, width = residual.shape
    _, cosine, _, query_gain, _ = fixed_args
    depth = query_gain.shape[1]
    length = cosine.shape[1]
    columns = projected.shape[2]
    heads = columns // depth - 2
    return pl.pallas_call(
        lambda *refs: back_kernel(most, *refs),
        out_shape=(
            shape((height, width)),
            shape((4, height, columns)),
            shape((8, 8, 128), F32),
            shape((2, 8, depth), F32),
            shape(up.shape[1:], F32),
            shape(up.shape[1:]),
        ),
        in_specs=[IN_VMEM] * 14 + [IN_ANY],
        out_specs=[IN_VMEM] * 5 + [IN_ANY],
        scratch_shapes=reduce_scratch(height, width)
        + [
            pltpu.VMEM((length, heads * depth), F32),
            pltpu.VMEM((length, depth), F32),
            pltpu.VMEM((length, depth), F32),
        ]
        + wire_scratch(REDUCE_KINDS + FOLD_KINDS, width // CHUNK)
        + [pltpu.VMEM(up.shape, B16), pltpu.SemaphoreType.DMA]
        + fold_scratch(*up.shape[1:]),
        compiler_params=remote_params(number),
        cost_estimate=cost(16 * height * hidden.shape[2] * width, 64 * height * width),
    )(upstream, hidden, w_back, residual, *fixed_args, projected, *saved, up)


def product_grad(left, right):
    return weight_grad(left, right).astype(B16)


def plane_device(
    tokens,
    seg_ids,
    w_query,
    w_key,
    w_value,
    w_out,
    w_gate,
    w_up,
    w_down,
    attn_gain,
    mlp_gain,
    query_gain,
    key_gain,
    cotangent,
):
    spot = lax.axis_index("tx")
    depth = query_gain.shape[0]
    length = seg_ids.shape[1]
    most = length // 2
    rows, width = tokens.shape
    head_width = w_query.shape[1] // 2
    kv_width = w_key.shape[1] // 2
    units = w_gate.shape[1] // 2

    gains = jnp.stack([attn_gain, mlp_gain])
    gains = jnp.concatenate([gains, swap_x(gains)], axis=1)
    seg_all = in_order(seg_ids, swap_x(seg_ids), 0)
    seg_all = jnp.where(lax.div(spot, 2) == 0, seg_all, seg_all[::-1])
    index = jnp.arange(length, dtype=jnp.int32)[None]
    edge = jnp.concatenate(
        [jnp.ones((2, 1), dtype=jnp.bool_), seg_all[:, 1:] != seg_all[:, :-1]], axis=1
    )
    starts = lax.cummax(jnp.where(edge, index, 0), axis=1)
    cosine, sine = rotary(index - starts, depth)
    cosine = jnp.concatenate([cosine, cosine], axis=-1)
    sine = jnp.concatenate([-sine, sine], axis=-1)
    fixed_args = (starts[:, :, None], cosine, sine, query_gain[None], key_gain[None])

    token_whole, w_project, w_branch = open_call(tokens, w_query, w_key, w_value, w_out, 0)
    first, first_scale, projected, mixed, query, keys, values, logs, grad_whole, w_back = front_call(
        token_whole, w_project, gains[0:1], fixed_args, most, cotangent, w_down, 1
    )
    residual, residual_whole, w_both = branch_call(mixed, w_branch, tokens, w_gate, w_up, 2)
    flat = (4 * rows, 2 * width)
    grad_flat = grad_whole.reshape(flat)
    second, hidden, unit_grads, second_scale, unit_stats = units_call(
        residual_whole.reshape(flat), grad_flat, w_both, w_back, gains[1:2]
    )
    tiles = lambda grad: grad.reshape(8, -1, grad.shape[1])
    (
        residual_grad,
        mlp_gain_part,
        branch_whole,
        down_mine,
        down_theirs,
        gate_mine,
        gate_theirs,
        up_tiles,
    ) = middle_call(
        unit_grads.reshape(4, rows, 2 * units),
        w_both,
        unit_stats,
        second_scale[:rows],
        residual,
        mlp_gain[None],
        cotangent,
        tiles(product_grad(grad_flat, hidden)),
        second.reshape(4, rows, 2 * width),
        3,
    )
    branch_flat = branch_whole.reshape(flat)
    upstream = backward_with(w_branch)(branch_flat).astype(B16).reshape(4, rows, head_width)
    out_tiles = tiles(product_grad(branch_flat, mixed.reshape(4 * rows, head_width)))
    output, proj_grads, proj_stats, gain_parts, up_mine, up_theirs = back_call(
        upstream,
        hidden.reshape(4, rows, units),
        w_back,
        residual,
        fixed_args,
        projected,
        (query, keys, values, logs),
        up_tiles,
        most,
        4,
    )
    extra = jnp.stack(
        [
            mlp_gain_part.reshape(8, 128),
            jnp.pad(jnp.sum(gain_parts[:, :2], axis=0), ((0, 6), (0, 0))),
        ]
    )
    input_grad, totals, out_mine, out_theirs, project_mine, project_theirs = last_call(
        proj_grads,
        w_project,
        proj_stats,
        first_scale,
        tokens,
        attn_gain[None],
        residual_grad,
        extra,
        out_tiles,
        first,
        5,
    )
    whole = lambda mine, theirs: in_order(mine, theirs.astype(F32), 1)
    attn_sums = totals[:8, :2].reshape(-1) / gains[0]
    attn_total = in_order(attn_sums[:width], attn_sums[width:], 0)
    mlp_total = in_order(totals[8].reshape(-1), totals[9].reshape(-1), 0)
    query_total, key_total = totals[10, 0], totals[10, 1]
    down_share = whole(down_mine, down_theirs).T
    out_share = whole(out_mine, out_theirs).T
    gate_share = whole(gate_mine, gate_theirs)
    up_share = whole(up_mine, up_theirs)
    ends = (0, head_width, head_width + kv_width, head_width + 2 * kv_width)
    query_share, key_share, value_share = (
        whole(project_mine[:, low:high], project_theirs[:, low:high])
        for low, high in zip(ends[:-1], ends[1:])
    )
    return (
        output,
        input_grad,
        query_share,
        key_share,
        value_share,
        out_share,
        gate_share,
        up_share,
        down_share,
        attn_total,
        mlp_total,
        query_total,
        key_total,
    )


def solution(mesh):
    placed = (
        P(("dp", "tx"), "ty"),
        P(("dp", "ty"), None),
        P("ty", "tx"),
        P("ty", "tx"),
        P("ty", "tx"),
        P("tx", "ty"),
        P("ty", "tx"),
        P("ty", "tx"),
        P("tx", "ty"),
        P("ty"),
        P("ty"),
        P(),
        P(),
        P(("dp", "tx"), "ty"),
    )
    return jax.shard_map(
        plane_device if fits(mesh) else general_device,
        mesh=mesh,
        in_specs=placed,
        out_specs=(
            P(("dp", "tx"), "ty"),
            P(("dp", "tx"), "ty"),
            P(("ty", "dp"), "tx"),
            P(("ty", "dp"), "tx"),
            P(("ty", "dp"), "tx"),
            P("tx", ("ty", "dp")),
            P(("ty", "dp"), "tx"),
            P(("ty", "dp"), "tx"),
            P("tx", ("ty", "dp")),
            P(),
            P(),
            P(),
            P(),
        ),
        check_vma=False,
    )
```

```python
import jax
import jax.numpy as jnp
from jax import lax
from jax.experimental import pallas as pl
from jax.experimental.pallas import tpu as pltpu
from jax.sharding import PartitionSpec as P

EPS = 1e-06
THETA = 1000000.0
NEG = -1e30
F32 = jnp.float32
B16 = jnp.bfloat16
MESH = pl.DeviceIdType.MESH


def width_sum(value):
    return lax.psum(value, "ty")


def token_gather(rows):
    return lax.all_gather(rows, "tx", axis=0, tiled=True)


def branch_gather(rows):
    return lax.all_gather(rows, "ty", axis=0, tiled=True)


def width_reduce(whole, apply):
    return lax.psum_scatter(apply(whole), "ty", scatter_dimension=0, tiled=True)


def head_reduce(whole, apply):
    return lax.psum_scatter(
        apply(whole).astype(jnp.bfloat16), "tx", scatter_dimension=0, tiled=True
    ).astype(jnp.float32)


def forward_with(weight):
    return lambda rows: jnp.dot(rows, weight, preferred_element_type=F32)


def backward_with(weight):
    return lambda rows: lax.dot_general(
        rows, weight, (((1,), (1,)), ((), ())), preferred_element_type=F32
    )


def weight_grad(left, right):
    return lax.dot_general(left, right, (((0,), (0,)), ((), ())), preferred_element_type=F32)


def norm_scale(rows):
    width = rows.shape[1] * lax.axis_size("ty")
    return lax.rsqrt(width_sum(jnp.sum(rows * rows, axis=1)) / width + EPS)


def norm_back(rows, scale, gain, upstream):
    width = rows.shape[1] * lax.axis_size("ty")
    inner = width_sum(jnp.sum(upstream * gain * rows, axis=1))
    back = scale[:, None] * gain * upstream - rows * (scale**3 * inner / width)[:, None]
    gain_part = jnp.sum(upstream * rows * scale[:, None], axis=0)
    return (back, gain_part)


def widen(part):
    whole = jnp.zeros((part.shape[0] * lax.axis_size("ty"),), F32)
    return lax.dynamic_update_slice_in_dim(whole, part, lax.axis_index("ty") * part.shape[0], 0)


def doc_positions(seg):
    count = seg.shape[-1]
    index = jnp.arange(count, dtype=jnp.int32)
    edge = jnp.concatenate([jnp.ones((1,), dtype=jnp.bool_), seg[1:] != seg[:-1]])
    first = lax.cummax(jnp.where(edge, index, jnp.zeros_like(index)), axis=0)
    return index - first


def rotary(positions, depth):
    half = depth // 2
    freq = THETA ** (-jnp.arange(half, dtype=F32) * 2.0 / depth)
    angle = positions.astype(F32)[..., None] * freq
    return (jnp.cos(angle), jnp.sin(angle))


def turn(value, gain, cosine, sine):
    normed = value * lax.rsqrt(jnp.mean(value * value, axis=-1, keepdims=True) + EPS) * gain
    half = value.shape[-1] // 2
    first = normed[..., :half]
    second = normed[..., half:]
    return jnp.concatenate(
        [first * cosine - second * sine, second * cosine + first * sine], axis=-1
    )


def block_scores(part, seq_keys, seq_ids, start, scale):
    block = part.shape[0]
    length = seq_ids.shape[0]
    index = jnp.arange(length, dtype=jnp.int32)
    rows = start + jnp.arange(block, dtype=jnp.int32)
    row_ids = lax.dynamic_slice_in_dim(seq_ids, start, block, 0)
    mask = (seq_ids[None, :] == row_ids[:, None]) & (index[None, :] <= rows[:, None])
    scores = jnp.einsum("qkgd,mkd->kgqm", part, seq_keys, preferred_element_type=F32) * scale
    return jnp.where(mask[None, None], scores, NEG)


def attend_forward(query, keys, values, seg, block):
    seqs, length, heads, depth = query.shape
    kv_heads = keys.shape[2]
    groups = heads // kv_heads
    scale = depth ** (-0.5)
    count = length // block
    starts = jnp.arange(count, dtype=jnp.int32) * block

    def one_sequence(operands):
        seq_query, seq_keys, seq_values, seq_ids = operands
        blocks = seq_query.reshape(count, block, kv_heads, groups, depth)

        def one_block(inputs):
            part, start = inputs
            scores = block_scores(part, seq_keys, seq_ids, start, scale)
            top = jnp.max(scores, axis=-1)
            weights = jnp.exp(scores - top[..., None])
            total = jnp.sum(weights, axis=-1)
            probs = (weights / total[..., None]).astype(B16)
            mixed = jnp.einsum("kgqm,mkd->qkgd", probs, seq_values, preferred_element_type=F32)
            return (mixed, top + jnp.log(total))

        mixed, logs = lax.map(one_block, (blocks, starts))
        return (mixed.reshape(length, heads * depth), logs)

    return lax.map(one_sequence, (query, keys, values, seg))


def attend_backward(query, keys, values, seg, logs, grad_out, block):
    seqs, length, heads, depth = query.shape
    kv_heads = keys.shape[2]
    groups = heads // kv_heads
    scale = depth ** (-0.5)
    count = length // block
    starts = jnp.arange(count, dtype=jnp.int32) * block

    def one_sequence(operands):
        seq_query, seq_keys, seq_values, seq_ids, seq_logs, seq_grad = operands
        blocks = seq_query.reshape(count, block, kv_heads, groups, depth)
        grads = seq_grad.reshape(count, block, kv_heads, groups, depth)

        def one_block(carry, inputs):
            key_acc, value_acc = carry
            part, grad_part, log_part, start = inputs
            scores = block_scores(part, seq_keys, seq_ids, start, scale)
            probs = jnp.exp(scores - log_part[..., None])
            value_acc = value_acc + jnp.einsum(
                "kgqm,qkgd->mkd", probs.astype(B16), grad_part, preferred_element_type=F32
            )
            prob_grad = jnp.einsum(
                "qkgd,mkd->kgqm", grad_part, seq_values, preferred_element_type=F32
            )
            delta = jnp.sum(probs * prob_grad, axis=-1, keepdims=True)
            score_grad = (probs * (prob_grad - delta)).astype(B16)
            query_grad = (
                jnp.einsum("kgqm,mkd->qkgd", score_grad, seq_keys, preferred_element_type=F32)
                * scale
            )
            key_acc = (
                key_acc
                + jnp.einsum("kgqm,qkgd->mkd", score_grad, part, preferred_element_type=F32) * scale
            )
            return ((key_acc, value_acc), query_grad)

        zeros = jnp.zeros((length, kv_heads, depth), F32)
        (key_grad, value_grad), query_grad = lax.scan(
            one_block, (zeros, zeros), (blocks, grads, seq_logs, starts)
        )
        return (query_grad.reshape(length, heads, depth), key_grad, value_grad)

    return lax.map(one_sequence, (query, keys, values, seg, logs, grad_out))


def general_device(
    tokens,
    seg_ids,
    w_query,
    w_key,
    w_value,
    w_out,
    w_gate,
    w_up,
    w_down,
    attn_gain,
    mlp_gain,
    query_gain,
    key_gain,
    cotangent,
):
    seqs, length = seg_ids.shape
    depth = query_gain.shape[0]
    query_width = w_query.shape[1]
    key_width = w_key.shape[1]
    units = w_gate.shape[1]
    block = min(512, length)
    inputs = tokens.astype(F32)
    first_scale = norm_scale(inputs)
    first_normed = (inputs * first_scale[:, None] * attn_gain).astype(B16)
    first_whole = token_gather(first_normed)
    w_project = jnp.concatenate([w_query, w_key, w_value], axis=1)
    projected = width_reduce(first_whole, forward_with(w_project))
    query_proj = projected[:, :query_width].reshape(seqs, length, -1, depth)
    key_proj = projected[:, query_width : query_width + key_width].reshape(seqs, length, -1, depth)
    values = projected[:, query_width + key_width :].astype(B16).reshape(seqs, length, -1, depth)
    positions = jax.vmap(doc_positions)(seg_ids)
    cosine, sine = rotary(positions, depth)
    cosine = cosine[:, :, None, :]
    sine = sine[:, :, None, :]
    query = turn(query_proj, query_gain, cosine, sine).astype(B16)
    keys = turn(key_proj, key_gain, cosine, sine).astype(B16)
    mixed, logs = attend_forward(query, keys, values, seg_ids, block)
    attended = mixed.reshape(seqs * length, -1).astype(B16)
    attended_whole = branch_gather(attended)
    residual = inputs + head_reduce(attended_whole, forward_with(w_out))
    second_scale = norm_scale(residual)
    second_normed = (residual * second_scale[:, None] * mlp_gain).astype(B16)
    second_whole = token_gather(second_normed)
    w_both = jnp.concatenate([w_gate, w_up], axis=1)
    gate_up = width_reduce(second_whole, forward_with(w_both))
    gate = gate_up[:, :units]
    upper = gate_up[:, units:]
    hidden = (jax.nn.silu(gate) * upper).astype(B16)
    hidden_whole = branch_gather(hidden)
    output = residual + head_reduce(hidden_whole, forward_with(w_down))
    grad_whole = token_gather(cotangent)
    hidden_grad = width_reduce(grad_whole, backward_with(w_down))
    down_grad = weight_grad(hidden_whole, grad_whole)
    gate_grad, up_grad = jax.vjp(lambda left, right: jax.nn.silu(left) * right, gate, upper)[1](
        hidden_grad
    )
    unit_grads = jnp.concatenate([gate_grad, up_grad], axis=1).astype(B16)
    unit_whole = branch_gather(unit_grads)
    second_grad = head_reduce(unit_whole, backward_with(w_both))
    both_grad = weight_grad(second_whole, unit_whole)
    gate_weight = both_grad[:, :units]
    up_weight = both_grad[:, units:]
    resid_norm_grad, mlp_gain_part = norm_back(residual, second_scale, mlp_gain, second_grad)
    residual_grad = cotangent.astype(F32) + resid_norm_grad
    residual_whole = token_gather(residual_grad.astype(B16))
    mixed_grad = width_reduce(residual_whole, backward_with(w_out)).astype(B16)
    out_grad = weight_grad(attended_whole, residual_whole)
    query_grad, key_grad, value_grad = attend_backward(
        query, keys, values, seg_ids, logs, mixed_grad.reshape(seqs, length, -1), block
    )
    query_proj_grad, query_gain_grad = jax.vjp(
        lambda value, gain: turn(value, gain, cosine, sine), query_proj, query_gain
    )[1](query_grad)
    key_proj_grad, key_gain_grad = jax.vjp(
        lambda value, gain: turn(value, gain, cosine, sine), key_proj, key_gain
    )[1](key_grad)
    rows = seqs * length
    proj_grad = jnp.concatenate(
        [
            query_proj_grad.reshape(rows, -1),
            key_proj_grad.reshape(rows, -1),
            value_grad.reshape(rows, -1),
        ],
        axis=1,
    ).astype(B16)
    proj_whole = branch_gather(proj_grad)
    first_grad = head_reduce(proj_whole, backward_with(w_project))
    project_grad = weight_grad(first_whole, proj_whole)
    query_weight = project_grad[:, :query_width]
    key_weight = project_grad[:, query_width : query_width + key_width]
    value_weight = project_grad[:, query_width + key_width :]
    input_norm_grad, attn_gain_part = norm_back(inputs, first_scale, attn_gain, first_grad)
    input_grad = (residual_grad + input_norm_grad).astype(B16)
    attn_total, mlp_total, query_total, key_total = lax.psum(
        (widen(attn_gain_part), widen(mlp_gain_part), query_gain_grad, key_gain_grad),
        ("dp", "tx", "ty"),
    )
    query_share, key_share, value_share, gate_share, up_share = (
        lax.psum_scatter(
            query_weight.astype(jnp.bfloat16), "dp", scatter_dimension=0, tiled=True
        ).astype(jnp.float32),
        lax.psum_scatter(
            key_weight.astype(jnp.bfloat16), "dp", scatter_dimension=0, tiled=True
        ).astype(jnp.float32),
        lax.psum_scatter(
            value_weight.astype(jnp.bfloat16), "dp", scatter_dimension=0, tiled=True
        ).astype(jnp.float32),
        lax.psum_scatter(
            gate_weight.astype(jnp.bfloat16), "dp", scatter_dimension=0, tiled=True
        ).astype(jnp.float32),
        lax.psum_scatter(
            up_weight.astype(jnp.bfloat16), "dp", scatter_dimension=0, tiled=True
        ).astype(jnp.float32),
    )
    out_share, down_share = (
        lax.psum_scatter(
            out_grad.astype(jnp.bfloat16), "dp", scatter_dimension=1, tiled=True
        ).astype(jnp.float32),
        lax.psum_scatter(
            down_grad.astype(jnp.bfloat16), "dp", scatter_dimension=1, tiled=True
        ).astype(jnp.float32),
    )
    return (
        output.astype(B16),
        input_grad,
        query_share,
        key_share,
        value_share,
        out_share,
        gate_share,
        up_share,
        down_share,
        attn_total,
        mlp_total,
        query_total,
        key_total,
    )


def fits(mesh):
    return mesh.shape["tx"] == 4 and mesh.shape["ty"] == 2 and mesh.shape["dp"] == 4


def swap_x(value):
    return lax.ppermute(value, "ty", [(0, 1), (1, 0)])


def in_order(mine, theirs, axis):
    first = lax.axis_index("ty") == 0
    return jnp.concatenate(
        [jnp.where(first, mine, theirs), jnp.where(first, theirs, mine)], axis=axis
    )


def spin(value, cosine, sine):
    return value * cosine + pltpu.roll(value, value.shape[1] // 2, 1) * sine


def spin_back(value, cosine, sine):
    return value * cosine + pltpu.roll(value * sine, value.shape[1] // 2, 1)


def head_scale(value):
    return lax.rsqrt(jnp.mean(value * value, axis=1, keepdims=True) + EPS)


def window(first, block, most):
    return max(0, first - most), first + block


def kept(first, block, low, high, starts):
    shape = (block, high - low)
    column = low + lax.broadcasted_iota(jnp.int32, shape, 1)
    row = first + lax.broadcasted_iota(jnp.int32, shape, 0)
    return (column >= starts) & (column <= row)


def rows_dot(left, right):
    return lax.dot_general(left, right, (((1,), (1,)), ((), ())), preferred_element_type=F32)


def stand(row):
    return jnp.transpose(jnp.broadcast_to(row, (row.shape[1], row.shape[1])))


def lie(column):
    return jnp.transpose(jnp.broadcast_to(column, (column.shape[0], column.shape[0])))[0:1]


def put_stats(stats_ref, tile, column):
    stats_ref[tile, 0:1, :] = lie(column[:128])
    stats_ref[tile, 1:2, :] = lie(column[128:])


BLOCK = 256


def attend_sequence(core, seq, most, projected, fixed_refs, mixed, saved_refs, between):
    starts_ref, cosine_ref, sine_ref, query_gain_ref, key_gain_ref = fixed_refs
    query_ref, key_ref, value_ref, log_ref = saved_refs
    rows = projected.shape[1]
    length = query_ref.shape[1]
    depth = key_ref.shape[2]
    heads = query_ref.shape[2] // depth
    scale = depth ** (-0.5)
    for half in range(2):
        place = 2 * lax.rem(core + half, 2) + seq
        for at in range(half * rows, (half + 1) * rows, BLOCK):
            inner = at - half * rows
            cosine = cosine_ref[seq, at : at + BLOCK, :]
            sine = sine_ref[seq, at : at + BLOCK, :]
            for head in range(heads + 2):
                lane = slice(head * depth, (head + 1) * depth)
                value = projected[place, inner : inner + BLOCK, lane]
                if head < heads:
                    normed = value * head_scale(value) * query_gain_ref[...]
                    query_ref[seq, at : at + BLOCK, lane] = spin(normed, cosine, sine).astype(B16)
                elif head == heads:
                    normed = value * head_scale(value) * key_gain_ref[...]
                    key_ref[seq, at : at + BLOCK, :] = spin(normed, cosine, sine).astype(B16)
                else:
                    value_ref[seq, at : at + BLOCK, :] = value.astype(B16)
    for first in range(0, length, BLOCK):
        between(first // BLOCK)
        low, high = window(first, BLOCK, most)
        mask = kept(first, BLOCK, low, high, starts_ref[seq, first : first + BLOCK, :])
        half, inner = divmod(first, rows)
        place = 2 * lax.rem(core + half, 2) + seq
        for head in range(heads):
            lane = slice(head * depth, (head + 1) * depth)
            query = query_ref[seq, first : first + BLOCK, lane]
            scores = rows_dot(query, key_ref[seq, low:high, :]) * scale
            scores = jnp.where(mask, scores, NEG)
            top = jnp.max(scores, axis=1, keepdims=True)
            weights = jnp.exp(scores - top)
            total = jnp.sum(weights, axis=1, keepdims=True)
            probs = (weights * (1.0 / total)).astype(B16)
            out = jnp.dot(probs, value_ref[seq, low:high, :], preferred_element_type=F32)
            mixed[place, inner : inner + BLOCK, lane] = out.astype(B16)
            log_ref[seq, head, first : first + BLOCK, :] = top + jnp.log(total)


def attend_sequence_back(
    core, seq, most, projected, upstream, fixed_refs, saved_refs, result, stats, gains, accs
):
    starts_ref, cosine_ref, sine_ref, query_gain_ref, key_gain_ref = fixed_refs
    query_ref, key_ref, value_ref, log_ref = saved_refs
    query_acc, key_acc, value_acc = accs
    rows = projected.shape[1]
    length = query_ref.shape[1]
    depth = key_ref.shape[2]
    heads = query_ref.shape[2] // depth
    scale = depth ** (-0.5)
    key_acc[...] = jnp.zeros_like(key_acc)
    value_acc[...] = jnp.zeros_like(value_acc)
    for first in range(0, length, BLOCK):
        low, high = window(first, BLOCK, most)
        mask = kept(first, BLOCK, low, high, starts_ref[seq, first : first + BLOCK, :])
        half, inner = divmod(first, rows)
        place = 2 * lax.rem(core + half, 2) + seq
        keys = key_ref[seq, low:high, :]
        values = value_ref[seq, low:high, :]
        for head in range(heads):
            lane = slice(head * depth, (head + 1) * depth)
            query = query_ref[seq, first : first + BLOCK, lane]
            grad = upstream[place, inner : inner + BLOCK, lane]
            scores = rows_dot(query, keys) * scale - log_ref[seq, head, first : first + BLOCK, :]
            probs = jnp.exp(jnp.where(mask, scores, NEG))
            prob_grad = rows_dot(grad, values)
            delta = jnp.sum(probs * prob_grad, axis=1, keepdims=True)
            score_grad = (probs * (prob_grad - delta)).astype(B16)
            query_acc[first : first + BLOCK, lane] = (
                jnp.dot(score_grad, keys, preferred_element_type=F32) * scale
            )
            key_acc[low:high, :] += weight_grad(score_grad, query) * scale
            value_acc[low:high, :] += weight_grad(probs.astype(B16), grad)
    query_total = jnp.zeros((1, depth), F32)
    key_total = jnp.zeros((1, depth), F32)
    for half in range(2):
        block = 2 * lax.rem(core + half, 2) + seq
        for at in range(half * rows, (half + 1) * rows, BLOCK):
            inner = at - half * rows
            cosine = cosine_ref[seq, at : at + BLOCK, :]
            sine = sine_ref[seq, at : at + BLOCK, :]
            total = jnp.zeros((BLOCK, 1), F32)
            for head in range(heads + 2):
                lane = slice(head * depth, (head + 1) * depth)
                value = projected[block, inner : inner + BLOCK, lane]
                if head == heads + 1:
                    back = value_acc[at : at + BLOCK, :].astype(B16)
                else:
                    if head < heads:
                        grad = query_acc[at : at + BLOCK, lane]
                        gain = query_gain_ref[...]
                    else:
                        grad = key_acc[at : at + BLOCK, :]
                        gain = key_gain_ref[...]
                    grad = spin_back(grad, cosine, sine)
                    rate = head_scale(value)
                    scaled = value * rate
                    share = jnp.sum(grad * scaled, axis=0, keepdims=True)
                    if head < heads:
                        query_total += share
                    else:
                        key_total += share
                    middle = jnp.mean(gain * grad * scaled, axis=1, keepdims=True)
                    back = (rate * (gain * grad - scaled * middle)).astype(B16)
                result[block, inner : inner + BLOCK, lane] = back
                total += jnp.sum(back.astype(F32) * value, axis=1, keepdims=True)
            put_stats(stats, 2 * block + inner // BLOCK, total)
    gains[seq, 0:1, :] = query_total
    gains[seq, 1:2, :] = key_total


def neighbours():
    spot = lax.axis_index("tx")
    core = lax.rem(spot, 2)
    return (
        {"ty": 1 - lax.axis_index("ty")},
        {"tx": lax.rem(spot + 2, 4)},
        {"tx": spot + 1 - 2 * core},
    )


def planes():
    plane = lax.axis_index("dp")
    return {"dp": plane + 1 - 2 * lax.rem(plane, 2)}, {"dp": lax.rem(plane + 2, 4)}


def greet(targets):
    barrier = pltpu.get_barrier_semaphore()
    for target in targets:
        pl.semaphore_signal(barrier, inc=1, device_id=target, device_id_type=MESH)
    pl.semaphore_wait(barrier, len(targets))


class Wires:
    def __init__(self, send_sems, recv_sems):
        self.send_sems = send_sems
        self.recv_sems = recv_sems

    def copy(self, kind, chunk, source, target, device):
        return pltpu.make_async_remote_copy(
            src_ref=source,
            dst_ref=target,
            send_sem=self.send_sems.at[kind, chunk],
            recv_sem=self.recv_sems.at[kind, chunk],
            device_id=device,
            device_id_type=MESH,
        )


CHUNK = 256
SIBLING, CORNER, FINAL_X, FINAL_Y = 0, 1, 2, 3
REDUCE_KINDS = 5
OUT_X, OUT_Y, OUT_CORNER, CORE_OWN, CORE_X, CORE_Y, CORE_CORNER = range(7)
GATHER_KINDS = 7
SHARE_X, SHARE_Z = 0, 1
SHARE_KINDS = 2


def lanes(chunk, half, width):
    return pl.ds(pl.multiple_of(half * width + chunk * CHUNK, CHUNK), CHUNK)


class Gather:
    def __init__(self, wires, base, whole, own, local_sem, most=4):
        self.wires, self.base, self.whole, self.own, self.local_sem = (
            wires,
            base,
            whole,
            own,
            local_sem,
        )
        self.most = most
        self.width = whole.shape[2] // 2
        self.count = self.width // CHUNK

    def place(self, block, chunk, half):
        return self.whole.at[block, :, lanes(chunk, half, self.width)]

    def copy(self, name, chunk):
        side, across, core = neighbours()
        at = self.place
        own = self.own.at[chunk]
        if name == "local":
            return pltpu.make_async_copy(own, at(0, chunk, 0), self.local_sem.at[chunk])
        kind, source, target, device = {
            "x": (OUT_X, own, at(0, chunk, 1), side),
            "y": (OUT_Y, own, at(1, chunk, 0), across),
            "core": (CORE_OWN, own, at(2, chunk, 0), core),
            "even": (OUT_CORNER, at(0, chunk, 1), at(1, chunk, 1), across),
            "odd": (OUT_CORNER, at(1, chunk, 0), at(1, chunk, 1), side),
            "core_x": (CORE_X, at(0, chunk, 1), at(2, chunk, 1), core),
            "core_y": (CORE_Y, at(1, chunk, 0), at(3, chunk, 0), core),
            "core_corner": (CORE_CORNER, at(1, chunk, 1), at(3, chunk, 1), core),
        }[name]
        return self.wires.copy(self.base + kind, chunk, source, target, device)

    def send(self, chunk):
        for name in ("x", "y", "core", "local"):
            self.copy(name, chunk).start()

    def relay(self, low=0, high=None):
        @pl.loop(low, self.count if high is None else high)
        def _(chunk):
            even = (lax.rem(chunk, 2) == 0) | (chunk >= self.most)
            self.copy("x", chunk).wait_recv()

            @pl.when(even)
            def _():
                self.copy("even", chunk).start()

            self.copy("core_x", chunk).start()
            self.copy("y", chunk).wait_recv()

            @pl.when(jnp.logical_not(even))
            def _():
                self.copy("odd", chunk).start()

            self.copy("core_y", chunk).start()

    def close(self):
        @pl.loop(0, self.count)
        def _(chunk):
            self.copy("even", chunk).wait_recv()
            self.copy("core_corner", chunk).start()

        @pl.loop(0, self.count)
        def _(chunk):
            for name in ("core", "core_x", "core_y", "core_corner"):
                self.copy(name, chunk).wait_recv()
            for name in ("x", "y", "core", "even", "core_x", "core_y", "core_corner"):
                self.copy(name, chunk).wait_send()
            self.copy("local", chunk).wait()


class Share:
    def __init__(self, wires, base, sources, whole, by_rows, local_sems, held=None):
        self.wires, self.base, self.sources, self.whole, self.by_rows, self.local_sems = (
            wires,
            base,
            sources,
            whole,
            by_rows,
            local_sems,
        )
        self.held = held or sources
        self.size = (whole.shape[0] // 2 if by_rows else whole.shape[0]) // 4

    def quarter(self, plane):
        start = plane * self.size
        if self.by_rows:
            rows = pl.ds(pl.multiple_of(self.whole.shape[0] // 2 + start, self.size), self.size)
            return self.whole.at[rows]
        width = self.whole.shape[1] // 2
        return self.whole.at[pl.ds(pl.multiple_of(start, self.size), self.size), width:]

    def cross(self, index):
        side, _, _ = neighbours()
        plane = lax.axis_index("dp")
        other = 1 - lax.axis_index("ty")
        source = self.sources[index]
        if self.by_rows:
            rows = pl.ds(pl.multiple_of(plane * self.size, self.size), self.size)
            columns = source.shape[1] // 2
            part = source.at[rows, pl.ds(pl.multiple_of(other * columns, columns), columns)]
            offset = sum(item.shape[1] // 2 for item in self.sources[:index])
            target = self.quarter(plane).at[:, offset : offset + columns]
        else:
            start = pl.multiple_of(other * (source.shape[0] // 2) + plane * self.size, self.size)
            part = source.at[pl.ds(start, self.size)]
            target = self.quarter(plane)
        return self.wires.copy(self.base + SHARE_X, index, part, target, side)

    def local(self, index):
        mine = lax.axis_index("ty")
        source = self.held[index]
        if self.by_rows:
            columns = source.shape[1] // 2
            offset = sum(item.shape[1] // 2 for item in self.sources[:index])
            part = source.at[:, pl.ds(pl.multiple_of(mine * columns, columns), columns)]
            target = self.whole.at[: self.whole.shape[0] // 2, offset : offset + columns]
        else:
            half = source.shape[0] // 2
            part = source.at[pl.ds(pl.multiple_of(mine * half, half), half)]
            target = self.whole.at[:, : self.whole.shape[1] // 2]
        return pltpu.make_async_copy(part, target, self.local_sems.at[index])

    def over(self, index):
        near, far = planes()
        plane = lax.axis_index("dp")
        owner = lax.rem(plane + 2, 4) if index == 2 else plane
        place = self.quarter(owner)
        return self.wires.copy(
            self.base + SHARE_Z, index, place, place, far if index == 0 else near
        )

    def start(self):
        for index in range(len(self.sources)):
            self.cross(index).start()
            self.local(index).start()

    def middle(self):
        for index in range(len(self.sources)):
            self.cross(index).wait_recv()
        self.over(0).start()
        self.over(1).start()

    def late(self):
        self.over(0).wait_recv()
        self.over(2).start()

    def close(self):
        self.over(1).wait_recv()
        self.over(2).wait_recv()
        for index in range(3):
            self.over(index).wait_send()
        for index in range(len(self.sources)):
            self.cross(index).wait_send()
            self.local(index).wait()


class Spread(Share):
    def __init__(self, wires, base, source, whole, local_sems, quarter):
        super().__init__(wires, base, (source,), whole, True, local_sems)
        self.piece = quarter

    def over(self, index):
        if index == 2:
            return super().over(index)
        near, far = planes()
        return self.wires.copy(
            self.base + SHARE_Z,
            index,
            self.piece,
            self.quarter(lax.axis_index("dp")),
            far if index == 0 else near,
        )

    def own(self):
        return pltpu.make_async_copy(
            self.piece, self.quarter(lax.axis_index("dp")), self.local_sems.at[1]
        )

    def start(self):
        self.over(0).start()
        self.over(1).start()
        self.local(0).start()
        self.own().start()

    def close(self):
        self.over(1).wait_recv()
        self.over(2).wait_recv()
        for index in range(3):
            self.over(index).wait_send()
        self.local(0).wait()
        self.own().wait()


FOLD_NEAR, FOLD_FAR, FOLD_X = 0, 1, 2
FOLD_KINDS = 3


class Fold:
    def __init__(self, wires, base, tiles, bufs, mine, theirs, first=None):
        self.wires, self.base, self.tiles, self.mine, self.theirs = (
            wires,
            base,
            tiles,
            mine,
            theirs,
        )
        self.first = tiles if first is None else first
        self.near_recv, self.far_recv = bufs
        plane = lax.axis_index("dp")
        self.low = lax.rem(plane, 2)
        self.high = lax.div(plane, 2)

    def index(self, half, high, low):
        return half * 4 + 2 * high + low

    def near(self, half, high):
        source = self.first.at[self.index(half, high, 1 - self.low)]
        slot = 2 * half + high
        return self.wires.copy(
            self.base + FOLD_NEAR, slot, source, self.near_recv.at[slot], planes()[0]
        )

    def far(self, half):
        source = self.tiles.at[self.index(half, 1 - self.high, self.low)]
        return self.wires.copy(
            self.base + FOLD_FAR, half, source, self.far_recv.at[half], planes()[1]
        )

    def cross(self):
        source = self.tiles.at[self.index(1, self.high, self.low)]
        return self.wires.copy(self.base + FOLD_X, 0, source, self.theirs, neighbours()[0])

    def start(self):
        for half in range(2):
            for high in range(2):
                self.near(half, high).start()

    def add(self, half, high):
        self.near(half, high).wait_recv()
        at = self.index(half, high, self.low)
        came = self.near_recv[2 * half + high].astype(F32)
        self.tiles[at] = (self.tiles[at].astype(F32) + came).astype(B16)

    def middle(self):
        @pl.loop(0, 2)
        def _(turn):
            half = 1 - turn
            self.add(half, 1 - self.high)
            self.far(half).start()

        @pl.loop(0, 2)
        def _(half):
            self.add(half, self.high)

    def late(self):
        at = self.index(1, self.high, self.low)
        self.far(1).wait_recv()
        self.tiles[at] = (self.tiles[at].astype(F32) + self.far_recv[1].astype(F32)).astype(B16)
        self.cross().start()
        self.far(0).wait_recv()
        at = self.index(0, self.high, self.low)
        self.mine[...] = self.tiles[at].astype(F32) + self.far_recv[0].astype(F32)

    def close(self):
        self.cross().wait_recv()
        for half in range(2):
            for high in range(2):
                self.near(half, high).wait_send()
            self.far(half).wait_send()
        self.cross().wait_send()


def fold_scratch(rows, columns):
    return [pltpu.VMEM((4, rows, columns), B16), pltpu.VMEM((2, rows, columns), B16)]


def turn_tile(step):
    low = lax.rem(lax.axis_index("dp"), 2)
    kept_now = lax.div(step, 4)
    low = kept_now * low + (1 - kept_now) * (1 - low)
    return lax.div(lax.rem(step, 4), 2) * 4 + 2 * lax.rem(step, 2) + low


class Reduce:
    def __init__(self, wires, rows_ref, weight_ref, transposed, bufs):
        self.wires, self.rows_ref, self.weight_ref, self.transposed = (
            wires,
            rows_ref,
            weight_ref,
            transposed,
        )
        (
            self.sibling_send,
            self.sibling_recv,
            self.kept_ref,
            self.out,
            self.corner_recv,
            self.x_recv,
            self.y_recv,
        ) = bufs
        self.rows = rows_ref.shape[1]
        self.width = (weight_ref.shape[0] if transposed else weight_ref.shape[1]) // 2
        self.count = self.width // CHUNK

    def product(self, block, chunk, half):
        left = self.rows_ref[block : block + 2].reshape(2 * self.rows, self.rows_ref.shape[2])
        at = lanes(chunk, half, self.width)
        if self.transposed:
            return rows_dot(left, self.weight_ref[at, :])
        return jnp.dot(left, self.weight_ref[:, at], preferred_element_type=F32)

    def sibling(self, chunk, half):
        return self.wires.copy(
            SIBLING + half * (REDUCE_KINDS - 1),
            chunk,
            self.sibling_send.at[lax.rem(chunk, 2), half],
            self.sibling_recv.at[chunk, half],
            neighbours()[2],
        )

    def corner(self, chunk, device):
        return self.wires.copy(
            CORNER, chunk, self.out.at[2, chunk], self.corner_recv.at[chunk], device
        )

    def final_x(self, chunk):
        return self.wires.copy(
            FINAL_X, chunk, self.out.at[0, chunk], self.x_recv.at[chunk], neighbours()[0]
        )

    def final_y(self, chunk):
        return self.wires.copy(
            FINAL_Y, chunk, self.out.at[1, chunk], self.y_recv.at[chunk], neighbours()[1]
        )

    def give(self, chunk):
        @pl.loop(0, 2)
        def _(turn):
            half = 1 - turn
            self.sibling_send[lax.rem(chunk, 2), half] = self.product(2, chunk, half).astype(B16)
            self.sibling(chunk, half).start()

    def take(self, chunk):
        rows = self.rows
        even = lax.rem(chunk, 2) == 0
        side, across, _ = neighbours()

        @pl.loop(0, 2)
        def _(turn):
            half = 1 - turn
            own = self.product(0, chunk, half)
            self.sibling(chunk, half).wait_recv()
            total = own + self.sibling_recv[chunk, half].astype(F32)

            @pl.when(half == 1)
            def _():
                self.out[2, chunk] = total[rows:].astype(B16)
                self.out[0, chunk] = total[:rows].astype(B16)

                @pl.when(even)
                def _():
                    self.corner(chunk, side).start()
                    self.final_x(chunk).start()

                @pl.when(jnp.logical_not(even))
                def _():
                    self.corner(chunk, across).start()

            @pl.when(half == 0)
            def _():
                self.kept_ref[chunk] = total[:rows]
                self.out[1, chunk] = total[rows:].astype(B16)

                @pl.when(jnp.logical_not(even))
                def _():
                    self.final_y(chunk).start()

    def start(self, between=(lambda: None, lambda: None)):
        self.give(0)
        self.take(0)
        self.give(1)
        self.take(1)
        between[0]()

        @pl.loop(2, self.count)
        def _(chunk):
            for half in range(2):
                self.sibling(chunk - 2, half).wait_send()
            self.give(chunk)
            self.take(chunk)

        between[1]()

    def middle(self):
        @pl.loop(0, self.count)
        def _(chunk):
            even = lax.rem(chunk, 2) == 0
            self.corner(chunk, neighbours()[0]).wait_recv()
            came = self.corner_recv[chunk].astype(F32)

            @pl.when(even)
            def _():
                self.out[1, chunk] = (self.out[1, chunk].astype(F32) + came).astype(B16)
                self.final_y(chunk).start()

            @pl.when(jnp.logical_not(even))
            def _():
                self.out[0, chunk] = (self.out[0, chunk].astype(F32) + came).astype(B16)
                self.final_x(chunk).start()

    def total(self, chunk):
        self.final_x(chunk).wait_recv()
        self.final_y(chunk).wait_recv()
        return (
            self.kept_ref[chunk] + self.x_recv[chunk].astype(F32) + self.y_recv[chunk].astype(F32)
        )

    def close(self):
        @pl.loop(self.count - 2, self.count)
        def _(chunk):
            for half in range(2):
                self.sibling(chunk, half).wait_send()

        @pl.loop(0, self.count)
        def _(chunk):
            self.corner(chunk, neighbours()[0]).wait_send()
            self.final_x(chunk).wait_send()
            self.final_y(chunk).wait_send()


def reduce_scratch(rows, width):
    count = width // CHUNK
    return [
        pltpu.VMEM((2, 2, 2 * rows, CHUNK), B16),
        pltpu.VMEM((count, 2, 2 * rows, CHUNK), B16),
        pltpu.VMEM((count, rows, CHUNK), F32),
        pltpu.VMEM((3, count, rows, CHUNK), B16),
        pltpu.VMEM((count, rows, CHUNK), B16),
        pltpu.VMEM((count, rows, CHUNK), B16),
        pltpu.VMEM((count, rows, CHUNK), B16),
    ]


def gather_scratch(rows, width):
    count = width // CHUNK
    return [pltpu.VMEM((count, rows, CHUNK), B16), pltpu.SemaphoreType.DMA((count,))]


def wire_scratch(kinds, count):
    return [pltpu.SemaphoreType.DMA((kinds, count))] * 2


IN_VMEM = pl.BlockSpec(memory_space=pltpu.VMEM)
IN_ANY = pl.BlockSpec(memory_space=pl.ANY)
VMEM_MOST = 60 * 1024 * 1024


def remote_params(number):
    return pltpu.CompilerParams(
        collective_id=number, has_side_effects=True, vmem_limit_bytes=VMEM_MOST
    )


def cost(flops, size):
    return pl.CostEstimate(flops=flops, bytes_accessed=size, transcendentals=0)


def shape(dims, kind=B16):
    return jax.ShapeDtypeStruct(dims, kind)


def cut(own, block_ref):
    for chunk in range(own.shape[0]):
        own[chunk] = block_ref[:, chunk * CHUNK : (chunk + 1) * CHUNK]


def open_kernel(
    tokens_ref,
    query_ref,
    key_ref,
    value_ref,
    out_ref,
    gains_ref,
    seg_ref,
    rate_ref,
    gains_all_ref,
    starts_ref,
    cosine_ref,
    sine_ref,
    whole_ref,
    project_ref,
    branch_ref,
    *scratch,
):
    own, gather_sem, send_sems, recv_sems, project_sem, branch_sem = scratch[:6]
    gains_recv, seg_recv, seg_all = scratch[6:]
    width = gains_ref.shape[1]
    length = seg_ref.shape[1]
    cut(own, tokens_ref)
    greet(neighbours() + planes())
    wires = Wires(send_sems, recv_sems)
    gather = Gather(wires, 0, whole_ref, own, gather_sem, 2)
    base = GATHER_KINDS + 2 * SHARE_KINDS
    side = neighbours()[0]
    gains = wires.copy(base, 0, gains_ref, gains_recv, side)
    segs = wires.copy(base, 1, seg_ref, seg_recv, side)
    shares = [
        Share(wires, GATHER_KINDS, (query_ref, key_ref, value_ref), project_ref, True, project_sem),
        Share(wires, GATHER_KINDS + SHARE_KINDS, (out_ref,), branch_ref, False, branch_sem),
    ]
    gains.start()
    segs.start()
    shares[0].start()
    shares[1].start()

    @pl.loop(0, gather.count)
    def _(chunk):
        gather.send(chunk)

    gains.wait()
    segs.wait()
    gains_all_ref[:, :width] = gains_ref[...]
    gains_all_ref[:, width:] = gains_recv[...]
    mine = lax.rem(lax.axis_index("ty") + lax.div(lax.axis_index("tx"), 2), 2)
    seg_all[pl.ds(mine, 1)] = seg_ref[...].astype(F32)[None]
    seg_all[pl.ds(1 - mine, 1)] = seg_recv[...].astype(F32)[None]

    shares[0].middle()
    shares[1].middle()

    @pl.loop(0, 2)
    def _(seq):
        for low in range(0, length, 128):
            here = stand(seg_all[seq, :, low : low + 128])
            before = jnp.zeros((128, 128), F32)
            for other in range(0, length, 128):
                before += (seg_all[seq, :, other : other + 128] < here).astype(F32)
            start = jnp.sum(before, axis=1, keepdims=True)
            at = slice(low, low + 128)
            starts_ref[seq, at, :] = start.astype(jnp.int32)
            row = lax.broadcasted_iota(jnp.int32, (128, 128), 0) + low
            lane = lax.broadcasted_iota(jnp.int32, (128, 128), 1)
            angle = (row.astype(F32) - start) * rate_ref[...]
            cosine_ref[seq, at, :] = jnp.cos(angle)
            sine = jnp.sin(angle)
            sine_ref[seq, at, :] = jnp.where(lane < 64, -sine, sine)

        @pl.when(seq == 0)
        def _():
            shares[0].late()
            shares[1].late()
            gather.relay(0, 2)

    gather.relay(2)
    gather.close()
    shares[0].close()
    shares[1].close()


def open_call(tokens, w_query, w_key, w_value, w_out, gains, seg_ids, rate, number):
    rows, width = tokens.shape
    columns = (w_query.shape[1] + w_key.shape[1] + w_value.shape[1]) // 2
    length = seg_ids.shape[1]
    return pl.pallas_call(
        open_kernel,
        out_shape=(
            shape((2, 2 * width), F32),
            shape((2, length, 1), jnp.int32),
            shape((2, length, 128), F32),
            shape((2, length, 128), F32),
            shape((4, rows, 2 * width)),
            shape((2 * width, columns)),
            shape((w_out.shape[0] // 2, 2 * width)),
        ),
        in_specs=[IN_VMEM] * 8,
        out_specs=(IN_VMEM,) * 4 + (IN_ANY,) * 3,
        scratch_shapes=gather_scratch(rows, width)
        + wire_scratch(GATHER_KINDS + 2 * SHARE_KINDS + 1, width // CHUNK)
        + [
            pltpu.SemaphoreType.DMA((3,)),
            pltpu.SemaphoreType.DMA((1,)),
            pltpu.VMEM((2, width), F32),
            pltpu.VMEM((1, length), jnp.int32),
            pltpu.VMEM((2, 1, length), F32),
        ],
        compiler_params=remote_params(number),
        cost_estimate=cost(0, 32 * rows * width),
    )(tokens, w_query, w_key, w_value, w_out, gains, seg_ids, rate)


def front_kernel(
    most,
    whole_ref,
    project_ref,
    gain_ref,
    starts_ref,
    cosine_ref,
    sine_ref,
    query_gain_ref,
    key_gain_ref,
    grad_ref,
    down_ref,
    gate_in_ref,
    first_ref,
    scale_ref,
    projected_ref,
    mixed_ref,
    query_ref,
    key_ref,
    value_ref,
    log_ref,
    grad_whole_ref,
    back_ref,
    gate_ref,
    *scratch,
):
    own, gather_sem, send_sems, recv_sems, back_sem, tokens, firsts, tile_sem = scratch
    core = lax.rem(lax.axis_index("tx"), 2)
    cut(own, grad_ref)
    rows = whole_ref.shape[1]

    def spot(ref, tile):
        at = pl.ds(pl.multiple_of(lax.rem(tile, rows // BLOCK) * BLOCK, BLOCK), BLOCK)
        return ref.at[lax.div(tile, rows // BLOCK), at, :]

    def fetch(tile):
        slot = lax.rem(tile, 2)
        return pltpu.make_async_copy(spot(whole_ref, tile), tokens.at[slot], tile_sem.at[0, slot])

    def store(tile):
        slot = lax.rem(tile, 2)
        return pltpu.make_async_copy(firsts.at[slot], spot(first_ref, tile), tile_sem.at[1, slot])

    fetch(0).start()
    greet(neighbours() + planes())
    wires = Wires(send_sems, recv_sems)
    gather = Gather(wires, 0, grad_whole_ref, own, gather_sem, 0)
    back = Share(wires, GATHER_KINDS, (down_ref,), back_ref, False, back_sem)
    size, columns = gate_ref.shape
    gate = wires.copy(
        GATHER_KINDS + SHARE_KINDS,
        0,
        gate_in_ref.at[
            pl.ds(pl.multiple_of(lax.axis_index("dp") * size, size), size),
            pl.ds(pl.multiple_of((1 - lax.axis_index("ty")) * columns, columns), columns),
        ],
        gate_ref,
        neighbours()[0],
    )
    back.start()
    gate.start()

    @pl.loop(0, gather.count)
    def _(chunk):
        gather.send(chunk)

    count = 4 * rows // BLOCK

    @pl.loop(0, count)
    def _(tile):
        slot = lax.rem(tile, 2)
        block = lax.div(tile, rows // BLOCK)
        at = pl.ds(pl.multiple_of(lax.rem(tile, rows // BLOCK) * BLOCK, BLOCK), BLOCK)

        @pl.when(tile < count - 1)
        def _():
            fetch(tile + 1).start()

        fetch(tile).wait()

        @pl.when(tile >= 2)
        def _():
            store(tile - 2).wait()

        value = tokens[slot].astype(F32)
        scale = lax.rsqrt(jnp.mean(value * value, axis=1, keepdims=True) + EPS)
        first = (value * scale * gain_ref[...]).astype(B16)
        firsts[slot] = first
        store(tile).start()
        projected_ref[block, at, :] = jnp.dot(
            first, project_ref[...], preferred_element_type=F32
        )

        @pl.when(block == 0)
        def _():
            scale_ref[at, :] = jnp.broadcast_to(scale, (BLOCK, 128))

        @pl.when(tile == count // 2)
        def _():
            back.middle()

    fixed_refs = (starts_ref, cosine_ref, sine_ref, query_gain_ref, key_gain_ref)
    saved_refs = (query_ref, key_ref, value_ref, log_ref)

    @pl.loop(0, 2)
    def _(seq):
        def between(turn):
            @pl.when(seq == 0)
            def _():
                if turn == 0:
                    back.late()
                gather.relay(turn, turn + 1)

        attend_sequence(
            core, seq, most, projected_ref, fixed_refs, mixed_ref, saved_refs, between
        )

    for tile in range(count - 2, count):
        store(tile).wait()
    gather.close()
    back.close()
    gate.wait()


def front_call(whole, w_project, gain, fixed_args, most, cotangent, w_down, w_gate, number):
    starts, cosine, sine, query_gain, key_gain = fixed_args
    rows, width = cotangent.shape
    length = cosine.shape[1]
    depth = query_gain.shape[1]
    columns = w_project.shape[1]
    heads = columns // depth - 2
    outs = (
        shape((4, rows, 2 * width)),
        shape((rows, 128), F32),
        shape((4, rows, columns), F32),
        shape((4, rows, heads * depth)),
        shape((2, length, heads * depth)),
        shape((2, length, depth)),
        shape((2, length, depth)),
        shape((2, heads, length, 1), F32),
        shape((4, rows, 2 * width)),
        shape((w_down.shape[0] // 2, 2 * width)),
        shape((width // 4, w_gate.shape[1] // 2)),
    )
    return pl.pallas_call(
        lambda *refs: front_kernel(most, *refs),
        out_shape=outs,
        in_specs=[IN_ANY] + [IN_VMEM] * 10,
        out_specs=[IN_ANY] + [IN_VMEM] * 7 + [IN_ANY] * 3,
        scratch_shapes=gather_scratch(rows, width)
        + wire_scratch(GATHER_KINDS + SHARE_KINDS + 1, width // CHUNK)
        + [
            pltpu.SemaphoreType.DMA((1,)),
            pltpu.VMEM((2, BLOCK, 2 * width), B16),
            pltpu.VMEM((2, BLOCK, 2 * width), B16),
            pltpu.SemaphoreType.DMA((2, 2)),
        ],
        compiler_params=remote_params(number),
        cost_estimate=cost(16 * rows * width * columns, 64 * rows * width),
    )(whole, w_project, gain, *fixed_args, cotangent, w_down, w_gate)


def branch_kernel(
    rows_in_ref,
    weight_in_ref,
    input_in_ref,
    up_in_ref,
    gate_in_ref,
    quarter_ref,
    residual_ref,
    whole_ref,
    up_ref,
    gate_ref,
    *scratch,
):
    bufs = scratch[:7]
    own, gather_sem, send_sems, recv_sems, up_sem = scratch[7:12]
    held, load_sem, gate_sem = scratch[12:17], scratch[17], scratch[18]
    rows_ref, weight_ref, input_ref, up_held, gate_held = held
    loads = Loads(
        (rows_in_ref, weight_in_ref, input_in_ref, up_in_ref, gate_in_ref), held, load_sem
    )
    loads.start()
    width = input_ref.shape[1]
    greet(neighbours() + planes())
    wires = Wires(send_sems, recv_sems)
    reduce = Reduce(wires, rows_ref, weight_ref, False, bufs)
    gather = Gather(wires, REDUCE_KINDS, whole_ref, own, gather_sem, 0)
    up = Share(
        wires, REDUCE_KINDS + GATHER_KINDS, (up_in_ref,), up_ref, True, up_sem, (up_held,)
    )
    gate = Spread(
        wires,
        REDUCE_KINDS + GATHER_KINDS + SHARE_KINDS,
        gate_held,
        gate_ref,
        gate_sem,
        quarter_ref,
    )
    loads.wait(0, 2)

    def between():
        loads.wait(2, 5)
        up.start()
        gate.start()

    reduce.start((between, gate.late))
    reduce.middle()
    up.middle()

    @pl.loop(0, width // CHUNK)
    def _(chunk):
        at = lanes(chunk, 0, width)
        residual = input_ref[:, at].astype(F32) + reduce.total(chunk)
        residual_ref[:, at] = residual
        own[chunk] = residual.astype(B16)
        gather.send(chunk)

    up.late()
    gather.relay()
    gather.close()
    up.close()
    gate.close()
    reduce.close()


def branch_call(rows, weight, inputs, w_up, w_gate, quarter, number):
    height, width = inputs.shape
    count = width // CHUNK
    loaded = (rows, weight, inputs, w_up, w_gate)
    return pl.pallas_call(
        branch_kernel,
        out_shape=(
            shape((height, width), F32),
            shape((4, height, 2 * width)),
            shape((2 * width, w_up.shape[1] // 2)),
            shape((2 * width, w_gate.shape[1] // 2)),
        ),
        in_specs=[IN_ANY] * 6,
        out_specs=(IN_VMEM, IN_ANY, IN_ANY, IN_ANY),
        scratch_shapes=reduce_scratch(height, width)
        + gather_scratch(height, width)
        + wire_scratch(REDUCE_KINDS + GATHER_KINDS + 2 * SHARE_KINDS, count)
        + [pltpu.SemaphoreType.DMA((1,))]
        + load_scratch(loaded)
        + [pltpu.SemaphoreType.DMA((2,))],
        compiler_params=remote_params(number),
        cost_estimate=cost(16 * height * rows.shape[2] * width, 64 * height * width),
    )(*loaded, quarter)


def units_kernel(
    whole_ref, grad_ref, gates_ref, uppers_ref, back_ref, gain_ref, second_ref, hidden_ref, unit_ref, scale_ref, stats_ref
):
    units = hidden_ref.shape[1]
    value = whole_ref[...].astype(F32)
    scale = lax.rsqrt(jnp.mean(value * value, axis=1, keepdims=True) + EPS)
    second = (value * scale * gain_ref[...]).astype(B16)
    second_ref[...] = second
    scale_ref[...] = jnp.broadcast_to(scale, scale_ref.shape)
    total = jnp.zeros((value.shape[0], 1), F32)
    for low in range(0, units, CHUNK):
        at = slice(low, low + CHUNK)
        beside = slice(units + low, units + low + CHUNK)
        gate = jnp.dot(second, gates_ref[:, at], preferred_element_type=F32)
        upper = jnp.dot(second, uppers_ref[:, at], preferred_element_type=F32)
        hidden_grad = rows_dot(grad_ref[...], back_ref[at, :])
        sigma = jax.nn.sigmoid(gate)
        passed = gate * sigma
        hidden_ref[:, at] = (passed * upper).astype(B16)
        gate_grad = (hidden_grad * upper * (sigma + passed * (1.0 - sigma))).astype(B16)
        up_grad = (hidden_grad * passed).astype(B16)
        unit_ref[:, at] = gate_grad
        unit_ref[:, beside] = up_grad
        total += jnp.sum(
            gate_grad.astype(F32) * gate + up_grad.astype(F32) * upper, axis=1, keepdims=True
        )
    stats_ref[...] = jnp.zeros_like(stats_ref)
    for tile in range(stats_ref.shape[0]):
        put_stats(stats_ref, tile, total[tile * BLOCK : (tile + 1) * BLOCK])


def units_call(whole, grad, w_gates, w_uppers, w_back, gain):
    tokens, width = whole.shape
    units = w_back.shape[0]
    size = 2 * BLOCK
    tiles = tokens // size

    def tile(columns):
        return pl.BlockSpec((size, columns), lambda i: (i, 0))

    def all_of(item):
        return pl.BlockSpec(item.shape, lambda i: (0, 0))

    return pl.pallas_call(
        units_kernel,
        out_shape=(
            shape((tokens, width)),
            shape((tokens, units)),
            shape((tokens, 2 * units)),
            shape((tokens, 128), F32),
            shape((2 * tiles, 8, 128), F32),
        ),
        grid=(tiles,),
        in_specs=[tile(width), tile(width)]
        + [all_of(item) for item in (w_gates, w_uppers, w_back, gain)],
        out_specs=(
            tile(width),
            tile(units),
            tile(2 * units),
            tile(128),
            pl.BlockSpec((2, 8, 128), lambda i: (i, 0, 0)),
        ),
        compiler_params=pltpu.CompilerParams(vmem_limit_bytes=VMEM_MOST),
        cost_estimate=cost(6 * tokens * width * units, 20 * tokens * width // 2),
    )(whole, grad, w_gates, w_uppers, w_back, gain)


class Loads:
    def __init__(self, sources, targets, sems):
        self.copies = [
            pltpu.make_async_copy(source, target, sems.at[index])
            for index, (source, target) in enumerate(zip(sources, targets))
        ]

    def start(self):
        for copy in self.copies:
            copy.start()

    def wait(self, low, high):
        for copy in self.copies[low:high]:
            copy.wait()


def load_scratch(items):
    return [pltpu.VMEM(item.shape, item.dtype) for item in items] + [
        pltpu.SemaphoreType.DMA((len(items),))
    ]


class Stats:
    def __init__(self, wires, base, ref, recv):
        self.ref, self.recv = ref, recv
        side, across, core = neighbours()
        self.hops = (
            lambda: wires.copy(base, 0, ref.at[4:8], recv.at[0:4], core),
            lambda: wires.copy(base, 1, ref.at[2:4], recv.at[4:6], across),
            lambda: wires.copy(base, 2, ref.at[0:2], recv.at[6:8], side),
        )
        self.spans = ((4, 0), (2, 4), (2, 6))

    def start(self, hop):
        self.hops[hop]().start()

    def finish(self, hop):
        self.hops[hop]().wait()
        size, at = self.spans[hop]
        self.ref[0:size] = self.ref[0:size] + self.recv[at : at + size]

    def step(self, hop):
        self.finish(hop)
        self.start(hop + 1)


def pull_columns(stats_ref, scale_ref, column_ref, width):
    for part in range(scale_ref.shape[0] // 128):
        at = slice(part * 128, (part + 1) * 128)
        scale = scale_ref[at, :]
        column_ref[at, :] = (
            stand(stats_ref[part // 2, part % 2 : part % 2 + 1, :]) * scale * scale / (2 * width)
        )


def pulled(reduce, chunk, refs, column_ref):
    scale_ref, value_ref, gain_ref, base_ref = refs
    at = lanes(chunk, 0, value_ref.shape[1])
    upstream = reduce.total(chunk)
    value = value_ref[:, at].astype(F32)
    scale = scale_ref[:, 0:1]
    back = scale * gain_ref[:, at] * upstream - value * column_ref[:, 0:1]
    return at, base_ref[:, at].astype(F32) + back, upstream * value * scale


def tile_columns(tile):
    return pl.ds(pl.multiple_of(tile * BLOCK, BLOCK), BLOCK)


SPLIT = 512


def middle_kernel(
    rows_in_ref,
    gates_in_ref,
    uppers_in_ref,
    value_in_ref,
    base_in_ref,
    branch_in_ref,
    mixed_in_ref,
    stats_in_ref,
    scale_ref,
    gain_ref,
    down_in_ref,
    second_ref,
    result_ref,
    gain_grad_ref,
    upstream_ref,
    out_ref,
    whole_ref,
    rest_ref,
    *refs,
):
    ends, scratch = refs[:6], refs[6:]
    bufs = scratch[:7]
    stats_ref, stats_recv, column_ref, send_sems, recv_sems, own, gather_sem = scratch[7:14]
    stream, stream_sem, down_sem, stage, stage_sem, upstream = scratch[14:20]
    tiles = scratch[20:29]
    weight_ref, rows_ref, value_ref, base_ref, branch_ref, mixed_ref = scratch[29:35]
    load_sem = scratch[35]
    rows, width = value_ref.shape
    columns = rows_ref.shape[2]
    half = tiles[0].shape[2]
    parts = [down_in_ref.at[:, :, index * half : (index + 1) * half] for index in range(2)]
    downs = [
        pltpu.make_async_copy(parts[index], tiles[3 * index], down_sem.at[index])
        for index in range(2)
    ]
    units = gates_in_ref.shape[1]
    loads = Loads(
        (
            rows_in_ref,
            gates_in_ref,
            uppers_in_ref,
            value_in_ref,
            base_in_ref,
            branch_in_ref,
            mixed_in_ref,
        ),
        (
            rows_ref,
            weight_ref.at[:, :units],
            weight_ref.at[:, units:],
            value_ref,
            base_ref,
            branch_ref,
            mixed_ref,
        ),
        load_sem,
    )

    def fetch(ref, step, tile):
        slot = lax.rem(step, 2)
        return pltpu.make_async_copy(
            ref.at[:, :, tile_columns(tile)], stream.at[slot], stream_sem.at[slot]
        )

    loads.start()
    for load in downs:
        load.start()
    fetch(second_ref, 0, turn_tile(0)).start()
    stats_ref[...] = stats_in_ref[...]
    greet(neighbours() + planes())
    wires = Wires(send_sems, recv_sems)
    base = REDUCE_KINDS + 1 + GATHER_KINDS
    folds = [
        Fold(
            wires,
            base + index * FOLD_KINDS,
            tiles[3 * index],
            tiles[3 * index + 1 : 3 * index + 3],
            ends[2 * index],
            ends[2 * index + 1],
            parts[index] if index < 2 else None,
        )
        for index in range(3)
    ]
    stats = Stats(wires, REDUCE_KINDS, stats_ref, stats_recv)
    folds[0].start()
    folds[1].start()
    stats.start(0)
    reduce = Reduce(wires, rows_ref, weight_ref, True, bufs)
    loads.wait(0, 3)
    reduce.start((lambda: stats.step(0), lambda: stats.step(1)))
    made = folds[2]

    def store(step):
        slot = lax.rem(step, 2)
        return pltpu.make_async_copy(
            stage.at[slot], rest_ref.at[turn_tile(step)], stage_sem.at[slot]
        )

    def make(step):
        slot = lax.rem(step, 2)

        @pl.when(step < 7)
        def _():
            fetch(second_ref, step + 1, turn_tile(step + 1)).start()

        fetch(second_ref, step, turn_tile(step)).wait()

        @pl.when(step >= 2)
        def _():
            store(step - 2).wait()

        left = stream[slot].reshape(4 * rows, BLOCK)
        flat = rows_ref[...].reshape(4 * rows, columns)
        made.tiles[turn_tile(step)] = weight_grad(left, flat[:, :SPLIT]).astype(B16)
        for low in range(SPLIT, columns, SPLIT):
            stage[slot, :, low - SPLIT : low] = weight_grad(
                left, flat[:, low : low + SPLIT]
            ).astype(B16)
        store(step).start()

    @pl.loop(0, 4)
    def _(step):
        make(step)
        made.near(lax.div(step, 2), lax.rem(step, 2)).start()

    reduce.middle()
    stats.finish(2)
    pull_columns(stats_ref, scale_ref, column_ref, width)

    @pl.loop(4, 8)
    def _(step):
        make(step)

    for load in downs:
        load.wait()
    folds[0].middle()
    folds[1].middle()
    loads.wait(3, 7)
    gather = Gather(wires, REDUCE_KINDS + 1, whole_ref, own, gather_sem)

    @pl.loop(0, width // CHUNK)
    def _(chunk):
        at, result, share = pulled(
            reduce, chunk, (scale_ref, value_ref, gain_ref, base_ref), column_ref
        )
        result_ref[:, at] = result
        own[chunk] = result.astype(B16)
        gather.send(chunk)
        gain_grad_ref[:, at] = jnp.sum(share, axis=0, keepdims=True)

    for step in (6, 7):
        store(step).wait()
    folds[2].middle()
    gather.relay()
    folds[0].late()
    folds[1].late()
    gather.close()
    folds[2].late()
    fetch(whole_ref, 0, 0).start()
    upstream[...] = jnp.zeros_like(upstream)

    @pl.loop(0, 8)
    def _(tile):
        @pl.when(tile < 7)
        def _():
            fetch(whole_ref, tile + 1, tile + 1).start()

        fetch(whole_ref, tile, tile).wait()
        left = stream[lax.rem(tile, 2)].reshape(4 * rows, BLOCK)
        upstream[...] += rows_dot(left, branch_ref[:, tile_columns(tile)])
        out_ref[tile] = weight_grad(left, mixed_ref[...].reshape(4 * rows, -1)).astype(B16)

    upstream_ref[...] = upstream[...].astype(B16).reshape(upstream_ref.shape)
    for fold in folds:
        fold.close()
    reduce.close()


def middle_call(
    rows, w_gates, w_uppers, stats, scale, value, gain, base, down, second, w_branch, mixed, number
):
    height, width = value.shape
    count = width // CHUNK
    columns = rows.shape[2]
    quarter, units = down.shape[1:]
    heads = mixed.shape[2]
    sizes = (units // 2, units // 2, SPLIT)
    ends, tiles = [], []
    for size in sizes:
        ends += [shape((quarter, size), F32), shape((quarter, size))]
        tiles += [pltpu.VMEM((8, quarter, size), B16)] + fold_scratch(quarter, size)
    loaded = (rows, w_gates, w_uppers, value, base, w_branch, mixed)
    return pl.pallas_call(
        middle_kernel,
        out_shape=[
            shape((height, width), F32),
            shape((1, width), F32),
            shape((4, height, heads)),
            shape((8, quarter, heads)),
            shape((4, height, 2 * width)),
            shape((8, quarter, columns - SPLIT)),
        ]
        + ends,
        in_specs=[IN_ANY] * 7 + [IN_VMEM] * 3 + [IN_ANY] * 2,
        out_specs=[IN_VMEM] * 4 + [IN_ANY] * 2 + [IN_VMEM, IN_ANY] * 3,
        scratch_shapes=reduce_scratch(height, width)
        + [
            pltpu.VMEM((8, 8, 128), F32),
            pltpu.VMEM((8, 8, 128), F32),
            pltpu.VMEM((height, 128), F32),
        ]
        + wire_scratch(REDUCE_KINDS + 1 + GATHER_KINDS + 3 * FOLD_KINDS, count)
        + gather_scratch(height, width)
        + [
            pltpu.VMEM((2, 4, height, BLOCK), B16),
            pltpu.SemaphoreType.DMA((2,)),
            pltpu.SemaphoreType.DMA((2,)),
            pltpu.VMEM((2, quarter, columns - SPLIT), B16),
            pltpu.SemaphoreType.DMA((2,)),
            pltpu.VMEM((4 * height, heads), F32),
        ]
        + tiles
        + [pltpu.VMEM((2 * width, columns), B16)]
        + load_scratch((rows,) + loaded[3:])[:-1]
        + [pltpu.SemaphoreType.DMA((len(loaded),))],
        compiler_params=remote_params(number),
        cost_estimate=cost(48 * height * units * width, 64 * height * width),
    )(*loaded, stats, scale, gain, down, second)


def last_kernel(
    rows_in_ref,
    weight_in_ref,
    value_in_ref,
    base_in_ref,
    stats_in_ref,
    scale_ref,
    gain_ref,
    extra_ref,
    out_in_ref,
    first_ref,
    result_ref,
    totals_ref,
    out_mine_ref,
    out_theirs_ref,
    project_mine_ref,
    project_theirs_ref,
    *scratch,
):
    bufs = scratch[:7]
    stats_ref, stats_recv, column_ref, send_sems, recv_sems = scratch[7:12]
    out_ref, project_ref, whole, sums_ref, sums_recv, load_sem = scratch[12:18]
    out_bufs, project_bufs = scratch[18:20], scratch[20:22]
    rows_ref, weight_ref, value_ref, base_ref = scratch[22:26]
    rows, width = value_ref.shape
    loads = Loads(
        (rows_in_ref, weight_in_ref, first_ref, value_in_ref, base_in_ref, out_in_ref),
        (rows_ref, weight_ref, whole, value_ref, base_ref, out_ref),
        load_sem,
    )
    loads.start()
    stats_ref[...] = stats_in_ref[...]
    sums_ref[...] = jnp.zeros_like(sums_ref)
    sums_ref[8] = extra_ref[0]
    sums_ref[9] = extra_ref[1]
    greet(neighbours() + planes())
    wires = Wires(send_sems, recv_sems)
    base = REDUCE_KINDS + 1
    out = Fold(wires, base, out_ref, out_bufs, out_mine_ref, out_theirs_ref, out_in_ref)
    project = Fold(
        wires, base + FOLD_KINDS, project_ref, project_bufs, project_mine_ref, project_theirs_ref
    )
    stats = Stats(wires, REDUCE_KINDS, stats_ref, stats_recv)
    stats.start(0)
    out.start()
    loads.wait(0, 2)

    def make(step):
        tile = turn_tile(step)
        left = whole[:, :, tile_columns(tile)].reshape(4 * rows, BLOCK)
        grad = weight_grad(left, rows_ref[...].reshape(4 * rows, rows_ref.shape[2]))
        project_ref[tile] = grad.astype(B16)
        share = jnp.sum(
            grad * weight_ref[tile_columns(tile), :].astype(F32), axis=1, keepdims=True
        )
        sums_ref[tile, 0:1, :] = lie(share[:128])
        sums_ref[tile, 1:2, :] = lie(share[128:])

    side, across, core = neighbours()
    near, far = planes()
    hops = [
        lambda hop=hop, device=device: wires.copy(
            base + 2 * FOLD_KINDS, hop, sums_ref, sums_recv.at[hop], device
        )
        for hop, device in enumerate((core, across, near, far))
    ]

    def add(hop):
        hops[hop]().wait()
        sums_ref[...] = sums_ref[...] + sums_recv[hop]

    reduce = Reduce(wires, rows_ref, weight_ref, True, bufs)
    reduce.start((lambda: stats.step(0), lambda: stats.step(1)))
    loads.wait(2, 3)

    @pl.loop(0, 4)
    def _(step):
        make(step)
        project.near(lax.div(step, 2), lax.rem(step, 2)).start()

    @pl.loop(4, 8)
    def _(step):
        make(step)

    hops[0]().start()
    loads.wait(3, 6)
    add(0)
    hops[1]().start()
    reduce.middle()
    out.middle()
    stats.finish(2)
    pull_columns(stats_ref, scale_ref, column_ref, width)
    add(1)
    hops[2]().start()
    project.middle()
    add(2)
    hops[3]().start()

    @pl.loop(0, width // CHUNK)
    def _(chunk):
        at, result, _ = pulled(
            reduce, chunk, (scale_ref, value_ref, gain_ref, base_ref), column_ref
        )
        result_ref[:, at] = result.astype(B16)

    out.late()
    project.late()
    add(3)
    move = wires.copy(base + 2 * FOLD_KINDS + 1, 0, sums_ref, sums_recv.at[4], side)
    move.start()
    move.wait()
    totals_ref[0:4] = sums_ref[0:4] + sums_recv[4, 4:8]
    totals_ref[4:8] = sums_ref[4:8] + sums_recv[4, 0:4]
    totals_ref[8] = sums_ref[8]
    totals_ref[9] = sums_recv[4, 8]
    totals_ref[10] = sums_ref[9] + sums_recv[4, 9]
    project.close()
    out.close()
    reduce.close()


def last_call(rows, weight, stats, scale, value, gain, base, extra, out, first, number):
    height, width = value.shape
    count = width // CHUNK
    quarter, branch = out.shape[1:]
    columns = rows.shape[2]
    return pl.pallas_call(
        last_kernel,
        out_shape=(
            shape((height, width)),
            shape((11, 8, 128), F32),
            shape((quarter, branch), F32),
            shape((quarter, branch)),
            shape((quarter, columns), F32),
            shape((quarter, columns)),
        ),
        in_specs=[IN_ANY] * 4 + [IN_VMEM] * 4 + [IN_ANY] * 2,
        out_specs=(IN_VMEM, IN_VMEM) + (IN_VMEM, IN_ANY) * 2,
        scratch_shapes=reduce_scratch(height, width)
        + [
            pltpu.VMEM((8, 8, 128), F32),
            pltpu.VMEM((8, 8, 128), F32),
            pltpu.VMEM((height, 128), F32),
        ]
        + wire_scratch(REDUCE_KINDS + 1 + 2 * FOLD_KINDS + 2, count)
        + [
            pltpu.VMEM((8, quarter, branch), B16),
            pltpu.VMEM((8, quarter, columns), B16),
            pltpu.VMEM((4, height, 2 * width), B16),
            pltpu.VMEM((10, 8, 128), F32),
            pltpu.VMEM((5, 10, 8, 128), F32),
            pltpu.SemaphoreType.DMA((6,)),
        ]
        + fold_scratch(quarter, branch)
        + fold_scratch(quarter, columns)
        + load_scratch((rows, weight, value, base))[:4],
        compiler_params=remote_params(number),
        cost_estimate=cost(32 * height * columns * width, 64 * height * width),
    )(rows, weight, value, base, stats, scale, gain, extra, out, first)


def back_kernel(
    most,
    query_gain_ref,
    key_gain_ref,
    *refs,
):
    operands, refs = refs[:12], refs[12:]
    rest_ref, refs = refs[0], refs[1:]
    output_ref, result_ref, stats_ref, gains_ref = refs[:4]
    ends, scratch = refs[4:8], refs[8:]
    bufs = scratch[:7]
    query_acc, key_acc, value_acc, send_sems, recv_sems, rest_sem = scratch[7:13]
    tiles = scratch[13:19]
    held, load_sem = scratch[19:31], scratch[31]
    hidden_ref, down_ref, upstream, starts_ref, cosine_ref, sine_ref = held[:6]
    projected_ref, query_ref, key_ref, value_ref, log_ref, residual_ref = held[6:]
    attend_loads = Loads(operands, held, load_sem)
    attend_loads.start()
    width = residual_ref.shape[1]
    core = lax.rem(lax.axis_index("tx"), 2)
    parts = [rest_ref.at[:, :, index * SPLIT : (index + 1) * SPLIT] for index in range(2)]
    loads = [
        pltpu.make_async_copy(parts[index], tiles[3 * index], rest_sem.at[index])
        for index in range(2)
    ]
    for load in loads:
        load.start()
    greet(neighbours() + planes())
    wires = Wires(send_sems, recv_sems)
    folds = [
        Fold(
            wires,
            REDUCE_KINDS + index * FOLD_KINDS,
            tiles[3 * index],
            tiles[3 * index + 1 : 3 * index + 3],
            ends[2 * index],
            ends[2 * index + 1],
            parts[index],
        )
        for index in range(2)
    ]
    for fold in folds:
        fold.start()
    reduce = Reduce(wires, hidden_ref, down_ref, False, bufs)
    attend_loads.wait(0, 2)
    reduce.start()
    attend_loads.wait(2, 12)
    for load in loads:
        load.wait()
    stats_ref[...] = jnp.zeros_like(stats_ref)
    fixed_refs = (starts_ref, cosine_ref, sine_ref, query_gain_ref, key_gain_ref)
    saved_refs = (query_ref, key_ref, value_ref, log_ref)

    @pl.loop(0, 2)
    def _(seq):
        attend_sequence_back(
            core,
            seq,
            most,
            projected_ref,
            upstream,
            fixed_refs,
            saved_refs,
            result_ref,
            stats_ref,
            gains_ref,
            (query_acc, key_acc, value_acc),
        )

        @pl.when(seq == 0)
        def _():
            reduce.middle()
            folds[0].middle()


    @pl.loop(0, width // CHUNK)
    def _(chunk):
        at = lanes(chunk, 0, width)
        output_ref[:, at] = (residual_ref[:, at] + reduce.total(chunk)).astype(B16)

    folds[1].middle()
    folds[0].late()
    folds[1].late()
    for fold in folds:
        fold.close()
    reduce.close()


def back_call(upstream, hidden, w_back, residual, fixed_args, projected, saved, rest, most, number):
    height, width = residual.shape
    _, cosine, _, query_gain, _ = fixed_args
    depth = query_gain.shape[1]
    length = cosine.shape[1]
    columns = projected.shape[2]
    heads = columns // depth - 2
    quarter = rest.shape[1]
    loaded = (hidden, w_back, upstream) + fixed_args[:3] + (projected,) + saved + (residual,)
    return pl.pallas_call(
        lambda *refs: back_kernel(most, *refs),
        out_shape=(
            shape((height, width)),
            shape((4, height, columns)),
            shape((8, 8, 128), F32),
            shape((2, 8, depth), F32),
        )
        + (shape((quarter, SPLIT), F32), shape((quarter, SPLIT))) * 2,
        in_specs=[IN_VMEM] * 2 + [IN_ANY] * 13,
        out_specs=[IN_VMEM] * 4 + [IN_VMEM, IN_ANY] * 2,
        scratch_shapes=reduce_scratch(height, width)
        + [
            pltpu.VMEM((length, heads * depth), F32),
            pltpu.VMEM((length, depth), F32),
            pltpu.VMEM((length, depth), F32),
        ]
        + wire_scratch(REDUCE_KINDS + 2 * FOLD_KINDS, width // CHUNK)
        + [pltpu.SemaphoreType.DMA((2,))]
        + ([pltpu.VMEM((8, quarter, SPLIT), B16)] + fold_scratch(quarter, SPLIT)) * 2
        + load_scratch(loaded),
        compiler_params=remote_params(number),
        cost_estimate=cost(16 * height * hidden.shape[2] * width, 64 * height * width),
    )(*fixed_args[3:], *loaded, rest)


def finish_kernel(place_ref, *refs):
    downs, both, out, project = refs[0:4], refs[4:10], refs[10:12], refs[12:14]
    totals_ref, gain_ref = refs[14:16]
    query_ref, key_ref, value_ref, out_ref, gate_ref, up_ref, down_ref = refs[16:23]
    attn_ref, mlp_ref = refs[23:]
    first = place_ref[0] == 0

    def ordered(mine, theirs):
        theirs = theirs.astype(F32)
        return jnp.where(first, mine, theirs), jnp.where(first, theirs, mine)

    def put(target, at, mine, theirs):
        half = target.shape[1] // 2
        low, high = ordered(mine, theirs)
        target[:, at : at + mine.shape[1]] = low
        target[:, half + at : half + at + mine.shape[1]] = high

    def put_turned(target, at, mine, theirs):
        half = target.shape[0] // 2
        low, high = ordered(mine, theirs)
        target[at : at + mine.shape[1], :] = low.T
        target[half + at : half + at + mine.shape[1], :] = high.T

    at = 0
    for index in (0, 2):
        put_turned(down_ref, at, downs[index][...], downs[index + 1][...])
        at += downs[index].shape[1]
    put_turned(out_ref, 0, out[0][...], out[1][...])
    at = 0
    for target in (query_ref, key_ref, value_ref):
        size = target.shape[1] // 2
        put(target, 0, project[0][:, at : at + size], project[1][:, at : at + size])
        at += size
    units = gate_ref.shape[1] // 2
    at = 0
    for index in (0, 2, 4):
        low = 0
        while low < both[index].shape[1]:
            size = min(both[index].shape[1] - low, units - at % units)
            put(
                gate_ref if at < units else up_ref,
                at % units,
                both[index][:, low : low + size],
                both[index + 1][:, low : low + size],
            )
            low += size
            at += size
    mine = jnp.concatenate([totals_ref[tile, 0:2] for tile in range(4)], axis=0)
    theirs = jnp.concatenate([totals_ref[tile, 0:2] for tile in range(4, 8)], axis=0)
    low, high = ordered(mine / gain_ref[0:8], theirs / gain_ref[8:16])
    attn_ref[0:8], attn_ref[8:16] = low, high
    low, high = ordered(totals_ref[8], totals_ref[9])
    mlp_ref[0:8], mlp_ref[8:16] = low, high


def finish_call(place, parts, totals, gain, sizes):
    quarter = parts[0].shape[0]
    queries, keys, branch, units = sizes
    return pl.pallas_call(
        finish_kernel,
        out_shape=(
            shape((quarter, queries), F32),
            shape((quarter, keys), F32),
            shape((quarter, keys), F32),
            shape((branch, quarter), F32),
            shape((quarter, units), F32),
            shape((quarter, units), F32),
            shape((units, quarter), F32),
            shape((16, 128), F32),
            shape((16, 128), F32),
        ),
        in_specs=[pl.BlockSpec(memory_space=pltpu.SMEM)] + [IN_VMEM] * (len(parts) + 2),
        out_specs=[IN_VMEM] * 9,
        compiler_params=pltpu.CompilerParams(vmem_limit_bytes=VMEM_MOST),
        cost_estimate=cost(0, 16 * 1024 * 1024),
    )(place, *parts, totals, gain)


def product_grad(left, right):
    return weight_grad(left, right).astype(B16)


def plane_device(
    tokens,
    seg_ids,
    w_query,
    w_key,
    w_value,
    w_out,
    w_gate,
    w_up,
    w_down,
    attn_gain,
    mlp_gain,
    query_gain,
    key_gain,
    cotangent,
):
    depth = query_gain.shape[0]
    most = seg_ids.shape[1] // 2
    rows, width = tokens.shape
    head_width = w_query.shape[1] // 2
    kv_width = w_key.shape[1] // 2
    units = w_gate.shape[1] // 2

    half = jnp.arange(depth // 2, dtype=F32)
    rate = THETA ** (-half * 2.0 / depth)
    rate = jnp.concatenate([rate, rate])[None]
    gains, starts, cosine, sine, token_whole, w_project, w_branch = open_call(
        tokens, w_query, w_key, w_value, w_out, jnp.stack([attn_gain, mlp_gain]), seg_ids, rate, 0
    )
    fixed_args = (starts, cosine, sine, query_gain[None], key_gain[None])
    (
        first,
        first_scale,
        projected,
        mixed,
        query,
        keys,
        values,
        logs,
        grad_whole,
        w_back,
        gate_quarter,
    ) = front_call(
        token_whole, w_project, gains[0:1], fixed_args, most, cotangent, w_down, w_gate, 1
    )
    residual, residual_whole, w_uppers, w_gates = branch_call(
        mixed, w_branch, tokens, w_up, w_gate, gate_quarter, 2
    )
    flat = (4 * rows, 2 * width)
    grad_flat = grad_whole.reshape(flat)
    second, hidden, unit_grads, second_scale, unit_stats = units_call(
        residual_whole.reshape(flat), grad_flat, w_gates, w_uppers, w_back, gains[1:2]
    )
    tiles = lambda grad: grad.reshape(8, -1, grad.shape[1])
    (
        residual_grad,
        mlp_gain_part,
        upstream,
        out_tiles,
        _,
        rest_tiles,
        *ends,
    ) = middle_call(
        unit_grads.reshape(4, rows, 2 * units),
        w_gates,
        w_uppers,
        unit_stats,
        second_scale[:rows],
        residual,
        mlp_gain[None],
        cotangent,
        tiles(product_grad(grad_flat, hidden)),
        second.reshape(4, rows, 2 * width),
        w_branch,
        mixed,
        3,
    )
    output, proj_grads, proj_stats, gain_parts, *rest_ends = back_call(
        upstream,
        hidden.reshape(4, rows, units),
        w_back,
        residual,
        fixed_args,
        projected,
        (query, keys, values, logs),
        rest_tiles,
        most,
        4,
    )
    extra = jnp.stack(
        [
            mlp_gain_part.reshape(8, 128),
            jnp.pad(jnp.sum(gain_parts[:, :2], axis=0), ((0, 6), (0, 0))),
        ]
    )
    input_grad, totals, out_mine, out_theirs, project_mine, project_theirs = last_call(
        proj_grads,
        w_project,
        proj_stats,
        first_scale,
        tokens,
        attn_gain[None],
        residual_grad,
        extra,
        out_tiles,
        first,
        5,
    )
    place = lax.axis_index("ty").reshape(1).astype(jnp.int32)
    (
        query_share,
        key_share,
        value_share,
        out_share,
        gate_share,
        up_share,
        down_share,
        attn_total,
        mlp_total,
    ) = finish_call(
        place,
        (*ends, *rest_ends, out_mine, out_theirs, project_mine, project_theirs),
        totals,
        gains[0].reshape(16, 128),
        (2 * head_width, 2 * kv_width, 2 * head_width, 2 * units),
    )
    attn_total, mlp_total = attn_total.reshape(-1), mlp_total.reshape(-1)
    query_total, key_total = totals[10, 0], totals[10, 1]
    return (
        output,
        input_grad,
        query_share,
        key_share,
        value_share,
        out_share,
        gate_share,
        up_share,
        down_share,
        attn_total,
        mlp_total,
        query_total,
        key_total,
    )


def solution(mesh):
    placed = (
        P(("dp", "tx"), "ty"),
        P(("dp", "ty"), None),
        P("ty", "tx"),
        P("ty", "tx"),
        P("ty", "tx"),
        P("tx", "ty"),
        P("ty", "tx"),
        P("ty", "tx"),
        P("tx", "ty"),
        P("ty"),
        P("ty"),
        P(),
        P(),
        P(("dp", "tx"), "ty"),
    )
    return jax.shard_map(
        plane_device if fits(mesh) else general_device,
        mesh=mesh,
        in_specs=placed,
        out_specs=(
            P(("dp", "tx"), "ty"),
            P(("dp", "tx"), "ty"),
            P(("ty", "dp"), "tx"),
            P(("ty", "dp"), "tx"),
            P(("ty", "dp"), "tx"),
            P("tx", ("ty", "dp")),
            P(("ty", "dp"), "tx"),
            P(("ty", "dp"), "tx"),
            P("tx", ("ty", "dp")),
            P(),
            P(),
            P(),
            P(),
        ),
        check_vma=False,
    )
```

```python
import jax
import jax.numpy as jnp
from jax import lax
from jax.experimental import pallas as pl
from jax.experimental.pallas import tpu as pltpu
from jax.sharding import PartitionSpec as P

EPS = 1e-06
THETA = 1000000.0
NEG = -1e30
F32 = jnp.float32
B16 = jnp.bfloat16
MESH = pl.DeviceIdType.MESH


def width_sum(value):
    return lax.psum(value, "ty")


def token_gather(rows):
    return lax.all_gather(rows, "tx", axis=0, tiled=True)


def branch_gather(rows):
    return lax.all_gather(rows, "ty", axis=0, tiled=True)


def width_reduce(whole, apply):
    return lax.psum_scatter(apply(whole), "ty", scatter_dimension=0, tiled=True)


def head_reduce(whole, apply):
    return lax.psum_scatter(
        apply(whole).astype(jnp.bfloat16), "tx", scatter_dimension=0, tiled=True
    ).astype(jnp.float32)


def forward_with(weight):
    return lambda rows: jnp.dot(rows, weight, preferred_element_type=F32)


def backward_with(weight):
    return lambda rows: lax.dot_general(
        rows, weight, (((1,), (1,)), ((), ())), preferred_element_type=F32
    )


def weight_grad(left, right):
    return lax.dot_general(left, right, (((0,), (0,)), ((), ())), preferred_element_type=F32)


def norm_scale(rows):
    width = rows.shape[1] * lax.axis_size("ty")
    return lax.rsqrt(width_sum(jnp.sum(rows * rows, axis=1)) / width + EPS)


def norm_back(rows, scale, gain, upstream):
    width = rows.shape[1] * lax.axis_size("ty")
    inner = width_sum(jnp.sum(upstream * gain * rows, axis=1))
    back = scale[:, None] * gain * upstream - rows * (scale**3 * inner / width)[:, None]
    gain_part = jnp.sum(upstream * rows * scale[:, None], axis=0)
    return (back, gain_part)


def widen(part):
    whole = jnp.zeros((part.shape[0] * lax.axis_size("ty"),), F32)
    return lax.dynamic_update_slice_in_dim(whole, part, lax.axis_index("ty") * part.shape[0], 0)


def doc_positions(seg):
    count = seg.shape[-1]
    index = jnp.arange(count, dtype=jnp.int32)
    edge = jnp.concatenate([jnp.ones((1,), dtype=jnp.bool_), seg[1:] != seg[:-1]])
    first = lax.cummax(jnp.where(edge, index, jnp.zeros_like(index)), axis=0)
    return index - first


def rotary(positions, depth):
    half = depth // 2
    freq = THETA ** (-jnp.arange(half, dtype=F32) * 2.0 / depth)
    angle = positions.astype(F32)[..., None] * freq
    return (jnp.cos(angle), jnp.sin(angle))


def turn(value, gain, cosine, sine):
    normed = value * lax.rsqrt(jnp.mean(value * value, axis=-1, keepdims=True) + EPS) * gain
    half = value.shape[-1] // 2
    first = normed[..., :half]
    second = normed[..., half:]
    return jnp.concatenate(
        [first * cosine - second * sine, second * cosine + first * sine], axis=-1
    )


def block_scores(part, seq_keys, seq_ids, start, scale):
    block = part.shape[0]
    length = seq_ids.shape[0]
    index = jnp.arange(length, dtype=jnp.int32)
    rows = start + jnp.arange(block, dtype=jnp.int32)
    row_ids = lax.dynamic_slice_in_dim(seq_ids, start, block, 0)
    mask = (seq_ids[None, :] == row_ids[:, None]) & (index[None, :] <= rows[:, None])
    scores = jnp.einsum("qkgd,mkd->kgqm", part, seq_keys, preferred_element_type=F32) * scale
    return jnp.where(mask[None, None], scores, NEG)


def attend_forward(query, keys, values, seg, block):
    seqs, length, heads, depth = query.shape
    kv_heads = keys.shape[2]
    groups = heads // kv_heads
    scale = depth ** (-0.5)
    count = length // block
    starts = jnp.arange(count, dtype=jnp.int32) * block

    def one_sequence(operands):
        seq_query, seq_keys, seq_values, seq_ids = operands
        blocks = seq_query.reshape(count, block, kv_heads, groups, depth)

        def one_block(inputs):
            part, start = inputs
            scores = block_scores(part, seq_keys, seq_ids, start, scale)
            top = jnp.max(scores, axis=-1)
            weights = jnp.exp(scores - top[..., None])
            total = jnp.sum(weights, axis=-1)
            probs = (weights / total[..., None]).astype(B16)
            mixed = jnp.einsum("kgqm,mkd->qkgd", probs, seq_values, preferred_element_type=F32)
            return (mixed, top + jnp.log(total))

        mixed, logs = lax.map(one_block, (blocks, starts))
        return (mixed.reshape(length, heads * depth), logs)

    return lax.map(one_sequence, (query, keys, values, seg))


def attend_backward(query, keys, values, seg, logs, grad_out, block):
    seqs, length, heads, depth = query.shape
    kv_heads = keys.shape[2]
    groups = heads // kv_heads
    scale = depth ** (-0.5)
    count = length // block
    starts = jnp.arange(count, dtype=jnp.int32) * block

    def one_sequence(operands):
        seq_query, seq_keys, seq_values, seq_ids, seq_logs, seq_grad = operands
        blocks = seq_query.reshape(count, block, kv_heads, groups, depth)
        grads = seq_grad.reshape(count, block, kv_heads, groups, depth)

        def one_block(carry, inputs):
            key_acc, value_acc = carry
            part, grad_part, log_part, start = inputs
            scores = block_scores(part, seq_keys, seq_ids, start, scale)
            probs = jnp.exp(scores - log_part[..., None])
            value_acc = value_acc + jnp.einsum(
                "kgqm,qkgd->mkd", probs.astype(B16), grad_part, preferred_element_type=F32
            )
            prob_grad = jnp.einsum(
                "qkgd,mkd->kgqm", grad_part, seq_values, preferred_element_type=F32
            )
            delta = jnp.sum(probs * prob_grad, axis=-1, keepdims=True)
            score_grad = (probs * (prob_grad - delta)).astype(B16)
            query_grad = (
                jnp.einsum("kgqm,mkd->qkgd", score_grad, seq_keys, preferred_element_type=F32)
                * scale
            )
            key_acc = (
                key_acc
                + jnp.einsum("kgqm,qkgd->mkd", score_grad, part, preferred_element_type=F32) * scale
            )
            return ((key_acc, value_acc), query_grad)

        zeros = jnp.zeros((length, kv_heads, depth), F32)
        (key_grad, value_grad), query_grad = lax.scan(
            one_block, (zeros, zeros), (blocks, grads, seq_logs, starts)
        )
        return (query_grad.reshape(length, heads, depth), key_grad, value_grad)

    return lax.map(one_sequence, (query, keys, values, seg, logs, grad_out))


def general_device(
    tokens,
    seg_ids,
    w_query,
    w_key,
    w_value,
    w_out,
    w_gate,
    w_up,
    w_down,
    attn_gain,
    mlp_gain,
    query_gain,
    key_gain,
    cotangent,
):
    seqs, length = seg_ids.shape
    depth = query_gain.shape[0]
    query_width = w_query.shape[1]
    key_width = w_key.shape[1]
    units = w_gate.shape[1]
    block = min(512, length)
    inputs = tokens.astype(F32)
    first_scale = norm_scale(inputs)
    first_normed = (inputs * first_scale[:, None] * attn_gain).astype(B16)
    first_whole = token_gather(first_normed)
    w_project = jnp.concatenate([w_query, w_key, w_value], axis=1)
    projected = width_reduce(first_whole, forward_with(w_project))
    query_proj = projected[:, :query_width].reshape(seqs, length, -1, depth)
    key_proj = projected[:, query_width : query_width + key_width].reshape(seqs, length, -1, depth)
    values = projected[:, query_width + key_width :].astype(B16).reshape(seqs, length, -1, depth)
    positions = jax.vmap(doc_positions)(seg_ids)
    cosine, sine = rotary(positions, depth)
    cosine = cosine[:, :, None, :]
    sine = sine[:, :, None, :]
    query = turn(query_proj, query_gain, cosine, sine).astype(B16)
    keys = turn(key_proj, key_gain, cosine, sine).astype(B16)
    mixed, logs = attend_forward(query, keys, values, seg_ids, block)
    attended = mixed.reshape(seqs * length, -1).astype(B16)
    attended_whole = branch_gather(attended)
    residual = inputs + head_reduce(attended_whole, forward_with(w_out))
    second_scale = norm_scale(residual)
    second_normed = (residual * second_scale[:, None] * mlp_gain).astype(B16)
    second_whole = token_gather(second_normed)
    w_both = jnp.concatenate([w_gate, w_up], axis=1)
    gate_up = width_reduce(second_whole, forward_with(w_both))
    gate = gate_up[:, :units]
    upper = gate_up[:, units:]
    hidden = (jax.nn.silu(gate) * upper).astype(B16)
    hidden_whole = branch_gather(hidden)
    output = residual + head_reduce(hidden_whole, forward_with(w_down))
    grad_whole = token_gather(cotangent)
    hidden_grad = width_reduce(grad_whole, backward_with(w_down))
    down_grad = weight_grad(hidden_whole, grad_whole)
    gate_grad, up_grad = jax.vjp(lambda left, right: jax.nn.silu(left) * right, gate, upper)[1](
        hidden_grad
    )
    unit_grads = jnp.concatenate([gate_grad, up_grad], axis=1).astype(B16)
    unit_whole = branch_gather(unit_grads)
    second_grad = head_reduce(unit_whole, backward_with(w_both))
    both_grad = weight_grad(second_whole, unit_whole)
    gate_weight = both_grad[:, :units]
    up_weight = both_grad[:, units:]
    resid_norm_grad, mlp_gain_part = norm_back(residual, second_scale, mlp_gain, second_grad)
    residual_grad = cotangent.astype(F32) + resid_norm_grad
    residual_whole = token_gather(residual_grad.astype(B16))
    mixed_grad = width_reduce(residual_whole, backward_with(w_out)).astype(B16)
    out_grad = weight_grad(attended_whole, residual_whole)
    query_grad, key_grad, value_grad = attend_backward(
        query, keys, values, seg_ids, logs, mixed_grad.reshape(seqs, length, -1), block
    )
    query_proj_grad, query_gain_grad = jax.vjp(
        lambda value, gain: turn(value, gain, cosine, sine), query_proj, query_gain
    )[1](query_grad)
    key_proj_grad, key_gain_grad = jax.vjp(
        lambda value, gain: turn(value, gain, cosine, sine), key_proj, key_gain
    )[1](key_grad)
    rows = seqs * length
    proj_grad = jnp.concatenate(
        [
            query_proj_grad.reshape(rows, -1),
            key_proj_grad.reshape(rows, -1),
            value_grad.reshape(rows, -1),
        ],
        axis=1,
    ).astype(B16)
    proj_whole = branch_gather(proj_grad)
    first_grad = head_reduce(proj_whole, backward_with(w_project))
    project_grad = weight_grad(first_whole, proj_whole)
    query_weight = project_grad[:, :query_width]
    key_weight = project_grad[:, query_width : query_width + key_width]
    value_weight = project_grad[:, query_width + key_width :]
    input_norm_grad, attn_gain_part = norm_back(inputs, first_scale, attn_gain, first_grad)
    input_grad = (residual_grad + input_norm_grad).astype(B16)
    attn_total, mlp_total, query_total, key_total = lax.psum(
        (widen(attn_gain_part), widen(mlp_gain_part), query_gain_grad, key_gain_grad),
        ("dp", "tx", "ty"),
    )
    query_share, key_share, value_share, gate_share, up_share = (
        lax.psum_scatter(
            query_weight.astype(jnp.bfloat16), "dp", scatter_dimension=0, tiled=True
        ).astype(jnp.float32),
        lax.psum_scatter(
            key_weight.astype(jnp.bfloat16), "dp", scatter_dimension=0, tiled=True
        ).astype(jnp.float32),
        lax.psum_scatter(
            value_weight.astype(jnp.bfloat16), "dp", scatter_dimension=0, tiled=True
        ).astype(jnp.float32),
        lax.psum_scatter(
            gate_weight.astype(jnp.bfloat16), "dp", scatter_dimension=0, tiled=True
        ).astype(jnp.float32),
        lax.psum_scatter(
            up_weight.astype(jnp.bfloat16), "dp", scatter_dimension=0, tiled=True
        ).astype(jnp.float32),
    )
    out_share, down_share = (
        lax.psum_scatter(
            out_grad.astype(jnp.bfloat16), "dp", scatter_dimension=1, tiled=True
        ).astype(jnp.float32),
        lax.psum_scatter(
            down_grad.astype(jnp.bfloat16), "dp", scatter_dimension=1, tiled=True
        ).astype(jnp.float32),
    )
    return (
        output.astype(B16),
        input_grad,
        query_share,
        key_share,
        value_share,
        out_share,
        gate_share,
        up_share,
        down_share,
        attn_total,
        mlp_total,
        query_total,
        key_total,
    )


def fits(mesh):
    return mesh.shape["tx"] == 4 and mesh.shape["ty"] == 2 and mesh.shape["dp"] == 4


def swap_x(value):
    return lax.ppermute(value, "ty", [(0, 1), (1, 0)])


def in_order(mine, theirs, axis):
    first = lax.axis_index("ty") == 0
    return jnp.concatenate(
        [jnp.where(first, mine, theirs), jnp.where(first, theirs, mine)], axis=axis
    )


def spin(value, cosine, sine):
    return value * cosine + pltpu.roll(value, value.shape[1] // 2, 1) * sine


def spin_back(value, cosine, sine):
    return value * cosine + pltpu.roll(value * sine, value.shape[1] // 2, 1)


def head_scale(value):
    return lax.rsqrt(jnp.mean(value * value, axis=1, keepdims=True) + EPS)


def window(first, block, most):
    return max(0, first - most), first + block


def kept(first, block, low, high, starts):
    shape = (block, high - low)
    column = low + lax.broadcasted_iota(jnp.int32, shape, 1)
    row = first + lax.broadcasted_iota(jnp.int32, shape, 0)
    return (column >= starts) & (column <= row)


def rows_dot(left, right):
    return lax.dot_general(left, right, (((1,), (1,)), ((), ())), preferred_element_type=F32)


def stand(row):
    return jnp.transpose(jnp.broadcast_to(row, (row.shape[1], row.shape[1])))


def lie(column):
    return jnp.transpose(jnp.broadcast_to(column, (column.shape[0], column.shape[0])))[0:1]


def put_stats(stats_ref, tile, column):
    stats_ref[tile, 0:1, :] = lie(column[:128])
    stats_ref[tile, 1:2, :] = lie(column[128:])


BLOCK = 256


def attend_sequence(core, seq, most, projected, fixed_refs, mixed, saved_refs, between):
    starts_ref, cosine_ref, sine_ref, query_gain_ref, key_gain_ref = fixed_refs
    query_ref, key_ref, value_ref, log_ref = saved_refs
    rows = projected.shape[1]
    length = query_ref.shape[1]
    depth = key_ref.shape[2]
    heads = query_ref.shape[2] // depth
    scale = depth ** (-0.5)
    for half in range(2):
        place = 2 * lax.rem(core + half, 2) + seq
        for at in range(half * rows, (half + 1) * rows, BLOCK):
            inner = at - half * rows
            cosine = cosine_ref[seq, at : at + BLOCK, :]
            sine = sine_ref[seq, at : at + BLOCK, :]
            for head in range(heads + 2):
                lane = slice(head * depth, (head + 1) * depth)
                value = projected[place, inner : inner + BLOCK, lane]
                if head < heads:
                    normed = value * head_scale(value) * query_gain_ref[...]
                    query_ref[seq, at : at + BLOCK, lane] = spin(normed, cosine, sine).astype(B16)
                elif head == heads:
                    normed = value * head_scale(value) * key_gain_ref[...]
                    key_ref[seq, at : at + BLOCK, :] = spin(normed, cosine, sine).astype(B16)
                else:
                    value_ref[seq, at : at + BLOCK, :] = value.astype(B16)
    for first in range(0, length, BLOCK):
        between(first // BLOCK)
        low, high = window(first, BLOCK, most)
        mask = kept(first, BLOCK, low, high, starts_ref[seq, first : first + BLOCK, :])
        half, inner = divmod(first, rows)
        place = 2 * lax.rem(core + half, 2) + seq
        for head in range(heads):
            lane = slice(head * depth, (head + 1) * depth)
            query = query_ref[seq, first : first + BLOCK, lane]
            scores = rows_dot(query, key_ref[seq, low:high, :]) * scale
            scores = jnp.where(mask, scores, NEG)
            top = jnp.max(scores, axis=1, keepdims=True)
            weights = jnp.exp(scores - top)
            total = jnp.sum(weights, axis=1, keepdims=True)
            probs = (weights * (1.0 / total)).astype(B16)
            out = jnp.dot(probs, value_ref[seq, low:high, :], preferred_element_type=F32)
            mixed[place, inner : inner + BLOCK, lane] = out.astype(B16)
            log_ref[seq, head, first : first + BLOCK, :] = top + jnp.log(total)


def attend_sequence_back(
    core, seq, most, projected, upstream, fixed_refs, saved_refs, result, stats, gains, accs
):
    starts_ref, cosine_ref, sine_ref, query_gain_ref, key_gain_ref = fixed_refs
    query_ref, key_ref, value_ref, log_ref = saved_refs
    query_acc, key_acc, value_acc = accs
    rows = projected.shape[1]
    length = query_ref.shape[1]
    depth = key_ref.shape[2]
    heads = query_ref.shape[2] // depth
    scale = depth ** (-0.5)
    key_acc[...] = jnp.zeros_like(key_acc)
    value_acc[...] = jnp.zeros_like(value_acc)
    for first in range(0, length, BLOCK):
        low, high = window(first, BLOCK, most)
        mask = kept(first, BLOCK, low, high, starts_ref[seq, first : first + BLOCK, :])
        half, inner = divmod(first, rows)
        place = 2 * lax.rem(core + half, 2) + seq
        keys = key_ref[seq, low:high, :]
        values = value_ref[seq, low:high, :]
        for head in range(heads):
            lane = slice(head * depth, (head + 1) * depth)
            query = query_ref[seq, first : first + BLOCK, lane]
            grad = upstream[place, inner : inner + BLOCK, lane]
            scores = rows_dot(query, keys) * scale - log_ref[seq, head, first : first + BLOCK, :]
            probs = jnp.exp(jnp.where(mask, scores, NEG))
            prob_grad = rows_dot(grad, values)
            delta = jnp.sum(probs * prob_grad, axis=1, keepdims=True)
            score_grad = (probs * (prob_grad - delta)).astype(B16)
            query_acc[first : first + BLOCK, lane] = (
                jnp.dot(score_grad, keys, preferred_element_type=F32) * scale
            )
            key_acc[low:high, :] += weight_grad(score_grad, query) * scale
            value_acc[low:high, :] += weight_grad(probs.astype(B16), grad)
    query_total = jnp.zeros((1, depth), F32)
    key_total = jnp.zeros((1, depth), F32)
    for half in range(2):
        block = 2 * lax.rem(core + half, 2) + seq
        for at in range(half * rows, (half + 1) * rows, BLOCK):
            inner = at - half * rows
            cosine = cosine_ref[seq, at : at + BLOCK, :]
            sine = sine_ref[seq, at : at + BLOCK, :]
            total = jnp.zeros((BLOCK, 1), F32)
            for head in range(heads + 2):
                lane = slice(head * depth, (head + 1) * depth)
                value = projected[block, inner : inner + BLOCK, lane]
                if head == heads + 1:
                    back = value_acc[at : at + BLOCK, :].astype(B16)
                else:
                    if head < heads:
                        grad = query_acc[at : at + BLOCK, lane]
                        gain = query_gain_ref[...]
                    else:
                        grad = key_acc[at : at + BLOCK, :]
                        gain = key_gain_ref[...]
                    grad = spin_back(grad, cosine, sine)
                    rate = head_scale(value)
                    scaled = value * rate
                    share = jnp.sum(grad * scaled, axis=0, keepdims=True)
                    if head < heads:
                        query_total += share
                    else:
                        key_total += share
                    middle = jnp.mean(gain * grad * scaled, axis=1, keepdims=True)
                    back = (rate * (gain * grad - scaled * middle)).astype(B16)
                result[block, inner : inner + BLOCK, lane] = back
                total += jnp.sum(back.astype(F32) * value, axis=1, keepdims=True)
            put_stats(stats, 2 * block + inner // BLOCK, total)
    gains[seq, 0:1, :] = query_total
    gains[seq, 1:2, :] = key_total


def neighbours():
    spot = lax.axis_index("tx")
    core = lax.rem(spot, 2)
    return (
        {"ty": 1 - lax.axis_index("ty")},
        {"tx": lax.rem(spot + 2, 4)},
        {"tx": spot + 1 - 2 * core},
    )


def planes():
    plane = lax.axis_index("dp")
    return {"dp": plane + 1 - 2 * lax.rem(plane, 2)}, {"dp": 3 - plane}


def inner():
    plane = lax.axis_index("dp")
    return (plane == 1) | (plane == 2)


def greet(targets):
    barrier = pltpu.get_barrier_semaphore()
    for target in targets:
        pl.semaphore_signal(barrier, inc=1, device_id=target, device_id_type=MESH)
    pl.semaphore_wait(barrier, len(targets))


class Wires:
    def __init__(self, send_sems, recv_sems):
        self.send_sems = send_sems
        self.recv_sems = recv_sems

    def copy(self, kind, chunk, source, target, device):
        return pltpu.make_async_remote_copy(
            src_ref=source,
            dst_ref=target,
            send_sem=self.send_sems.at[kind, chunk],
            recv_sem=self.recv_sems.at[kind, chunk],
            device_id=device,
            device_id_type=MESH,
        )


CHUNK = 256
SIBLING, CORNER, FINAL_X, FINAL_Y = 0, 1, 2, 3
REDUCE_KINDS = 5
OUT_X, OUT_Y, OUT_CORNER, CORE_OWN, CORE_X, CORE_Y, CORE_CORNER = range(7)
GATHER_KINDS = 7
SHARE_X, SHARE_NEAR, SHARE_MIDDLE = 0, 1, 2
SHARE_KINDS = 3


def lanes(chunk, half, width):
    return pl.ds(pl.multiple_of(half * width + chunk * CHUNK, CHUNK), CHUNK)


class Gather:
    def __init__(self, wires, base, whole, own, local_sem, most=4):
        self.wires, self.base, self.whole, self.own, self.local_sem = (
            wires,
            base,
            whole,
            own,
            local_sem,
        )
        self.most = most
        self.width = whole.shape[2] // 2
        self.count = self.width // CHUNK

    def place(self, block, chunk, half):
        return self.whole.at[block, :, lanes(chunk, half, self.width)]

    def copy(self, name, chunk):
        side, across, core = neighbours()
        at = self.place
        own = self.own.at[chunk]
        if name == "local":
            return pltpu.make_async_copy(own, at(0, chunk, 0), self.local_sem.at[chunk])
        kind, source, target, device = {
            "x": (OUT_X, own, at(0, chunk, 1), side),
            "y": (OUT_Y, own, at(1, chunk, 0), across),
            "core": (CORE_OWN, own, at(2, chunk, 0), core),
            "even": (OUT_CORNER, at(0, chunk, 1), at(1, chunk, 1), across),
            "odd": (OUT_CORNER, at(1, chunk, 0), at(1, chunk, 1), side),
            "core_x": (CORE_X, at(0, chunk, 1), at(2, chunk, 1), core),
            "core_y": (CORE_Y, at(1, chunk, 0), at(3, chunk, 0), core),
            "core_corner": (CORE_CORNER, at(1, chunk, 1), at(3, chunk, 1), core),
        }[name]
        return self.wires.copy(self.base + kind, chunk, source, target, device)

    def send(self, chunk):
        for name in ("x", "y", "core", "local"):
            self.copy(name, chunk).start()

    def relay(self, low=0, high=None):
        @pl.loop(low, self.count if high is None else high)
        def _(chunk):
            even = (lax.rem(chunk, 2) == 0) | (chunk >= self.most)
            self.copy("x", chunk).wait_recv()

            @pl.when(even)
            def _():
                self.copy("even", chunk).start()

            self.copy("core_x", chunk).start()
            self.copy("y", chunk).wait_recv()

            @pl.when(jnp.logical_not(even))
            def _():
                self.copy("odd", chunk).start()

            self.copy("core_y", chunk).start()

    def close(self):
        @pl.loop(0, self.count)
        def _(chunk):
            self.copy("even", chunk).wait_recv()
            self.copy("core_corner", chunk).start()

        @pl.loop(0, self.count)
        def _(chunk):
            for name in ("core", "core_x", "core_y", "core_corner"):
                self.copy(name, chunk).wait_recv()
            for name in ("x", "y", "core", "even", "core_x", "core_y", "core_corner"):
                self.copy(name, chunk).wait_send()
            self.copy("local", chunk).wait()


class Share:
    def __init__(self, wires, base, sources, whole, by_rows, local_sems, held=None):
        self.wires, self.base, self.sources, self.whole, self.by_rows, self.local_sems = (
            wires,
            base,
            sources,
            whole,
            by_rows,
            local_sems,
        )
        self.held = held or sources
        self.size = (whole.shape[0] // 2 if by_rows else whole.shape[0]) // 4

    def quarter(self, plane):
        start = plane * self.size
        if self.by_rows:
            rows = pl.ds(pl.multiple_of(self.whole.shape[0] // 2 + start, self.size), self.size)
            return self.whole.at[rows]
        width = self.whole.shape[1] // 2
        return self.whole.at[pl.ds(pl.multiple_of(start, self.size), self.size), width:]

    def cross(self, index):
        side, _, _ = neighbours()
        plane = lax.axis_index("dp")
        other = 1 - lax.axis_index("ty")
        source = self.sources[index]
        if self.by_rows:
            rows = pl.ds(pl.multiple_of(plane * self.size, self.size), self.size)
            columns = source.shape[1] // 2
            part = source.at[rows, pl.ds(pl.multiple_of(other * columns, columns), columns)]
            offset = sum(item.shape[1] // 2 for item in self.sources[:index])
            target = self.quarter(plane).at[:, offset : offset + columns]
        else:
            start = pl.multiple_of(other * (source.shape[0] // 2) + plane * self.size, self.size)
            part = source.at[pl.ds(start, self.size)]
            target = self.quarter(plane)
        return self.wires.copy(self.base + SHARE_X, index, part, target, side)

    def local(self, index):
        mine = lax.axis_index("ty")
        source = self.held[index]
        if self.by_rows:
            columns = source.shape[1] // 2
            offset = sum(item.shape[1] // 2 for item in self.sources[:index])
            part = source.at[:, pl.ds(pl.multiple_of(mine * columns, columns), columns)]
            target = self.whole.at[: self.whole.shape[0] // 2, offset : offset + columns]
        else:
            half = source.shape[0] // 2
            part = source.at[pl.ds(pl.multiple_of(mine * half, half), half)]
            target = self.whole.at[:, : self.whole.shape[1] // 2]
        return pltpu.make_async_copy(part, target, self.local_sems.at[index])

    def piece_of(self, owner):
        place = self.quarter(owner)
        return place, place

    def over(self, near, index):
        beside, mirror = planes()
        plane = lax.axis_index("dp")
        other = 3 - plane
        if near:
            owner = (plane, other, other + 1 - 2 * lax.rem(other, 2))[index]
        else:
            owner = (plane, plane + 1 - 2 * lax.rem(plane, 2))[index]
        source, target = self.piece_of(owner) if index else self.own_piece()
        return self.wires.copy(
            self.base + (SHARE_NEAR if near else SHARE_MIDDLE),
            index,
            source,
            target,
            beside if near else mirror,
        )

    def own_piece(self):
        return self.piece_of(lax.axis_index("dp"))

    def start(self):
        for index in range(len(self.sources)):
            self.cross(index).start()
            self.local(index).start()

    def send_own(self):
        self.over(True, 0).start()

        @pl.when(inner())
        def _():
            self.over(False, 0).start()

    def middle(self):
        for index in range(len(self.sources)):
            self.cross(index).wait_recv()
        self.send_own()

    def late(self):
        @pl.when(inner())
        def _():
            self.over(True, 0).wait_recv()
            self.over(False, 1).start()
            self.over(False, 0).wait_recv()
            self.over(True, 1).start()

    def later(self):
        @pl.when(inner())
        def _():
            self.over(False, 1).wait_recv()
            self.over(True, 2).start()

    def close_planes(self):
        self.over(True, 0).wait_send()

        @pl.when(inner())
        def _():
            self.over(True, 1).wait_send()
            self.over(True, 2).wait_send()
            self.over(False, 0).wait_send()
            self.over(False, 1).wait_send()

        @pl.when(jnp.logical_not(inner()))
        def _():
            for index in range(3):
                self.over(True, index).wait_recv()

    def close(self):
        self.close_planes()
        for index in range(len(self.sources)):
            self.cross(index).wait_send()
            self.local(index).wait()


class Spread(Share):
    def __init__(self, wires, base, source, whole, local_sems, quarter):
        super().__init__(wires, base, (source,), whole, True, local_sems)
        self.piece = quarter

    def own_piece(self):
        return self.piece, self.quarter(lax.axis_index("dp"))

    def own(self):
        return pltpu.make_async_copy(
            self.piece, self.quarter(lax.axis_index("dp")), self.local_sems.at[1]
        )

    def start(self):
        self.send_own()
        self.local(0).start()
        self.own().start()

    def close(self):
        self.close_planes()
        self.local(0).wait()
        self.own().wait()


FOLD_END, FOLD_MIDDLE, FOLD_BACK, FOLD_X = 0, 2, 4, 5
FOLD_KINDS = 6


def side():
    return lax.div(lax.axis_index("dp"), 2)


def turn_shard(turn):
    return 3 * (1 - side()) + turn * (2 * side() - 1)


class Fold:
    def __init__(self, wires, base, tiles, bufs, mine, theirs, first=None):
        self.wires, self.base, self.tiles, self.mine, self.theirs = (
            wires,
            base,
            tiles,
            mine,
            theirs,
        )
        self.first = tiles if first is None else first
        (self.recv,) = bufs
        self.near, self.mirror = planes()

    def send(self, kind, half, slot, source, target, device):
        target = self.recv.at[2 * target + half]
        return self.wires.copy(self.base + kind, slot, source, target, device)

    def end(self, half, turn):
        source = self.first.at[4 * half + turn_shard(turn)]
        return self.send(FOLD_END + half, half, turn, source, turn, self.near)

    def across(self, half, turn):
        source = self.recv.at[2 * turn + half]
        return self.send(FOLD_MIDDLE + half, half, turn, source, 3 + turn, self.mirror)

    def back(self, half):
        return self.send(FOLD_BACK, half, half, self.recv.at[6 + half], 0, self.near)

    def cross(self):
        source = self.tiles.at[4 + lax.axis_index("dp")]
        return self.wires.copy(self.base + FOLD_X, 0, source, self.theirs, neighbours()[0])

    def add(self, slot, half, shard):
        self.recv[2 * slot + half] = (
            self.recv[2 * slot + half].astype(F32) + self.tiles[4 * half + shard].astype(F32)
        ).astype(B16)

    def begin(self, turn, half):
        @pl.when(jnp.logical_not(inner()))
        def _():
            self.end(half, turn).start()

    def start(self):
        for turn in range(3):
            for half in (1, 0):
                self.begin(turn, half)

    def pass_on(self, turn):
        @pl.when(inner())
        def _():
            for half in (1, 0):
                self.end(half, turn).wait_recv()
                self.add(turn, half, turn_shard(turn))
                self.across(half, turn).start()

    def step(self):
        self.pass_on(0)

    def middle(self):
        self.pass_on(1)

        @pl.when(inner())
        def _():
            for half in (1, 0):
                self.across(half, 0).wait_recv()
                self.add(3, half, 3 * side())
                self.back(half).start()

    def late(self):
        plane = lax.axis_index("dp")
        for half in (1, 0):

            @pl.when(inner())
            def _():
                self.end(half, 2).wait_recv()
                self.across(half, 1).wait_recv()
                self.add(2, half, plane)

            @pl.when(jnp.logical_not(inner()))
            def _():
                self.back(half).wait_recv()

            at = 4 * half + plane
            middle = inner().astype(jnp.int32)
            total = self.recv[4 * middle + half].astype(F32)
            other = jnp.where(
                inner(), self.recv[8 * middle + half].astype(F32), self.tiles[at].astype(F32)
            )
            total = total + other
            if half == 1:
                self.tiles[at] = total.astype(B16)
                self.cross().start()
            else:
                self.mine[...] = total

    def close(self):
        self.cross().wait_recv()

        @pl.when(inner())
        def _():
            for half in range(2):
                self.across(half, 0).wait_send()
                self.across(half, 1).wait_send()
                self.back(half).wait_send()

        @pl.when(jnp.logical_not(inner()))
        def _():
            for half in range(2):
                for turn in range(3):
                    self.end(half, turn).wait_send()

        self.cross().wait_send()


def fold_scratch(rows, columns):
    return [pltpu.VMEM((10, rows, columns), B16)]


def turn_tile(step):
    return 4 * (1 - lax.rem(step, 2)) + turn_shard(lax.div(step, 2))


def make_tiles(fold, make, low, high):
    @pl.loop(low, high)
    def _(step):
        make(step)

        @pl.when(step < 6)
        def _():
            half = 1 - lax.rem(step, 2)
            turn = lax.div(step, 2)
            for side_half in range(2):

                @pl.when(half == side_half)
                def _():
                    fold.begin(turn, side_half)


class Reduce:
    def __init__(self, wires, rows_ref, weight_ref, transposed, bufs):
        self.wires, self.rows_ref, self.weight_ref, self.transposed = (
            wires,
            rows_ref,
            weight_ref,
            transposed,
        )
        (
            self.sibling_send,
            self.sibling_recv,
            self.kept_ref,
            self.out,
            self.corner_recv,
            self.x_recv,
            self.y_recv,
        ) = bufs
        self.rows = rows_ref.shape[1]
        self.width = (weight_ref.shape[0] if transposed else weight_ref.shape[1]) // 2
        self.count = self.width // CHUNK

    def product(self, block, chunk, half):
        left = self.rows_ref[block : block + 2].reshape(2 * self.rows, self.rows_ref.shape[2])
        at = lanes(chunk, half, self.width)
        if self.transposed:
            return rows_dot(left, self.weight_ref[at, :])
        return jnp.dot(left, self.weight_ref[:, at], preferred_element_type=F32)

    def sibling(self, chunk, half):
        return self.wires.copy(
            SIBLING + half * (REDUCE_KINDS - 1),
            chunk,
            self.sibling_send.at[lax.rem(chunk, 2), half],
            self.sibling_recv.at[chunk, half],
            neighbours()[2],
        )

    def corner(self, chunk, device):
        return self.wires.copy(
            CORNER, chunk, self.out.at[2, chunk], self.corner_recv.at[chunk], device
        )

    def final_x(self, chunk):
        return self.wires.copy(
            FINAL_X, chunk, self.out.at[0, chunk], self.x_recv.at[chunk], neighbours()[0]
        )

    def final_y(self, chunk):
        return self.wires.copy(
            FINAL_Y, chunk, self.out.at[1, chunk], self.y_recv.at[chunk], neighbours()[1]
        )

    def give(self, chunk):
        @pl.loop(0, 2)
        def _(turn):
            half = 1 - turn
            self.sibling_send[lax.rem(chunk, 2), half] = self.product(2, chunk, half).astype(B16)
            self.sibling(chunk, half).start()

    def take(self, chunk):
        rows = self.rows
        even = lax.rem(chunk, 2) == 0
        side, across, _ = neighbours()

        @pl.loop(0, 2)
        def _(turn):
            half = 1 - turn
            own = self.product(0, chunk, half)
            self.sibling(chunk, half).wait_recv()
            total = own + self.sibling_recv[chunk, half].astype(F32)

            @pl.when(half == 1)
            def _():
                self.out[2, chunk] = total[rows:].astype(B16)
                self.out[0, chunk] = total[:rows].astype(B16)

                @pl.when(even)
                def _():
                    self.corner(chunk, side).start()
                    self.final_x(chunk).start()

                @pl.when(jnp.logical_not(even))
                def _():
                    self.corner(chunk, across).start()

            @pl.when(half == 0)
            def _():
                self.kept_ref[chunk] = total[:rows]
                self.out[1, chunk] = total[rows:].astype(B16)

                @pl.when(jnp.logical_not(even))
                def _():
                    self.final_y(chunk).start()

    def start(self, between=(lambda: None, lambda: None)):
        self.give(0)
        self.take(0)
        self.give(1)
        self.take(1)
        between[0]()

        @pl.loop(2, self.count)
        def _(chunk):
            for half in range(2):
                self.sibling(chunk - 2, half).wait_send()
            self.give(chunk)
            self.take(chunk)

        between[1]()

    def middle(self):
        @pl.loop(0, self.count)
        def _(chunk):
            even = lax.rem(chunk, 2) == 0
            self.corner(chunk, neighbours()[0]).wait_recv()
            came = self.corner_recv[chunk].astype(F32)

            @pl.when(even)
            def _():
                self.out[1, chunk] = (self.out[1, chunk].astype(F32) + came).astype(B16)
                self.final_y(chunk).start()

            @pl.when(jnp.logical_not(even))
            def _():
                self.out[0, chunk] = (self.out[0, chunk].astype(F32) + came).astype(B16)
                self.final_x(chunk).start()

    def total(self, chunk):
        self.final_x(chunk).wait_recv()
        self.final_y(chunk).wait_recv()
        return (
            self.kept_ref[chunk] + self.x_recv[chunk].astype(F32) + self.y_recv[chunk].astype(F32)
        )

    def close(self):
        @pl.loop(self.count - 2, self.count)
        def _(chunk):
            for half in range(2):
                self.sibling(chunk, half).wait_send()

        @pl.loop(0, self.count)
        def _(chunk):
            self.corner(chunk, neighbours()[0]).wait_send()
            self.final_x(chunk).wait_send()
            self.final_y(chunk).wait_send()


def reduce_scratch(rows, width):
    count = width // CHUNK
    return [
        pltpu.VMEM((2, 2, 2 * rows, CHUNK), B16),
        pltpu.VMEM((count, 2, 2 * rows, CHUNK), B16),
        pltpu.VMEM((count, rows, CHUNK), F32),
        pltpu.VMEM((3, count, rows, CHUNK), B16),
        pltpu.VMEM((count, rows, CHUNK), B16),
        pltpu.VMEM((count, rows, CHUNK), B16),
        pltpu.VMEM((count, rows, CHUNK), B16),
    ]


def gather_scratch(rows, width):
    count = width // CHUNK
    return [pltpu.VMEM((count, rows, CHUNK), B16), pltpu.SemaphoreType.DMA((count,))]


def wire_scratch(kinds, count):
    return [pltpu.SemaphoreType.DMA((kinds, count))] * 2


IN_VMEM = pl.BlockSpec(memory_space=pltpu.VMEM)
IN_ANY = pl.BlockSpec(memory_space=pl.ANY)
VMEM_MOST = 60 * 1024 * 1024


def remote_params(number):
    return pltpu.CompilerParams(
        collective_id=number, has_side_effects=True, vmem_limit_bytes=VMEM_MOST
    )


def cost(flops, size):
    return pl.CostEstimate(flops=flops, bytes_accessed=size, transcendentals=0)


def shape(dims, kind=B16):
    return jax.ShapeDtypeStruct(dims, kind)


def cut(own, block_ref):
    for chunk in range(own.shape[0]):
        own[chunk] = block_ref[:, chunk * CHUNK : (chunk + 1) * CHUNK]


def open_kernel(
    tokens_ref,
    query_ref,
    key_ref,
    value_ref,
    out_ref,
    gains_ref,
    seg_ref,
    rate_ref,
    gains_all_ref,
    starts_ref,
    cosine_ref,
    sine_ref,
    whole_ref,
    project_ref,
    branch_ref,
    *scratch,
):
    own, gather_sem, send_sems, recv_sems, project_sem, branch_sem = scratch[:6]
    gains_recv, seg_recv, seg_all = scratch[6:]
    width = gains_ref.shape[1]
    length = seg_ref.shape[1]
    cut(own, tokens_ref)
    greet(neighbours() + planes())
    wires = Wires(send_sems, recv_sems)
    gather = Gather(wires, 0, whole_ref, own, gather_sem, 2)
    base = GATHER_KINDS + 2 * SHARE_KINDS
    side = neighbours()[0]
    gains = wires.copy(base, 0, gains_ref, gains_recv, side)
    segs = wires.copy(base, 1, seg_ref, seg_recv, side)
    shares = [
        Share(wires, GATHER_KINDS, (query_ref, key_ref, value_ref), project_ref, True, project_sem),
        Share(wires, GATHER_KINDS + SHARE_KINDS, (out_ref,), branch_ref, False, branch_sem),
    ]
    gains.start()
    segs.start()
    shares[0].start()
    shares[1].start()

    @pl.loop(0, gather.count)
    def _(chunk):
        gather.send(chunk)

    gains.wait()
    segs.wait()
    gains_all_ref[:, :width] = gains_ref[...]
    gains_all_ref[:, width:] = gains_recv[...]
    mine = lax.rem(lax.axis_index("ty") + lax.div(lax.axis_index("tx"), 2), 2)
    seg_all[pl.ds(mine, 1)] = seg_ref[...].astype(F32)[None]
    seg_all[pl.ds(1 - mine, 1)] = seg_recv[...].astype(F32)[None]

    shares[0].middle()
    shares[1].middle()

    @pl.loop(0, 2)
    def _(seq):
        for low in range(0, length, 128):
            here = stand(seg_all[seq, :, low : low + 128])
            before = jnp.zeros((128, 128), F32)
            for other in range(0, length, 128):
                before += (seg_all[seq, :, other : other + 128] < here).astype(F32)
            start = jnp.sum(before, axis=1, keepdims=True)
            at = slice(low, low + 128)
            starts_ref[seq, at, :] = start.astype(jnp.int32)
            row = lax.broadcasted_iota(jnp.int32, (128, 128), 0) + low
            lane = lax.broadcasted_iota(jnp.int32, (128, 128), 1)
            angle = (row.astype(F32) - start) * rate_ref[...]
            cosine_ref[seq, at, :] = jnp.cos(angle)
            sine = jnp.sin(angle)
            sine_ref[seq, at, :] = jnp.where(lane < 64, -sine, sine)

        @pl.when(seq == 0)
        def _():
            shares[0].late()
            shares[1].late()
            gather.relay(0, 2)
            shares[0].later()
            shares[1].later()

    gather.relay(2)
    gather.close()
    shares[0].close()
    shares[1].close()


def open_call(tokens, w_query, w_key, w_value, w_out, gains, seg_ids, rate, number):
    rows, width = tokens.shape
    columns = (w_query.shape[1] + w_key.shape[1] + w_value.shape[1]) // 2
    length = seg_ids.shape[1]
    return pl.pallas_call(
        open_kernel,
        out_shape=(
            shape((2, 2 * width), F32),
            shape((2, length, 1), jnp.int32),
            shape((2, length, 128), F32),
            shape((2, length, 128), F32),
            shape((4, rows, 2 * width)),
            shape((2 * width, columns)),
            shape((w_out.shape[0] // 2, 2 * width)),
        ),
        in_specs=[IN_VMEM] * 8,
        out_specs=(IN_VMEM,) * 4 + (IN_ANY,) * 3,
        scratch_shapes=gather_scratch(rows, width)
        + wire_scratch(GATHER_KINDS + 2 * SHARE_KINDS + 1, width // CHUNK)
        + [
            pltpu.SemaphoreType.DMA((3,)),
            pltpu.SemaphoreType.DMA((1,)),
            pltpu.VMEM((2, width), F32),
            pltpu.VMEM((1, length), jnp.int32),
            pltpu.VMEM((2, 1, length), F32),
        ],
        compiler_params=remote_params(number),
        cost_estimate=cost(0, 32 * rows * width),
    )(tokens, w_query, w_key, w_value, w_out, gains, seg_ids, rate)


def front_kernel(
    most,
    whole_ref,
    project_ref,
    gain_ref,
    starts_ref,
    cosine_ref,
    sine_ref,
    query_gain_ref,
    key_gain_ref,
    grad_ref,
    down_ref,
    gate_in_ref,
    first_ref,
    scale_ref,
    projected_ref,
    mixed_ref,
    query_ref,
    key_ref,
    value_ref,
    log_ref,
    grad_whole_ref,
    back_ref,
    gate_ref,
    *scratch,
):
    own, gather_sem, send_sems, recv_sems, back_sem, tokens, firsts, tile_sem = scratch
    core = lax.rem(lax.axis_index("tx"), 2)
    cut(own, grad_ref)
    rows = whole_ref.shape[1]

    def spot(ref, tile):
        at = pl.ds(pl.multiple_of(lax.rem(tile, rows // BLOCK) * BLOCK, BLOCK), BLOCK)
        return ref.at[lax.div(tile, rows // BLOCK), at, :]

    def fetch(tile):
        slot = lax.rem(tile, 2)
        return pltpu.make_async_copy(spot(whole_ref, tile), tokens.at[slot], tile_sem.at[0, slot])

    def store(tile):
        slot = lax.rem(tile, 2)
        return pltpu.make_async_copy(firsts.at[slot], spot(first_ref, tile), tile_sem.at[1, slot])

    fetch(0).start()
    greet(neighbours() + planes())
    wires = Wires(send_sems, recv_sems)
    gather = Gather(wires, 0, grad_whole_ref, own, gather_sem, 0)
    back = Share(wires, GATHER_KINDS, (down_ref,), back_ref, False, back_sem)
    size, columns = gate_ref.shape
    gate = wires.copy(
        GATHER_KINDS + SHARE_KINDS,
        0,
        gate_in_ref.at[
            pl.ds(pl.multiple_of(lax.axis_index("dp") * size, size), size),
            pl.ds(pl.multiple_of((1 - lax.axis_index("ty")) * columns, columns), columns),
        ],
        gate_ref,
        neighbours()[0],
    )
    back.start()
    gate.start()

    @pl.loop(0, gather.count)
    def _(chunk):
        gather.send(chunk)

    count = 4 * rows // BLOCK

    @pl.loop(0, count)
    def _(tile):
        slot = lax.rem(tile, 2)
        block = lax.div(tile, rows // BLOCK)
        at = pl.ds(pl.multiple_of(lax.rem(tile, rows // BLOCK) * BLOCK, BLOCK), BLOCK)

        @pl.when(tile < count - 1)
        def _():
            fetch(tile + 1).start()

        fetch(tile).wait()

        @pl.when(tile >= 2)
        def _():
            store(tile - 2).wait()

        value = tokens[slot].astype(F32)
        scale = lax.rsqrt(jnp.mean(value * value, axis=1, keepdims=True) + EPS)
        first = (value * scale * gain_ref[...]).astype(B16)
        firsts[slot] = first
        store(tile).start()
        projected_ref[block, at, :] = jnp.dot(
            first, project_ref[...], preferred_element_type=F32
        )

        @pl.when(block == 0)
        def _():
            scale_ref[at, :] = jnp.broadcast_to(scale, (BLOCK, 128))

        @pl.when(tile == count // 2)
        def _():
            back.middle()

    fixed_refs = (starts_ref, cosine_ref, sine_ref, query_gain_ref, key_gain_ref)
    saved_refs = (query_ref, key_ref, value_ref, log_ref)

    @pl.loop(0, 2)
    def _(seq):
        def between(turn):
            @pl.when(seq == 0)
            def _():
                if turn == 0:
                    back.late()
                elif turn == 2:
                    back.later()
                gather.relay(turn, turn + 1)

        attend_sequence(
            core, seq, most, projected_ref, fixed_refs, mixed_ref, saved_refs, between
        )

    for tile in range(count - 2, count):
        store(tile).wait()
    gather.close()
    back.close()
    gate.wait()


def front_call(whole, w_project, gain, fixed_args, most, cotangent, w_down, w_gate, number):
    starts, cosine, sine, query_gain, key_gain = fixed_args
    rows, width = cotangent.shape
    length = cosine.shape[1]
    depth = query_gain.shape[1]
    columns = w_project.shape[1]
    heads = columns // depth - 2
    outs = (
        shape((4, rows, 2 * width)),
        shape((rows, 128), F32),
        shape((4, rows, columns), F32),
        shape((4, rows, heads * depth)),
        shape((2, length, heads * depth)),
        shape((2, length, depth)),
        shape((2, length, depth)),
        shape((2, heads, length, 1), F32),
        shape((4, rows, 2 * width)),
        shape((w_down.shape[0] // 2, 2 * width)),
        shape((width // 4, w_gate.shape[1] // 2)),
    )
    return pl.pallas_call(
        lambda *refs: front_kernel(most, *refs),
        out_shape=outs,
        in_specs=[IN_ANY] + [IN_VMEM] * 10,
        out_specs=[IN_ANY] + [IN_VMEM] * 7 + [IN_ANY] * 3,
        scratch_shapes=gather_scratch(rows, width)
        + wire_scratch(GATHER_KINDS + SHARE_KINDS + 1, width // CHUNK)
        + [
            pltpu.SemaphoreType.DMA((1,)),
            pltpu.VMEM((2, BLOCK, 2 * width), B16),
            pltpu.VMEM((2, BLOCK, 2 * width), B16),
            pltpu.SemaphoreType.DMA((2, 2)),
        ],
        compiler_params=remote_params(number),
        cost_estimate=cost(16 * rows * width * columns, 64 * rows * width),
    )(whole, w_project, gain, *fixed_args, cotangent, w_down, w_gate)


def branch_kernel(
    rows_in_ref,
    weight_in_ref,
    input_in_ref,
    up_in_ref,
    gate_in_ref,
    quarter_ref,
    residual_ref,
    whole_ref,
    up_ref,
    gate_ref,
    *scratch,
):
    bufs = scratch[:7]
    own, gather_sem, send_sems, recv_sems, up_sem = scratch[7:12]
    held, load_sem, gate_sem = scratch[12:17], scratch[17], scratch[18]
    rows_ref, weight_ref, input_ref, up_held, gate_held = held
    loads = Loads(
        (rows_in_ref, weight_in_ref, input_in_ref, up_in_ref, gate_in_ref), held, load_sem
    )
    loads.start()
    width = input_ref.shape[1]
    greet(neighbours() + planes())
    wires = Wires(send_sems, recv_sems)
    reduce = Reduce(wires, rows_ref, weight_ref, False, bufs)
    gather = Gather(wires, REDUCE_KINDS, whole_ref, own, gather_sem, 0)
    up = Share(
        wires, REDUCE_KINDS + GATHER_KINDS, (up_in_ref,), up_ref, True, up_sem, (up_held,)
    )
    gate = Spread(
        wires,
        REDUCE_KINDS + GATHER_KINDS + SHARE_KINDS,
        gate_held,
        gate_ref,
        gate_sem,
        quarter_ref,
    )
    loads.wait(0, 2)

    def between():
        loads.wait(2, 5)
        up.start()
        gate.start()

    reduce.start((between, gate.late))
    up.middle()
    reduce.middle()
    gate.later()

    @pl.loop(0, width // CHUNK)
    def _(chunk):
        at = lanes(chunk, 0, width)
        residual = input_ref[:, at].astype(F32) + reduce.total(chunk)
        residual_ref[:, at] = residual
        own[chunk] = residual.astype(B16)
        gather.send(chunk)

    up.late()
    gather.relay()
    up.later()
    gather.close()
    up.close()
    gate.close()
    reduce.close()


def branch_call(rows, weight, inputs, w_up, w_gate, quarter, number):
    height, width = inputs.shape
    count = width // CHUNK
    loaded = (rows, weight, inputs, w_up, w_gate)
    return pl.pallas_call(
        branch_kernel,
        out_shape=(
            shape((height, width), F32),
            shape((4, height, 2 * width)),
            shape((2 * width, w_up.shape[1] // 2)),
            shape((2 * width, w_gate.shape[1] // 2)),
        ),
        in_specs=[IN_ANY] * 6,
        out_specs=(IN_VMEM, IN_ANY, IN_ANY, IN_ANY),
        scratch_shapes=reduce_scratch(height, width)
        + gather_scratch(height, width)
        + wire_scratch(REDUCE_KINDS + GATHER_KINDS + 2 * SHARE_KINDS, count)
        + [pltpu.SemaphoreType.DMA((1,))]
        + load_scratch(loaded)
        + [pltpu.SemaphoreType.DMA((2,))],
        compiler_params=remote_params(number),
        cost_estimate=cost(16 * height * rows.shape[2] * width, 64 * height * width),
    )(*loaded, quarter)


def units_kernel(
    whole_ref, grad_ref, gates_ref, uppers_ref, back_ref, gain_ref, second_ref, hidden_ref, unit_ref, scale_ref, stats_ref
):
    units = hidden_ref.shape[1]
    value = whole_ref[...].astype(F32)
    scale = lax.rsqrt(jnp.mean(value * value, axis=1, keepdims=True) + EPS)
    second = (value * scale * gain_ref[...]).astype(B16)
    second_ref[...] = second
    scale_ref[...] = jnp.broadcast_to(scale, scale_ref.shape)
    total = jnp.zeros((value.shape[0], 1), F32)
    for low in range(0, units, CHUNK):
        at = slice(low, low + CHUNK)
        beside = slice(units + low, units + low + CHUNK)
        gate = jnp.dot(second, gates_ref[:, at], preferred_element_type=F32)
        upper = jnp.dot(second, uppers_ref[:, at], preferred_element_type=F32)
        hidden_grad = rows_dot(grad_ref[...], back_ref[at, :])
        sigma = jax.nn.sigmoid(gate)
        passed = gate * sigma
        hidden_ref[:, at] = (passed * upper).astype(B16)
        gate_grad = (hidden_grad * upper * (sigma + passed * (1.0 - sigma))).astype(B16)
        up_grad = (hidden_grad * passed).astype(B16)
        unit_ref[:, at] = gate_grad
        unit_ref[:, beside] = up_grad
        total += jnp.sum(
            gate_grad.astype(F32) * gate + up_grad.astype(F32) * upper, axis=1, keepdims=True
        )
    stats_ref[...] = jnp.zeros_like(stats_ref)
    for tile in range(stats_ref.shape[0]):
        put_stats(stats_ref, tile, total[tile * BLOCK : (tile + 1) * BLOCK])


def units_call(whole, grad, w_gates, w_uppers, w_back, gain):
    tokens, width = whole.shape
    units = w_back.shape[0]
    size = 2 * BLOCK
    tiles = tokens // size

    def tile(columns):
        return pl.BlockSpec((size, columns), lambda i: (i, 0))

    def all_of(item):
        return pl.BlockSpec(item.shape, lambda i: (0, 0))

    return pl.pallas_call(
        units_kernel,
        out_shape=(
            shape((tokens, width)),
            shape((tokens, units)),
            shape((tokens, 2 * units)),
            shape((tokens, 128), F32),
            shape((2 * tiles, 8, 128), F32),
        ),
        grid=(tiles,),
        in_specs=[tile(width), tile(width)]
        + [all_of(item) for item in (w_gates, w_uppers, w_back, gain)],
        out_specs=(
            tile(width),
            tile(units),
            tile(2 * units),
            tile(128),
            pl.BlockSpec((2, 8, 128), lambda i: (i, 0, 0)),
        ),
        compiler_params=pltpu.CompilerParams(vmem_limit_bytes=VMEM_MOST),
        cost_estimate=cost(6 * tokens * width * units, 20 * tokens * width // 2),
    )(whole, grad, w_gates, w_uppers, w_back, gain)


class Loads:
    def __init__(self, sources, targets, sems):
        self.copies = [
            pltpu.make_async_copy(source, target, sems.at[index])
            for index, (source, target) in enumerate(zip(sources, targets))
        ]

    def start(self):
        for copy in self.copies:
            copy.start()

    def wait(self, low, high):
        for copy in self.copies[low:high]:
            copy.wait()


def load_scratch(items):
    return [pltpu.VMEM(item.shape, item.dtype) for item in items] + [
        pltpu.SemaphoreType.DMA((len(items),))
    ]


class Stats:
    def __init__(self, wires, base, ref, recv):
        self.ref, self.recv = ref, recv
        side, across, core = neighbours()
        self.hops = (
            lambda: wires.copy(base, 0, ref.at[4:8], recv.at[0:4], core),
            lambda: wires.copy(base, 1, ref.at[2:4], recv.at[4:6], across),
            lambda: wires.copy(base, 2, ref.at[0:2], recv.at[6:8], side),
        )
        self.spans = ((4, 0), (2, 4), (2, 6))

    def start(self, hop):
        self.hops[hop]().start()

    def finish(self, hop):
        self.hops[hop]().wait()
        size, at = self.spans[hop]
        self.ref[0:size] = self.ref[0:size] + self.recv[at : at + size]

    def step(self, hop):
        self.finish(hop)
        self.start(hop + 1)


def pull_columns(stats_ref, scale_ref, column_ref, width):
    for part in range(scale_ref.shape[0] // 128):
        at = slice(part * 128, (part + 1) * 128)
        scale = scale_ref[at, :]
        column_ref[at, :] = (
            stand(stats_ref[part // 2, part % 2 : part % 2 + 1, :]) * scale * scale / (2 * width)
        )


def pulled(reduce, chunk, refs, column_ref):
    scale_ref, value_ref, gain_ref, base_ref = refs
    at = lanes(chunk, 0, value_ref.shape[1])
    upstream = reduce.total(chunk)
    value = value_ref[:, at].astype(F32)
    scale = scale_ref[:, 0:1]
    back = scale * gain_ref[:, at] * upstream - value * column_ref[:, 0:1]
    return at, base_ref[:, at].astype(F32) + back, upstream * value * scale


def tile_columns(tile):
    return pl.ds(pl.multiple_of(tile * BLOCK, BLOCK), BLOCK)


SPLIT = 512


def middle_kernel(
    rows_in_ref,
    gates_in_ref,
    uppers_in_ref,
    value_in_ref,
    base_in_ref,
    branch_in_ref,
    mixed_in_ref,
    stats_in_ref,
    scale_ref,
    gain_ref,
    down_in_ref,
    second_ref,
    result_ref,
    gain_grad_ref,
    upstream_ref,
    out_ref,
    whole_ref,
    rest_ref,
    *refs,
):
    ends, scratch = refs[:4], refs[4:]
    bufs = scratch[:7]
    stats_ref, stats_recv, column_ref, send_sems, recv_sems, own, gather_sem = scratch[7:14]
    stream, stream_sem, down_sem, stage, stage_sem, upstream = scratch[14:20]
    down_tiles, down_recv, made_tiles, made_recv = scratch[20:24]
    weight_ref, rows_ref, value_ref, base_ref, branch_ref, mixed_ref = scratch[24:30]
    load_sem = scratch[30]
    rows, width = value_ref.shape
    columns = rows_ref.shape[2]
    load = pltpu.make_async_copy(down_in_ref, down_tiles, down_sem)
    units = gates_in_ref.shape[1]
    loads = Loads(
        (
            rows_in_ref,
            gates_in_ref,
            uppers_in_ref,
            value_in_ref,
            base_in_ref,
            branch_in_ref,
            mixed_in_ref,
        ),
        (
            rows_ref,
            weight_ref.at[:, :units],
            weight_ref.at[:, units:],
            value_ref,
            base_ref,
            branch_ref,
            mixed_ref,
        ),
        load_sem,
    )

    def fetch(ref, step, tile):
        slot = lax.rem(step, 2)
        return pltpu.make_async_copy(
            ref.at[:, :, tile_columns(tile)], stream.at[slot], stream_sem.at[slot]
        )

    loads.start()
    load.start()
    fetch(second_ref, 0, turn_tile(0)).start()
    stats_ref[...] = stats_in_ref[...]
    greet(neighbours() + planes())
    wires = Wires(send_sems, recv_sems)
    base = REDUCE_KINDS + 1 + GATHER_KINDS
    down = Fold(wires, base, down_tiles, (down_recv,), ends[0], ends[1], down_in_ref)
    made = Fold(wires, base + FOLD_KINDS, made_tiles, (made_recv,), ends[2], ends[3])
    stats = Stats(wires, REDUCE_KINDS, stats_ref, stats_recv)
    down.start()
    stats.start(0)
    reduce = Reduce(wires, rows_ref, weight_ref, True, bufs)
    loads.wait(0, 3)
    reduce.start((lambda: stats.step(0), lambda: stats.step(1)))
    load.wait()
    down.step()

    def store(step):
        slot = lax.rem(step, 2)
        return pltpu.make_async_copy(
            stage.at[slot], rest_ref.at[turn_tile(step)], stage_sem.at[slot]
        )

    def make(step):
        slot = lax.rem(step, 2)

        @pl.when(step < 7)
        def _():
            fetch(second_ref, step + 1, turn_tile(step + 1)).start()

        fetch(second_ref, step, turn_tile(step)).wait()

        @pl.when(step >= 2)
        def _():
            store(step - 2).wait()

        left = stream[slot].reshape(4 * rows, BLOCK)
        flat = rows_ref[...].reshape(4 * rows, columns)
        made.tiles[turn_tile(step)] = weight_grad(left, flat[:, :SPLIT]).astype(B16)
        for low in range(SPLIT, columns, SPLIT):
            stage[slot, :, low - SPLIT : low] = weight_grad(
                left, flat[:, low : low + SPLIT]
            ).astype(B16)
        store(step).start()

    make_tiles(made, make, 0, 4)
    reduce.middle()
    stats.finish(2)
    pull_columns(stats_ref, scale_ref, column_ref, width)
    down.middle()
    make_tiles(made, make, 4, 8)
    loads.wait(3, 7)
    gather = Gather(wires, REDUCE_KINDS + 1, whole_ref, own, gather_sem)

    @pl.loop(0, width // CHUNK)
    def _(chunk):
        at, result, share = pulled(
            reduce, chunk, (scale_ref, value_ref, gain_ref, base_ref), column_ref
        )
        result_ref[:, at] = result
        own[chunk] = result.astype(B16)
        gather.send(chunk)
        gain_grad_ref[:, at] = jnp.sum(share, axis=0, keepdims=True)

    for step in (6, 7):
        store(step).wait()
    down.late()
    gather.relay(0, 2)
    made.step()
    gather.relay(2)
    made.middle()
    gather.close()
    made.late()
    fetch(whole_ref, 0, 0).start()
    upstream[...] = jnp.zeros_like(upstream)

    @pl.loop(0, 8)
    def _(tile):
        @pl.when(tile < 7)
        def _():
            fetch(whole_ref, tile + 1, tile + 1).start()

        fetch(whole_ref, tile, tile).wait()
        left = stream[lax.rem(tile, 2)].reshape(4 * rows, BLOCK)
        upstream[...] += rows_dot(left, branch_ref[:, tile_columns(tile)])
        out_ref[tile] = weight_grad(left, mixed_ref[...].reshape(4 * rows, -1)).astype(B16)

    upstream_ref[...] = upstream[...].astype(B16).reshape(upstream_ref.shape)
    down.close()
    made.close()
    reduce.close()


def middle_call(
    rows, w_gates, w_uppers, stats, scale, value, gain, base, down, second, w_branch, mixed, number
):
    height, width = value.shape
    count = width // CHUNK
    columns = rows.shape[2]
    quarter, units = down.shape[1:]
    heads = mixed.shape[2]
    sizes = (units, SPLIT)
    ends, tiles = [], []
    for size in sizes:
        ends += [shape((quarter, size), F32), shape((quarter, size))]
        tiles += [pltpu.VMEM((8, quarter, size), B16)] + fold_scratch(quarter, size)
    loaded = (rows, w_gates, w_uppers, value, base, w_branch, mixed)
    return pl.pallas_call(
        middle_kernel,
        out_shape=[
            shape((height, width), F32),
            shape((1, width), F32),
            shape((4, height, heads)),
            shape((8, quarter, heads)),
            shape((4, height, 2 * width)),
            shape((8, quarter, columns - SPLIT)),
        ]
        + ends,
        in_specs=[IN_ANY] * 7 + [IN_VMEM] * 3 + [IN_ANY] * 2,
        out_specs=[IN_VMEM] * 4 + [IN_ANY] * 2 + [IN_VMEM, IN_ANY] * 2,
        scratch_shapes=reduce_scratch(height, width)
        + [
            pltpu.VMEM((8, 8, 128), F32),
            pltpu.VMEM((8, 8, 128), F32),
            pltpu.VMEM((height, 128), F32),
        ]
        + wire_scratch(REDUCE_KINDS + 1 + GATHER_KINDS + 2 * FOLD_KINDS, count)
        + gather_scratch(height, width)
        + [
            pltpu.VMEM((2, 4, height, BLOCK), B16),
            pltpu.SemaphoreType.DMA((2,)),
            pltpu.SemaphoreType.DMA,
            pltpu.VMEM((2, quarter, columns - SPLIT), B16),
            pltpu.SemaphoreType.DMA((2,)),
            pltpu.VMEM((4 * height, heads), F32),
        ]
        + tiles
        + [pltpu.VMEM((2 * width, columns), B16)]
        + load_scratch((rows,) + loaded[3:])[:-1]
        + [pltpu.SemaphoreType.DMA((len(loaded),))],
        compiler_params=remote_params(number),
        cost_estimate=cost(48 * height * units * width, 64 * height * width),
    )(*loaded, stats, scale, gain, down, second)


def last_kernel(
    rows_in_ref,
    weight_in_ref,
    value_in_ref,
    base_in_ref,
    stats_in_ref,
    scale_ref,
    gain_ref,
    extra_ref,
    out_in_ref,
    first_ref,
    result_ref,
    totals_ref,
    out_mine_ref,
    out_theirs_ref,
    project_mine_ref,
    project_theirs_ref,
    *scratch,
):
    bufs = scratch[:7]
    stats_ref, stats_recv, column_ref, send_sems, recv_sems = scratch[7:12]
    out_ref, project_ref, whole, sums_ref, sums_recv, load_sem = scratch[12:18]
    out_bufs, project_bufs = scratch[18:19], scratch[19:20]
    rows_ref, weight_ref, value_ref, base_ref = scratch[20:24]
    rows, width = value_ref.shape
    loads = Loads(
        (rows_in_ref, weight_in_ref, first_ref, value_in_ref, base_in_ref, out_in_ref),
        (rows_ref, weight_ref, whole, value_ref, base_ref, out_ref),
        load_sem,
    )
    loads.start()
    stats_ref[...] = stats_in_ref[...]
    sums_ref[...] = jnp.zeros_like(sums_ref)
    sums_ref[8] = extra_ref[0]
    sums_ref[9] = extra_ref[1]
    greet(neighbours() + planes())
    wires = Wires(send_sems, recv_sems)
    base = REDUCE_KINDS + 1
    out = Fold(wires, base, out_ref, out_bufs, out_mine_ref, out_theirs_ref, out_in_ref)
    project = Fold(
        wires, base + FOLD_KINDS, project_ref, project_bufs, project_mine_ref, project_theirs_ref
    )
    stats = Stats(wires, REDUCE_KINDS, stats_ref, stats_recv)
    stats.start(0)
    out.start()
    loads.wait(0, 2)

    def make(step):
        tile = turn_tile(step)
        left = whole[:, :, tile_columns(tile)].reshape(4 * rows, BLOCK)
        grad = weight_grad(left, rows_ref[...].reshape(4 * rows, rows_ref.shape[2]))
        project_ref[tile] = grad.astype(B16)
        share = jnp.sum(
            grad * weight_ref[tile_columns(tile), :].astype(F32), axis=1, keepdims=True
        )
        sums_ref[tile, 0:1, :] = lie(share[:128])
        sums_ref[tile, 1:2, :] = lie(share[128:])

    side, across, core = neighbours()
    near, far = planes()
    hops = [
        lambda hop=hop, device=device: wires.copy(
            base + 2 * FOLD_KINDS, hop, sums_ref, sums_recv.at[hop], device
        )
        for hop, device in enumerate((core, across, near, far))
    ]

    def add(hop):
        hops[hop]().wait()
        sums_ref[...] = sums_ref[...] + sums_recv[hop]

    reduce = Reduce(wires, rows_ref, weight_ref, True, bufs)
    reduce.start((lambda: stats.step(0), lambda: stats.step(1)))
    loads.wait(2, 3)
    make_tiles(project, make, 0, 8)
    hops[0]().start()
    loads.wait(3, 6)
    out.step()
    add(0)
    hops[1]().start()
    reduce.middle()
    out.middle()
    project.step()
    stats.finish(2)
    pull_columns(stats_ref, scale_ref, column_ref, width)
    add(1)
    hops[2]().start()
    project.middle()
    add(2)
    hops[3]().start()

    @pl.loop(0, width // CHUNK)
    def _(chunk):
        at, result, _ = pulled(
            reduce, chunk, (scale_ref, value_ref, gain_ref, base_ref), column_ref
        )
        result_ref[:, at] = result.astype(B16)

    out.late()
    project.late()
    add(3)
    move = wires.copy(base + 2 * FOLD_KINDS + 1, 0, sums_ref, sums_recv.at[4], side)
    move.start()
    move.wait()
    totals_ref[0:4] = sums_ref[0:4] + sums_recv[4, 4:8]
    totals_ref[4:8] = sums_ref[4:8] + sums_recv[4, 0:4]
    totals_ref[8] = sums_ref[8]
    totals_ref[9] = sums_recv[4, 8]
    totals_ref[10] = sums_ref[9] + sums_recv[4, 9]
    project.close()
    out.close()
    reduce.close()


def last_call(rows, weight, stats, scale, value, gain, base, extra, out, first, number):
    height, width = value.shape
    count = width // CHUNK
    quarter, branch = out.shape[1:]
    columns = rows.shape[2]
    return pl.pallas_call(
        last_kernel,
        out_shape=(
            shape((height, width)),
            shape((11, 8, 128), F32),
            shape((quarter, branch), F32),
            shape((quarter, branch)),
            shape((quarter, columns), F32),
            shape((quarter, columns)),
        ),
        in_specs=[IN_ANY] * 4 + [IN_VMEM] * 4 + [IN_ANY] * 2,
        out_specs=(IN_VMEM, IN_VMEM) + (IN_VMEM, IN_ANY) * 2,
        scratch_shapes=reduce_scratch(height, width)
        + [
            pltpu.VMEM((8, 8, 128), F32),
            pltpu.VMEM((8, 8, 128), F32),
            pltpu.VMEM((height, 128), F32),
        ]
        + wire_scratch(REDUCE_KINDS + 1 + 2 * FOLD_KINDS + 2, count)
        + [
            pltpu.VMEM((8, quarter, branch), B16),
            pltpu.VMEM((8, quarter, columns), B16),
            pltpu.VMEM((4, height, 2 * width), B16),
            pltpu.VMEM((10, 8, 128), F32),
            pltpu.VMEM((5, 10, 8, 128), F32),
            pltpu.SemaphoreType.DMA((6,)),
        ]
        + fold_scratch(quarter, branch)
        + fold_scratch(quarter, columns)
        + load_scratch((rows, weight, value, base))[:4],
        compiler_params=remote_params(number),
        cost_estimate=cost(32 * height * columns * width, 64 * height * width),
    )(rows, weight, value, base, stats, scale, gain, extra, out, first)


def back_kernel(
    most,
    query_gain_ref,
    key_gain_ref,
    *refs,
):
    operands, refs = refs[:12], refs[12:]
    rest_ref, refs = refs[0], refs[1:]
    output_ref, result_ref, stats_ref, gains_ref = refs[:4]
    ends, scratch = refs[4:6], refs[6:]
    bufs = scratch[:7]
    query_acc, key_acc, value_acc, send_sems, recv_sems, rest_sem = scratch[7:13]
    tiles, fold_recv = scratch[13:15]
    held, load_sem = scratch[15:27], scratch[27]
    hidden_ref, down_ref, upstream, starts_ref, cosine_ref, sine_ref = held[:6]
    projected_ref, query_ref, key_ref, value_ref, log_ref, residual_ref = held[6:]
    attend_loads = Loads(operands, held, load_sem)
    attend_loads.start()
    width = residual_ref.shape[1]
    core = lax.rem(lax.axis_index("tx"), 2)
    load = pltpu.make_async_copy(rest_ref, tiles, rest_sem)
    load.start()
    greet(neighbours() + planes())
    wires = Wires(send_sems, recv_sems)
    fold = Fold(wires, REDUCE_KINDS, tiles, (fold_recv,), ends[0], ends[1], rest_ref)
    fold.start()
    reduce = Reduce(wires, hidden_ref, down_ref, False, bufs)
    attend_loads.wait(0, 2)
    reduce.start()
    attend_loads.wait(2, 12)
    load.wait()
    stats_ref[...] = jnp.zeros_like(stats_ref)
    fixed_refs = (starts_ref, cosine_ref, sine_ref, query_gain_ref, key_gain_ref)
    saved_refs = (query_ref, key_ref, value_ref, log_ref)

    @pl.loop(0, 2)
    def _(seq):
        attend_sequence_back(
            core,
            seq,
            most,
            projected_ref,
            upstream,
            fixed_refs,
            saved_refs,
            result_ref,
            stats_ref,
            gains_ref,
            (query_acc, key_acc, value_acc),
        )

        @pl.when(seq == 0)
        def _():
            reduce.middle()
            fold.step()

    fold.middle()


    @pl.loop(0, width // CHUNK)
    def _(chunk):
        at = lanes(chunk, 0, width)
        output_ref[:, at] = (residual_ref[:, at] + reduce.total(chunk)).astype(B16)

    fold.late()
    fold.close()
    reduce.close()


def back_call(upstream, hidden, w_back, residual, fixed_args, projected, saved, rest, most, number):
    height, width = residual.shape
    _, cosine, _, query_gain, _ = fixed_args
    depth = query_gain.shape[1]
    length = cosine.shape[1]
    columns = projected.shape[2]
    heads = columns // depth - 2
    quarter, columns_left = rest.shape[1:]
    loaded = (hidden, w_back, upstream) + fixed_args[:3] + (projected,) + saved + (residual,)
    return pl.pallas_call(
        lambda *refs: back_kernel(most, *refs),
        out_shape=(
            shape((height, width)),
            shape((4, height, columns)),
            shape((8, 8, 128), F32),
            shape((2, 8, depth), F32),
        )
        + (shape((quarter, columns_left), F32), shape((quarter, columns_left))),
        in_specs=[IN_VMEM] * 2 + [IN_ANY] * 13,
        out_specs=[IN_VMEM] * 5 + [IN_ANY],
        scratch_shapes=reduce_scratch(height, width)
        + [
            pltpu.VMEM((length, heads * depth), F32),
            pltpu.VMEM((length, depth), F32),
            pltpu.VMEM((length, depth), F32),
        ]
        + wire_scratch(REDUCE_KINDS + FOLD_KINDS, width // CHUNK)
        + [pltpu.SemaphoreType.DMA, pltpu.VMEM(rest.shape, B16)]
        + fold_scratch(quarter, columns_left)
        + load_scratch(loaded),
        compiler_params=remote_params(number),
        cost_estimate=cost(16 * height * hidden.shape[2] * width, 64 * height * width),
    )(*fixed_args[3:], *loaded, rest)


def finish_kernel(place_ref, *refs):
    downs, both, out, project = refs[0:2], refs[2:6], refs[6:8], refs[8:10]
    totals_ref, gain_ref = refs[10:12]
    query_ref, key_ref, value_ref, out_ref, gate_ref, up_ref, down_ref = refs[12:19]
    attn_ref, mlp_ref = refs[19:]
    first = place_ref[0] == 0

    def ordered(mine, theirs):
        theirs = theirs.astype(F32)
        return jnp.where(first, mine, theirs), jnp.where(first, theirs, mine)

    def put(target, at, mine, theirs):
        half = target.shape[1] // 2
        low, high = ordered(mine, theirs)
        target[:, at : at + mine.shape[1]] = low
        target[:, half + at : half + at + mine.shape[1]] = high

    def put_turned(target, at, mine, theirs):
        half = target.shape[0] // 2
        low, high = ordered(mine, theirs)
        target[at : at + mine.shape[1], :] = low.T
        target[half + at : half + at + mine.shape[1], :] = high.T

    put_turned(down_ref, 0, downs[0][...], downs[1][...])
    put_turned(out_ref, 0, out[0][...], out[1][...])
    at = 0
    for target in (query_ref, key_ref, value_ref):
        size = target.shape[1] // 2
        put(target, 0, project[0][:, at : at + size], project[1][:, at : at + size])
        at += size
    units = gate_ref.shape[1] // 2
    at = 0
    for index in (0, 2):
        low = 0
        while low < both[index].shape[1]:
            size = min(both[index].shape[1] - low, units - at % units)
            put(
                gate_ref if at < units else up_ref,
                at % units,
                both[index][:, low : low + size],
                both[index + 1][:, low : low + size],
            )
            low += size
            at += size
    mine = jnp.concatenate([totals_ref[tile, 0:2] for tile in range(4)], axis=0)
    theirs = jnp.concatenate([totals_ref[tile, 0:2] for tile in range(4, 8)], axis=0)
    low, high = ordered(mine / gain_ref[0:8], theirs / gain_ref[8:16])
    attn_ref[0:8], attn_ref[8:16] = low, high
    low, high = ordered(totals_ref[8], totals_ref[9])
    mlp_ref[0:8], mlp_ref[8:16] = low, high


def finish_call(place, parts, totals, gain, sizes):
    quarter = parts[0].shape[0]
    queries, keys, branch, units = sizes
    return pl.pallas_call(
        finish_kernel,
        out_shape=(
            shape((quarter, queries), F32),
            shape((quarter, keys), F32),
            shape((quarter, keys), F32),
            shape((branch, quarter), F32),
            shape((quarter, units), F32),
            shape((quarter, units), F32),
            shape((units, quarter), F32),
            shape((16, 128), F32),
            shape((16, 128), F32),
        ),
        in_specs=[pl.BlockSpec(memory_space=pltpu.SMEM)] + [IN_VMEM] * (len(parts) + 2),
        out_specs=[IN_VMEM] * 9,
        compiler_params=pltpu.CompilerParams(vmem_limit_bytes=VMEM_MOST),
        cost_estimate=cost(0, 16 * 1024 * 1024),
    )(place, *parts, totals, gain)


def product_grad(left, right):
    return weight_grad(left, right).astype(B16)


def plane_device(
    tokens,
    seg_ids,
    w_query,
    w_key,
    w_value,
    w_out,
    w_gate,
    w_up,
    w_down,
    attn_gain,
    mlp_gain,
    query_gain,
    key_gain,
    cotangent,
):
    depth = query_gain.shape[0]
    most = seg_ids.shape[1] // 2
    rows, width = tokens.shape
    head_width = w_query.shape[1] // 2
    kv_width = w_key.shape[1] // 2
    units = w_gate.shape[1] // 2

    half = jnp.arange(depth // 2, dtype=F32)
    rate = THETA ** (-half * 2.0 / depth)
    rate = jnp.concatenate([rate, rate])[None]
    gains, starts, cosine, sine, token_whole, w_project, w_branch = open_call(
        tokens, w_query, w_key, w_value, w_out, jnp.stack([attn_gain, mlp_gain]), seg_ids, rate, 0
    )
    fixed_args = (starts, cosine, sine, query_gain[None], key_gain[None])
    (
        first,
        first_scale,
        projected,
        mixed,
        query,
        keys,
        values,
        logs,
        grad_whole,
        w_back,
        gate_quarter,
    ) = front_call(
        token_whole, w_project, gains[0:1], fixed_args, most, cotangent, w_down, w_gate, 1
    )
    residual, residual_whole, w_uppers, w_gates = branch_call(
        mixed, w_branch, tokens, w_up, w_gate, gate_quarter, 2
    )
    flat = (4 * rows, 2 * width)
    grad_flat = grad_whole.reshape(flat)
    second, hidden, unit_grads, second_scale, unit_stats = units_call(
        residual_whole.reshape(flat), grad_flat, w_gates, w_uppers, w_back, gains[1:2]
    )
    tiles = lambda grad: grad.reshape(8, -1, grad.shape[1])
    (
        residual_grad,
        mlp_gain_part,
        upstream,
        out_tiles,
        _,
        rest_tiles,
        *ends,
    ) = middle_call(
        unit_grads.reshape(4, rows, 2 * units),
        w_gates,
        w_uppers,
        unit_stats,
        second_scale[:rows],
        residual,
        mlp_gain[None],
        cotangent,
        tiles(product_grad(grad_flat, hidden)),
        second.reshape(4, rows, 2 * width),
        w_branch,
        mixed,
        3,
    )
    output, proj_grads, proj_stats, gain_parts, *rest_ends = back_call(
        upstream,
        hidden.reshape(4, rows, units),
        w_back,
        residual,
        fixed_args,
        projected,
        (query, keys, values, logs),
        rest_tiles,
        most,
        4,
    )
    extra = jnp.stack(
        [
            mlp_gain_part.reshape(8, 128),
            jnp.pad(jnp.sum(gain_parts[:, :2], axis=0), ((0, 6), (0, 0))),
        ]
    )
    input_grad, totals, out_mine, out_theirs, project_mine, project_theirs = last_call(
        proj_grads,
        w_project,
        proj_stats,
        first_scale,
        tokens,
        attn_gain[None],
        residual_grad,
        extra,
        out_tiles,
        first,
        5,
    )
    place = lax.axis_index("ty").reshape(1).astype(jnp.int32)
    (
        query_share,
        key_share,
        value_share,
        out_share,
        gate_share,
        up_share,
        down_share,
        attn_total,
        mlp_total,
    ) = finish_call(
        place,
        (*ends, *rest_ends, out_mine, out_theirs, project_mine, project_theirs),
        totals,
        gains[0].reshape(16, 128),
        (2 * head_width, 2 * kv_width, 2 * head_width, 2 * units),
    )
    attn_total, mlp_total = attn_total.reshape(-1), mlp_total.reshape(-1)
    query_total, key_total = totals[10, 0], totals[10, 1]
    return (
        output,
        input_grad,
        query_share,
        key_share,
        value_share,
        out_share,
        gate_share,
        up_share,
        down_share,
        attn_total,
        mlp_total,
        query_total,
        key_total,
    )


def solution(mesh):
    placed = (
        P(("dp", "tx"), "ty"),
        P(("dp", "ty"), None),
        P("ty", "tx"),
        P("ty", "tx"),
        P("ty", "tx"),
        P("tx", "ty"),
        P("ty", "tx"),
        P("ty", "tx"),
        P("tx", "ty"),
        P("ty"),
        P("ty"),
        P(),
        P(),
        P(("dp", "tx"), "ty"),
    )
    return jax.shard_map(
        plane_device if fits(mesh) else general_device,
        mesh=mesh,
        in_specs=placed,
        out_specs=(
            P(("dp", "tx"), "ty"),
            P(("dp", "tx"), "ty"),
            P(("ty", "dp"), "tx"),
            P(("ty", "dp"), "tx"),
            P(("ty", "dp"), "tx"),
            P("tx", ("ty", "dp")),
            P(("ty", "dp"), "tx"),
            P(("ty", "dp"), "tx"),
            P("tx", ("ty", "dp")),
            P(),
            P(),
            P(),
            P(),
        ),
        check_vma=False,
    )
```

```python
import jax
import jax.numpy as jnp
from jax import lax
from jax.experimental import pallas as pl
from jax.experimental.pallas import tpu as pltpu
from jax.sharding import PartitionSpec as P

EPS = 1e-06
THETA = 1000000.0
NEG = -1e30
F32 = jnp.float32
B16 = jnp.bfloat16
MESH = pl.DeviceIdType.MESH


def width_sum(value):
    return lax.psum(value, "ty")


def token_gather(rows):
    return lax.all_gather(rows, "tx", axis=0, tiled=True)


def branch_gather(rows):
    return lax.all_gather(rows, "ty", axis=0, tiled=True)


def width_reduce(whole, apply):
    return lax.psum_scatter(apply(whole), "ty", scatter_dimension=0, tiled=True)


def head_reduce(whole, apply):
    return lax.psum_scatter(
        apply(whole).astype(jnp.bfloat16), "tx", scatter_dimension=0, tiled=True
    ).astype(jnp.float32)


def forward_with(weight):
    return lambda rows: jnp.dot(rows, weight, preferred_element_type=F32)


def backward_with(weight):
    return lambda rows: lax.dot_general(
        rows, weight, (((1,), (1,)), ((), ())), preferred_element_type=F32
    )


def weight_grad(left, right):
    return lax.dot_general(left, right, (((0,), (0,)), ((), ())), preferred_element_type=F32)


def norm_scale(rows):
    width = rows.shape[1] * lax.axis_size("ty")
    return lax.rsqrt(width_sum(jnp.sum(rows * rows, axis=1)) / width + EPS)


def norm_back(rows, scale, gain, upstream):
    width = rows.shape[1] * lax.axis_size("ty")
    inner = width_sum(jnp.sum(upstream * gain * rows, axis=1))
    back = scale[:, None] * gain * upstream - rows * (scale**3 * inner / width)[:, None]
    gain_part = jnp.sum(upstream * rows * scale[:, None], axis=0)
    return (back, gain_part)


def widen(part):
    whole = jnp.zeros((part.shape[0] * lax.axis_size("ty"),), F32)
    return lax.dynamic_update_slice_in_dim(whole, part, lax.axis_index("ty") * part.shape[0], 0)


def doc_positions(seg):
    count = seg.shape[-1]
    index = jnp.arange(count, dtype=jnp.int32)
    edge = jnp.concatenate([jnp.ones((1,), dtype=jnp.bool_), seg[1:] != seg[:-1]])
    first = lax.cummax(jnp.where(edge, index, jnp.zeros_like(index)), axis=0)
    return index - first


def rotary(positions, depth):
    half = depth // 2
    freq = THETA ** (-jnp.arange(half, dtype=F32) * 2.0 / depth)
    angle = positions.astype(F32)[..., None] * freq
    return (jnp.cos(angle), jnp.sin(angle))


def turn(value, gain, cosine, sine):
    normed = value * lax.rsqrt(jnp.mean(value * value, axis=-1, keepdims=True) + EPS) * gain
    half = value.shape[-1] // 2
    first = normed[..., :half]
    second = normed[..., half:]
    return jnp.concatenate(
        [first * cosine - second * sine, second * cosine + first * sine], axis=-1
    )


def block_scores(part, seq_keys, seq_ids, start, scale):
    block = part.shape[0]
    length = seq_ids.shape[0]
    index = jnp.arange(length, dtype=jnp.int32)
    rows = start + jnp.arange(block, dtype=jnp.int32)
    row_ids = lax.dynamic_slice_in_dim(seq_ids, start, block, 0)
    mask = (seq_ids[None, :] == row_ids[:, None]) & (index[None, :] <= rows[:, None])
    scores = jnp.einsum("qkgd,mkd->kgqm", part, seq_keys, preferred_element_type=F32) * scale
    return jnp.where(mask[None, None], scores, NEG)


def attend_forward(query, keys, values, seg, block):
    seqs, length, heads, depth = query.shape
    kv_heads = keys.shape[2]
    groups = heads // kv_heads
    scale = depth ** (-0.5)
    count = length // block
    starts = jnp.arange(count, dtype=jnp.int32) * block

    def one_sequence(operands):
        seq_query, seq_keys, seq_values, seq_ids = operands
        blocks = seq_query.reshape(count, block, kv_heads, groups, depth)

        def one_block(inputs):
            part, start = inputs
            scores = block_scores(part, seq_keys, seq_ids, start, scale)
            top = jnp.max(scores, axis=-1)
            weights = jnp.exp(scores - top[..., None])
            total = jnp.sum(weights, axis=-1)
            probs = (weights / total[..., None]).astype(B16)
            mixed = jnp.einsum("kgqm,mkd->qkgd", probs, seq_values, preferred_element_type=F32)
            return (mixed, top + jnp.log(total))

        mixed, logs = lax.map(one_block, (blocks, starts))
        return (mixed.reshape(length, heads * depth), logs)

    return lax.map(one_sequence, (query, keys, values, seg))


def attend_backward(query, keys, values, seg, logs, grad_out, block):
    seqs, length, heads, depth = query.shape
    kv_heads = keys.shape[2]
    groups = heads // kv_heads
    scale = depth ** (-0.5)
    count = length // block
    starts = jnp.arange(count, dtype=jnp.int32) * block

    def one_sequence(operands):
        seq_query, seq_keys, seq_values, seq_ids, seq_logs, seq_grad = operands
        blocks = seq_query.reshape(count, block, kv_heads, groups, depth)
        grads = seq_grad.reshape(count, block, kv_heads, groups, depth)

        def one_block(carry, inputs):
            key_acc, value_acc = carry
            part, grad_part, log_part, start = inputs
            scores = block_scores(part, seq_keys, seq_ids, start, scale)
            probs = jnp.exp(scores - log_part[..., None])
            value_acc = value_acc + jnp.einsum(
                "kgqm,qkgd->mkd", probs.astype(B16), grad_part, preferred_element_type=F32
            )
            prob_grad = jnp.einsum(
                "qkgd,mkd->kgqm", grad_part, seq_values, preferred_element_type=F32
            )
            delta = jnp.sum(probs * prob_grad, axis=-1, keepdims=True)
            score_grad = (probs * (prob_grad - delta)).astype(B16)
            query_grad = (
                jnp.einsum("kgqm,mkd->qkgd", score_grad, seq_keys, preferred_element_type=F32)
                * scale
            )
            key_acc = (
                key_acc
                + jnp.einsum("kgqm,qkgd->mkd", score_grad, part, preferred_element_type=F32) * scale
            )
            return ((key_acc, value_acc), query_grad)

        zeros = jnp.zeros((length, kv_heads, depth), F32)
        (key_grad, value_grad), query_grad = lax.scan(
            one_block, (zeros, zeros), (blocks, grads, seq_logs, starts)
        )
        return (query_grad.reshape(length, heads, depth), key_grad, value_grad)

    return lax.map(one_sequence, (query, keys, values, seg, logs, grad_out))


def general_device(
    tokens,
    seg_ids,
    w_query,
    w_key,
    w_value,
    w_out,
    w_gate,
    w_up,
    w_down,
    attn_gain,
    mlp_gain,
    query_gain,
    key_gain,
    cotangent,
):
    seqs, length = seg_ids.shape
    depth = query_gain.shape[0]
    query_width = w_query.shape[1]
    key_width = w_key.shape[1]
    units = w_gate.shape[1]
    block = min(512, length)
    inputs = tokens.astype(F32)
    first_scale = norm_scale(inputs)
    first_normed = (inputs * first_scale[:, None] * attn_gain).astype(B16)
    first_whole = token_gather(first_normed)
    w_project = jnp.concatenate([w_query, w_key, w_value], axis=1)
    projected = width_reduce(first_whole, forward_with(w_project))
    query_proj = projected[:, :query_width].reshape(seqs, length, -1, depth)
    key_proj = projected[:, query_width : query_width + key_width].reshape(seqs, length, -1, depth)
    values = projected[:, query_width + key_width :].astype(B16).reshape(seqs, length, -1, depth)
    positions = jax.vmap(doc_positions)(seg_ids)
    cosine, sine = rotary(positions, depth)
    cosine = cosine[:, :, None, :]
    sine = sine[:, :, None, :]
    query = turn(query_proj, query_gain, cosine, sine).astype(B16)
    keys = turn(key_proj, key_gain, cosine, sine).astype(B16)
    mixed, logs = attend_forward(query, keys, values, seg_ids, block)
    attended = mixed.reshape(seqs * length, -1).astype(B16)
    attended_whole = branch_gather(attended)
    residual = inputs + head_reduce(attended_whole, forward_with(w_out))
    second_scale = norm_scale(residual)
    second_normed = (residual * second_scale[:, None] * mlp_gain).astype(B16)
    second_whole = token_gather(second_normed)
    w_both = jnp.concatenate([w_gate, w_up], axis=1)
    gate_up = width_reduce(second_whole, forward_with(w_both))
    gate = gate_up[:, :units]
    upper = gate_up[:, units:]
    hidden = (jax.nn.silu(gate) * upper).astype(B16)
    hidden_whole = branch_gather(hidden)
    output = residual + head_reduce(hidden_whole, forward_with(w_down))
    grad_whole = token_gather(cotangent)
    hidden_grad = width_reduce(grad_whole, backward_with(w_down))
    down_grad = weight_grad(hidden_whole, grad_whole)
    gate_grad, up_grad = jax.vjp(lambda left, right: jax.nn.silu(left) * right, gate, upper)[1](
        hidden_grad
    )
    unit_grads = jnp.concatenate([gate_grad, up_grad], axis=1).astype(B16)
    unit_whole = branch_gather(unit_grads)
    second_grad = head_reduce(unit_whole, backward_with(w_both))
    both_grad = weight_grad(second_whole, unit_whole)
    gate_weight = both_grad[:, :units]
    up_weight = both_grad[:, units:]
    resid_norm_grad, mlp_gain_part = norm_back(residual, second_scale, mlp_gain, second_grad)
    residual_grad = cotangent.astype(F32) + resid_norm_grad
    residual_whole = token_gather(residual_grad.astype(B16))
    mixed_grad = width_reduce(residual_whole, backward_with(w_out)).astype(B16)
    out_grad = weight_grad(attended_whole, residual_whole)
    query_grad, key_grad, value_grad = attend_backward(
        query, keys, values, seg_ids, logs, mixed_grad.reshape(seqs, length, -1), block
    )
    query_proj_grad, query_gain_grad = jax.vjp(
        lambda value, gain: turn(value, gain, cosine, sine), query_proj, query_gain
    )[1](query_grad)
    key_proj_grad, key_gain_grad = jax.vjp(
        lambda value, gain: turn(value, gain, cosine, sine), key_proj, key_gain
    )[1](key_grad)
    rows = seqs * length
    proj_grad = jnp.concatenate(
        [
            query_proj_grad.reshape(rows, -1),
            key_proj_grad.reshape(rows, -1),
            value_grad.reshape(rows, -1),
        ],
        axis=1,
    ).astype(B16)
    proj_whole = branch_gather(proj_grad)
    first_grad = head_reduce(proj_whole, backward_with(w_project))
    project_grad = weight_grad(first_whole, proj_whole)
    query_weight = project_grad[:, :query_width]
    key_weight = project_grad[:, query_width : query_width + key_width]
    value_weight = project_grad[:, query_width + key_width :]
    input_norm_grad, attn_gain_part = norm_back(inputs, first_scale, attn_gain, first_grad)
    input_grad = (residual_grad + input_norm_grad).astype(B16)
    attn_total, mlp_total, query_total, key_total = lax.psum(
        (widen(attn_gain_part), widen(mlp_gain_part), query_gain_grad, key_gain_grad),
        ("dp", "tx", "ty"),
    )
    query_share, key_share, value_share, gate_share, up_share = (
        lax.psum_scatter(
            query_weight.astype(jnp.bfloat16), "dp", scatter_dimension=0, tiled=True
        ).astype(jnp.float32),
        lax.psum_scatter(
            key_weight.astype(jnp.bfloat16), "dp", scatter_dimension=0, tiled=True
        ).astype(jnp.float32),
        lax.psum_scatter(
            value_weight.astype(jnp.bfloat16), "dp", scatter_dimension=0, tiled=True
        ).astype(jnp.float32),
        lax.psum_scatter(
            gate_weight.astype(jnp.bfloat16), "dp", scatter_dimension=0, tiled=True
        ).astype(jnp.float32),
        lax.psum_scatter(
            up_weight.astype(jnp.bfloat16), "dp", scatter_dimension=0, tiled=True
        ).astype(jnp.float32),
    )
    out_share, down_share = (
        lax.psum_scatter(
            out_grad.astype(jnp.bfloat16), "dp", scatter_dimension=1, tiled=True
        ).astype(jnp.float32),
        lax.psum_scatter(
            down_grad.astype(jnp.bfloat16), "dp", scatter_dimension=1, tiled=True
        ).astype(jnp.float32),
    )
    return (
        output.astype(B16),
        input_grad,
        query_share,
        key_share,
        value_share,
        out_share,
        gate_share,
        up_share,
        down_share,
        attn_total,
        mlp_total,
        query_total,
        key_total,
    )


def fits(mesh):
    return mesh.shape["tx"] == 4 and mesh.shape["ty"] == 2 and mesh.shape["dp"] == 4


def swap_x(value):
    return lax.ppermute(value, "ty", [(0, 1), (1, 0)])


def in_order(mine, theirs, axis):
    first = lax.axis_index("ty") == 0
    return jnp.concatenate(
        [jnp.where(first, mine, theirs), jnp.where(first, theirs, mine)], axis=axis
    )


def spin(value, cosine, sine):
    return value * cosine + pltpu.roll(value, value.shape[1] // 2, 1) * sine


def spin_back(value, cosine, sine):
    return value * cosine + pltpu.roll(value * sine, value.shape[1] // 2, 1)


def head_scale(value):
    return lax.rsqrt(jnp.mean(value * value, axis=1, keepdims=True) + EPS)


def window(first, block, most):
    return max(0, first - most), first + block


def kept(first, block, low, high, starts):
    shape = (block, high - low)
    column = low + lax.broadcasted_iota(jnp.int32, shape, 1)
    row = first + lax.broadcasted_iota(jnp.int32, shape, 0)
    return (column >= starts) & (column <= row)


def rows_dot(left, right):
    return lax.dot_general(left, right, (((1,), (1,)), ((), ())), preferred_element_type=F32)


def stand(row):
    return jnp.transpose(jnp.broadcast_to(row, (row.shape[1], row.shape[1])))


def lie(column):
    return jnp.transpose(jnp.broadcast_to(column, (column.shape[0], column.shape[0])))[0:1]


def put_stats(stats_ref, tile, column):
    stats_ref[tile, 0:1, :] = lie(column[:128])
    stats_ref[tile, 1:2, :] = lie(column[128:])


BLOCK = 256


def attend_sequence(core, seq, most, projected, fixed_refs, mixed, saved_refs, between):
    starts_ref, cosine_ref, sine_ref, query_gain_ref, key_gain_ref = fixed_refs
    query_ref, key_ref, value_ref, log_ref = saved_refs
    rows = projected.shape[1]
    length = query_ref.shape[1]
    depth = key_ref.shape[2]
    heads = query_ref.shape[2] // depth
    scale = depth ** (-0.5)
    for half in range(2):
        place = 2 * lax.rem(core + half, 2) + seq
        for at in range(half * rows, (half + 1) * rows, BLOCK):
            inner = at - half * rows
            cosine = cosine_ref[seq, at : at + BLOCK, :]
            sine = sine_ref[seq, at : at + BLOCK, :]
            for head in range(heads + 2):
                lane = slice(head * depth, (head + 1) * depth)
                value = projected[place, inner : inner + BLOCK, lane]
                if head < heads:
                    normed = value * head_scale(value) * query_gain_ref[...]
                    query_ref[seq, at : at + BLOCK, lane] = spin(normed, cosine, sine).astype(B16)
                elif head == heads:
                    normed = value * head_scale(value) * key_gain_ref[...]
                    key_ref[seq, at : at + BLOCK, :] = spin(normed, cosine, sine).astype(B16)
                else:
                    value_ref[seq, at : at + BLOCK, :] = value.astype(B16)
    for first in range(0, length, BLOCK):
        between(first // BLOCK)
        low, high = window(first, BLOCK, most)
        mask = kept(first, BLOCK, low, high, starts_ref[seq, first : first + BLOCK, :])
        half, inner = divmod(first, rows)
        place = 2 * lax.rem(core + half, 2) + seq
        for head in range(heads):
            lane = slice(head * depth, (head + 1) * depth)
            query = query_ref[seq, first : first + BLOCK, lane]
            scores = rows_dot(query, key_ref[seq, low:high, :]) * scale
            scores = jnp.where(mask, scores, NEG)
            top = jnp.max(scores, axis=1, keepdims=True)
            weights = jnp.exp(scores - top)
            total = jnp.sum(weights, axis=1, keepdims=True)
            probs = (weights * (1.0 / total)).astype(B16)
            out = jnp.dot(probs, value_ref[seq, low:high, :], preferred_element_type=F32)
            mixed[place, inner : inner + BLOCK, lane] = out.astype(B16)
            log_ref[seq, head, first : first + BLOCK, :] = top + jnp.log(total)


def attend_sequence_back(
    core, seq, most, projected, upstream, fixed_refs, saved_refs, result, stats, gains, accs
):
    starts_ref, cosine_ref, sine_ref, query_gain_ref, key_gain_ref = fixed_refs
    query_ref, key_ref, value_ref, log_ref = saved_refs
    query_acc, key_acc, value_acc = accs
    rows = projected.shape[1]
    length = query_ref.shape[1]
    depth = key_ref.shape[2]
    heads = query_ref.shape[2] // depth
    scale = depth ** (-0.5)
    key_acc[...] = jnp.zeros_like(key_acc)
    value_acc[...] = jnp.zeros_like(value_acc)
    for first in range(0, length, BLOCK):
        low, high = window(first, BLOCK, most)
        mask = kept(first, BLOCK, low, high, starts_ref[seq, first : first + BLOCK, :])
        half, inner = divmod(first, rows)
        place = 2 * lax.rem(core + half, 2) + seq
        keys = key_ref[seq, low:high, :]
        values = value_ref[seq, low:high, :]
        for head in range(heads):
            lane = slice(head * depth, (head + 1) * depth)
            query = query_ref[seq, first : first + BLOCK, lane]
            grad = upstream[place, inner : inner + BLOCK, lane]
            scores = rows_dot(query, keys) * scale - log_ref[seq, head, first : first + BLOCK, :]
            probs = jnp.exp(jnp.where(mask, scores, NEG))
            prob_grad = rows_dot(grad, values)
            delta = jnp.sum(probs * prob_grad, axis=1, keepdims=True)
            score_grad = (probs * (prob_grad - delta)).astype(B16)
            query_acc[first : first + BLOCK, lane] = (
                jnp.dot(score_grad, keys, preferred_element_type=F32) * scale
            )
            key_acc[low:high, :] += weight_grad(score_grad, query) * scale
            value_acc[low:high, :] += weight_grad(probs.astype(B16), grad)
    query_total = jnp.zeros((1, depth), F32)
    key_total = jnp.zeros((1, depth), F32)
    for half in range(2):
        block = 2 * lax.rem(core + half, 2) + seq
        for at in range(half * rows, (half + 1) * rows, BLOCK):
            inner = at - half * rows
            cosine = cosine_ref[seq, at : at + BLOCK, :]
            sine = sine_ref[seq, at : at + BLOCK, :]
            total = jnp.zeros((BLOCK, 1), F32)
            for head in range(heads + 2):
                lane = slice(head * depth, (head + 1) * depth)
                value = projected[block, inner : inner + BLOCK, lane]
                if head == heads + 1:
                    back = value_acc[at : at + BLOCK, :].astype(B16)
                else:
                    if head < heads:
                        grad = query_acc[at : at + BLOCK, lane]
                        gain = query_gain_ref[...]
                    else:
                        grad = key_acc[at : at + BLOCK, :]
                        gain = key_gain_ref[...]
                    grad = spin_back(grad, cosine, sine)
                    rate = head_scale(value)
                    scaled = value * rate
                    share = jnp.sum(grad * scaled, axis=0, keepdims=True)
                    if head < heads:
                        query_total += share
                    else:
                        key_total += share
                    middle = jnp.mean(gain * grad * scaled, axis=1, keepdims=True)
                    back = (rate * (gain * grad - scaled * middle)).astype(B16)
                result[block, inner : inner + BLOCK, lane] = back
                total += jnp.sum(back.astype(F32) * value, axis=1, keepdims=True)
            put_stats(stats, 2 * block + inner // BLOCK, total)
    gains[seq, 0:1, :] = query_total
    gains[seq, 1:2, :] = key_total


def neighbours():
    spot = lax.axis_index("tx")
    core = lax.rem(spot, 2)
    return (
        {"ty": 1 - lax.axis_index("ty")},
        {"tx": lax.rem(spot + 2, 4)},
        {"tx": spot + 1 - 2 * core},
    )


def planes():
    plane = lax.axis_index("dp")
    return {"dp": plane + 1 - 2 * lax.rem(plane, 2)}, {"dp": 3 - plane}


def inner():
    plane = lax.axis_index("dp")
    return (plane == 1) | (plane == 2)


def greet(targets):
    barrier = pltpu.get_barrier_semaphore()
    for target in targets:
        pl.semaphore_signal(barrier, inc=1, device_id=target, device_id_type=MESH)
    pl.semaphore_wait(barrier, len(targets))


class Wires:
    def __init__(self, send_sems, recv_sems):
        self.send_sems = send_sems
        self.recv_sems = recv_sems

    def copy(self, kind, chunk, source, target, device):
        return pltpu.make_async_remote_copy(
            src_ref=source,
            dst_ref=target,
            send_sem=self.send_sems.at[kind, chunk],
            recv_sem=self.recv_sems.at[kind, chunk],
            device_id=device,
            device_id_type=MESH,
        )


CHUNK = 256
SIBLING, CORNER, FINAL_X, FINAL_Y = 0, 1, 2, 3
REDUCE_KINDS = 5
OUT_X, OUT_Y, OUT_CORNER, CORE_OWN, CORE_X, CORE_Y, CORE_CORNER = range(7)
GATHER_KINDS = 7
SHARE_X, SHARE_NEAR, SHARE_MIDDLE = 0, 1, 2
SHARE_KINDS = 3


def lanes(chunk, half, width):
    return pl.ds(pl.multiple_of(half * width + chunk * CHUNK, CHUNK), CHUNK)


class Gather:
    def __init__(self, wires, base, whole, own, local_sem, most=4):
        self.wires, self.base, self.whole, self.own, self.local_sem = (
            wires,
            base,
            whole,
            own,
            local_sem,
        )
        self.most = most
        self.width = whole.shape[2] // 2
        self.count = self.width // CHUNK

    def place(self, block, chunk, half):
        return self.whole.at[block, :, lanes(chunk, half, self.width)]

    def copy(self, name, chunk):
        side, across, core = neighbours()
        at = self.place
        own = self.own.at[chunk]
        if name == "local":
            return pltpu.make_async_copy(own, at(0, chunk, 0), self.local_sem.at[chunk])
        kind, source, target, device = {
            "x": (OUT_X, own, at(0, chunk, 1), side),
            "y": (OUT_Y, own, at(1, chunk, 0), across),
            "core": (CORE_OWN, own, at(2, chunk, 0), core),
            "even": (OUT_CORNER, at(0, chunk, 1), at(1, chunk, 1), across),
            "odd": (OUT_CORNER, at(1, chunk, 0), at(1, chunk, 1), side),
            "core_x": (CORE_X, at(0, chunk, 1), at(2, chunk, 1), core),
            "core_y": (CORE_Y, at(1, chunk, 0), at(3, chunk, 0), core),
            "core_corner": (CORE_CORNER, at(1, chunk, 1), at(3, chunk, 1), core),
        }[name]
        return self.wires.copy(self.base + kind, chunk, source, target, device)

    def send(self, chunk):
        for name in ("x", "y", "core", "local"):
            self.copy(name, chunk).start()

    def relay(self, low=0, high=None):
        @pl.loop(low, self.count if high is None else high)
        def _(chunk):
            even = (lax.rem(chunk, 2) == 0) | (chunk >= self.most)
            self.copy("x", chunk).wait_recv()

            @pl.when(even)
            def _():
                self.copy("even", chunk).start()

            self.copy("core_x", chunk).start()
            self.copy("y", chunk).wait_recv()

            @pl.when(jnp.logical_not(even))
            def _():
                self.copy("odd", chunk).start()

            self.copy("core_y", chunk).start()

    def close(self):
        @pl.loop(0, self.count)
        def _(chunk):
            self.copy("even", chunk).wait_recv()
            self.copy("core_corner", chunk).start()

        @pl.loop(0, self.count)
        def _(chunk):
            for name in ("core", "core_x", "core_y", "core_corner"):
                self.copy(name, chunk).wait_recv()
            for name in ("x", "y", "core", "even", "core_x", "core_y", "core_corner"):
                self.copy(name, chunk).wait_send()
            self.copy("local", chunk).wait()


class Share:
    def __init__(self, wires, base, sources, whole, by_rows, local_sems, held=None):
        self.wires, self.base, self.sources, self.whole, self.by_rows, self.local_sems = (
            wires,
            base,
            sources,
            whole,
            by_rows,
            local_sems,
        )
        self.held = held or sources
        self.size = (whole.shape[0] // 2 if by_rows else whole.shape[0]) // 4

    def quarter(self, plane):
        start = plane * self.size
        if self.by_rows:
            rows = pl.ds(pl.multiple_of(self.whole.shape[0] // 2 + start, self.size), self.size)
            return self.whole.at[rows]
        width = self.whole.shape[1] // 2
        return self.whole.at[pl.ds(pl.multiple_of(start, self.size), self.size), width:]

    def cross(self, index):
        side, _, _ = neighbours()
        plane = lax.axis_index("dp")
        other = 1 - lax.axis_index("ty")
        source = self.sources[index]
        if self.by_rows:
            rows = pl.ds(pl.multiple_of(plane * self.size, self.size), self.size)
            columns = source.shape[1] // 2
            part = source.at[rows, pl.ds(pl.multiple_of(other * columns, columns), columns)]
            offset = sum(item.shape[1] // 2 for item in self.sources[:index])
            target = self.quarter(plane).at[:, offset : offset + columns]
        else:
            start = pl.multiple_of(other * (source.shape[0] // 2) + plane * self.size, self.size)
            part = source.at[pl.ds(start, self.size)]
            target = self.quarter(plane)
        return self.wires.copy(self.base + SHARE_X, index, part, target, side)

    def local(self, index):
        mine = lax.axis_index("ty")
        source = self.held[index]
        if self.by_rows:
            columns = source.shape[1] // 2
            offset = sum(item.shape[1] // 2 for item in self.sources[:index])
            part = source.at[:, pl.ds(pl.multiple_of(mine * columns, columns), columns)]
            target = self.whole.at[: self.whole.shape[0] // 2, offset : offset + columns]
        else:
            half = source.shape[0] // 2
            part = source.at[pl.ds(pl.multiple_of(mine * half, half), half)]
            target = self.whole.at[:, : self.whole.shape[1] // 2]
        return pltpu.make_async_copy(part, target, self.local_sems.at[index])

    def piece_of(self, owner):
        place = self.quarter(owner)
        return place, place

    def over(self, near, index):
        beside, mirror = planes()
        plane = lax.axis_index("dp")
        other = 3 - plane
        if near:
            owner = (plane, other, other + 1 - 2 * lax.rem(other, 2))[index]
        else:
            owner = (plane, plane + 1 - 2 * lax.rem(plane, 2))[index]
        source, target = self.piece_of(owner) if index else self.own_piece()
        return self.wires.copy(
            self.base + (SHARE_NEAR if near else SHARE_MIDDLE),
            index,
            source,
            target,
            beside if near else mirror,
        )

    def own_piece(self):
        return self.piece_of(lax.axis_index("dp"))

    def start(self):
        for index in range(len(self.sources)):
            self.cross(index).start()
            self.local(index).start()

    def send_own(self):
        self.over(True, 0).start()

        @pl.when(inner())
        def _():
            self.over(False, 0).start()

    def middle(self):
        for index in range(len(self.sources)):
            self.cross(index).wait_recv()
        self.send_own()

    def late(self):
        @pl.when(inner())
        def _():
            self.over(True, 0).wait_recv()
            self.over(False, 1).start()
            self.over(False, 0).wait_recv()
            self.over(True, 1).start()

    def later(self):
        @pl.when(inner())
        def _():
            self.over(False, 1).wait_recv()
            self.over(True, 2).start()

    def close_planes(self):
        self.over(True, 0).wait_send()

        @pl.when(inner())
        def _():
            self.over(True, 1).wait_send()
            self.over(True, 2).wait_send()
            self.over(False, 0).wait_send()
            self.over(False, 1).wait_send()

        @pl.when(jnp.logical_not(inner()))
        def _():
            for index in range(3):
                self.over(True, index).wait_recv()

    def close(self):
        self.close_planes()
        for index in range(len(self.sources)):
            self.cross(index).wait_send()
            self.local(index).wait()


class Spread(Share):
    def __init__(self, wires, base, source, whole, local_sems, quarter):
        super().__init__(wires, base, (source,), whole, True, local_sems)
        self.piece = quarter

    def own_piece(self):
        return self.piece, self.quarter(lax.axis_index("dp"))

    def own(self):
        return pltpu.make_async_copy(
            self.piece, self.quarter(lax.axis_index("dp")), self.local_sems.at[1]
        )

    def start(self):
        self.send_own()
        self.local(0).start()
        self.own().start()

    def close(self):
        self.close_planes()
        self.local(0).wait()
        self.own().wait()


FOLD_END, FOLD_MIDDLE, FOLD_BACK, FOLD_X = 0, 2, 4, 5
FOLD_KINDS = 6


def side():
    return lax.div(lax.axis_index("dp"), 2)


def turn_shard(turn):
    return 3 * (1 - side()) + turn * (2 * side() - 1)


class Fold:
    def __init__(self, wires, base, tiles, bufs, mine, theirs, first=None):
        self.wires, self.base, self.tiles, self.mine, self.theirs = (
            wires,
            base,
            tiles,
            mine,
            theirs,
        )
        self.first = tiles if first is None else first
        (self.recv,) = bufs
        self.near, self.mirror = planes()

    def send(self, kind, half, slot, source, target, device):
        target = self.recv.at[2 * target + half]
        return self.wires.copy(self.base + kind, slot, source, target, device)

    def end(self, half, turn):
        source = self.first.at[4 * half + turn_shard(turn)]
        return self.send(FOLD_END + half, half, turn, source, turn, self.near)

    def across(self, half, turn):
        source = self.recv.at[2 * turn + half]
        return self.send(FOLD_MIDDLE + half, half, turn, source, 3 + turn, self.mirror)

    def back(self, half):
        return self.send(FOLD_BACK, half, half, self.recv.at[6 + half], 0, self.near)

    def cross(self):
        source = self.tiles.at[4 + lax.axis_index("dp")]
        return self.wires.copy(self.base + FOLD_X, 0, source, self.theirs, neighbours()[0])

    def add(self, slot, half, shard):
        self.recv[2 * slot + half] = (
            self.recv[2 * slot + half].astype(F32) + self.tiles[4 * half + shard].astype(F32)
        ).astype(B16)

    def begin(self, turn, half):
        @pl.when(jnp.logical_not(inner()))
        def _():
            self.end(half, turn).start()

    def start(self):
        for turn in range(3):
            for half in (1, 0):
                self.begin(turn, half)

    def pass_on(self, turn):
        @pl.when(inner())
        def _():
            for half in (1, 0):
                self.end(half, turn).wait_recv()
                self.add(turn, half, turn_shard(turn))
                self.across(half, turn).start()

    def step(self):
        self.pass_on(0)

    def middle(self):
        self.pass_on(1)

        @pl.when(inner())
        def _():
            for half in (1, 0):
                self.across(half, 0).wait_recv()
                self.add(3, half, 3 * side())
                self.back(half).start()

    def late(self):
        plane = lax.axis_index("dp")
        for half in (1, 0):

            @pl.when(inner())
            def _():
                self.end(half, 2).wait_recv()
                self.across(half, 1).wait_recv()
                self.add(2, half, plane)

            @pl.when(jnp.logical_not(inner()))
            def _():
                self.back(half).wait_recv()

            at = 4 * half + plane
            middle = inner().astype(jnp.int32)
            total = self.recv[4 * middle + half].astype(F32)
            other = jnp.where(
                inner(), self.recv[8 * middle + half].astype(F32), self.tiles[at].astype(F32)
            )
            total = total + other
            if half == 1:
                self.tiles[at] = total.astype(B16)
                self.cross().start()
            else:
                self.mine[...] = total

    def close(self):
        self.cross().wait_recv()

        @pl.when(inner())
        def _():
            for half in range(2):
                self.across(half, 0).wait_send()
                self.across(half, 1).wait_send()
                self.back(half).wait_send()

        @pl.when(jnp.logical_not(inner()))
        def _():
            for half in range(2):
                for turn in range(3):
                    self.end(half, turn).wait_send()

        self.cross().wait_send()


def fold_scratch(rows, columns):
    return [pltpu.VMEM((10, rows, columns), B16)]


def turn_tile(step):
    return 4 * (1 - lax.rem(step, 2)) + turn_shard(lax.div(step, 2))


def make_tiles(fold, make, low, high):
    @pl.loop(low, high)
    def _(step):
        make(step)

        @pl.when(step < 6)
        def _():
            half = 1 - lax.rem(step, 2)
            turn = lax.div(step, 2)
            for side_half in range(2):

                @pl.when(half == side_half)
                def _():
                    fold.begin(turn, side_half)


class Reduce:
    def __init__(self, wires, rows_ref, weight_ref, transposed, bufs):
        self.wires, self.rows_ref, self.weight_ref, self.transposed = (
            wires,
            rows_ref,
            weight_ref,
            transposed,
        )
        (
            self.sibling_send,
            self.sibling_recv,
            self.kept_ref,
            self.out,
            self.corner_recv,
            self.x_recv,
            self.y_recv,
        ) = bufs
        self.rows = rows_ref.shape[1]
        self.width = (weight_ref.shape[0] if transposed else weight_ref.shape[1]) // 2
        self.count = self.width // CHUNK

    def product(self, block, chunk, half):
        left = self.rows_ref[block : block + 2].reshape(2 * self.rows, self.rows_ref.shape[2])
        at = lanes(chunk, half, self.width)
        if self.transposed:
            return rows_dot(left, self.weight_ref[at, :])
        return jnp.dot(left, self.weight_ref[:, at], preferred_element_type=F32)

    def sibling(self, chunk, half):
        return self.wires.copy(
            SIBLING + half * (REDUCE_KINDS - 1),
            chunk,
            self.sibling_send.at[lax.rem(chunk, 2), half],
            self.sibling_recv.at[chunk, half],
            neighbours()[2],
        )

    def corner(self, chunk, device):
        return self.wires.copy(
            CORNER, chunk, self.out.at[2, chunk], self.corner_recv.at[chunk], device
        )

    def final_x(self, chunk):
        return self.wires.copy(
            FINAL_X, chunk, self.out.at[0, chunk], self.x_recv.at[chunk], neighbours()[0]
        )

    def final_y(self, chunk):
        return self.wires.copy(
            FINAL_Y, chunk, self.out.at[1, chunk], self.y_recv.at[chunk], neighbours()[1]
        )

    def give(self, chunk):
        @pl.loop(0, 2)
        def _(turn):
            half = 1 - turn
            self.sibling_send[lax.rem(chunk, 2), half] = self.product(2, chunk, half).astype(B16)
            self.sibling(chunk, half).start()

    def take(self, chunk):
        rows = self.rows
        even = lax.rem(chunk, 2) == 0
        side, across, _ = neighbours()

        @pl.loop(0, 2)
        def _(turn):
            half = 1 - turn
            own = self.product(0, chunk, half)
            self.sibling(chunk, half).wait_recv()
            total = own + self.sibling_recv[chunk, half].astype(F32)

            @pl.when(half == 1)
            def _():
                self.out[2, chunk] = total[rows:].astype(B16)
                self.out[0, chunk] = total[:rows].astype(B16)

                @pl.when(even)
                def _():
                    self.corner(chunk, side).start()
                    self.final_x(chunk).start()

                @pl.when(jnp.logical_not(even))
                def _():
                    self.corner(chunk, across).start()

            @pl.when(half == 0)
            def _():
                self.kept_ref[chunk] = total[:rows]
                self.out[1, chunk] = total[rows:].astype(B16)

                @pl.when(jnp.logical_not(even))
                def _():
                    self.final_y(chunk).start()

    def start(self, between=(lambda: None, lambda: None)):
        self.give(0)
        self.rest(between)

    def rest(self, between):
        self.take(0)
        self.give(1)
        self.take(1)
        between[0]()

        @pl.loop(2, self.count)
        def _(chunk):
            for half in range(2):
                self.sibling(chunk - 2, half).wait_send()
            self.give(chunk)
            self.take(chunk)

        between[1]()

    def middle(self):
        @pl.loop(0, self.count)
        def _(chunk):
            even = lax.rem(chunk, 2) == 0
            self.corner(chunk, neighbours()[0]).wait_recv()
            came = self.corner_recv[chunk].astype(F32)

            @pl.when(even)
            def _():
                self.out[1, chunk] = (self.out[1, chunk].astype(F32) + came).astype(B16)
                self.final_y(chunk).start()

            @pl.when(jnp.logical_not(even))
            def _():
                self.out[0, chunk] = (self.out[0, chunk].astype(F32) + came).astype(B16)
                self.final_x(chunk).start()

    def total(self, chunk):
        self.final_x(chunk).wait_recv()
        self.final_y(chunk).wait_recv()
        return (
            self.kept_ref[chunk] + self.x_recv[chunk].astype(F32) + self.y_recv[chunk].astype(F32)
        )

    def close(self):
        @pl.loop(self.count - 2, self.count)
        def _(chunk):
            for half in range(2):
                self.sibling(chunk, half).wait_send()

        @pl.loop(0, self.count)
        def _(chunk):
            self.corner(chunk, neighbours()[0]).wait_send()
            self.final_x(chunk).wait_send()
            self.final_y(chunk).wait_send()


def reduce_scratch(rows, width):
    count = width // CHUNK
    return [
        pltpu.VMEM((2, 2, 2 * rows, CHUNK), B16),
        pltpu.VMEM((count, 2, 2 * rows, CHUNK), B16),
        pltpu.VMEM((count, rows, CHUNK), F32),
        pltpu.VMEM((3, count, rows, CHUNK), B16),
        pltpu.VMEM((count, rows, CHUNK), B16),
        pltpu.VMEM((count, rows, CHUNK), B16),
        pltpu.VMEM((count, rows, CHUNK), B16),
    ]


def gather_scratch(rows, width):
    count = width // CHUNK
    return [pltpu.VMEM((count, rows, CHUNK), B16), pltpu.SemaphoreType.DMA((count,))]


def wire_scratch(kinds, count):
    return [pltpu.SemaphoreType.DMA((kinds, count))] * 2


IN_VMEM = pl.BlockSpec(memory_space=pltpu.VMEM)
IN_ANY = pl.BlockSpec(memory_space=pl.ANY)
VMEM_MOST = 60 * 1024 * 1024


def remote_params(number):
    return pltpu.CompilerParams(
        collective_id=number, has_side_effects=True, vmem_limit_bytes=VMEM_MOST
    )


def cost(flops, size):
    return pl.CostEstimate(flops=flops, bytes_accessed=size, transcendentals=0)


def shape(dims, kind=B16):
    return jax.ShapeDtypeStruct(dims, kind)


def cut(own, block_ref):
    for chunk in range(own.shape[0]):
        own[chunk] = block_ref[:, chunk * CHUNK : (chunk + 1) * CHUNK]


def open_kernel(
    tokens_ref,
    query_ref,
    key_ref,
    value_ref,
    out_ref,
    attn_ref,
    mlp_ref,
    seg_ref,
    rate_ref,
    attn_all_ref,
    mlp_all_ref,
    starts_ref,
    cosine_ref,
    sine_ref,
    whole_ref,
    project_ref,
    branch_ref,
    *scratch,
):
    own, gather_sem, send_sems, recv_sems, project_sem, branch_sem = scratch[:6]
    attn_recv, mlp_recv, seg_recv, seg_all = scratch[6:]
    width = attn_ref.shape[1]
    length = seg_ref.shape[1]
    cut(own, tokens_ref)
    greet(neighbours() + planes())
    wires = Wires(send_sems, recv_sems)
    gather = Gather(wires, 0, whole_ref, own, gather_sem, 2)
    base = GATHER_KINDS + 2 * SHARE_KINDS
    side = neighbours()[0]
    small = [
        wires.copy(base, index, source, target, side)
        for index, (source, target) in enumerate(
            ((attn_ref, attn_recv), (mlp_ref, mlp_recv), (seg_ref, seg_recv))
        )
    ]
    shares = [
        Share(wires, GATHER_KINDS, (query_ref, key_ref, value_ref), project_ref, True, project_sem),
        Share(wires, GATHER_KINDS + SHARE_KINDS, (out_ref,), branch_ref, False, branch_sem),
    ]
    for copy in small:
        copy.start()
    shares[0].start()
    shares[1].start()

    @pl.loop(0, gather.count)
    def _(chunk):
        gather.send(chunk)

    for copy in small:
        copy.wait()
    attn_all_ref[:, :width] = attn_ref[...]
    attn_all_ref[:, width:] = attn_recv[...]
    mlp_all_ref[:, :width] = mlp_ref[...]
    mlp_all_ref[:, width:] = mlp_recv[...]
    mine = lax.rem(lax.axis_index("ty") + lax.div(lax.axis_index("tx"), 2), 2)
    seg_all[pl.ds(mine, 1)] = seg_ref[...].astype(F32)[None]
    seg_all[pl.ds(1 - mine, 1)] = seg_recv[...].astype(F32)[None]

    shares[0].middle()
    shares[1].middle()

    @pl.loop(0, 2)
    def _(seq):
        for low in range(0, length, 128):
            here = stand(seg_all[seq, :, low : low + 128])
            before = jnp.zeros((128, 128), F32)
            for other in range(0, length, 128):
                before += (seg_all[seq, :, other : other + 128] < here).astype(F32)
            start = jnp.sum(before, axis=1, keepdims=True)
            at = slice(low, low + 128)
            starts_ref[seq, at, :] = start.astype(jnp.int32)
            row = lax.broadcasted_iota(jnp.int32, (128, 128), 0) + low
            lane = lax.broadcasted_iota(jnp.int32, (128, 128), 1)
            angle = (row.astype(F32) - start) * rate_ref[...]
            cosine_ref[seq, at, :] = jnp.cos(angle)
            sine = jnp.sin(angle)
            sine_ref[seq, at, :] = jnp.where(lane < 64, -sine, sine)

        @pl.when(seq == 0)
        def _():
            shares[0].late()
            shares[1].late()
            gather.relay(0, 2)
            shares[0].later()
            shares[1].later()

    gather.relay(2)
    gather.close()
    shares[0].close()
    shares[1].close()


def open_call(tokens, w_query, w_key, w_value, w_out, attn_gain, mlp_gain, seg_ids, rate, number):
    rows, width = tokens.shape
    columns = (w_query.shape[1] + w_key.shape[1] + w_value.shape[1]) // 2
    length = seg_ids.shape[1]
    return pl.pallas_call(
        open_kernel,
        out_shape=(
            shape((1, 2 * width), F32),
            shape((1, 2 * width), F32),
            shape((2, length, 1), jnp.int32),
            shape((2, length, 128), F32),
            shape((2, length, 128), F32),
            shape((4, rows, 2 * width)),
            shape((2 * width, columns)),
            shape((w_out.shape[0] // 2, 2 * width)),
        ),
        in_specs=[IN_VMEM] * 9,
        out_specs=(IN_VMEM,) * 5 + (IN_ANY,) * 3,
        scratch_shapes=gather_scratch(rows, width)
        + wire_scratch(GATHER_KINDS + 2 * SHARE_KINDS + 1, width // CHUNK)
        + [
            pltpu.SemaphoreType.DMA((3,)),
            pltpu.SemaphoreType.DMA((1,)),
            pltpu.VMEM((1, width), F32),
            pltpu.VMEM((1, width), F32),
            pltpu.VMEM((1, length), jnp.int32),
            pltpu.VMEM((2, 1, length), F32),
        ],
        compiler_params=remote_params(number),
        cost_estimate=cost(0, 32 * rows * width),
    )(tokens, w_query, w_key, w_value, w_out, attn_gain, mlp_gain, seg_ids, rate)


def front_kernel(
    most,
    whole_ref,
    project_ref,
    gain_ref,
    query_gain_ref,
    key_gain_ref,
    grad_ref,
    starts_in_ref,
    cosine_in_ref,
    sine_in_ref,
    down_in_ref,
    gate_in_ref,
    first_ref,
    scale_ref,
    projected_ref,
    mixed_ref,
    query_ref,
    key_ref,
    value_ref,
    log_ref,
    grad_whole_ref,
    back_ref,
    gate_ref,
    *scratch,
):
    own, gather_sem, send_sems, recv_sems, back_sem, tokens, firsts, tile_sem = scratch[:8]
    down_ref, starts_ref, cosine_ref, sine_ref = scratch[8:12]
    loads = Loads(
        (down_in_ref, starts_in_ref, cosine_in_ref, sine_in_ref), scratch[8:12], scratch[12]
    )
    core = lax.rem(lax.axis_index("tx"), 2)
    cut(own, grad_ref)
    rows = whole_ref.shape[1]

    def spot(ref, tile):
        at = pl.ds(pl.multiple_of(lax.rem(tile, rows // BLOCK) * BLOCK, BLOCK), BLOCK)
        return ref.at[lax.div(tile, rows // BLOCK), at, :]

    def fetch(tile):
        slot = lax.rem(tile, 2)
        return pltpu.make_async_copy(spot(whole_ref, tile), tokens.at[slot], tile_sem.at[0, slot])

    def store(tile):
        slot = lax.rem(tile, 2)
        return pltpu.make_async_copy(firsts.at[slot], spot(first_ref, tile), tile_sem.at[1, slot])

    fetch(0).start()
    loads.start()
    greet(neighbours() + planes())
    wires = Wires(send_sems, recv_sems)
    gather = Gather(wires, 0, grad_whole_ref, own, gather_sem, 0)
    back = Share(wires, GATHER_KINDS, (down_in_ref,), back_ref, False, back_sem, (down_ref,))
    size, columns = gate_ref.shape
    gate = wires.copy(
        GATHER_KINDS + SHARE_KINDS,
        0,
        gate_in_ref.at[
            pl.ds(pl.multiple_of(lax.axis_index("dp") * size, size), size),
            pl.ds(pl.multiple_of((1 - lax.axis_index("ty")) * columns, columns), columns),
        ],
        gate_ref,
        neighbours()[0],
    )
    back.cross(0).start()
    gate.start()

    @pl.loop(0, gather.count)
    def _(chunk):
        gather.send(chunk)

    loads.wait(0, 1)
    back.local(0).start()
    count = 4 * rows // BLOCK

    @pl.loop(0, count)
    def _(tile):
        slot = lax.rem(tile, 2)
        block = lax.div(tile, rows // BLOCK)
        at = pl.ds(pl.multiple_of(lax.rem(tile, rows // BLOCK) * BLOCK, BLOCK), BLOCK)

        @pl.when(tile < count - 1)
        def _():
            fetch(tile + 1).start()

        fetch(tile).wait()

        @pl.when(tile >= 2)
        def _():
            store(tile - 2).wait()

        value = tokens[slot].astype(F32)
        scale = lax.rsqrt(jnp.mean(value * value, axis=1, keepdims=True) + EPS)
        first = (value * scale * gain_ref[...]).astype(B16)
        firsts[slot] = first
        store(tile).start()
        projected_ref[block, at, :] = jnp.dot(
            first, project_ref[...], preferred_element_type=F32
        )

        @pl.when(block == 0)
        def _():
            scale_ref[at, :] = jnp.broadcast_to(scale, (BLOCK, 128))

        @pl.when(tile == count // 2)
        def _():
            back.middle()

    loads.wait(1, 4)
    fixed_refs = (starts_ref, cosine_ref, sine_ref, query_gain_ref, key_gain_ref)
    saved_refs = (query_ref, key_ref, value_ref, log_ref)

    @pl.loop(0, 2)
    def _(seq):
        def between(turn):
            @pl.when(seq == 0)
            def _():
                if turn == 0:
                    back.late()
                elif turn == 2:
                    back.later()
                gather.relay(turn, turn + 1)

        attend_sequence(
            core, seq, most, projected_ref, fixed_refs, mixed_ref, saved_refs, between
        )

    for tile in range(count - 2, count):
        store(tile).wait()
    gather.close()
    back.close()
    gate.wait()


def front_call(whole, w_project, gain, fixed_args, most, cotangent, w_down, w_gate, number):
    starts, cosine, sine, query_gain, key_gain = fixed_args
    rows, width = cotangent.shape
    length = cosine.shape[1]
    depth = query_gain.shape[1]
    columns = w_project.shape[1]
    heads = columns // depth - 2
    outs = (
        shape((4, rows, 2 * width)),
        shape((rows, 128), F32),
        shape((4, rows, columns), F32),
        shape((4, rows, heads * depth)),
        shape((2, length, heads * depth)),
        shape((2, length, depth)),
        shape((2, length, depth)),
        shape((2, heads, length, 1), F32),
        shape((4, rows, 2 * width)),
        shape((w_down.shape[0] // 2, 2 * width)),
        shape((width // 4, w_gate.shape[1] // 2)),
    )
    return pl.pallas_call(
        lambda *refs: front_kernel(most, *refs),
        out_shape=outs,
        in_specs=[IN_ANY] + [IN_VMEM] * 5 + [IN_ANY] * 5,
        out_specs=[IN_ANY] + [IN_VMEM] * 7 + [IN_ANY] * 3,
        scratch_shapes=gather_scratch(rows, width)
        + wire_scratch(GATHER_KINDS + SHARE_KINDS + 1, width // CHUNK)
        + [
            pltpu.SemaphoreType.DMA((1,)),
            pltpu.VMEM((2, BLOCK, 2 * width), B16),
            pltpu.VMEM((2, BLOCK, 2 * width), B16),
            pltpu.SemaphoreType.DMA((2, 2)),
        ]
        + load_scratch((w_down, starts, cosine, sine)),
        compiler_params=remote_params(number),
        cost_estimate=cost(16 * rows * width * columns, 64 * rows * width),
    )(whole, w_project, gain, query_gain, key_gain, cotangent, starts, cosine, sine, w_down, w_gate)


def branch_kernel(
    rows_in_ref,
    weight_in_ref,
    input_in_ref,
    up_in_ref,
    gate_in_ref,
    quarter_ref,
    residual_ref,
    whole_ref,
    up_ref,
    gate_ref,
    *scratch,
):
    bufs = scratch[:7]
    own, gather_sem, send_sems, recv_sems, up_sem = scratch[7:12]
    held, load_sem, gate_sem = scratch[12:17], scratch[17], scratch[18]
    rows_ref, weight_ref, input_ref, up_held, gate_held = held
    loads = Loads(
        (rows_in_ref, weight_in_ref, input_in_ref, up_in_ref, gate_in_ref), held, load_sem
    )
    loads.start()
    width = input_ref.shape[1]
    greet(neighbours() + planes())
    wires = Wires(send_sems, recv_sems)
    reduce = Reduce(wires, rows_ref, weight_ref, False, bufs)
    gather = Gather(wires, REDUCE_KINDS, whole_ref, own, gather_sem, 0)
    up = Share(
        wires, REDUCE_KINDS + GATHER_KINDS, (up_in_ref,), up_ref, True, up_sem, (up_held,)
    )
    gate = Spread(
        wires,
        REDUCE_KINDS + GATHER_KINDS + SHARE_KINDS,
        gate_held,
        gate_ref,
        gate_sem,
        quarter_ref,
    )
    loads.wait(0, 2)

    def between():
        loads.wait(2, 5)
        up.start()
        gate.start()

    reduce.start((between, gate.late))
    up.middle()
    reduce.middle()
    gate.later()

    @pl.loop(0, width // CHUNK)
    def _(chunk):
        at = lanes(chunk, 0, width)
        residual = input_ref[:, at].astype(F32) + reduce.total(chunk)
        residual_ref[:, at] = residual
        own[chunk] = residual.astype(B16)
        gather.send(chunk)

    up.late()
    gather.relay()
    up.later()
    gather.close()
    up.close()
    gate.close()
    reduce.close()


def branch_call(rows, weight, inputs, w_up, w_gate, quarter, number):
    height, width = inputs.shape
    count = width // CHUNK
    loaded = (rows, weight, inputs, w_up, w_gate)
    return pl.pallas_call(
        branch_kernel,
        out_shape=(
            shape((height, width), F32),
            shape((4, height, 2 * width)),
            shape((2 * width, w_up.shape[1] // 2)),
            shape((2 * width, w_gate.shape[1] // 2)),
        ),
        in_specs=[IN_ANY] * 6,
        out_specs=(IN_VMEM, IN_ANY, IN_ANY, IN_ANY),
        scratch_shapes=reduce_scratch(height, width)
        + gather_scratch(height, width)
        + wire_scratch(REDUCE_KINDS + GATHER_KINDS + 2 * SHARE_KINDS, count)
        + [pltpu.SemaphoreType.DMA((1,))]
        + load_scratch(loaded)
        + [pltpu.SemaphoreType.DMA((2,))],
        compiler_params=remote_params(number),
        cost_estimate=cost(16 * height * rows.shape[2] * width, 64 * height * width),
    )(*loaded, quarter)


def units_kernel(
    whole_ref, grad_ref, gates_ref, uppers_ref, back_ref, gain_ref, second_ref, hidden_ref, unit_ref, scale_ref, stats_ref
):
    units = hidden_ref.shape[1]
    value = whole_ref[...].astype(F32)
    scale = lax.rsqrt(jnp.mean(value * value, axis=1, keepdims=True) + EPS)
    second = (value * scale * gain_ref[...]).astype(B16)
    second_ref[...] = second
    scale_ref[...] = jnp.broadcast_to(scale, scale_ref.shape)
    total = jnp.zeros((value.shape[0], 1), F32)
    for low in range(0, units, CHUNK):
        at = slice(low, low + CHUNK)
        beside = slice(units + low, units + low + CHUNK)
        gate = jnp.dot(second, gates_ref[:, at], preferred_element_type=F32)
        upper = jnp.dot(second, uppers_ref[:, at], preferred_element_type=F32)
        hidden_grad = rows_dot(grad_ref[...], back_ref[at, :])
        sigma = jax.nn.sigmoid(gate)
        passed = gate * sigma
        hidden_ref[:, at] = (passed * upper).astype(B16)
        gate_grad = (hidden_grad * upper * (sigma + passed * (1.0 - sigma))).astype(B16)
        up_grad = (hidden_grad * passed).astype(B16)
        unit_ref[:, at] = gate_grad
        unit_ref[:, beside] = up_grad
        total += jnp.sum(
            gate_grad.astype(F32) * gate + up_grad.astype(F32) * upper, axis=1, keepdims=True
        )
    stats_ref[...] = jnp.zeros_like(stats_ref)
    for tile in range(stats_ref.shape[0]):
        put_stats(stats_ref, tile, total[tile * BLOCK : (tile + 1) * BLOCK])


def units_call(whole, grad, w_gates, w_uppers, w_back, gain):
    tokens, width = whole.shape
    units = w_back.shape[0]
    size = 2 * BLOCK
    tiles = tokens // size

    def tile(columns):
        return pl.BlockSpec((size, columns), lambda i: (i, 0))

    def all_of(item):
        return pl.BlockSpec(item.shape, lambda i: (0, 0))

    return pl.pallas_call(
        units_kernel,
        out_shape=(
            shape((tokens, width)),
            shape((tokens, units)),
            shape((tokens, 2 * units)),
            shape((tokens, 128), F32),
            shape((2 * tiles, 8, 128), F32),
        ),
        grid=(tiles,),
        in_specs=[tile(width), tile(width)]
        + [all_of(item) for item in (w_gates, w_uppers, w_back, gain)],
        out_specs=(
            tile(width),
            tile(units),
            tile(2 * units),
            tile(128),
            pl.BlockSpec((2, 8, 128), lambda i: (i, 0, 0)),
        ),
        compiler_params=pltpu.CompilerParams(vmem_limit_bytes=VMEM_MOST),
        cost_estimate=cost(6 * tokens * width * units, 20 * tokens * width // 2),
    )(whole, grad, w_gates, w_uppers, w_back, gain)


class Loads:
    def __init__(self, sources, targets, sems):
        self.copies = [
            pltpu.make_async_copy(source, target, sems.at[index])
            for index, (source, target) in enumerate(zip(sources, targets))
        ]

    def start(self):
        for copy in self.copies:
            copy.start()

    def wait(self, low, high):
        for copy in self.copies[low:high]:
            copy.wait()


def load_scratch(items):
    return [pltpu.VMEM(item.shape, item.dtype) for item in items] + [
        pltpu.SemaphoreType.DMA((len(items),))
    ]


class Stats:
    def __init__(self, wires, base, ref, recv):
        self.ref, self.recv = ref, recv
        side, across, core = neighbours()
        self.hops = (
            lambda: wires.copy(base, 0, ref.at[4:8], recv.at[0:4], core),
            lambda: wires.copy(base, 1, ref.at[2:4], recv.at[4:6], across),
            lambda: wires.copy(base, 2, ref.at[0:2], recv.at[6:8], side),
        )
        self.spans = ((4, 0), (2, 4), (2, 6))

    def start(self, hop):
        self.hops[hop]().start()

    def finish(self, hop):
        self.hops[hop]().wait()
        size, at = self.spans[hop]
        self.ref[0:size] = self.ref[0:size] + self.recv[at : at + size]

    def step(self, hop):
        self.finish(hop)
        self.start(hop + 1)


def pull_columns(stats_ref, scale_ref, column_ref, width):
    for part in range(scale_ref.shape[0] // 128):
        at = slice(part * 128, (part + 1) * 128)
        scale = scale_ref[at, :]
        column_ref[at, :] = (
            stand(stats_ref[part // 2, part % 2 : part % 2 + 1, :]) * scale * scale / (2 * width)
        )


def pulled(reduce, chunk, refs, column_ref):
    scale_ref, value_ref, gain_ref, base_ref = refs
    at = lanes(chunk, 0, value_ref.shape[1])
    upstream = reduce.total(chunk)
    value = value_ref[:, at].astype(F32)
    scale = scale_ref[:, 0:1]
    back = scale * gain_ref[:, at] * upstream - value * column_ref[:, 0:1]
    return at, base_ref[:, at].astype(F32) + back, upstream * value * scale


def tile_columns(tile):
    return pl.ds(pl.multiple_of(tile * BLOCK, BLOCK), BLOCK)


SPLIT = 512


def middle_kernel(
    rows_in_ref,
    gates_in_ref,
    uppers_in_ref,
    value_in_ref,
    base_in_ref,
    hidden_in_ref,
    scale_in_ref,
    stats_in_ref,
    gain_ref,
    grad_ref,
    second_ref,
    result_ref,
    gain_grad_ref,
    whole_ref,
    rest_ref,
    *refs,
):
    ends, scratch = refs[:4], refs[4:]
    bufs = scratch[:7]
    stats_ref, stats_recv, column_ref, send_sems, recv_sems, own, gather_sem = scratch[7:14]
    stream, stream_sem, stage, stage_sem = scratch[14:18]
    down_tiles, down_recv, made_tiles, made_recv = scratch[18:22]
    weight_ref, hidden_ref, rows_ref, value_ref, base_ref, scale_ref = scratch[22:28]
    load_sem = scratch[28]
    rows, width = value_ref.shape
    columns = rows_ref.shape[2]
    units = gates_in_ref.shape[1]
    loads = Loads(
        (
            hidden_in_ref,
            rows_in_ref,
            gates_in_ref,
            uppers_in_ref,
            scale_in_ref.at[pl.ds(0, rows)],
            value_in_ref,
            base_in_ref,
        ),
        (
            hidden_ref,
            rows_ref,
            weight_ref.at[:, :units],
            weight_ref.at[:, units:],
            scale_ref,
            value_ref,
            base_ref,
        ),
        load_sem,
    )

    def fetch(ref, step, tile):
        slot = lax.rem(step, 2)
        return pltpu.make_async_copy(
            ref.at[:, :, tile_columns(tile)], stream.at[slot], stream_sem.at[slot]
        )

    fetch(grad_ref, 0, turn_tile(0)).start()
    loads.start()
    stats_ref[...] = stats_in_ref[...]
    greet(neighbours() + planes())
    wires = Wires(send_sems, recv_sems)
    base = REDUCE_KINDS + 1 + GATHER_KINDS
    down = Fold(wires, base, down_tiles, (down_recv,), ends[0], ends[1])
    made = Fold(wires, base + FOLD_KINDS, made_tiles, (made_recv,), ends[2], ends[3])
    stats = Stats(wires, REDUCE_KINDS, stats_ref, stats_recv)
    def make_down(step):
        @pl.when(step < 7)
        def _():
            fetch(grad_ref, step + 1, turn_tile(step + 1)).start()

        fetch(grad_ref, step, turn_tile(step)).wait()
        left = stream[lax.rem(step, 2)].reshape(4 * rows, BLOCK)
        down_tiles[turn_tile(step)] = weight_grad(
            left, hidden_ref[...].reshape(4 * rows, units)
        ).astype(B16)

    stats.start(0)
    loads.wait(0, 1)
    make_tiles(down, make_down, 0, 2)
    reduce = Reduce(wires, rows_ref, weight_ref, True, bufs)
    loads.wait(1, 4)

    def first_part():
        stats.step(0)
        make_tiles(down, make_down, 2, 4)

    def second_part():
        stats.step(1)
        make_tiles(down, make_down, 4, 8)

    reduce.start((first_part, second_part))
    fetch(second_ref, 0, turn_tile(0)).start()
    down.step()

    def store(step):
        slot = lax.rem(step, 2)
        return pltpu.make_async_copy(
            stage.at[slot], rest_ref.at[turn_tile(step)], stage_sem.at[slot]
        )

    def make(step):
        slot = lax.rem(step, 2)

        @pl.when(step < 7)
        def _():
            fetch(second_ref, step + 1, turn_tile(step + 1)).start()

        fetch(second_ref, step, turn_tile(step)).wait()

        @pl.when(step >= 2)
        def _():
            store(step - 2).wait()

        left = stream[slot].reshape(4 * rows, BLOCK)
        flat = rows_ref[...].reshape(4 * rows, columns)
        made.tiles[turn_tile(step)] = weight_grad(left, flat[:, :SPLIT]).astype(B16)
        for low in range(SPLIT, columns, SPLIT):
            stage[slot, :, low - SPLIT : low] = weight_grad(
                left, flat[:, low : low + SPLIT]
            ).astype(B16)
        store(step).start()

    make_tiles(made, make, 0, 4)
    reduce.middle()
    loads.wait(4, 7)
    stats.finish(2)
    pull_columns(stats_ref, scale_ref, column_ref, width)
    down.middle()
    make_tiles(made, make, 4, 8)
    gather = Gather(wires, REDUCE_KINDS + 1, whole_ref, own, gather_sem)

    @pl.loop(0, width // CHUNK)
    def _(chunk):
        at, result, share = pulled(
            reduce, chunk, (scale_ref, value_ref, gain_ref, base_ref), column_ref
        )
        result_ref[:, at] = result
        own[chunk] = result.astype(B16)
        gather.send(chunk)
        gain_grad_ref[:, at] = jnp.sum(share, axis=0, keepdims=True)

    for step in (6, 7):
        store(step).wait()
    down.late()
    gather.relay(0, 2)
    made.step()
    gather.relay(2)
    made.middle()
    gather.close()
    made.late()
    down.close()
    made.close()
    reduce.close()


def middle_call(
    rows, w_gates, w_uppers, stats, scale, value, gain, base, hidden, grad, second, number
):
    height, width = value.shape
    count = width // CHUNK
    columns = rows.shape[2]
    quarter, units = width // 4, hidden.shape[2]
    sizes = (units, SPLIT)
    ends, tiles = [], []
    for size in sizes:
        ends += [shape((quarter, size), F32), shape((quarter, size))]
        tiles += [pltpu.VMEM((8, quarter, size), B16)] + fold_scratch(quarter, size)
    loaded = (rows, w_gates, w_uppers, value, base, hidden, scale)
    return pl.pallas_call(
        middle_kernel,
        out_shape=[
            shape((height, width), F32),
            shape((1, width), F32),
            shape((4, height, 2 * width)),
            shape((8, quarter, columns - SPLIT)),
        ]
        + ends,
        in_specs=[IN_ANY] * 7 + [IN_VMEM] * 2 + [IN_ANY] * 2,
        out_specs=[IN_VMEM] * 2 + [IN_ANY] * 2 + [IN_VMEM, IN_ANY] * 2,
        scratch_shapes=reduce_scratch(height, width)
        + [
            pltpu.VMEM((8, 8, 128), F32),
            pltpu.VMEM((8, 8, 128), F32),
            pltpu.VMEM((height, 128), F32),
        ]
        + wire_scratch(REDUCE_KINDS + 1 + GATHER_KINDS + 2 * FOLD_KINDS, count)
        + gather_scratch(height, width)
        + [
            pltpu.VMEM((2, 4, height, BLOCK), B16),
            pltpu.SemaphoreType.DMA((2,)),
            pltpu.VMEM((2, quarter, columns - SPLIT), B16),
            pltpu.SemaphoreType.DMA((2,)),
        ]
        + tiles
        + [pltpu.VMEM((2 * width, columns), B16)]
        + load_scratch((hidden, rows, value, base))[:-1]
        + [pltpu.VMEM((height, 128), F32)]
        + [pltpu.SemaphoreType.DMA((len(loaded),))],
        compiler_params=remote_params(number),
        cost_estimate=cost(48 * height * units * width, 64 * height * width),
    )(*loaded, stats, gain, grad, second)


def last_kernel(
    rows_in_ref,
    weight_in_ref,
    value_in_ref,
    base_in_ref,
    stats_in_ref,
    scale_ref,
    gain_ref,
    extra_ref,
    out_in_ref,
    project_in_ref,
    result_ref,
    totals_ref,
    out_mine_ref,
    out_theirs_ref,
    project_mine_ref,
    project_theirs_ref,
    *scratch,
):
    bufs = scratch[:7]
    stats_ref, stats_recv, column_ref, send_sems, recv_sems = scratch[7:12]
    out_ref, project_ref, sums_ref, sums_recv, load_sem = scratch[12:17]
    out_bufs, project_bufs = scratch[17:18], scratch[18:19]
    rows_ref, weight_ref, value_ref, base_ref = scratch[19:23]
    rows, width = value_ref.shape
    loads = Loads(
        (project_in_ref, weight_in_ref, rows_in_ref, value_in_ref, base_in_ref, out_in_ref),
        (project_ref, weight_ref, rows_ref, value_ref, base_ref, out_ref),
        load_sem,
    )
    loads.start()
    stats_ref[...] = stats_in_ref[...]
    sums_ref[...] = jnp.zeros_like(sums_ref)
    sums_ref[8] = extra_ref[0]
    sums_ref[9] = extra_ref[1]
    greet(neighbours() + planes())
    wires = Wires(send_sems, recv_sems)
    base = REDUCE_KINDS + 1
    out = Fold(wires, base, out_ref, out_bufs, out_mine_ref, out_theirs_ref, out_in_ref)
    project = Fold(
        wires,
        base + FOLD_KINDS,
        project_ref,
        project_bufs,
        project_mine_ref,
        project_theirs_ref,
        project_in_ref,
    )
    stats = Stats(wires, REDUCE_KINDS, stats_ref, stats_recv)
    stats.start(0)
    out.start()
    loads.wait(0, 2)

    @pl.loop(0, 8)
    def _(tile):
        share = jnp.sum(
            project_ref[tile].astype(F32) * weight_ref[tile_columns(tile), :].astype(F32),
            axis=1,
            keepdims=True,
        )
        sums_ref[tile, 0:1, :] = lie(share[:128])
        sums_ref[tile, 1:2, :] = lie(share[128:])

    side_device, across, core = neighbours()
    near, mirror = planes()

    def hop(index):
        slot, device = ((0, core), (1, across), (2, near), (3, mirror), (2, near))[index]
        kind, chunk = divmod(index, 4)
        return wires.copy(
            base + 2 * FOLD_KINDS + kind, chunk, sums_ref, sums_recv.at[slot], device
        )

    def add(slot):
        sums_ref[...] = sums_ref[...] + sums_recv[slot]

    reduce = Reduce(wires, rows_ref, weight_ref, True, bufs)
    loads.wait(2, 3)
    hop(0).start()
    reduce.give(0)
    hop(0).wait()
    add(0)
    hop(1).start()
    stats.step(0)

    def after_two():
        hop(1).wait()
        add(1)

        @pl.when(jnp.logical_not(inner()))
        def _():
            hop(2).start()

        project.start()
        stats.step(1)

    reduce.rest((after_two, lambda: None))
    loads.wait(3, 6)
    out.step()
    ends_line = jnp.logical_not(inner())

    @pl.when(inner())
    def _():
        hop(2).wait_recv()
        add(2)
        hop(3).start()

    out.middle()
    reduce.middle()
    stats.finish(2)
    pull_columns(stats_ref, scale_ref, column_ref, width)

    @pl.when(inner())
    def _():
        hop(3).wait()
        add(3)
        hop(4).start()

    project.step()
    project.middle()

    @pl.loop(0, width // CHUNK)
    def _(chunk):
        at, result, _ = pulled(
            reduce, chunk, (scale_ref, value_ref, gain_ref, base_ref), column_ref
        )
        result_ref[:, at] = result.astype(B16)

    @pl.when(inner())
    def _():
        hop(4).wait_send()

    @pl.when(ends_line)
    def _():
        hop(2).wait_send()
        hop(4).wait_recv()
        sums_ref[...] = sums_recv[2]

    move = wires.copy(base + 2 * FOLD_KINDS + 1, 1, sums_ref, sums_recv.at[4], side_device)
    move.start()
    out.late()
    project.late()
    move.wait()
    totals_ref[0:4] = sums_ref[0:4] + sums_recv[4, 4:8]
    totals_ref[4:8] = sums_ref[4:8] + sums_recv[4, 0:4]
    totals_ref[8] = sums_ref[8]
    totals_ref[9] = sums_recv[4, 8]
    totals_ref[10] = sums_ref[9] + sums_recv[4, 9]
    project.close()
    out.close()
    reduce.close()


def last_call(rows, weight, stats, scale, value, gain, base, extra, out, project, number):
    height, width = value.shape
    count = width // CHUNK
    quarter, branch = out.shape[1:]
    columns = rows.shape[2]
    return pl.pallas_call(
        last_kernel,
        out_shape=(
            shape((height, width)),
            shape((11, 8, 128), F32),
            shape((quarter, branch), F32),
            shape((quarter, branch)),
            shape((quarter, columns), F32),
            shape((quarter, columns)),
        ),
        in_specs=[IN_ANY] * 4 + [IN_VMEM] * 4 + [IN_ANY] * 2,
        out_specs=(IN_VMEM, IN_VMEM) + (IN_VMEM, IN_ANY) * 2,
        scratch_shapes=reduce_scratch(height, width)
        + [
            pltpu.VMEM((8, 8, 128), F32),
            pltpu.VMEM((8, 8, 128), F32),
            pltpu.VMEM((height, 128), F32),
        ]
        + wire_scratch(REDUCE_KINDS + 1 + 2 * FOLD_KINDS + 2, count)
        + [
            pltpu.VMEM((8, quarter, branch), B16),
            pltpu.VMEM((8, quarter, columns), B16),
            pltpu.VMEM((10, 8, 128), F32),
            pltpu.VMEM((5, 10, 8, 128), F32),
            pltpu.SemaphoreType.DMA((6,)),
        ]
        + fold_scratch(quarter, branch)
        + fold_scratch(quarter, columns)
        + load_scratch((rows, weight, value, base))[:4],
        compiler_params=remote_params(number),
        cost_estimate=cost(32 * height * columns * width, 64 * height * width),
    )(rows, weight, value, base, stats, scale, gain, extra, out, project)


def back_kernel(
    most,
    query_gain_ref,
    key_gain_ref,
    *refs,
):
    operands, refs = refs[:13], refs[13:]
    rest_ref, whole_ref, first_ref = refs[:3]
    output_ref, result_ref, stats_ref, gains_ref, out_ref, project_ref = refs[3:9]
    ends, scratch = refs[9:11], refs[11:]
    bufs = scratch[:7]
    key_acc, value_acc, send_sems, recv_sems, rest_sem = scratch[7:12]
    tiles, fold_recv = scratch[12:14]
    held, load_sem = scratch[14:27], scratch[27]
    upstream, acc, stream, stream_sem, stage, stage_sem = scratch[28:]
    hidden_ref, down_ref, branch_ref, mixed_ref, starts_ref, cosine_ref, sine_ref = held[:7]
    projected_ref, query_ref, key_ref, value_ref, log_ref, residual_ref = held[7:]
    attend_loads = Loads(operands, held, load_sem)
    attend_loads.start()
    width = residual_ref.shape[1]
    rows = residual_ref.shape[0]

    def fetch(ref, tile):
        slot = lax.rem(tile, 2)
        return pltpu.make_async_copy(
            ref.at[:, :, tile_columns(tile)], stream.at[slot], stream_sem.at[slot]
        )

    def each_tile(ref, target, right, work):
        columns = target.shape[2]

        def store(tile):
            slot = lax.rem(tile, 2)
            return pltpu.make_async_copy(
                stage.at[slot, :, :columns], target.at[tile], stage_sem.at[slot]
            )

        @pl.loop(0, 8)
        def _(tile):
            @pl.when(tile < 7)
            def _():
                fetch(ref, tile + 1).start()

            fetch(ref, tile).wait()

            @pl.when(tile >= 2)
            def _():
                store(tile - 2).wait()

            left = stream[lax.rem(tile, 2)].reshape(4 * rows, BLOCK)
            work(tile, left)
            stage[lax.rem(tile, 2), :, :columns] = weight_grad(
                left, right[...].reshape(4 * rows, columns)
            ).astype(B16)
            store(tile).start()

        for tile in (6, 7):
            store(tile).wait()

    fetch(whole_ref, 0).start()
    core = lax.rem(lax.axis_index("tx"), 2)
    load = pltpu.make_async_copy(rest_ref, tiles, rest_sem)
    load.start()
    greet(neighbours() + planes())
    wires = Wires(send_sems, recv_sems)
    fold = Fold(wires, REDUCE_KINDS, tiles, (fold_recv,), ends[0], ends[1], rest_ref)
    fold.start()
    reduce = Reduce(wires, hidden_ref, down_ref, False, bufs)
    attend_loads.wait(0, 2)
    reduce.start()
    attend_loads.wait(2, 13)
    load.wait()
    acc[...] = jnp.zeros_like(acc)

    def branch_work(tile, left):
        acc[...] += rows_dot(left, branch_ref[:, tile_columns(tile)])

    each_tile(whole_ref, out_ref, mixed_ref, branch_work)
    fetch(first_ref, 0).start()
    upstream[...] = acc[...].astype(B16).reshape(upstream.shape)
    fold.step()
    stats_ref[...] = jnp.zeros_like(stats_ref)
    fixed_refs = (starts_ref, cosine_ref, sine_ref, query_gain_ref, key_gain_ref)
    saved_refs = (query_ref, key_ref, value_ref, log_ref)

    @pl.loop(0, 2)
    def _(seq):
        attend_sequence_back(
            core,
            seq,
            most,
            projected_ref,
            upstream,
            fixed_refs,
            saved_refs,
            result_ref,
            stats_ref,
            gains_ref,
            (acc, key_acc, value_acc),
        )

        @pl.when(seq == 0)
        def _():
            reduce.middle()

    fold.middle()

    each_tile(first_ref, project_ref, result_ref, lambda tile, left: None)


    @pl.loop(0, width // CHUNK)
    def _(chunk):
        at = lanes(chunk, 0, width)
        output_ref[:, at] = (residual_ref[:, at] + reduce.total(chunk)).astype(B16)

    fold.late()
    fold.close()
    reduce.close()


def back_call(
    whole, first, w_branch, mixed, hidden, w_back, residual, fixed_args, projected, saved, rest, most, number
):
    height, width = residual.shape
    _, cosine, _, query_gain, _ = fixed_args
    depth = query_gain.shape[1]
    length = cosine.shape[1]
    columns = projected.shape[2]
    heads = columns // depth - 2
    quarter, columns_left = rest.shape[1:]
    loaded = (hidden, w_back, w_branch, mixed) + fixed_args[:3] + (projected,) + saved + (residual,)
    return pl.pallas_call(
        lambda *refs: back_kernel(most, *refs),
        out_shape=(
            shape((height, width)),
            shape((4, height, columns)),
            shape((8, 8, 128), F32),
            shape((2, 8, depth), F32),
            shape((8, quarter, heads * depth)),
            shape((8, quarter, columns)),
        )
        + (shape((quarter, columns_left), F32), shape((quarter, columns_left))),
        in_specs=[IN_VMEM] * 2 + [IN_ANY] * 16,
        out_specs=[IN_VMEM] * 4 + [IN_ANY] * 2 + [IN_VMEM, IN_ANY],
        scratch_shapes=reduce_scratch(height, width)
        + [
            pltpu.VMEM((length, depth), F32),
            pltpu.VMEM((length, depth), F32),
        ]
        + wire_scratch(REDUCE_KINDS + FOLD_KINDS, width // CHUNK)
        + [pltpu.SemaphoreType.DMA, pltpu.VMEM(rest.shape, B16)]
        + fold_scratch(quarter, columns_left)
        + load_scratch(loaded)
        + [
            pltpu.VMEM((4, height, heads * depth), B16),
            pltpu.VMEM((4 * height, heads * depth), F32),
            pltpu.VMEM((2, 4, height, BLOCK), B16),
            pltpu.SemaphoreType.DMA((2,)),
            pltpu.VMEM((2, quarter, columns), B16),
            pltpu.SemaphoreType.DMA((2,)),
        ],
        compiler_params=remote_params(number),
        cost_estimate=cost(16 * height * hidden.shape[2] * width, 64 * height * width),
    )(*fixed_args[3:], *loaded, rest, whole, first)


def finish_kernel(place_ref, *refs):
    downs, both, out, project = refs[0:2], refs[2:6], refs[6:8], refs[8:10]
    totals_ref, gain_ref = refs[10:12]
    query_ref, key_ref, value_ref, out_ref, gate_ref, up_ref, down_ref = refs[12:19]
    attn_ref, mlp_ref = refs[19:]
    first = place_ref[0] == 0

    def ordered(mine, theirs):
        theirs = theirs.astype(F32)
        return jnp.where(first, mine, theirs), jnp.where(first, theirs, mine)

    def put(target, at, mine, theirs):
        half = target.shape[1] // 2
        low, high = ordered(mine, theirs)
        target[:, at : at + mine.shape[1]] = low
        target[:, half + at : half + at + mine.shape[1]] = high

    def put_turned(target, at, mine, theirs):
        half = target.shape[0] // 2
        low, high = ordered(mine, theirs)
        target[at : at + mine.shape[1], :] = low.T
        target[half + at : half + at + mine.shape[1], :] = high.T

    put_turned(down_ref, 0, downs[0][...], downs[1][...])
    put_turned(out_ref, 0, out[0][...], out[1][...])
    at = 0
    for target in (query_ref, key_ref, value_ref):
        size = target.shape[1] // 2
        put(target, 0, project[0][:, at : at + size], project[1][:, at : at + size])
        at += size
    units = gate_ref.shape[1] // 2
    at = 0
    for index in (0, 2):
        low = 0
        while low < both[index].shape[1]:
            size = min(both[index].shape[1] - low, units - at % units)
            put(
                gate_ref if at < units else up_ref,
                at % units,
                both[index][:, low : low + size],
                both[index + 1][:, low : low + size],
            )
            low += size
            at += size
    mine = jnp.concatenate([totals_ref[tile, 0:2] for tile in range(4)], axis=0)
    theirs = jnp.concatenate([totals_ref[tile, 0:2] for tile in range(4, 8)], axis=0)
    low, high = ordered(mine / gain_ref[0:8], theirs / gain_ref[8:16])
    attn_ref[0:8], attn_ref[8:16] = low, high
    low, high = ordered(totals_ref[8], totals_ref[9])
    mlp_ref[0:8], mlp_ref[8:16] = low, high


def finish_call(place, parts, totals, gain, sizes):
    quarter = parts[0].shape[0]
    queries, keys, branch, units = sizes
    return pl.pallas_call(
        finish_kernel,
        out_shape=(
            shape((quarter, queries), F32),
            shape((quarter, keys), F32),
            shape((quarter, keys), F32),
            shape((branch, quarter), F32),
            shape((quarter, units), F32),
            shape((quarter, units), F32),
            shape((units, quarter), F32),
            shape((16, 128), F32),
            shape((16, 128), F32),
        ),
        in_specs=[pl.BlockSpec(memory_space=pltpu.SMEM)] + [IN_VMEM] * (len(parts) + 2),
        out_specs=[IN_VMEM] * 9,
        compiler_params=pltpu.CompilerParams(vmem_limit_bytes=VMEM_MOST),
        cost_estimate=cost(0, 16 * 1024 * 1024),
    )(place, *parts, totals, gain)


def plane_device(
    tokens,
    seg_ids,
    w_query,
    w_key,
    w_value,
    w_out,
    w_gate,
    w_up,
    w_down,
    attn_gain,
    mlp_gain,
    query_gain,
    key_gain,
    cotangent,
):
    depth = query_gain.shape[0]
    most = seg_ids.shape[1] // 2
    rows, width = tokens.shape
    head_width = w_query.shape[1] // 2
    kv_width = w_key.shape[1] // 2
    units = w_gate.shape[1] // 2

    half = jnp.arange(depth // 2, dtype=F32)
    rate = THETA ** (-half * 2.0 / depth)
    rate = jnp.concatenate([rate, rate])[None]
    attn_row, mlp_row, starts, cosine, sine, token_whole, w_project, w_branch = open_call(
        tokens, w_query, w_key, w_value, w_out, attn_gain[None], mlp_gain[None], seg_ids, rate, 0
    )
    fixed_args = (starts, cosine, sine, query_gain[None], key_gain[None])
    (
        first,
        first_scale,
        projected,
        mixed,
        query,
        keys,
        values,
        logs,
        grad_whole,
        w_back,
        gate_quarter,
    ) = front_call(
        token_whole, w_project, attn_row, fixed_args, most, cotangent, w_down, w_gate, 1
    )
    residual, residual_whole, w_uppers, w_gates = branch_call(
        mixed, w_branch, tokens, w_up, w_gate, gate_quarter, 2
    )
    flat = (4 * rows, 2 * width)
    grad_flat = grad_whole.reshape(flat)
    second, hidden, unit_grads, second_scale, unit_stats = units_call(
        residual_whole.reshape(flat), grad_flat, w_gates, w_uppers, w_back, mlp_row
    )
    (
        residual_grad,
        mlp_gain_part,
        branch_whole,
        rest_tiles,
        *ends,
    ) = middle_call(
        unit_grads.reshape(4, rows, 2 * units),
        w_gates,
        w_uppers,
        unit_stats,
        second_scale,
        residual,
        mlp_gain[None],
        cotangent,
        hidden.reshape(4, rows, units),
        grad_whole,
        second.reshape(4, rows, 2 * width),
        3,
    )
    output, proj_grads, proj_stats, gain_parts, out_tiles, project_tiles, *rest_ends = back_call(
        branch_whole,
        first,
        w_branch,
        mixed,
        hidden.reshape(4, rows, units),
        w_back,
        residual,
        fixed_args,
        projected,
        (query, keys, values, logs),
        rest_tiles,
        most,
        4,
    )
    extra = jnp.stack(
        [
            mlp_gain_part.reshape(8, 128),
            jnp.pad(jnp.sum(gain_parts[:, :2], axis=0), ((0, 6), (0, 0))),
        ]
    )
    input_grad, totals, out_mine, out_theirs, project_mine, project_theirs = last_call(
        proj_grads,
        w_project,
        proj_stats,
        first_scale,
        tokens,
        attn_gain[None],
        residual_grad,
        extra,
        out_tiles,
        project_tiles,
        5,
    )
    place = lax.axis_index("ty").reshape(1).astype(jnp.int32)
    (
        query_share,
        key_share,
        value_share,
        out_share,
        gate_share,
        up_share,
        down_share,
        attn_total,
        mlp_total,
    ) = finish_call(
        place,
        (*ends, *rest_ends, out_mine, out_theirs, project_mine, project_theirs),
        totals,
        attn_row.reshape(16, 128),
        (2 * head_width, 2 * kv_width, 2 * head_width, 2 * units),
    )
    attn_total, mlp_total = attn_total.reshape(-1), mlp_total.reshape(-1)
    query_total, key_total = totals[10, 0], totals[10, 1]
    return (
        output,
        input_grad,
        query_share,
        key_share,
        value_share,
        out_share,
        gate_share,
        up_share,
        down_share,
        attn_total,
        mlp_total,
        query_total,
        key_total,
    )


def solution(mesh):
    placed = (
        P(("dp", "tx"), "ty"),
        P(("dp", "ty"), None),
        P("ty", "tx"),
        P("ty", "tx"),
        P("ty", "tx"),
        P("tx", "ty"),
        P("ty", "tx"),
        P("ty", "tx"),
        P("tx", "ty"),
        P("ty"),
        P("ty"),
        P(),
        P(),
        P(("dp", "tx"), "ty"),
    )
    return jax.shard_map(
        plane_device if fits(mesh) else general_device,
        mesh=mesh,
        in_specs=placed,
        out_specs=(
            P(("dp", "tx"), "ty"),
            P(("dp", "tx"), "ty"),
            P(("ty", "dp"), "tx"),
            P(("ty", "dp"), "tx"),
            P(("ty", "dp"), "tx"),
            P("tx", ("ty", "dp")),
            P(("ty", "dp"), "tx"),
            P(("ty", "dp"), "tx"),
            P("tx", ("ty", "dp")),
            P(),
            P(),
            P(),
            P(),
        ),
        check_vma=False,
    )
```

```python
import jax
import jax.numpy as jnp
from jax import lax
from jax.experimental import pallas as pl
from jax.experimental.pallas import tpu as pltpu
from jax.sharding import PartitionSpec as P

EPS = 1e-06
THETA = 1000000.0
NEG = -1e30
F32 = jnp.float32
B16 = jnp.bfloat16
MESH = pl.DeviceIdType.MESH


def width_sum(value):
    return lax.psum(value, "ty")


def token_gather(rows):
    return lax.all_gather(rows, "tx", axis=0, tiled=True)


def branch_gather(rows):
    return lax.all_gather(rows, "ty", axis=0, tiled=True)


def width_reduce(whole, apply):
    return lax.psum_scatter(apply(whole), "ty", scatter_dimension=0, tiled=True)


def head_reduce(whole, apply):
    return lax.psum_scatter(
        apply(whole).astype(jnp.bfloat16), "tx", scatter_dimension=0, tiled=True
    ).astype(jnp.float32)


def forward_with(weight):
    return lambda rows: jnp.dot(rows, weight, preferred_element_type=F32)


def backward_with(weight):
    return lambda rows: lax.dot_general(
        rows, weight, (((1,), (1,)), ((), ())), preferred_element_type=F32
    )


def weight_grad(left, right):
    return lax.dot_general(left, right, (((0,), (0,)), ((), ())), preferred_element_type=F32)


def norm_scale(rows):
    width = rows.shape[1] * lax.axis_size("ty")
    return lax.rsqrt(width_sum(jnp.sum(rows * rows, axis=1)) / width + EPS)


def norm_back(rows, scale, gain, upstream):
    width = rows.shape[1] * lax.axis_size("ty")
    inner = width_sum(jnp.sum(upstream * gain * rows, axis=1))
    back = scale[:, None] * gain * upstream - rows * (scale**3 * inner / width)[:, None]
    gain_part = jnp.sum(upstream * rows * scale[:, None], axis=0)
    return (back, gain_part)


def widen(part):
    whole = jnp.zeros((part.shape[0] * lax.axis_size("ty"),), F32)
    return lax.dynamic_update_slice_in_dim(whole, part, lax.axis_index("ty") * part.shape[0], 0)


def doc_positions(seg):
    count = seg.shape[-1]
    index = jnp.arange(count, dtype=jnp.int32)
    edge = jnp.concatenate([jnp.ones((1,), dtype=jnp.bool_), seg[1:] != seg[:-1]])
    first = lax.cummax(jnp.where(edge, index, jnp.zeros_like(index)), axis=0)
    return index - first


def rotary(positions, depth):
    half = depth // 2
    freq = THETA ** (-jnp.arange(half, dtype=F32) * 2.0 / depth)
    angle = positions.astype(F32)[..., None] * freq
    return (jnp.cos(angle), jnp.sin(angle))


def turn(value, gain, cosine, sine):
    normed = value * lax.rsqrt(jnp.mean(value * value, axis=-1, keepdims=True) + EPS) * gain
    half = value.shape[-1] // 2
    first = normed[..., :half]
    second = normed[..., half:]
    return jnp.concatenate(
        [first * cosine - second * sine, second * cosine + first * sine], axis=-1
    )


def block_scores(part, seq_keys, seq_ids, start, scale):
    block = part.shape[0]
    length = seq_ids.shape[0]
    index = jnp.arange(length, dtype=jnp.int32)
    rows = start + jnp.arange(block, dtype=jnp.int32)
    row_ids = lax.dynamic_slice_in_dim(seq_ids, start, block, 0)
    mask = (seq_ids[None, :] == row_ids[:, None]) & (index[None, :] <= rows[:, None])
    scores = jnp.einsum("qkgd,mkd->kgqm", part, seq_keys, preferred_element_type=F32) * scale
    return jnp.where(mask[None, None], scores, NEG)


def attend_forward(query, keys, values, seg, block):
    seqs, length, heads, depth = query.shape
    kv_heads = keys.shape[2]
    groups = heads // kv_heads
    scale = depth ** (-0.5)
    count = length // block
    starts = jnp.arange(count, dtype=jnp.int32) * block

    def one_sequence(operands):
        seq_query, seq_keys, seq_values, seq_ids = operands
        blocks = seq_query.reshape(count, block, kv_heads, groups, depth)

        def one_block(inputs):
            part, start = inputs
            scores = block_scores(part, seq_keys, seq_ids, start, scale)
            top = jnp.max(scores, axis=-1)
            weights = jnp.exp(scores - top[..., None])
            total = jnp.sum(weights, axis=-1)
            probs = (weights / total[..., None]).astype(B16)
            mixed = jnp.einsum("kgqm,mkd->qkgd", probs, seq_values, preferred_element_type=F32)
            return (mixed, top + jnp.log(total))

        mixed, logs = lax.map(one_block, (blocks, starts))
        return (mixed.reshape(length, heads * depth), logs)

    return lax.map(one_sequence, (query, keys, values, seg))


def attend_backward(query, keys, values, seg, logs, grad_out, block):
    seqs, length, heads, depth = query.shape
    kv_heads = keys.shape[2]
    groups = heads // kv_heads
    scale = depth ** (-0.5)
    count = length // block
    starts = jnp.arange(count, dtype=jnp.int32) * block

    def one_sequence(operands):
        seq_query, seq_keys, seq_values, seq_ids, seq_logs, seq_grad = operands
        blocks = seq_query.reshape(count, block, kv_heads, groups, depth)
        grads = seq_grad.reshape(count, block, kv_heads, groups, depth)

        def one_block(carry, inputs):
            key_acc, value_acc = carry
            part, grad_part, log_part, start = inputs
            scores = block_scores(part, seq_keys, seq_ids, start, scale)
            probs = jnp.exp(scores - log_part[..., None])
            value_acc = value_acc + jnp.einsum(
                "kgqm,qkgd->mkd", probs.astype(B16), grad_part, preferred_element_type=F32
            )
            prob_grad = jnp.einsum(
                "qkgd,mkd->kgqm", grad_part, seq_values, preferred_element_type=F32
            )
            delta = jnp.sum(probs * prob_grad, axis=-1, keepdims=True)
            score_grad = (probs * (prob_grad - delta)).astype(B16)
            query_grad = (
                jnp.einsum("kgqm,mkd->qkgd", score_grad, seq_keys, preferred_element_type=F32)
                * scale
            )
            key_acc = (
                key_acc
                + jnp.einsum("kgqm,qkgd->mkd", score_grad, part, preferred_element_type=F32) * scale
            )
            return ((key_acc, value_acc), query_grad)

        zeros = jnp.zeros((length, kv_heads, depth), F32)
        (key_grad, value_grad), query_grad = lax.scan(
            one_block, (zeros, zeros), (blocks, grads, seq_logs, starts)
        )
        return (query_grad.reshape(length, heads, depth), key_grad, value_grad)

    return lax.map(one_sequence, (query, keys, values, seg, logs, grad_out))


def general_device(
    tokens,
    seg_ids,
    w_query,
    w_key,
    w_value,
    w_out,
    w_gate,
    w_up,
    w_down,
    attn_gain,
    mlp_gain,
    query_gain,
    key_gain,
    cotangent,
):
    seqs, length = seg_ids.shape
    depth = query_gain.shape[0]
    query_width = w_query.shape[1]
    key_width = w_key.shape[1]
    units = w_gate.shape[1]
    block = min(512, length)
    inputs = tokens.astype(F32)
    first_scale = norm_scale(inputs)
    first_normed = (inputs * first_scale[:, None] * attn_gain).astype(B16)
    first_whole = token_gather(first_normed)
    w_project = jnp.concatenate([w_query, w_key, w_value], axis=1)
    projected = width_reduce(first_whole, forward_with(w_project))
    query_proj = projected[:, :query_width].reshape(seqs, length, -1, depth)
    key_proj = projected[:, query_width : query_width + key_width].reshape(seqs, length, -1, depth)
    values = projected[:, query_width + key_width :].astype(B16).reshape(seqs, length, -1, depth)
    positions = jax.vmap(doc_positions)(seg_ids)
    cosine, sine = rotary(positions, depth)
    cosine = cosine[:, :, None, :]
    sine = sine[:, :, None, :]
    query = turn(query_proj, query_gain, cosine, sine).astype(B16)
    keys = turn(key_proj, key_gain, cosine, sine).astype(B16)
    mixed, logs = attend_forward(query, keys, values, seg_ids, block)
    attended = mixed.reshape(seqs * length, -1).astype(B16)
    attended_whole = branch_gather(attended)
    residual = inputs + head_reduce(attended_whole, forward_with(w_out))
    second_scale = norm_scale(residual)
    second_normed = (residual * second_scale[:, None] * mlp_gain).astype(B16)
    second_whole = token_gather(second_normed)
    w_both = jnp.concatenate([w_gate, w_up], axis=1)
    gate_up = width_reduce(second_whole, forward_with(w_both))
    gate = gate_up[:, :units]
    upper = gate_up[:, units:]
    hidden = (jax.nn.silu(gate) * upper).astype(B16)
    hidden_whole = branch_gather(hidden)
    output = residual + head_reduce(hidden_whole, forward_with(w_down))
    grad_whole = token_gather(cotangent)
    hidden_grad = width_reduce(grad_whole, backward_with(w_down))
    down_grad = weight_grad(hidden_whole, grad_whole)
    gate_grad, up_grad = jax.vjp(lambda left, right: jax.nn.silu(left) * right, gate, upper)[1](
        hidden_grad
    )
    unit_grads = jnp.concatenate([gate_grad, up_grad], axis=1).astype(B16)
    unit_whole = branch_gather(unit_grads)
    second_grad = head_reduce(unit_whole, backward_with(w_both))
    both_grad = weight_grad(second_whole, unit_whole)
    gate_weight = both_grad[:, :units]
    up_weight = both_grad[:, units:]
    resid_norm_grad, mlp_gain_part = norm_back(residual, second_scale, mlp_gain, second_grad)
    residual_grad = cotangent.astype(F32) + resid_norm_grad
    residual_whole = token_gather(residual_grad.astype(B16))
    mixed_grad = width_reduce(residual_whole, backward_with(w_out)).astype(B16)
    out_grad = weight_grad(attended_whole, residual_whole)
    query_grad, key_grad, value_grad = attend_backward(
        query, keys, values, seg_ids, logs, mixed_grad.reshape(seqs, length, -1), block
    )
    query_proj_grad, query_gain_grad = jax.vjp(
        lambda value, gain: turn(value, gain, cosine, sine), query_proj, query_gain
    )[1](query_grad)
    key_proj_grad, key_gain_grad = jax.vjp(
        lambda value, gain: turn(value, gain, cosine, sine), key_proj, key_gain
    )[1](key_grad)
    rows = seqs * length
    proj_grad = jnp.concatenate(
        [
            query_proj_grad.reshape(rows, -1),
            key_proj_grad.reshape(rows, -1),
            value_grad.reshape(rows, -1),
        ],
        axis=1,
    ).astype(B16)
    proj_whole = branch_gather(proj_grad)
    first_grad = head_reduce(proj_whole, backward_with(w_project))
    project_grad = weight_grad(first_whole, proj_whole)
    query_weight = project_grad[:, :query_width]
    key_weight = project_grad[:, query_width : query_width + key_width]
    value_weight = project_grad[:, query_width + key_width :]
    input_norm_grad, attn_gain_part = norm_back(inputs, first_scale, attn_gain, first_grad)
    input_grad = (residual_grad + input_norm_grad).astype(B16)
    attn_total, mlp_total, query_total, key_total = lax.psum(
        (widen(attn_gain_part), widen(mlp_gain_part), query_gain_grad, key_gain_grad),
        ("dp", "tx", "ty"),
    )
    query_share, key_share, value_share, gate_share, up_share = (
        lax.psum_scatter(
            query_weight.astype(jnp.bfloat16), "dp", scatter_dimension=0, tiled=True
        ).astype(jnp.float32),
        lax.psum_scatter(
            key_weight.astype(jnp.bfloat16), "dp", scatter_dimension=0, tiled=True
        ).astype(jnp.float32),
        lax.psum_scatter(
            value_weight.astype(jnp.bfloat16), "dp", scatter_dimension=0, tiled=True
        ).astype(jnp.float32),
        lax.psum_scatter(
            gate_weight.astype(jnp.bfloat16), "dp", scatter_dimension=0, tiled=True
        ).astype(jnp.float32),
        lax.psum_scatter(
            up_weight.astype(jnp.bfloat16), "dp", scatter_dimension=0, tiled=True
        ).astype(jnp.float32),
    )
    out_share, down_share = (
        lax.psum_scatter(
            out_grad.astype(jnp.bfloat16), "dp", scatter_dimension=1, tiled=True
        ).astype(jnp.float32),
        lax.psum_scatter(
            down_grad.astype(jnp.bfloat16), "dp", scatter_dimension=1, tiled=True
        ).astype(jnp.float32),
    )
    return (
        output.astype(B16),
        input_grad,
        query_share,
        key_share,
        value_share,
        out_share,
        gate_share,
        up_share,
        down_share,
        attn_total,
        mlp_total,
        query_total,
        key_total,
    )


def fits(mesh):
    return mesh.shape["tx"] == 4 and mesh.shape["ty"] == 2 and mesh.shape["dp"] == 4


def swap_x(value):
    return lax.ppermute(value, "ty", [(0, 1), (1, 0)])


def in_order(mine, theirs, axis):
    first = lax.axis_index("ty") == 0
    return jnp.concatenate(
        [jnp.where(first, mine, theirs), jnp.where(first, theirs, mine)], axis=axis
    )


def spin(value, cosine, sine):
    return value * cosine + pltpu.roll(value, value.shape[1] // 2, 1) * sine


def spin_back(value, cosine, sine):
    return value * cosine + pltpu.roll(value * sine, value.shape[1] // 2, 1)


def head_scale(value):
    return lax.rsqrt(jnp.mean(value * value, axis=1, keepdims=True) + EPS)


def window(first, block, most):
    return max(0, first - most), first + block


def kept(first, block, low, high, starts):
    shape = (block, high - low)
    column = low + lax.broadcasted_iota(jnp.int32, shape, 1)
    row = first + lax.broadcasted_iota(jnp.int32, shape, 0)
    return (column >= starts) & (column <= row)


def rows_dot(left, right):
    return lax.dot_general(left, right, (((1,), (1,)), ((), ())), preferred_element_type=F32)


def stand(row):
    return jnp.transpose(jnp.broadcast_to(row, (row.shape[1], row.shape[1])))


def lie(column):
    return jnp.transpose(jnp.broadcast_to(column, (column.shape[0], column.shape[0])))[0:1]


def put_stats(stats_ref, tile, column):
    stats_ref[tile, 0:1, :] = lie(column[:128])
    stats_ref[tile, 1:2, :] = lie(column[128:])


BLOCK = 256


def attend_sequence(core, seq, most, projected, fixed_refs, mixed, saved_refs, between):
    starts_ref, cosine_ref, sine_ref, query_gain_ref, key_gain_ref = fixed_refs
    query_ref, key_ref, value_ref, log_ref = saved_refs
    rows = projected.shape[1]
    length = query_ref.shape[1]
    depth = key_ref.shape[2]
    heads = query_ref.shape[2] // depth
    scale = depth ** (-0.5)
    for half in range(2):
        place = 2 * lax.rem(core + half, 2) + seq
        for at in range(half * rows, (half + 1) * rows, BLOCK):
            inner = at - half * rows
            cosine = cosine_ref[seq, at : at + BLOCK, :]
            sine = sine_ref[seq, at : at + BLOCK, :]
            for head in range(heads + 2):
                lane = slice(head * depth, (head + 1) * depth)
                value = projected[place, inner : inner + BLOCK, lane]
                if head < heads:
                    normed = value * head_scale(value) * query_gain_ref[...]
                    query_ref[seq, at : at + BLOCK, lane] = spin(normed, cosine, sine).astype(B16)
                elif head == heads:
                    normed = value * head_scale(value) * key_gain_ref[...]
                    key_ref[seq, at : at + BLOCK, :] = spin(normed, cosine, sine).astype(B16)
                else:
                    value_ref[seq, at : at + BLOCK, :] = value.astype(B16)
    for first in range(0, length, BLOCK):
        between(first // BLOCK)
        low, high = window(first, BLOCK, most)
        mask = kept(first, BLOCK, low, high, starts_ref[seq, first : first + BLOCK, :])
        half, inner = divmod(first, rows)
        place = 2 * lax.rem(core + half, 2) + seq
        for head in range(heads):
            lane = slice(head * depth, (head + 1) * depth)
            query = query_ref[seq, first : first + BLOCK, lane]
            scores = rows_dot(query, key_ref[seq, low:high, :]) * scale
            scores = jnp.where(mask, scores, NEG)
            top = jnp.max(scores, axis=1, keepdims=True)
            weights = jnp.exp(scores - top)
            total = jnp.sum(weights, axis=1, keepdims=True)
            probs = (weights * (1.0 / total)).astype(B16)
            out = jnp.dot(probs, value_ref[seq, low:high, :], preferred_element_type=F32)
            mixed[place, inner : inner + BLOCK, lane] = out.astype(B16)
            log_ref[seq, head, first : first + BLOCK, :] = top + jnp.log(total)


def attend_sequence_back(
    core, seq, most, projected, upstream, fixed_refs, saved_refs, result, stats, gains, accs
):
    starts_ref, cosine_ref, sine_ref, query_gain_ref, key_gain_ref = fixed_refs
    query_ref, key_ref, value_ref, log_ref = saved_refs
    query_acc, key_acc, value_acc = accs
    rows = projected.shape[1]
    length = query_ref.shape[1]
    depth = key_ref.shape[2]
    heads = query_ref.shape[2] // depth
    scale = depth ** (-0.5)
    key_acc[...] = jnp.zeros_like(key_acc)
    value_acc[...] = jnp.zeros_like(value_acc)
    for first in range(0, length, BLOCK):
        low, high = window(first, BLOCK, most)
        mask = kept(first, BLOCK, low, high, starts_ref[seq, first : first + BLOCK, :])
        half, inner = divmod(first, rows)
        place = 2 * lax.rem(core + half, 2) + seq
        keys = key_ref[seq, low:high, :]
        values = value_ref[seq, low:high, :]
        for head in range(heads):
            lane = slice(head * depth, (head + 1) * depth)
            query = query_ref[seq, first : first + BLOCK, lane]
            grad = upstream[place, inner : inner + BLOCK, lane]
            scores = rows_dot(query, keys) * scale - log_ref[seq, head, first : first + BLOCK, :]
            probs = jnp.exp(jnp.where(mask, scores, NEG))
            prob_grad = rows_dot(grad, values)
            delta = jnp.sum(probs * prob_grad, axis=1, keepdims=True)
            score_grad = (probs * (prob_grad - delta)).astype(B16)
            query_acc[first : first + BLOCK, lane] = (
                jnp.dot(score_grad, keys, preferred_element_type=F32) * scale
            )
            key_acc[low:high, :] += weight_grad(score_grad, query) * scale
            value_acc[low:high, :] += weight_grad(probs.astype(B16), grad)
    query_total = jnp.zeros((1, depth), F32)
    key_total = jnp.zeros((1, depth), F32)
    for half in range(2):
        block = 2 * lax.rem(core + half, 2) + seq
        for at in range(half * rows, (half + 1) * rows, BLOCK):
            inner = at - half * rows
            cosine = cosine_ref[seq, at : at + BLOCK, :]
            sine = sine_ref[seq, at : at + BLOCK, :]
            total = jnp.zeros((BLOCK, 1), F32)
            for head in range(heads + 2):
                lane = slice(head * depth, (head + 1) * depth)
                value = projected[block, inner : inner + BLOCK, lane]
                if head == heads + 1:
                    back = value_acc[at : at + BLOCK, :].astype(B16)
                else:
                    if head < heads:
                        grad = query_acc[at : at + BLOCK, lane]
                        gain = query_gain_ref[...]
                    else:
                        grad = key_acc[at : at + BLOCK, :]
                        gain = key_gain_ref[...]
                    grad = spin_back(grad, cosine, sine)
                    rate = head_scale(value)
                    scaled = value * rate
                    share = jnp.sum(grad * scaled, axis=0, keepdims=True)
                    if head < heads:
                        query_total += share
                    else:
                        key_total += share
                    middle = jnp.mean(gain * grad * scaled, axis=1, keepdims=True)
                    back = (rate * (gain * grad - scaled * middle)).astype(B16)
                result[block, inner : inner + BLOCK, lane] = back
                total += jnp.sum(back.astype(F32) * value, axis=1, keepdims=True)
            put_stats(stats, 2 * block + inner // BLOCK, total)
    gains[seq, 0:1, :] = query_total
    gains[seq, 1:2, :] = key_total


def neighbours():
    spot = lax.axis_index("tx")
    core = lax.rem(spot, 2)
    return (
        {"ty": 1 - lax.axis_index("ty")},
        {"tx": lax.rem(spot + 2, 4)},
        {"tx": spot + 1 - 2 * core},
    )


def planes():
    plane = lax.axis_index("dp")
    return {"dp": plane + 1 - 2 * lax.rem(plane, 2)}, {"dp": 3 - plane}


def inner():
    plane = lax.axis_index("dp")
    return (plane == 1) | (plane == 2)


def greet(targets):
    barrier = pltpu.get_barrier_semaphore()
    for target in targets:
        pl.semaphore_signal(barrier, inc=1, device_id=target, device_id_type=MESH)
    pl.semaphore_wait(barrier, len(targets))


class Wires:
    def __init__(self, send_sems, recv_sems):
        self.send_sems = send_sems
        self.recv_sems = recv_sems

    def copy(self, kind, chunk, source, target, device):
        return pltpu.make_async_remote_copy(
            src_ref=source,
            dst_ref=target,
            send_sem=self.send_sems.at[kind, chunk],
            recv_sem=self.recv_sems.at[kind, chunk],
            device_id=device,
            device_id_type=MESH,
        )


CHUNK = 256
SIBLING, CORNER, FINAL_X, FINAL_Y = 0, 1, 2, 3
REDUCE_KINDS = 5
OUT_X, OUT_Y, OUT_CORNER, CORE_OWN, CORE_X, CORE_Y, CORE_CORNER = range(7)
GATHER_KINDS = 7
SHARE_X, SHARE_NEAR, SHARE_MIDDLE = 0, 1, 2
SHARE_KINDS = 3


def lanes(chunk, half, width):
    return pl.ds(pl.multiple_of(half * width + chunk * CHUNK, CHUNK), CHUNK)


class Gather:
    def __init__(self, wires, base, whole, own, local_sem, most=4):
        self.wires, self.base, self.whole, self.own, self.local_sem = (
            wires,
            base,
            whole,
            own,
            local_sem,
        )
        self.most = most
        self.width = whole.shape[2] // 2
        self.count = self.width // CHUNK

    def place(self, block, chunk, half):
        return self.whole.at[block, :, lanes(chunk, half, self.width)]

    def copy(self, name, chunk):
        side, across, core = neighbours()
        at = self.place
        own = self.own.at[chunk]
        if name == "local":
            return pltpu.make_async_copy(own, at(0, chunk, 0), self.local_sem.at[chunk])
        kind, source, target, device = {
            "x": (OUT_X, own, at(0, chunk, 1), side),
            "y": (OUT_Y, own, at(1, chunk, 0), across),
            "core": (CORE_OWN, own, at(2, chunk, 0), core),
            "even": (OUT_CORNER, at(0, chunk, 1), at(1, chunk, 1), across),
            "odd": (OUT_CORNER, at(1, chunk, 0), at(1, chunk, 1), side),
            "core_x": (CORE_X, at(0, chunk, 1), at(2, chunk, 1), core),
            "core_y": (CORE_Y, at(1, chunk, 0), at(3, chunk, 0), core),
            "core_corner": (CORE_CORNER, at(1, chunk, 1), at(3, chunk, 1), core),
        }[name]
        return self.wires.copy(self.base + kind, chunk, source, target, device)

    def send(self, chunk):
        for name in ("x", "y", "core", "local"):
            self.copy(name, chunk).start()

    def relay(self, low=0, high=None):
        @pl.loop(low, self.count if high is None else high)
        def _(chunk):
            even = (lax.rem(chunk, 2) == 0) | (chunk >= self.most)
            self.copy("x", chunk).wait_recv()

            @pl.when(even)
            def _():
                self.copy("even", chunk).start()

            self.copy("core_x", chunk).start()
            self.copy("y", chunk).wait_recv()

            @pl.when(jnp.logical_not(even))
            def _():
                self.copy("odd", chunk).start()

            self.copy("core_y", chunk).start()

    def close(self):
        @pl.loop(0, self.count)
        def _(chunk):
            self.copy("even", chunk).wait_recv()
            self.copy("core_corner", chunk).start()

        @pl.loop(0, self.count)
        def _(chunk):
            for name in ("core", "core_x", "core_y", "core_corner"):
                self.copy(name, chunk).wait_recv()
            for name in ("x", "y", "core", "even", "core_x", "core_y", "core_corner"):
                self.copy(name, chunk).wait_send()
            self.copy("local", chunk).wait()


class Share:
    def __init__(self, wires, base, sources, whole, by_rows, local_sems, held=None):
        self.wires, self.base, self.sources, self.whole, self.by_rows, self.local_sems = (
            wires,
            base,
            sources,
            whole,
            by_rows,
            local_sems,
        )
        self.held = held or sources
        self.size = (whole.shape[0] // 2 if by_rows else whole.shape[0]) // 4

    def quarter(self, plane):
        start = plane * self.size
        if self.by_rows:
            rows = pl.ds(pl.multiple_of(self.whole.shape[0] // 2 + start, self.size), self.size)
            return self.whole.at[rows]
        width = self.whole.shape[1] // 2
        return self.whole.at[pl.ds(pl.multiple_of(start, self.size), self.size), width:]

    def cross(self, index):
        side, _, _ = neighbours()
        plane = lax.axis_index("dp")
        other = 1 - lax.axis_index("ty")
        source = self.sources[index]
        if self.by_rows:
            rows = pl.ds(pl.multiple_of(plane * self.size, self.size), self.size)
            columns = source.shape[1] // 2
            part = source.at[rows, pl.ds(pl.multiple_of(other * columns, columns), columns)]
            offset = sum(item.shape[1] // 2 for item in self.sources[:index])
            target = self.quarter(plane).at[:, offset : offset + columns]
        else:
            start = pl.multiple_of(other * (source.shape[0] // 2) + plane * self.size, self.size)
            part = source.at[pl.ds(start, self.size)]
            target = self.quarter(plane)
        return self.wires.copy(self.base + SHARE_X, index, part, target, side)

    def local(self, index):
        mine = lax.axis_index("ty")
        source = self.held[index]
        if self.by_rows:
            columns = source.shape[1] // 2
            offset = sum(item.shape[1] // 2 for item in self.sources[:index])
            part = source.at[:, pl.ds(pl.multiple_of(mine * columns, columns), columns)]
            target = self.whole.at[: self.whole.shape[0] // 2, offset : offset + columns]
        else:
            half = source.shape[0] // 2
            part = source.at[pl.ds(pl.multiple_of(mine * half, half), half)]
            target = self.whole.at[:, : self.whole.shape[1] // 2]
        return pltpu.make_async_copy(part, target, self.local_sems.at[index])

    def piece_of(self, owner):
        place = self.quarter(owner)
        return place, place

    def over(self, near, index):
        beside, mirror = planes()
        plane = lax.axis_index("dp")
        other = 3 - plane
        if near:
            owner = (plane, other, other + 1 - 2 * lax.rem(other, 2))[index]
        else:
            owner = (plane, plane + 1 - 2 * lax.rem(plane, 2))[index]
        source, target = self.piece_of(owner) if index else self.own_piece()
        return self.wires.copy(
            self.base + (SHARE_NEAR if near else SHARE_MIDDLE),
            index,
            source,
            target,
            beside if near else mirror,
        )

    def own_piece(self):
        return self.piece_of(lax.axis_index("dp"))

    def start(self):
        for index in range(len(self.sources)):
            self.cross(index).start()
            self.local(index).start()

    def send_own(self):
        self.over(True, 0).start()

        @pl.when(inner())
        def _():
            self.over(False, 0).start()

    def middle(self):
        for index in range(len(self.sources)):
            self.cross(index).wait_recv()
        self.send_own()

    def late(self):
        @pl.when(inner())
        def _():
            self.over(True, 0).wait_recv()
            self.over(False, 1).start()
            self.over(False, 0).wait_recv()
            self.over(True, 1).start()

    def later(self):
        @pl.when(inner())
        def _():
            self.over(False, 1).wait_recv()
            self.over(True, 2).start()

    def close_planes(self):
        self.over(True, 0).wait_send()

        @pl.when(inner())
        def _():
            self.over(True, 1).wait_send()
            self.over(True, 2).wait_send()
            self.over(False, 0).wait_send()
            self.over(False, 1).wait_send()

        @pl.when(jnp.logical_not(inner()))
        def _():
            for index in range(3):
                self.over(True, index).wait_recv()

    def close(self):
        self.close_planes()
        for index in range(len(self.sources)):
            self.cross(index).wait_send()
            self.local(index).wait()


class Spread(Share):
    def __init__(self, wires, base, source, whole, local_sems, quarter):
        super().__init__(wires, base, (source,), whole, True, local_sems)
        self.piece = quarter

    def own_piece(self):
        return self.piece, self.quarter(lax.axis_index("dp"))

    def own(self):
        return pltpu.make_async_copy(
            self.piece, self.quarter(lax.axis_index("dp")), self.local_sems.at[1]
        )

    def start(self):
        self.send_own()
        self.local(0).start()
        self.own().start()

    def close(self):
        self.close_planes()
        self.local(0).wait()
        self.own().wait()


FOLD_END, FOLD_MIDDLE, FOLD_BACK, FOLD_X = 0, 2, 4, 5
FOLD_KINDS = 6


def side():
    return lax.div(lax.axis_index("dp"), 2)


def turn_shard(turn):
    return 3 * (1 - side()) + turn * (2 * side() - 1)


class Fold:
    def __init__(self, wires, base, tiles, bufs, mine, theirs, first=None):
        self.wires, self.base, self.tiles, self.mine, self.theirs = (
            wires,
            base,
            tiles,
            mine,
            theirs,
        )
        self.first = tiles if first is None else first
        (self.recv,) = bufs
        self.near, self.mirror = planes()

    def send(self, kind, half, slot, source, target, device):
        target = self.recv.at[2 * target + half]
        return self.wires.copy(self.base + kind, slot, source, target, device)

    def end(self, half, turn):
        source = self.first.at[4 * half + turn_shard(turn)]
        return self.send(FOLD_END + half, half, turn, source, turn, self.near)

    def across(self, half, turn):
        source = self.recv.at[2 * turn + half]
        return self.send(FOLD_MIDDLE + half, half, turn, source, 3 + turn, self.mirror)

    def back(self, half):
        return self.send(FOLD_BACK, half, half, self.recv.at[6 + half], 0, self.near)

    def cross(self):
        source = self.tiles.at[4 + lax.axis_index("dp")]
        return self.wires.copy(self.base + FOLD_X, 0, source, self.theirs, neighbours()[0])

    def add(self, slot, half, shard):
        self.recv[2 * slot + half] = (
            self.recv[2 * slot + half].astype(F32) + self.tiles[4 * half + shard].astype(F32)
        ).astype(B16)

    def begin(self, turn, half):
        @pl.when(jnp.logical_not(inner()))
        def _():
            self.end(half, turn).start()

    def start(self):
        for turn in range(3):
            for half in (1, 0):
                self.begin(turn, half)

    def pass_on(self, turn):
        @pl.when(inner())
        def _():
            for half in (1, 0):
                self.end(half, turn).wait_recv()
                self.add(turn, half, turn_shard(turn))
                self.across(half, turn).start()

    def step(self):
        self.pass_on(0)

    def middle(self):
        self.pass_on(1)

        @pl.when(inner())
        def _():
            for half in (1, 0):
                self.across(half, 0).wait_recv()
                self.add(3, half, 3 * side())
                self.back(half).start()

    def late(self):
        plane = lax.axis_index("dp")
        for half in (1, 0):

            @pl.when(inner())
            def _():
                self.end(half, 2).wait_recv()
                self.across(half, 1).wait_recv()
                self.add(2, half, plane)

            @pl.when(jnp.logical_not(inner()))
            def _():
                self.back(half).wait_recv()

            at = 4 * half + plane
            middle = inner().astype(jnp.int32)
            total = self.recv[4 * middle + half].astype(F32)
            other = jnp.where(
                inner(), self.recv[8 * middle + half].astype(F32), self.tiles[at].astype(F32)
            )
            total = total + other
            if half == 1:
                self.tiles[at] = total.astype(B16)
                self.cross().start()
            else:
                self.mine[...] = total

    def close(self):
        self.cross().wait_recv()

        @pl.when(inner())
        def _():
            for half in range(2):
                self.across(half, 0).wait_send()
                self.across(half, 1).wait_send()
                self.back(half).wait_send()

        @pl.when(jnp.logical_not(inner()))
        def _():
            for half in range(2):
                for turn in range(3):
                    self.end(half, turn).wait_send()

        self.cross().wait_send()


def fold_scratch(rows, columns):
    return [pltpu.VMEM((10, rows, columns), B16)]


def turn_tile(step):
    return 4 * (1 - lax.rem(step, 2)) + turn_shard(lax.div(step, 2))


def make_tiles(fold, make, low, high):
    @pl.loop(low, high)
    def _(step):
        make(step)

        @pl.when(step < 6)
        def _():
            half = 1 - lax.rem(step, 2)
            turn = lax.div(step, 2)
            for side_half in range(2):

                @pl.when(half == side_half)
                def _():
                    fold.begin(turn, side_half)


class Reduce:
    def __init__(self, wires, rows_ref, weight_ref, transposed, bufs):
        self.wires, self.rows_ref, self.weight_ref, self.transposed = (
            wires,
            rows_ref,
            weight_ref,
            transposed,
        )
        (
            self.sibling_send,
            self.sibling_recv,
            self.kept_ref,
            self.out,
            self.corner_recv,
            self.x_recv,
            self.y_recv,
        ) = bufs
        self.rows = rows_ref.shape[1]
        self.width = (weight_ref.shape[0] if transposed else weight_ref.shape[1]) // 2
        self.count = self.width // CHUNK

    def product(self, block, chunk, half):
        left = self.rows_ref[block : block + 2].reshape(2 * self.rows, self.rows_ref.shape[2])
        at = lanes(chunk, half, self.width)
        if self.transposed:
            return rows_dot(left, self.weight_ref[at, :])
        return jnp.dot(left, self.weight_ref[:, at], preferred_element_type=F32)

    def sibling(self, chunk, half):
        return self.wires.copy(
            SIBLING + half * (REDUCE_KINDS - 1),
            chunk,
            self.sibling_send.at[lax.rem(chunk, 2), half],
            self.sibling_recv.at[chunk, half],
            neighbours()[2],
        )

    def corner(self, chunk, device):
        return self.wires.copy(
            CORNER, chunk, self.out.at[2, chunk], self.corner_recv.at[chunk], device
        )

    def final_x(self, chunk):
        return self.wires.copy(
            FINAL_X, chunk, self.out.at[0, chunk], self.x_recv.at[chunk], neighbours()[0]
        )

    def final_y(self, chunk):
        return self.wires.copy(
            FINAL_Y, chunk, self.out.at[1, chunk], self.y_recv.at[chunk], neighbours()[1]
        )

    def give(self, chunk):
        @pl.loop(0, 2)
        def _(turn):
            half = 1 - turn
            self.sibling_send[lax.rem(chunk, 2), half] = self.product(2, chunk, half).astype(B16)
            self.sibling(chunk, half).start()

    def take(self, chunk):
        rows = self.rows
        even = lax.rem(chunk, 2) == 0
        side, across, _ = neighbours()

        @pl.loop(0, 2)
        def _(turn):
            half = 1 - turn
            own = self.product(0, chunk, half)
            self.sibling(chunk, half).wait_recv()
            total = own + self.sibling_recv[chunk, half].astype(F32)

            @pl.when(half == 1)
            def _():
                self.out[2, chunk] = total[rows:].astype(B16)
                self.out[0, chunk] = total[:rows].astype(B16)

                @pl.when(even)
                def _():
                    self.corner(chunk, side).start()
                    self.final_x(chunk).start()

                @pl.when(jnp.logical_not(even))
                def _():
                    self.corner(chunk, across).start()

            @pl.when(half == 0)
            def _():
                self.kept_ref[chunk] = total[:rows]
                self.out[1, chunk] = total[rows:].astype(B16)

                @pl.when(jnp.logical_not(even))
                def _():
                    self.final_y(chunk).start()

    def start(self, between=(lambda: None, lambda: None)):
        self.give(0)
        self.rest(between)

    def rest(self, between):
        self.take(0)
        self.give(1)
        self.take(1)
        between[0]()

        @pl.loop(2, self.count)
        def _(chunk):
            for half in range(2):
                self.sibling(chunk - 2, half).wait_send()
            self.give(chunk)
            self.take(chunk)
            self.middle(chunk - 2, chunk - 1)

        between[1]()

    def middle(self, low=None, high=None):
        @pl.loop(self.count - 2 if low is None else low, self.count if high is None else high)
        def _(chunk):
            even = lax.rem(chunk, 2) == 0
            self.corner(chunk, neighbours()[0]).wait_recv()
            came = self.corner_recv[chunk].astype(F32)

            @pl.when(even)
            def _():
                self.out[1, chunk] = (self.out[1, chunk].astype(F32) + came).astype(B16)
                self.final_y(chunk).start()

            @pl.when(jnp.logical_not(even))
            def _():
                self.out[0, chunk] = (self.out[0, chunk].astype(F32) + came).astype(B16)
                self.final_x(chunk).start()

    def total(self, chunk):
        self.final_x(chunk).wait_recv()
        self.final_y(chunk).wait_recv()
        return (
            self.kept_ref[chunk] + self.x_recv[chunk].astype(F32) + self.y_recv[chunk].astype(F32)
        )

    def close(self):
        @pl.loop(self.count - 2, self.count)
        def _(chunk):
            for half in range(2):
                self.sibling(chunk, half).wait_send()

        @pl.loop(0, self.count)
        def _(chunk):
            self.corner(chunk, neighbours()[0]).wait_send()
            self.final_x(chunk).wait_send()
            self.final_y(chunk).wait_send()


def reduce_scratch(rows, width):
    count = width // CHUNK
    return [
        pltpu.VMEM((2, 2, 2 * rows, CHUNK), B16),
        pltpu.VMEM((count, 2, 2 * rows, CHUNK), B16),
        pltpu.VMEM((count, rows, CHUNK), F32),
        pltpu.VMEM((3, count, rows, CHUNK), B16),
        pltpu.VMEM((count, rows, CHUNK), B16),
        pltpu.VMEM((count, rows, CHUNK), B16),
        pltpu.VMEM((count, rows, CHUNK), B16),
    ]


def gather_scratch(rows, width):
    count = width // CHUNK
    return [pltpu.VMEM((count, rows, CHUNK), B16), pltpu.SemaphoreType.DMA((count,))]


def wire_scratch(kinds, count):
    return [pltpu.SemaphoreType.DMA((kinds, count))] * 2


IN_VMEM = pl.BlockSpec(memory_space=pltpu.VMEM)
IN_ANY = pl.BlockSpec(memory_space=pl.ANY)
VMEM_MOST = 60 * 1024 * 1024


def remote_params(number):
    return pltpu.CompilerParams(
        collective_id=number, has_side_effects=True, vmem_limit_bytes=VMEM_MOST
    )


def cost(flops, size):
    return pl.CostEstimate(flops=flops, bytes_accessed=size, transcendentals=0)


def shape(dims, kind=B16):
    return jax.ShapeDtypeStruct(dims, kind)


def cut(own, block_ref):
    for chunk in range(own.shape[0]):
        own[chunk] = block_ref[:, chunk * CHUNK : (chunk + 1) * CHUNK]


def open_kernel(
    tokens_ref,
    query_ref,
    key_ref,
    value_ref,
    out_ref,
    attn_ref,
    mlp_ref,
    seg_ref,
    rate_ref,
    attn_all_ref,
    mlp_all_ref,
    starts_ref,
    cosine_ref,
    sine_ref,
    whole_ref,
    project_ref,
    branch_ref,
    *scratch,
):
    own, gather_sem, send_sems, recv_sems, project_sem, branch_sem = scratch[:6]
    attn_recv, mlp_recv, seg_recv, seg_all = scratch[6:]
    width = attn_ref.shape[1]
    length = seg_ref.shape[1]
    cut(own, tokens_ref)
    greet(neighbours() + planes())
    wires = Wires(send_sems, recv_sems)
    gather = Gather(wires, 0, whole_ref, own, gather_sem, 2)
    base = GATHER_KINDS + 2 * SHARE_KINDS
    side = neighbours()[0]
    small = [
        wires.copy(base, index, source, target, side)
        for index, (source, target) in enumerate(
            ((attn_ref, attn_recv), (mlp_ref, mlp_recv), (seg_ref, seg_recv))
        )
    ]
    shares = [
        Share(wires, GATHER_KINDS, (query_ref, key_ref, value_ref), project_ref, True, project_sem),
        Share(wires, GATHER_KINDS + SHARE_KINDS, (out_ref,), branch_ref, False, branch_sem),
    ]
    for copy in small:
        copy.start()
    shares[0].start()
    shares[1].start()

    @pl.loop(0, gather.count)
    def _(chunk):
        gather.send(chunk)

    for copy in small:
        copy.wait()
    attn_all_ref[:, :width] = attn_ref[...]
    attn_all_ref[:, width:] = attn_recv[...]
    mlp_all_ref[:, :width] = mlp_ref[...]
    mlp_all_ref[:, width:] = mlp_recv[...]
    mine = lax.rem(lax.axis_index("ty") + lax.div(lax.axis_index("tx"), 2), 2)
    seg_all[pl.ds(mine, 1)] = seg_ref[...].astype(F32)[None]
    seg_all[pl.ds(1 - mine, 1)] = seg_recv[...].astype(F32)[None]

    shares[0].middle()
    shares[1].middle()

    def between(seq, piece):
        @pl.when(seq == 0)
        def _():
            if piece == 4:
                gather.relay(0, 1)
            elif piece == 6:
                shares[0].late()
                shares[1].late()

        @pl.when(seq == 1)
        def _():
            if piece == 0:
                gather.relay(1, 2)
            elif piece == 2:
                shares[0].later()
                shares[1].later()
            elif piece == 3:
                gather.relay(2, 3)
            elif piece == 6:
                gather.relay(3, 4)

    @pl.loop(0, 2)
    def _(seq):
        for low in range(0, length, 128):
            between(seq, low // 128)
            here = stand(seg_all[seq, :, low : low + 128])
            before = jnp.zeros((128, 128), F32)
            for other in range(0, length, 128):
                before += (seg_all[seq, :, other : other + 128] < here).astype(F32)
            start = jnp.sum(before, axis=1, keepdims=True)
            at = slice(low, low + 128)
            starts_ref[seq, at, :] = start.astype(jnp.int32)
            row = lax.broadcasted_iota(jnp.int32, (128, 128), 0) + low
            lane = lax.broadcasted_iota(jnp.int32, (128, 128), 1)
            angle = (row.astype(F32) - start) * rate_ref[...]
            cosine_ref[seq, at, :] = jnp.cos(angle)
            sine = jnp.sin(angle)
            sine_ref[seq, at, :] = jnp.where(lane < 64, -sine, sine)

    gather.close()
    shares[0].close()
    shares[1].close()


def open_call(tokens, w_query, w_key, w_value, w_out, attn_gain, mlp_gain, seg_ids, rate, number):
    rows, width = tokens.shape
    columns = (w_query.shape[1] + w_key.shape[1] + w_value.shape[1]) // 2
    length = seg_ids.shape[1]
    return pl.pallas_call(
        open_kernel,
        out_shape=(
            shape((1, 2 * width), F32),
            shape((1, 2 * width), F32),
            shape((2, length, 1), jnp.int32),
            shape((2, length, 128), F32),
            shape((2, length, 128), F32),
            shape((4, rows, 2 * width)),
            shape((2 * width, columns)),
            shape((w_out.shape[0] // 2, 2 * width)),
        ),
        in_specs=[IN_VMEM] * 9,
        out_specs=(IN_VMEM,) * 5 + (IN_ANY,) * 3,
        scratch_shapes=gather_scratch(rows, width)
        + wire_scratch(GATHER_KINDS + 2 * SHARE_KINDS + 1, width // CHUNK)
        + [
            pltpu.SemaphoreType.DMA((3,)),
            pltpu.SemaphoreType.DMA((1,)),
            pltpu.VMEM((1, width), F32),
            pltpu.VMEM((1, width), F32),
            pltpu.VMEM((1, length), jnp.int32),
            pltpu.VMEM((2, 1, length), F32),
        ],
        compiler_params=remote_params(number),
        cost_estimate=cost(0, 32 * rows * width),
    )(tokens, w_query, w_key, w_value, w_out, attn_gain, mlp_gain, seg_ids, rate)


def front_kernel(
    most,
    whole_ref,
    project_ref,
    gain_ref,
    query_gain_ref,
    key_gain_ref,
    grad_ref,
    starts_in_ref,
    cosine_in_ref,
    sine_in_ref,
    down_in_ref,
    gate_in_ref,
    first_ref,
    scale_ref,
    projected_ref,
    mixed_ref,
    query_ref,
    key_ref,
    value_ref,
    log_ref,
    grad_whole_ref,
    back_ref,
    gate_ref,
    *scratch,
):
    own, gather_sem, send_sems, recv_sems, back_sem, tokens, firsts, tile_sem = scratch[:8]
    down_ref, starts_ref, cosine_ref, sine_ref = scratch[8:12]
    loads = Loads(
        (down_in_ref, starts_in_ref, cosine_in_ref, sine_in_ref), scratch[8:12], scratch[12]
    )
    core = lax.rem(lax.axis_index("tx"), 2)
    cut(own, grad_ref)
    rows = whole_ref.shape[1]

    def spot(ref, tile):
        at = pl.ds(pl.multiple_of(lax.rem(tile, rows // BLOCK) * BLOCK, BLOCK), BLOCK)
        return ref.at[lax.div(tile, rows // BLOCK), at, :]

    def fetch(tile):
        slot = lax.rem(tile, 2)
        return pltpu.make_async_copy(spot(whole_ref, tile), tokens.at[slot], tile_sem.at[0, slot])

    def store(tile):
        slot = lax.rem(tile, 2)
        return pltpu.make_async_copy(firsts.at[slot], spot(first_ref, tile), tile_sem.at[1, slot])

    fetch(0).start()
    loads.start()
    greet(neighbours() + planes())
    wires = Wires(send_sems, recv_sems)
    gather = Gather(wires, 0, grad_whole_ref, own, gather_sem, 0)
    back = Share(wires, GATHER_KINDS, (down_in_ref,), back_ref, False, back_sem, (down_ref,))
    size, columns = gate_ref.shape
    gate = wires.copy(
        GATHER_KINDS + SHARE_KINDS,
        0,
        gate_in_ref.at[
            pl.ds(pl.multiple_of(lax.axis_index("dp") * size, size), size),
            pl.ds(pl.multiple_of((1 - lax.axis_index("ty")) * columns, columns), columns),
        ],
        gate_ref,
        neighbours()[0],
    )
    back.cross(0).start()

    @pl.loop(0, gather.count)
    def _(chunk):
        gather.send(chunk)

    gate.start()

    loads.wait(0, 1)
    back.local(0).start()
    count = 4 * rows // BLOCK

    @pl.loop(0, count)
    def _(tile):
        slot = lax.rem(tile, 2)
        block = lax.div(tile, rows // BLOCK)
        at = pl.ds(pl.multiple_of(lax.rem(tile, rows // BLOCK) * BLOCK, BLOCK), BLOCK)

        @pl.when(tile < count - 1)
        def _():
            fetch(tile + 1).start()

        fetch(tile).wait()

        @pl.when(tile >= 2)
        def _():
            store(tile - 2).wait()

        value = tokens[slot].astype(F32)
        scale = lax.rsqrt(jnp.mean(value * value, axis=1, keepdims=True) + EPS)
        first = (value * scale * gain_ref[...]).astype(B16)
        firsts[slot] = first
        store(tile).start()
        projected_ref[block, at, :] = jnp.dot(
            first, project_ref[...], preferred_element_type=F32
        )

        @pl.when(block == 0)
        def _():
            scale_ref[at, :] = jnp.broadcast_to(scale, (BLOCK, 128))

        @pl.when(tile == count // 2)
        def _():
            back.middle()

    loads.wait(1, 4)
    fixed_refs = (starts_ref, cosine_ref, sine_ref, query_gain_ref, key_gain_ref)
    saved_refs = (query_ref, key_ref, value_ref, log_ref)

    @pl.loop(0, 2)
    def _(seq):
        def between(turn):
            @pl.when(seq == 0)
            def _():
                if turn == 0:
                    gather.relay(0, 1)
                elif turn == 1:
                    back.late()
                elif turn == 2:
                    gather.relay(1, 2)
                else:
                    back.later()

            @pl.when(seq == 1)
            def _():
                if turn < 2:
                    gather.relay(turn + 2, turn + 3)

        attend_sequence(
            core, seq, most, projected_ref, fixed_refs, mixed_ref, saved_refs, between
        )

    for tile in range(count - 2, count):
        store(tile).wait()
    gather.close()
    back.close()
    gate.wait()


def front_call(whole, w_project, gain, fixed_args, most, cotangent, w_down, w_gate, number):
    starts, cosine, sine, query_gain, key_gain = fixed_args
    rows, width = cotangent.shape
    length = cosine.shape[1]
    depth = query_gain.shape[1]
    columns = w_project.shape[1]
    heads = columns // depth - 2
    outs = (
        shape((4, rows, 2 * width)),
        shape((rows, 128), F32),
        shape((4, rows, columns), F32),
        shape((4, rows, heads * depth)),
        shape((2, length, heads * depth)),
        shape((2, length, depth)),
        shape((2, length, depth)),
        shape((2, heads, length, 1), F32),
        shape((4, rows, 2 * width)),
        shape((w_down.shape[0] // 2, 2 * width)),
        shape((width // 4, w_gate.shape[1] // 2)),
    )
    return pl.pallas_call(
        lambda *refs: front_kernel(most, *refs),
        out_shape=outs,
        in_specs=[IN_ANY] + [IN_VMEM] * 5 + [IN_ANY] * 5,
        out_specs=[IN_ANY] + [IN_VMEM] * 7 + [IN_ANY] * 3,
        scratch_shapes=gather_scratch(rows, width)
        + wire_scratch(GATHER_KINDS + SHARE_KINDS + 1, width // CHUNK)
        + [
            pltpu.SemaphoreType.DMA((1,)),
            pltpu.VMEM((2, BLOCK, 2 * width), B16),
            pltpu.VMEM((2, BLOCK, 2 * width), B16),
            pltpu.SemaphoreType.DMA((2, 2)),
        ]
        + load_scratch((w_down, starts, cosine, sine)),
        compiler_params=remote_params(number),
        cost_estimate=cost(16 * rows * width * columns, 64 * rows * width),
    )(whole, w_project, gain, query_gain, key_gain, cotangent, starts, cosine, sine, w_down, w_gate)


def branch_kernel(
    rows_in_ref,
    weight_in_ref,
    input_in_ref,
    up_in_ref,
    gate_in_ref,
    quarter_ref,
    residual_ref,
    whole_ref,
    up_ref,
    gate_ref,
    *scratch,
):
    bufs = scratch[:7]
    own, gather_sem, send_sems, recv_sems, up_sem = scratch[7:12]
    held, load_sem, gate_sem = scratch[12:17], scratch[17], scratch[18]
    rows_ref, weight_ref, input_ref, up_held, gate_held = held
    loads = Loads(
        (rows_in_ref, weight_in_ref, input_in_ref, up_in_ref, gate_in_ref), held, load_sem
    )
    loads.start()
    width = input_ref.shape[1]
    greet(neighbours() + planes())
    wires = Wires(send_sems, recv_sems)
    reduce = Reduce(wires, rows_ref, weight_ref, False, bufs)
    gather = Gather(wires, REDUCE_KINDS, whole_ref, own, gather_sem, 2)
    up = Share(
        wires, REDUCE_KINDS + GATHER_KINDS, (up_in_ref,), up_ref, True, up_sem, (up_held,)
    )
    gate = Spread(
        wires,
        REDUCE_KINDS + GATHER_KINDS + SHARE_KINDS,
        gate_held,
        gate_ref,
        gate_sem,
        quarter_ref,
    )
    loads.wait(0, 2)

    def between():
        loads.wait(2, 5)
        up.start()
        gate.start()

    reduce.start((between, gate.late))
    up.middle()
    reduce.middle()
    gate.later()

    @pl.loop(0, width // CHUNK)
    def _(chunk):
        at = lanes(chunk, 0, width)
        residual = input_ref[:, at].astype(F32) + reduce.total(chunk)
        residual_ref[:, at] = residual
        own[chunk] = residual.astype(B16)
        gather.send(chunk)

    up.late()
    gather.relay()
    up.later()
    gather.close()
    up.close()
    gate.close()
    reduce.close()


def branch_call(rows, weight, inputs, w_up, w_gate, quarter, number):
    height, width = inputs.shape
    count = width // CHUNK
    loaded = (rows, weight, inputs, w_up, w_gate)
    return pl.pallas_call(
        branch_kernel,
        out_shape=(
            shape((height, width), F32),
            shape((4, height, 2 * width)),
            shape((2 * width, w_up.shape[1] // 2)),
            shape((2 * width, w_gate.shape[1] // 2)),
        ),
        in_specs=[IN_ANY] * 6,
        out_specs=(IN_VMEM, IN_ANY, IN_ANY, IN_ANY),
        scratch_shapes=reduce_scratch(height, width)
        + gather_scratch(height, width)
        + wire_scratch(REDUCE_KINDS + GATHER_KINDS + 2 * SHARE_KINDS, count)
        + [pltpu.SemaphoreType.DMA((1,))]
        + load_scratch(loaded)
        + [pltpu.SemaphoreType.DMA((2,))],
        compiler_params=remote_params(number),
        cost_estimate=cost(16 * height * rows.shape[2] * width, 64 * height * width),
    )(*loaded, quarter)


def units_kernel(
    whole_ref, grad_ref, gates_ref, uppers_ref, back_ref, gain_ref, second_ref, hidden_ref, unit_ref, scale_ref, stats_ref
):
    units = hidden_ref.shape[1]
    value = whole_ref[...].astype(F32)
    scale = lax.rsqrt(jnp.mean(value * value, axis=1, keepdims=True) + EPS)
    second = (value * scale * gain_ref[...]).astype(B16)
    second_ref[...] = second
    scale_ref[...] = jnp.broadcast_to(scale, scale_ref.shape)
    total = jnp.zeros((value.shape[0], 1), F32)
    for low in range(0, units, CHUNK):
        at = slice(low, low + CHUNK)
        beside = slice(units + low, units + low + CHUNK)
        gate = jnp.dot(second, gates_ref[:, at], preferred_element_type=F32)
        upper = jnp.dot(second, uppers_ref[:, at], preferred_element_type=F32)
        hidden_grad = rows_dot(grad_ref[...], back_ref[at, :])
        sigma = jax.nn.sigmoid(gate)
        passed = gate * sigma
        hidden_ref[:, at] = (passed * upper).astype(B16)
        gate_grad = (hidden_grad * upper * (sigma + passed * (1.0 - sigma))).astype(B16)
        up_grad = (hidden_grad * passed).astype(B16)
        unit_ref[:, at] = gate_grad
        unit_ref[:, beside] = up_grad
        total += jnp.sum(
            gate_grad.astype(F32) * gate + up_grad.astype(F32) * upper, axis=1, keepdims=True
        )
    stats_ref[...] = jnp.zeros_like(stats_ref)
    for tile in range(stats_ref.shape[0]):
        put_stats(stats_ref, tile, total[tile * BLOCK : (tile + 1) * BLOCK])


def units_call(whole, grad, w_gates, w_uppers, w_back, gain):
    tokens, width = whole.shape
    units = w_back.shape[0]
    size = 2 * BLOCK
    tiles = tokens // size

    def tile(columns):
        return pl.BlockSpec((size, columns), lambda i: (i, 0))

    def all_of(item):
        return pl.BlockSpec(item.shape, lambda i: (0, 0))

    return pl.pallas_call(
        units_kernel,
        out_shape=(
            shape((tokens, width)),
            shape((tokens, units)),
            shape((tokens, 2 * units)),
            shape((tokens, 128), F32),
            shape((2 * tiles, 8, 128), F32),
        ),
        grid=(tiles,),
        in_specs=[tile(width), tile(width)]
        + [all_of(item) for item in (w_gates, w_uppers, w_back, gain)],
        out_specs=(
            tile(width),
            tile(units),
            tile(2 * units),
            tile(128),
            pl.BlockSpec((2, 8, 128), lambda i: (i, 0, 0)),
        ),
        compiler_params=pltpu.CompilerParams(vmem_limit_bytes=VMEM_MOST),
        cost_estimate=cost(6 * tokens * width * units, 20 * tokens * width // 2),
    )(whole, grad, w_gates, w_uppers, w_back, gain)


class Loads:
    def __init__(self, sources, targets, sems):
        self.copies = [
            pltpu.make_async_copy(source, target, sems.at[index])
            for index, (source, target) in enumerate(zip(sources, targets))
        ]

    def start(self):
        for copy in self.copies:
            copy.start()

    def wait(self, low, high):
        for copy in self.copies[low:high]:
            copy.wait()


def load_scratch(items):
    return [pltpu.VMEM(item.shape, item.dtype) for item in items] + [
        pltpu.SemaphoreType.DMA((len(items),))
    ]


class Stats:
    def __init__(self, wires, base, ref, recv):
        self.ref, self.recv = ref, recv
        side, across, core = neighbours()
        self.hops = (
            lambda: wires.copy(base, 0, ref.at[4:8], recv.at[0:4], core),
            lambda: wires.copy(base, 1, ref.at[2:4], recv.at[4:6], across),
            lambda: wires.copy(base, 2, ref.at[0:2], recv.at[6:8], side),
        )
        self.spans = ((4, 0), (2, 4), (2, 6))

    def start(self, hop):
        self.hops[hop]().start()

    def finish(self, hop):
        self.hops[hop]().wait()
        size, at = self.spans[hop]
        self.ref[0:size] = self.ref[0:size] + self.recv[at : at + size]

    def step(self, hop):
        self.finish(hop)
        self.start(hop + 1)


def pull_columns(stats_ref, scale_ref, column_ref, width):
    for part in range(scale_ref.shape[0] // 128):
        at = slice(part * 128, (part + 1) * 128)
        scale = scale_ref[at, :]
        column_ref[at, :] = (
            stand(stats_ref[part // 2, part % 2 : part % 2 + 1, :]) * scale * scale / (2 * width)
        )


def pulled(reduce, chunk, refs, column_ref):
    scale_ref, value_ref, gain_ref, base_ref = refs
    at = lanes(chunk, 0, value_ref.shape[1])
    upstream = reduce.total(chunk)
    value = value_ref[:, at].astype(F32)
    scale = scale_ref[:, 0:1]
    back = scale * gain_ref[:, at] * upstream - value * column_ref[:, 0:1]
    return at, base_ref[:, at].astype(F32) + back, upstream * value * scale


def tile_columns(tile):
    return pl.ds(pl.multiple_of(tile * BLOCK, BLOCK), BLOCK)


SPLIT = 512


def middle_kernel(
    rows_in_ref,
    gates_in_ref,
    uppers_in_ref,
    value_in_ref,
    base_in_ref,
    hidden_in_ref,
    scale_in_ref,
    stats_in_ref,
    gain_ref,
    grad_ref,
    second_ref,
    result_ref,
    gain_grad_ref,
    whole_ref,
    rest_ref,
    *refs,
):
    ends, scratch = refs[:4], refs[4:]
    bufs = scratch[:7]
    stats_ref, stats_recv, column_ref, send_sems, recv_sems, own, gather_sem = scratch[7:14]
    stream, stream_sem, stage, stage_sem = scratch[14:18]
    down_tiles, down_recv, made_tiles, made_recv = scratch[18:22]
    weight_ref, hidden_ref, rows_ref, value_ref, base_ref, scale_ref = scratch[22:28]
    load_sem = scratch[28]
    rows, width = value_ref.shape
    columns = rows_ref.shape[2]
    units = gates_in_ref.shape[1]
    loads = Loads(
        (
            hidden_in_ref,
            rows_in_ref,
            gates_in_ref,
            uppers_in_ref,
            scale_in_ref.at[pl.ds(0, rows)],
            value_in_ref,
            base_in_ref,
        ),
        (
            hidden_ref,
            rows_ref,
            weight_ref.at[:, :units],
            weight_ref.at[:, units:],
            scale_ref,
            value_ref,
            base_ref,
        ),
        load_sem,
    )

    def fetch(ref, step, tile):
        slot = lax.rem(step, 2)
        return pltpu.make_async_copy(
            ref.at[:, :, tile_columns(tile)], stream.at[slot], stream_sem.at[slot]
        )

    fetch(grad_ref, 0, turn_tile(0)).start()
    loads.start()
    stats_ref[...] = stats_in_ref[...]
    greet(neighbours() + planes())
    wires = Wires(send_sems, recv_sems)
    base = REDUCE_KINDS + 1 + GATHER_KINDS
    down = Fold(wires, base, down_tiles, (down_recv,), ends[0], ends[1])
    made = Fold(wires, base + FOLD_KINDS, made_tiles, (made_recv,), ends[2], ends[3])
    stats = Stats(wires, REDUCE_KINDS, stats_ref, stats_recv)
    def make_down(step):
        @pl.when(step < 7)
        def _():
            fetch(grad_ref, step + 1, turn_tile(step + 1)).start()

        fetch(grad_ref, step, turn_tile(step)).wait()
        left = stream[lax.rem(step, 2)].reshape(4 * rows, BLOCK)
        down_tiles[turn_tile(step)] = weight_grad(
            left, hidden_ref[...].reshape(4 * rows, units)
        ).astype(B16)

    stats.start(0)
    loads.wait(0, 1)
    make_tiles(down, make_down, 0, 2)
    reduce = Reduce(wires, rows_ref, weight_ref, True, bufs)
    loads.wait(1, 4)

    def first_part():
        stats.step(0)
        make_tiles(down, make_down, 2, 4)

    def second_part():
        down.step()
        stats.step(1)
        make_tiles(down, make_down, 4, 6)

    reduce.start((first_part, second_part))
    reduce.middle()
    make_tiles(down, make_down, 6, 8)
    fetch(second_ref, 0, turn_tile(0)).start()

    def store(step):
        slot = lax.rem(step, 2)
        return pltpu.make_async_copy(
            stage.at[slot], rest_ref.at[turn_tile(step)], stage_sem.at[slot]
        )

    def make(step):
        slot = lax.rem(step, 2)

        @pl.when(step < 7)
        def _():
            fetch(second_ref, step + 1, turn_tile(step + 1)).start()

        fetch(second_ref, step, turn_tile(step)).wait()

        @pl.when(step >= 2)
        def _():
            store(step - 2).wait()

        left = stream[slot].reshape(4 * rows, BLOCK)
        flat = rows_ref[...].reshape(4 * rows, columns)
        made.tiles[turn_tile(step)] = weight_grad(left, flat[:, :SPLIT]).astype(B16)
        for low in range(SPLIT, columns, SPLIT):
            stage[slot, :, low - SPLIT : low] = weight_grad(
                left, flat[:, low : low + SPLIT]
            ).astype(B16)
        store(step).start()

    make_tiles(made, make, 0, 4)
    loads.wait(4, 7)
    stats.finish(2)
    pull_columns(stats_ref, scale_ref, column_ref, width)
    gather = Gather(wires, REDUCE_KINDS + 1, whole_ref, own, gather_sem, 2)

    @pl.loop(0, width // CHUNK)
    def _(chunk):
        at, result, share = pulled(
            reduce, chunk, (scale_ref, value_ref, gain_ref, base_ref), column_ref
        )
        result_ref[:, at] = result
        own[chunk] = result.astype(B16)
        gather.send(chunk)
        gain_grad_ref[:, at] = jnp.sum(share, axis=0, keepdims=True)

    down.middle()
    make_tiles(made, make, 4, 8)
    for step in (6, 7):
        store(step).wait()
    gather.relay(0, 3)
    down.late()
    made.step()
    gather.relay(3)
    made.middle()
    gather.close()
    made.late()
    down.close()
    made.close()
    reduce.close()


def middle_call(
    rows, w_gates, w_uppers, stats, scale, value, gain, base, hidden, grad, second, number
):
    height, width = value.shape
    count = width // CHUNK
    columns = rows.shape[2]
    quarter, units = width // 4, hidden.shape[2]
    sizes = (units, SPLIT)
    ends, tiles = [], []
    for size in sizes:
        ends += [shape((quarter, size), F32), shape((quarter, size))]
        tiles += [pltpu.VMEM((8, quarter, size), B16)] + fold_scratch(quarter, size)
    loaded = (rows, w_gates, w_uppers, value, base, hidden, scale)
    return pl.pallas_call(
        middle_kernel,
        out_shape=[
            shape((height, width), F32),
            shape((1, width), F32),
            shape((4, height, 2 * width)),
            shape((8, quarter, columns - SPLIT)),
        ]
        + ends,
        in_specs=[IN_ANY] * 7 + [IN_VMEM] * 2 + [IN_ANY] * 2,
        out_specs=[IN_VMEM] * 2 + [IN_ANY] * 2 + [IN_VMEM, IN_ANY] * 2,
        scratch_shapes=reduce_scratch(height, width)
        + [
            pltpu.VMEM((8, 8, 128), F32),
            pltpu.VMEM((8, 8, 128), F32),
            pltpu.VMEM((height, 128), F32),
        ]
        + wire_scratch(REDUCE_KINDS + 1 + GATHER_KINDS + 2 * FOLD_KINDS, count)
        + gather_scratch(height, width)
        + [
            pltpu.VMEM((2, 4, height, BLOCK), B16),
            pltpu.SemaphoreType.DMA((2,)),
            pltpu.VMEM((2, quarter, columns - SPLIT), B16),
            pltpu.SemaphoreType.DMA((2,)),
        ]
        + tiles
        + [pltpu.VMEM((2 * width, columns), B16)]
        + load_scratch((hidden, rows, value, base))[:-1]
        + [pltpu.VMEM((height, 128), F32)]
        + [pltpu.SemaphoreType.DMA((len(loaded),))],
        compiler_params=remote_params(number),
        cost_estimate=cost(48 * height * units * width, 64 * height * width),
    )(*loaded, stats, gain, grad, second)


def last_kernel(
    rows_in_ref,
    weight_in_ref,
    value_in_ref,
    base_in_ref,
    stats_in_ref,
    scale_ref,
    gain_ref,
    extra_ref,
    out_in_ref,
    project_in_ref,
    result_ref,
    totals_ref,
    out_mine_ref,
    out_theirs_ref,
    project_mine_ref,
    project_theirs_ref,
    *scratch,
):
    bufs = scratch[:7]
    stats_ref, stats_recv, column_ref, send_sems, recv_sems = scratch[7:12]
    out_ref, project_ref, sums_ref, sums_recv, load_sem = scratch[12:17]
    out_bufs, project_bufs = scratch[17:18], scratch[18:19]
    rows_ref, weight_ref, value_ref, base_ref = scratch[19:23]
    rows, width = value_ref.shape
    loads = Loads(
        (project_in_ref, weight_in_ref, rows_in_ref, value_in_ref, base_in_ref, out_in_ref),
        (project_ref, weight_ref, rows_ref, value_ref, base_ref, out_ref),
        load_sem,
    )
    loads.start()
    stats_ref[...] = stats_in_ref[...]
    sums_ref[...] = jnp.zeros_like(sums_ref)
    sums_ref[8] = extra_ref[0]
    sums_ref[9] = extra_ref[1]
    greet(neighbours() + planes())
    wires = Wires(send_sems, recv_sems)
    base = REDUCE_KINDS + 1
    out = Fold(wires, base, out_ref, out_bufs, out_mine_ref, out_theirs_ref, out_in_ref)
    project = Fold(
        wires,
        base + FOLD_KINDS,
        project_ref,
        project_bufs,
        project_mine_ref,
        project_theirs_ref,
        project_in_ref,
    )
    stats = Stats(wires, REDUCE_KINDS, stats_ref, stats_recv)
    stats.start(0)
    out.start()
    loads.wait(0, 2)

    @pl.loop(0, 8)
    def _(tile):
        share = jnp.sum(
            project_ref[tile].astype(F32) * weight_ref[tile_columns(tile), :].astype(F32),
            axis=1,
            keepdims=True,
        )
        sums_ref[tile, 0:1, :] = lie(share[:128])
        sums_ref[tile, 1:2, :] = lie(share[128:])

    side_device, across, core = neighbours()
    near, mirror = planes()

    def hop(index):
        slot, device = ((0, core), (1, across), (2, near), (3, mirror), (2, near))[index]
        kind, chunk = divmod(index, 4)
        return wires.copy(
            base + 2 * FOLD_KINDS + kind, chunk, sums_ref, sums_recv.at[slot], device
        )

    def add(slot):
        sums_ref[...] = sums_ref[...] + sums_recv[slot]

    reduce = Reduce(wires, rows_ref, weight_ref, True, bufs)
    loads.wait(2, 3)
    hop(0).start()
    reduce.give(0)
    hop(0).wait()
    add(0)
    hop(1).start()
    stats.step(0)

    def after_two():
        hop(1).wait()
        add(1)

        @pl.when(jnp.logical_not(inner()))
        def _():
            hop(2).start()

        project.start()
        stats.step(1)

    reduce.rest((after_two, lambda: None))
    loads.wait(3, 6)
    out.step()
    ends_line = jnp.logical_not(inner())

    @pl.when(inner())
    def _():
        hop(2).wait_recv()
        add(2)
        hop(3).start()

    out.middle()
    reduce.middle()
    stats.finish(2)
    pull_columns(stats_ref, scale_ref, column_ref, width)

    @pl.when(inner())
    def _():
        hop(3).wait()
        add(3)
        hop(4).start()

    project.step()
    project.middle()

    @pl.loop(0, width // CHUNK)
    def _(chunk):
        at, result, _ = pulled(
            reduce, chunk, (scale_ref, value_ref, gain_ref, base_ref), column_ref
        )
        result_ref[:, at] = result.astype(B16)

    @pl.when(inner())
    def _():
        hop(4).wait_send()

    @pl.when(ends_line)
    def _():
        hop(2).wait_send()
        hop(4).wait_recv()
        sums_ref[...] = sums_recv[2]

    move = wires.copy(base + 2 * FOLD_KINDS + 1, 1, sums_ref, sums_recv.at[4], side_device)
    move.start()
    out.late()
    project.late()
    move.wait()
    totals_ref[0:4] = sums_ref[0:4] + sums_recv[4, 4:8]
    totals_ref[4:8] = sums_ref[4:8] + sums_recv[4, 0:4]
    totals_ref[8] = sums_ref[8]
    totals_ref[9] = sums_recv[4, 8]
    totals_ref[10] = sums_ref[9] + sums_recv[4, 9]
    project.close()
    out.close()
    reduce.close()


def last_call(rows, weight, stats, scale, value, gain, base, extra, out, project, number):
    height, width = value.shape
    count = width // CHUNK
    quarter, branch = out.shape[1:]
    columns = rows.shape[2]
    return pl.pallas_call(
        last_kernel,
        out_shape=(
            shape((height, width)),
            shape((11, 8, 128), F32),
            shape((quarter, branch), F32),
            shape((quarter, branch)),
            shape((quarter, columns), F32),
            shape((quarter, columns)),
        ),
        in_specs=[IN_ANY] * 4 + [IN_VMEM] * 4 + [IN_ANY] * 2,
        out_specs=(IN_VMEM, IN_VMEM) + (IN_VMEM, IN_ANY) * 2,
        scratch_shapes=reduce_scratch(height, width)
        + [
            pltpu.VMEM((8, 8, 128), F32),
            pltpu.VMEM((8, 8, 128), F32),
            pltpu.VMEM((height, 128), F32),
        ]
        + wire_scratch(REDUCE_KINDS + 1 + 2 * FOLD_KINDS + 2, count)
        + [
            pltpu.VMEM((8, quarter, branch), B16),
            pltpu.VMEM((8, quarter, columns), B16),
            pltpu.VMEM((10, 8, 128), F32),
            pltpu.VMEM((5, 10, 8, 128), F32),
            pltpu.SemaphoreType.DMA((6,)),
        ]
        + fold_scratch(quarter, branch)
        + fold_scratch(quarter, columns)
        + load_scratch((rows, weight, value, base))[:4],
        compiler_params=remote_params(number),
        cost_estimate=cost(32 * height * columns * width, 64 * height * width),
    )(rows, weight, value, base, stats, scale, gain, extra, out, project)


def back_kernel(
    most,
    query_gain_ref,
    key_gain_ref,
    *refs,
):
    operands, refs = refs[:13], refs[13:]
    rest_ref, whole_ref, first_ref = refs[:3]
    output_ref, result_ref, stats_ref, gains_ref, out_ref, project_ref = refs[3:9]
    ends, scratch = refs[9:11], refs[11:]
    bufs = scratch[:7]
    key_acc, value_acc, send_sems, recv_sems, rest_sem = scratch[7:12]
    tiles, fold_recv = scratch[12:14]
    held, load_sem = scratch[14:27], scratch[27]
    upstream, acc, stream, stream_sem, stage, stage_sem = scratch[28:]
    hidden_ref, down_ref, branch_ref, mixed_ref, starts_ref, cosine_ref, sine_ref = held[:7]
    projected_ref, query_ref, key_ref, value_ref, log_ref, residual_ref = held[7:]
    attend_loads = Loads(operands, held, load_sem)
    attend_loads.start()
    width = residual_ref.shape[1]
    rows = residual_ref.shape[0]

    def fetch(ref, tile):
        slot = lax.rem(tile, 2)
        return pltpu.make_async_copy(
            ref.at[:, :, tile_columns(tile)], stream.at[slot], stream_sem.at[slot]
        )

    def each_tile(ref, target, right, work):
        columns = target.shape[2]

        def store(tile):
            slot = lax.rem(tile, 2)
            return pltpu.make_async_copy(
                stage.at[slot, :, :columns], target.at[tile], stage_sem.at[slot]
            )

        @pl.loop(0, 8)
        def _(tile):
            @pl.when(tile < 7)
            def _():
                fetch(ref, tile + 1).start()

            fetch(ref, tile).wait()

            @pl.when(tile >= 2)
            def _():
                store(tile - 2).wait()

            left = stream[lax.rem(tile, 2)].reshape(4 * rows, BLOCK)
            work(tile, left)
            stage[lax.rem(tile, 2), :, :columns] = weight_grad(
                left, right[...].reshape(4 * rows, columns)
            ).astype(B16)
            store(tile).start()

        for tile in (6, 7):
            store(tile).wait()

    fetch(whole_ref, 0).start()
    core = lax.rem(lax.axis_index("tx"), 2)
    load = pltpu.make_async_copy(rest_ref, tiles, rest_sem)
    load.start()
    greet(neighbours() + planes())
    wires = Wires(send_sems, recv_sems)
    fold = Fold(wires, REDUCE_KINDS, tiles, (fold_recv,), ends[0], ends[1], rest_ref)
    fold.start()
    reduce = Reduce(wires, hidden_ref, down_ref, False, bufs)
    attend_loads.wait(0, 2)
    reduce.start()
    attend_loads.wait(2, 13)
    load.wait()
    acc[...] = jnp.zeros_like(acc)

    def branch_work(tile, left):
        acc[...] += rows_dot(left, branch_ref[:, tile_columns(tile)])

    each_tile(whole_ref, out_ref, mixed_ref, branch_work)
    fetch(first_ref, 0).start()
    upstream[...] = acc[...].astype(B16).reshape(upstream.shape)
    fold.step()
    stats_ref[...] = jnp.zeros_like(stats_ref)
    fixed_refs = (starts_ref, cosine_ref, sine_ref, query_gain_ref, key_gain_ref)
    saved_refs = (query_ref, key_ref, value_ref, log_ref)

    @pl.loop(0, 2)
    def _(seq):
        attend_sequence_back(
            core,
            seq,
            most,
            projected_ref,
            upstream,
            fixed_refs,
            saved_refs,
            result_ref,
            stats_ref,
            gains_ref,
            (acc, key_acc, value_acc),
        )

        @pl.when(seq == 0)
        def _():
            reduce.middle()

    fold.middle()

    each_tile(first_ref, project_ref, result_ref, lambda tile, left: None)


    @pl.loop(0, width // CHUNK)
    def _(chunk):
        at = lanes(chunk, 0, width)
        output_ref[:, at] = (residual_ref[:, at] + reduce.total(chunk)).astype(B16)

    fold.late()
    fold.close()
    reduce.close()


def back_call(
    whole, first, w_branch, mixed, hidden, w_back, residual, fixed_args, projected, saved, rest, most, number
):
    height, width = residual.shape
    _, cosine, _, query_gain, _ = fixed_args
    depth = query_gain.shape[1]
    length = cosine.shape[1]
    columns = projected.shape[2]
    heads = columns // depth - 2
    quarter, columns_left = rest.shape[1:]
    loaded = (hidden, w_back, w_branch, mixed) + fixed_args[:3] + (projected,) + saved + (residual,)
    return pl.pallas_call(
        lambda *refs: back_kernel(most, *refs),
        out_shape=(
            shape((height, width)),
            shape((4, height, columns)),
            shape((8, 8, 128), F32),
            shape((2, 8, depth), F32),
            shape((8, quarter, heads * depth)),
            shape((8, quarter, columns)),
        )
        + (shape((quarter, columns_left), F32), shape((quarter, columns_left))),
        in_specs=[IN_VMEM] * 2 + [IN_ANY] * 16,
        out_specs=[IN_VMEM] * 4 + [IN_ANY] * 2 + [IN_VMEM, IN_ANY],
        scratch_shapes=reduce_scratch(height, width)
        + [
            pltpu.VMEM((length, depth), F32),
            pltpu.VMEM((length, depth), F32),
        ]
        + wire_scratch(REDUCE_KINDS + FOLD_KINDS, width // CHUNK)
        + [pltpu.SemaphoreType.DMA, pltpu.VMEM(rest.shape, B16)]
        + fold_scratch(quarter, columns_left)
        + load_scratch(loaded)
        + [
            pltpu.VMEM((4, height, heads * depth), B16),
            pltpu.VMEM((4 * height, heads * depth), F32),
            pltpu.VMEM((2, 4, height, BLOCK), B16),
            pltpu.SemaphoreType.DMA((2,)),
            pltpu.VMEM((2, quarter, columns), B16),
            pltpu.SemaphoreType.DMA((2,)),
        ],
        compiler_params=remote_params(number),
        cost_estimate=cost(16 * height * hidden.shape[2] * width, 64 * height * width),
    )(*fixed_args[3:], *loaded, rest, whole, first)


def finish_kernel(place_ref, *refs):
    downs, both, out, project = refs[0:2], refs[2:6], refs[6:8], refs[8:10]
    totals_ref, gain_ref = refs[10:12]
    query_ref, key_ref, value_ref, out_ref, gate_ref, up_ref, down_ref = refs[12:19]
    attn_ref, mlp_ref = refs[19:]
    first = place_ref[0] == 0

    def ordered(mine, theirs):
        theirs = theirs.astype(F32)
        return jnp.where(first, mine, theirs), jnp.where(first, theirs, mine)

    def put(target, at, mine, theirs):
        half = target.shape[1] // 2
        low, high = ordered(mine, theirs)
        target[:, at : at + mine.shape[1]] = low
        target[:, half + at : half + at + mine.shape[1]] = high

    def put_turned(target, at, mine, theirs):
        half = target.shape[0] // 2
        low, high = ordered(mine, theirs)
        target[at : at + mine.shape[1], :] = low.T
        target[half + at : half + at + mine.shape[1], :] = high.T

    put_turned(down_ref, 0, downs[0][...], downs[1][...])
    put_turned(out_ref, 0, out[0][...], out[1][...])
    at = 0
    for target in (query_ref, key_ref, value_ref):
        size = target.shape[1] // 2
        put(target, 0, project[0][:, at : at + size], project[1][:, at : at + size])
        at += size
    units = gate_ref.shape[1] // 2
    at = 0
    for index in (0, 2):
        low = 0
        while low < both[index].shape[1]:
            size = min(both[index].shape[1] - low, units - at % units)
            put(
                gate_ref if at < units else up_ref,
                at % units,
                both[index][:, low : low + size],
                both[index + 1][:, low : low + size],
            )
            low += size
            at += size
    mine = jnp.concatenate([totals_ref[tile, 0:2] for tile in range(4)], axis=0)
    theirs = jnp.concatenate([totals_ref[tile, 0:2] for tile in range(4, 8)], axis=0)
    low, high = ordered(mine / gain_ref[0:8], theirs / gain_ref[8:16])
    attn_ref[0:8], attn_ref[8:16] = low, high
    low, high = ordered(totals_ref[8], totals_ref[9])
    mlp_ref[0:8], mlp_ref[8:16] = low, high


def finish_call(place, parts, totals, gain, sizes):
    quarter = parts[0].shape[0]
    queries, keys, branch, units = sizes
    return pl.pallas_call(
        finish_kernel,
        out_shape=(
            shape((quarter, queries), F32),
            shape((quarter, keys), F32),
            shape((quarter, keys), F32),
            shape((branch, quarter), F32),
            shape((quarter, units), F32),
            shape((quarter, units), F32),
            shape((units, quarter), F32),
            shape((16, 128), F32),
            shape((16, 128), F32),
        ),
        in_specs=[pl.BlockSpec(memory_space=pltpu.SMEM)] + [IN_VMEM] * (len(parts) + 2),
        out_specs=[IN_VMEM] * 9,
        compiler_params=pltpu.CompilerParams(vmem_limit_bytes=VMEM_MOST),
        cost_estimate=cost(0, 16 * 1024 * 1024),
    )(place, *parts, totals, gain)


def plane_device(
    tokens,
    seg_ids,
    w_query,
    w_key,
    w_value,
    w_out,
    w_gate,
    w_up,
    w_down,
    attn_gain,
    mlp_gain,
    query_gain,
    key_gain,
    cotangent,
):
    depth = query_gain.shape[0]
    most = seg_ids.shape[1] // 2
    rows, width = tokens.shape
    head_width = w_query.shape[1] // 2
    kv_width = w_key.shape[1] // 2
    units = w_gate.shape[1] // 2

    half = jnp.arange(depth // 2, dtype=F32)
    rate = THETA ** (-half * 2.0 / depth)
    rate = jnp.concatenate([rate, rate])[None]
    attn_row, mlp_row, starts, cosine, sine, token_whole, w_project, w_branch = open_call(
        tokens, w_query, w_key, w_value, w_out, attn_gain[None], mlp_gain[None], seg_ids, rate, 0
    )
    fixed_args = (starts, cosine, sine, query_gain[None], key_gain[None])
    (
        first,
        first_scale,
        projected,
        mixed,
        query,
        keys,
        values,
        logs,
        grad_whole,
        w_back,
        gate_quarter,
    ) = front_call(
        token_whole, w_project, attn_row, fixed_args, most, cotangent, w_down, w_gate, 1
    )
    residual, residual_whole, w_uppers, w_gates = branch_call(
        mixed, w_branch, tokens, w_up, w_gate, gate_quarter, 2
    )
    flat = (4 * rows, 2 * width)
    grad_flat = grad_whole.reshape(flat)
    second, hidden, unit_grads, second_scale, unit_stats = units_call(
        residual_whole.reshape(flat), grad_flat, w_gates, w_uppers, w_back, mlp_row
    )
    (
        residual_grad,
        mlp_gain_part,
        branch_whole,
        rest_tiles,
        *ends,
    ) = middle_call(
        unit_grads.reshape(4, rows, 2 * units),
        w_gates,
        w_uppers,
        unit_stats,
        second_scale,
        residual,
        mlp_gain[None],
        cotangent,
        hidden.reshape(4, rows, units),
        grad_whole,
        second.reshape(4, rows, 2 * width),
        3,
    )
    output, proj_grads, proj_stats, gain_parts, out_tiles, project_tiles, *rest_ends = back_call(
        branch_whole,
        first,
        w_branch,
        mixed,
        hidden.reshape(4, rows, units),
        w_back,
        residual,
        fixed_args,
        projected,
        (query, keys, values, logs),
        rest_tiles,
        most,
        4,
    )
    extra = jnp.stack(
        [
            mlp_gain_part.reshape(8, 128),
            jnp.pad(jnp.sum(gain_parts[:, :2], axis=0), ((0, 6), (0, 0))),
        ]
    )
    input_grad, totals, out_mine, out_theirs, project_mine, project_theirs = last_call(
        proj_grads,
        w_project,
        proj_stats,
        first_scale,
        tokens,
        attn_gain[None],
        residual_grad,
        extra,
        out_tiles,
        project_tiles,
        5,
    )
    place = lax.axis_index("ty").reshape(1).astype(jnp.int32)
    (
        query_share,
        key_share,
        value_share,
        out_share,
        gate_share,
        up_share,
        down_share,
        attn_total,
        mlp_total,
    ) = finish_call(
        place,
        (*ends, *rest_ends, out_mine, out_theirs, project_mine, project_theirs),
        totals,
        attn_row.reshape(16, 128),
        (2 * head_width, 2 * kv_width, 2 * head_width, 2 * units),
    )
    attn_total, mlp_total = attn_total.reshape(-1), mlp_total.reshape(-1)
    query_total, key_total = totals[10, 0], totals[10, 1]
    return (
        output,
        input_grad,
        query_share,
        key_share,
        value_share,
        out_share,
        gate_share,
        up_share,
        down_share,
        attn_total,
        mlp_total,
        query_total,
        key_total,
    )


def solution(mesh):
    placed = (
        P(("dp", "tx"), "ty"),
        P(("dp", "ty"), None),
        P("ty", "tx"),
        P("ty", "tx"),
        P("ty", "tx"),
        P("tx", "ty"),
        P("ty", "tx"),
        P("ty", "tx"),
        P("tx", "ty"),
        P("ty"),
        P("ty"),
        P(),
        P(),
        P(("dp", "tx"), "ty"),
    )
    return jax.shard_map(
        plane_device if fits(mesh) else general_device,
        mesh=mesh,
        in_specs=placed,
        out_specs=(
            P(("dp", "tx"), "ty"),
            P(("dp", "tx"), "ty"),
            P(("ty", "dp"), "tx"),
            P(("ty", "dp"), "tx"),
            P(("ty", "dp"), "tx"),
            P("tx", ("ty", "dp")),
            P(("ty", "dp"), "tx"),
            P(("ty", "dp"), "tx"),
            P("tx", ("ty", "dp")),
            P(),
            P(),
            P(),
            P(),
        ),
        check_vma=False,
    )
```

```python
import jax
import jax.numpy as jnp
import numpy as np
from jax import lax
from jax.experimental import pallas as pl
from jax.experimental.pallas import tpu as pltpu
from jax.sharding import PartitionSpec as P

EPS = 1e-06
THETA = 1000000.0
NEG = -1e30
F32 = jnp.float32
B16 = jnp.bfloat16
MESH = pl.DeviceIdType.MESH


def width_sum(value):
    return lax.psum(value, "ty")


def token_gather(rows):
    return lax.all_gather(rows, "tx", axis=0, tiled=True)


def branch_gather(rows):
    return lax.all_gather(rows, "ty", axis=0, tiled=True)


def width_reduce(whole, apply):
    return lax.psum_scatter(apply(whole), "ty", scatter_dimension=0, tiled=True)


def head_reduce(whole, apply):
    return lax.psum_scatter(
        apply(whole).astype(jnp.bfloat16), "tx", scatter_dimension=0, tiled=True
    ).astype(jnp.float32)


def forward_with(weight):
    return lambda rows: jnp.dot(rows, weight, preferred_element_type=F32)


def backward_with(weight):
    return lambda rows: lax.dot_general(
        rows, weight, (((1,), (1,)), ((), ())), preferred_element_type=F32
    )


def weight_grad(left, right):
    return lax.dot_general(left, right, (((0,), (0,)), ((), ())), preferred_element_type=F32)


def norm_scale(rows):
    width = rows.shape[1] * lax.axis_size("ty")
    return lax.rsqrt(width_sum(jnp.sum(rows * rows, axis=1)) / width + EPS)


def norm_back(rows, scale, gain, upstream):
    width = rows.shape[1] * lax.axis_size("ty")
    inner = width_sum(jnp.sum(upstream * gain * rows, axis=1))
    back = scale[:, None] * gain * upstream - rows * (scale**3 * inner / width)[:, None]
    gain_part = jnp.sum(upstream * rows * scale[:, None], axis=0)
    return (back, gain_part)


def widen(part):
    whole = jnp.zeros((part.shape[0] * lax.axis_size("ty"),), F32)
    return lax.dynamic_update_slice_in_dim(whole, part, lax.axis_index("ty") * part.shape[0], 0)


def doc_positions(seg):
    count = seg.shape[-1]
    index = jnp.arange(count, dtype=jnp.int32)
    edge = jnp.concatenate([jnp.ones((1,), dtype=jnp.bool_), seg[1:] != seg[:-1]])
    first = lax.cummax(jnp.where(edge, index, jnp.zeros_like(index)), axis=0)
    return index - first


def rotary(positions, depth):
    half = depth // 2
    freq = THETA ** (-jnp.arange(half, dtype=F32) * 2.0 / depth)
    angle = positions.astype(F32)[..., None] * freq
    return (jnp.cos(angle), jnp.sin(angle))


def turn(value, gain, cosine, sine):
    normed = value * lax.rsqrt(jnp.mean(value * value, axis=-1, keepdims=True) + EPS) * gain
    half = value.shape[-1] // 2
    first = normed[..., :half]
    second = normed[..., half:]
    return jnp.concatenate(
        [first * cosine - second * sine, second * cosine + first * sine], axis=-1
    )


def block_scores(part, seq_keys, seq_ids, start, scale):
    block = part.shape[0]
    length = seq_ids.shape[0]
    index = jnp.arange(length, dtype=jnp.int32)
    rows = start + jnp.arange(block, dtype=jnp.int32)
    row_ids = lax.dynamic_slice_in_dim(seq_ids, start, block, 0)
    mask = (seq_ids[None, :] == row_ids[:, None]) & (index[None, :] <= rows[:, None])
    scores = jnp.einsum("qkgd,mkd->kgqm", part, seq_keys, preferred_element_type=F32) * scale
    return jnp.where(mask[None, None], scores, NEG)


def attend_forward(query, keys, values, seg, block):
    seqs, length, heads, depth = query.shape
    kv_heads = keys.shape[2]
    groups = heads // kv_heads
    scale = depth ** (-0.5)
    count = length // block
    starts = jnp.arange(count, dtype=jnp.int32) * block

    def one_sequence(operands):
        seq_query, seq_keys, seq_values, seq_ids = operands
        blocks = seq_query.reshape(count, block, kv_heads, groups, depth)

        def one_block(inputs):
            part, start = inputs
            scores = block_scores(part, seq_keys, seq_ids, start, scale)
            top = jnp.max(scores, axis=-1)
            weights = jnp.exp(scores - top[..., None])
            total = jnp.sum(weights, axis=-1)
            probs = (weights / total[..., None]).astype(B16)
            mixed = jnp.einsum("kgqm,mkd->qkgd", probs, seq_values, preferred_element_type=F32)
            return (mixed, top + jnp.log(total))

        mixed, logs = lax.map(one_block, (blocks, starts))
        return (mixed.reshape(length, heads * depth), logs)

    return lax.map(one_sequence, (query, keys, values, seg))


def attend_backward(query, keys, values, seg, logs, grad_out, block):
    seqs, length, heads, depth = query.shape
    kv_heads = keys.shape[2]
    groups = heads // kv_heads
    scale = depth ** (-0.5)
    count = length // block
    starts = jnp.arange(count, dtype=jnp.int32) * block

    def one_sequence(operands):
        seq_query, seq_keys, seq_values, seq_ids, seq_logs, seq_grad = operands
        blocks = seq_query.reshape(count, block, kv_heads, groups, depth)
        grads = seq_grad.reshape(count, block, kv_heads, groups, depth)

        def one_block(carry, inputs):
            key_acc, value_acc = carry
            part, grad_part, log_part, start = inputs
            scores = block_scores(part, seq_keys, seq_ids, start, scale)
            probs = jnp.exp(scores - log_part[..., None])
            value_acc = value_acc + jnp.einsum(
                "kgqm,qkgd->mkd", probs.astype(B16), grad_part, preferred_element_type=F32
            )
            prob_grad = jnp.einsum(
                "qkgd,mkd->kgqm", grad_part, seq_values, preferred_element_type=F32
            )
            delta = jnp.sum(probs * prob_grad, axis=-1, keepdims=True)
            score_grad = (probs * (prob_grad - delta)).astype(B16)
            query_grad = (
                jnp.einsum("kgqm,mkd->qkgd", score_grad, seq_keys, preferred_element_type=F32)
                * scale
            )
            key_acc = (
                key_acc
                + jnp.einsum("kgqm,qkgd->mkd", score_grad, part, preferred_element_type=F32) * scale
            )
            return ((key_acc, value_acc), query_grad)

        zeros = jnp.zeros((length, kv_heads, depth), F32)
        (key_grad, value_grad), query_grad = lax.scan(
            one_block, (zeros, zeros), (blocks, grads, seq_logs, starts)
        )
        return (query_grad.reshape(length, heads, depth), key_grad, value_grad)

    return lax.map(one_sequence, (query, keys, values, seg, logs, grad_out))


def general_device(
    tokens,
    seg_ids,
    w_query,
    w_key,
    w_value,
    w_out,
    w_gate,
    w_up,
    w_down,
    attn_gain,
    mlp_gain,
    query_gain,
    key_gain,
    cotangent,
):
    seqs, length = seg_ids.shape
    depth = query_gain.shape[0]
    query_width = w_query.shape[1]
    key_width = w_key.shape[1]
    units = w_gate.shape[1]
    block = min(512, length)
    inputs = tokens.astype(F32)
    first_scale = norm_scale(inputs)
    first_normed = (inputs * first_scale[:, None] * attn_gain).astype(B16)
    first_whole = token_gather(first_normed)
    w_project = jnp.concatenate([w_query, w_key, w_value], axis=1)
    projected = width_reduce(first_whole, forward_with(w_project))
    query_proj = projected[:, :query_width].reshape(seqs, length, -1, depth)
    key_proj = projected[:, query_width : query_width + key_width].reshape(seqs, length, -1, depth)
    values = projected[:, query_width + key_width :].astype(B16).reshape(seqs, length, -1, depth)
    positions = jax.vmap(doc_positions)(seg_ids)
    cosine, sine = rotary(positions, depth)
    cosine = cosine[:, :, None, :]
    sine = sine[:, :, None, :]
    query = turn(query_proj, query_gain, cosine, sine).astype(B16)
    keys = turn(key_proj, key_gain, cosine, sine).astype(B16)
    mixed, logs = attend_forward(query, keys, values, seg_ids, block)
    attended = mixed.reshape(seqs * length, -1).astype(B16)
    attended_whole = branch_gather(attended)
    residual = inputs + head_reduce(attended_whole, forward_with(w_out))
    second_scale = norm_scale(residual)
    second_normed = (residual * second_scale[:, None] * mlp_gain).astype(B16)
    second_whole = token_gather(second_normed)
    w_both = jnp.concatenate([w_gate, w_up], axis=1)
    gate_up = width_reduce(second_whole, forward_with(w_both))
    gate = gate_up[:, :units]
    upper = gate_up[:, units:]
    hidden = (jax.nn.silu(gate) * upper).astype(B16)
    hidden_whole = branch_gather(hidden)
    output = residual + head_reduce(hidden_whole, forward_with(w_down))
    grad_whole = token_gather(cotangent)
    hidden_grad = width_reduce(grad_whole, backward_with(w_down))
    down_grad = weight_grad(hidden_whole, grad_whole)
    gate_grad, up_grad = jax.vjp(lambda left, right: jax.nn.silu(left) * right, gate, upper)[1](
        hidden_grad
    )
    unit_grads = jnp.concatenate([gate_grad, up_grad], axis=1).astype(B16)
    unit_whole = branch_gather(unit_grads)
    second_grad = head_reduce(unit_whole, backward_with(w_both))
    both_grad = weight_grad(second_whole, unit_whole)
    gate_weight = both_grad[:, :units]
    up_weight = both_grad[:, units:]
    resid_norm_grad, mlp_gain_part = norm_back(residual, second_scale, mlp_gain, second_grad)
    residual_grad = cotangent.astype(F32) + resid_norm_grad
    residual_whole = token_gather(residual_grad.astype(B16))
    mixed_grad = width_reduce(residual_whole, backward_with(w_out)).astype(B16)
    out_grad = weight_grad(attended_whole, residual_whole)
    query_grad, key_grad, value_grad = attend_backward(
        query, keys, values, seg_ids, logs, mixed_grad.reshape(seqs, length, -1), block
    )
    query_proj_grad, query_gain_grad = jax.vjp(
        lambda value, gain: turn(value, gain, cosine, sine), query_proj, query_gain
    )[1](query_grad)
    key_proj_grad, key_gain_grad = jax.vjp(
        lambda value, gain: turn(value, gain, cosine, sine), key_proj, key_gain
    )[1](key_grad)
    rows = seqs * length
    proj_grad = jnp.concatenate(
        [
            query_proj_grad.reshape(rows, -1),
            key_proj_grad.reshape(rows, -1),
            value_grad.reshape(rows, -1),
        ],
        axis=1,
    ).astype(B16)
    proj_whole = branch_gather(proj_grad)
    first_grad = head_reduce(proj_whole, backward_with(w_project))
    project_grad = weight_grad(first_whole, proj_whole)
    query_weight = project_grad[:, :query_width]
    key_weight = project_grad[:, query_width : query_width + key_width]
    value_weight = project_grad[:, query_width + key_width :]
    input_norm_grad, attn_gain_part = norm_back(inputs, first_scale, attn_gain, first_grad)
    input_grad = (residual_grad + input_norm_grad).astype(B16)
    attn_total, mlp_total, query_total, key_total = lax.psum(
        (widen(attn_gain_part), widen(mlp_gain_part), query_gain_grad, key_gain_grad),
        ("dp", "tx", "ty"),
    )
    query_share, key_share, value_share, gate_share, up_share = (
        lax.psum_scatter(
            query_weight.astype(jnp.bfloat16), "dp", scatter_dimension=0, tiled=True
        ).astype(jnp.float32),
        lax.psum_scatter(
            key_weight.astype(jnp.bfloat16), "dp", scatter_dimension=0, tiled=True
        ).astype(jnp.float32),
        lax.psum_scatter(
            value_weight.astype(jnp.bfloat16), "dp", scatter_dimension=0, tiled=True
        ).astype(jnp.float32),
        lax.psum_scatter(
            gate_weight.astype(jnp.bfloat16), "dp", scatter_dimension=0, tiled=True
        ).astype(jnp.float32),
        lax.psum_scatter(
            up_weight.astype(jnp.bfloat16), "dp", scatter_dimension=0, tiled=True
        ).astype(jnp.float32),
    )
    out_share, down_share = (
        lax.psum_scatter(
            out_grad.astype(jnp.bfloat16), "dp", scatter_dimension=1, tiled=True
        ).astype(jnp.float32),
        lax.psum_scatter(
            down_grad.astype(jnp.bfloat16), "dp", scatter_dimension=1, tiled=True
        ).astype(jnp.float32),
    )
    return (
        output.astype(B16),
        input_grad,
        query_share,
        key_share,
        value_share,
        out_share,
        gate_share,
        up_share,
        down_share,
        attn_total,
        mlp_total,
        query_total,
        key_total,
    )


def fits(mesh):
    return mesh.shape["tx"] == 4 and mesh.shape["ty"] == 2 and mesh.shape["dp"] == 4


def swap_x(value):
    return lax.ppermute(value, "ty", [(0, 1), (1, 0)])


def in_order(mine, theirs, axis):
    first = lax.axis_index("ty") == 0
    return jnp.concatenate(
        [jnp.where(first, mine, theirs), jnp.where(first, theirs, mine)], axis=axis
    )


def spin(value, cosine, sine):
    return value * cosine + pltpu.roll(value, value.shape[1] // 2, 1) * sine


def spin_back(value, cosine, sine):
    return value * cosine + pltpu.roll(value * sine, value.shape[1] // 2, 1)


def head_scale(value):
    return lax.rsqrt(jnp.mean(value * value, axis=1, keepdims=True) + EPS)


def window(first, block, most):
    return max(0, first - most), first + block


def kept(first, block, low, high, starts):
    shape = (block, high - low)
    column = low + lax.broadcasted_iota(jnp.int32, shape, 1)
    row = first + lax.broadcasted_iota(jnp.int32, shape, 0)
    return (column >= starts) & (column <= row)


def rows_dot(left, right):
    return lax.dot_general(left, right, (((1,), (1,)), ((), ())), preferred_element_type=F32)


def stand(row):
    return jnp.transpose(jnp.broadcast_to(row, (row.shape[1], row.shape[1])))


def lie(column):
    return jnp.transpose(jnp.broadcast_to(column, (column.shape[0], column.shape[0])))[0:1]


def put_stats(stats_ref, tile, column):
    stats_ref[tile, 0:1, :] = lie(column[:128])
    stats_ref[tile, 1:2, :] = lie(column[128:])


BLOCK = 256


def attend_sequence(core, seq, most, projected, fixed_refs, mixed, saved_refs, between):
    starts_ref, cosine_ref, sine_ref, query_gain_ref, key_gain_ref = fixed_refs
    query_ref, key_ref, value_ref, log_ref = saved_refs
    rows = projected.shape[1]
    length = query_ref.shape[1]
    depth = key_ref.shape[2]
    heads = query_ref.shape[2] // depth
    scale = depth ** (-0.5)
    for half in range(2):
        place = 2 * lax.rem(core + half, 2) + seq
        for at in range(half * rows, (half + 1) * rows, BLOCK):
            inner = at - half * rows
            cosine = cosine_ref[seq, at : at + BLOCK, :]
            sine = sine_ref[seq, at : at + BLOCK, :]
            for head in range(heads + 2):
                lane = slice(head * depth, (head + 1) * depth)
                value = projected[place, inner : inner + BLOCK, lane]
                if head < heads:
                    normed = value * head_scale(value) * query_gain_ref[...]
                    query_ref[seq, at : at + BLOCK, lane] = spin(normed, cosine, sine).astype(B16)
                elif head == heads:
                    normed = value * head_scale(value) * key_gain_ref[...]
                    key_ref[seq, at : at + BLOCK, :] = spin(normed, cosine, sine).astype(B16)
                else:
                    value_ref[seq, at : at + BLOCK, :] = value.astype(B16)
    for first in range(0, length, BLOCK):
        between(first // BLOCK)
        low, high = window(first, BLOCK, most)
        mask = kept(first, BLOCK, low, high, starts_ref[seq, first : first + BLOCK, :])
        half, inner = divmod(first, rows)
        place = 2 * lax.rem(core + half, 2) + seq
        for head in range(heads):
            lane = slice(head * depth, (head + 1) * depth)
            query = query_ref[seq, first : first + BLOCK, lane]
            scores = rows_dot(query, key_ref[seq, low:high, :]) * scale
            scores = jnp.where(mask, scores, NEG)
            top = jnp.max(scores, axis=1, keepdims=True)
            weights = jnp.exp(scores - top)
            total = jnp.sum(weights, axis=1, keepdims=True)
            probs = (weights * (1.0 / total)).astype(B16)
            out = jnp.dot(probs, value_ref[seq, low:high, :], preferred_element_type=F32)
            mixed[place, inner : inner + BLOCK, lane] = out.astype(B16)
            log_ref[seq, head, first : first + BLOCK, :] = top + jnp.log(total)


def attend_sequence_back(
    core, seq, most, projected, upstream, fixed_refs, saved_refs, result, stats, gains, accs
):
    starts_ref, cosine_ref, sine_ref, query_gain_ref, key_gain_ref = fixed_refs
    query_ref, key_ref, value_ref, log_ref = saved_refs
    query_acc, key_acc, value_acc = accs
    rows = projected.shape[1]
    length = query_ref.shape[1]
    depth = key_ref.shape[2]
    heads = query_ref.shape[2] // depth
    scale = depth ** (-0.5)
    key_acc[...] = jnp.zeros_like(key_acc)
    value_acc[...] = jnp.zeros_like(value_acc)
    for first in range(0, length, BLOCK):
        low, high = window(first, BLOCK, most)
        mask = kept(first, BLOCK, low, high, starts_ref[seq, first : first + BLOCK, :])
        half, inner = divmod(first, rows)
        place = 2 * lax.rem(core + half, 2) + seq
        keys = key_ref[seq, low:high, :]
        values = value_ref[seq, low:high, :]
        for head in range(heads):
            lane = slice(head * depth, (head + 1) * depth)
            query = query_ref[seq, first : first + BLOCK, lane]
            grad = upstream[place, inner : inner + BLOCK, lane]
            scores = rows_dot(query, keys) * scale - log_ref[seq, head, first : first + BLOCK, :]
            probs = jnp.exp(jnp.where(mask, scores, NEG))
            prob_grad = rows_dot(grad, values)
            delta = jnp.sum(probs * prob_grad, axis=1, keepdims=True)
            score_grad = (probs * (prob_grad - delta)).astype(B16)
            query_acc[first : first + BLOCK, lane] = (
                jnp.dot(score_grad, keys, preferred_element_type=F32) * scale
            )
            key_acc[low:high, :] += weight_grad(score_grad, query) * scale
            value_acc[low:high, :] += weight_grad(probs.astype(B16), grad)
    query_total = jnp.zeros((1, depth), F32)
    key_total = jnp.zeros((1, depth), F32)
    for half in range(2):
        block = 2 * lax.rem(core + half, 2) + seq
        for at in range(half * rows, (half + 1) * rows, BLOCK):
            inner = at - half * rows
            cosine = cosine_ref[seq, at : at + BLOCK, :]
            sine = sine_ref[seq, at : at + BLOCK, :]
            total = jnp.zeros((BLOCK, 1), F32)
            for head in range(heads + 2):
                lane = slice(head * depth, (head + 1) * depth)
                value = projected[block, inner : inner + BLOCK, lane]
                if head == heads + 1:
                    back = value_acc[at : at + BLOCK, :].astype(B16)
                else:
                    if head < heads:
                        grad = query_acc[at : at + BLOCK, lane]
                        gain = query_gain_ref[...]
                    else:
                        grad = key_acc[at : at + BLOCK, :]
                        gain = key_gain_ref[...]
                    grad = spin_back(grad, cosine, sine)
                    rate = head_scale(value)
                    scaled = value * rate
                    share = jnp.sum(grad * scaled, axis=0, keepdims=True)
                    if head < heads:
                        query_total += share
                    else:
                        key_total += share
                    middle = jnp.mean(gain * grad * scaled, axis=1, keepdims=True)
                    back = (rate * (gain * grad - scaled * middle)).astype(B16)
                result[block, inner : inner + BLOCK, lane] = back
                total += jnp.sum(back.astype(F32) * value, axis=1, keepdims=True)
            put_stats(stats, 2 * block + inner // BLOCK, total)
    gains[seq, 0:1, :] = query_total
    gains[seq, 1:2, :] = key_total


def neighbours():
    spot = lax.axis_index("tx")
    core = lax.rem(spot, 2)
    return (
        {"ty": 1 - lax.axis_index("ty")},
        {"tx": lax.rem(spot + 2, 4)},
        {"tx": spot + 1 - 2 * core},
    )


def planes():
    plane = lax.axis_index("dp")
    return {"dp": plane + 1 - 2 * lax.rem(plane, 2)}, {"dp": 3 - plane}


def inner():
    plane = lax.axis_index("dp")
    return (plane == 1) | (plane == 2)


def greet(targets):
    barrier = pltpu.get_barrier_semaphore()
    for target in targets:
        pl.semaphore_signal(barrier, inc=1, device_id=target, device_id_type=MESH)
    pl.semaphore_wait(barrier, len(targets))


class Wires:
    def __init__(self, send_sems, recv_sems):
        self.send_sems = send_sems
        self.recv_sems = recv_sems

    def copy(self, kind, chunk, source, target, device):
        return pltpu.make_async_remote_copy(
            src_ref=source,
            dst_ref=target,
            send_sem=self.send_sems.at[kind, chunk],
            recv_sem=self.recv_sems.at[kind, chunk],
            device_id=device,
            device_id_type=MESH,
        )


CHUNK = 256
SIBLING, CORNER, FINAL_X, FINAL_Y = 0, 1, 2, 3
REDUCE_KINDS = 5
OUT_X, OUT_Y, OUT_CORNER, CORE_OWN, CORE_X, CORE_Y, CORE_CORNER = range(7)
GATHER_KINDS = 7
SHARE_X, SHARE_NEAR, SHARE_MIDDLE = 0, 1, 2
SHARE_KINDS = 3


def lanes(chunk, half, width):
    return pl.ds(pl.multiple_of(half * width + chunk * CHUNK, CHUNK), CHUNK)


class Gather:
    def __init__(self, wires, base, whole, own, local_sem, most=4):
        self.wires, self.base, self.whole, self.own, self.local_sem = (
            wires,
            base,
            whole,
            own,
            local_sem,
        )
        self.most = most
        self.width = whole.shape[2] // 2
        self.count = self.width // CHUNK

    def place(self, block, chunk, half):
        return self.whole.at[block, :, lanes(chunk, half, self.width)]

    def copy(self, name, chunk):
        side, across, core = neighbours()
        at = self.place
        own = self.own.at[chunk]
        if name == "local":
            return pltpu.make_async_copy(own, at(0, chunk, 0), self.local_sem.at[chunk])
        kind, source, target, device = {
            "x": (OUT_X, own, at(0, chunk, 1), side),
            "y": (OUT_Y, own, at(1, chunk, 0), across),
            "core": (CORE_OWN, own, at(2, chunk, 0), core),
            "even": (OUT_CORNER, at(0, chunk, 1), at(1, chunk, 1), across),
            "odd": (OUT_CORNER, at(1, chunk, 0), at(1, chunk, 1), side),
            "core_x": (CORE_X, at(0, chunk, 1), at(2, chunk, 1), core),
            "core_y": (CORE_Y, at(1, chunk, 0), at(3, chunk, 0), core),
            "core_corner": (CORE_CORNER, at(1, chunk, 1), at(3, chunk, 1), core),
        }[name]
        return self.wires.copy(self.base + kind, chunk, source, target, device)

    def send(self, chunk):
        for name in ("x", "y", "core", "local"):
            self.copy(name, chunk).start()

    def relay(self, low=0, high=None):
        @pl.loop(low, self.count if high is None else high)
        def _(chunk):
            even = (lax.rem(chunk, 2) == 0) | (chunk >= self.most)
            self.copy("x", chunk).wait_recv()

            @pl.when(even)
            def _():
                self.copy("even", chunk).start()

            self.copy("core_x", chunk).start()
            self.copy("y", chunk).wait_recv()

            @pl.when(jnp.logical_not(even))
            def _():
                self.copy("odd", chunk).start()

            self.copy("core_y", chunk).start()

    def close(self):
        @pl.loop(0, self.count)
        def _(chunk):
            self.copy("even", chunk).wait_recv()
            self.copy("core_corner", chunk).start()

        @pl.loop(0, self.count)
        def _(chunk):
            for name in ("core", "core_x", "core_y", "core_corner"):
                self.copy(name, chunk).wait_recv()
            for name in ("x", "y", "core", "even", "core_x", "core_y", "core_corner"):
                self.copy(name, chunk).wait_send()
            self.copy("local", chunk).wait()


class Share:
    def __init__(self, wires, base, sources, whole, by_rows, local_sems, held=None):
        self.wires, self.base, self.sources, self.whole, self.by_rows, self.local_sems = (
            wires,
            base,
            sources,
            whole,
            by_rows,
            local_sems,
        )
        self.held = held or sources
        self.size = (whole.shape[0] // 2 if by_rows else whole.shape[0]) // 4

    def quarter(self, plane):
        start = plane * self.size
        if self.by_rows:
            rows = pl.ds(pl.multiple_of(self.whole.shape[0] // 2 + start, self.size), self.size)
            return self.whole.at[rows]
        width = self.whole.shape[1] // 2
        return self.whole.at[pl.ds(pl.multiple_of(start, self.size), self.size), width:]

    def cross(self, index):
        side, _, _ = neighbours()
        plane = lax.axis_index("dp")
        other = 1 - lax.axis_index("ty")
        source = self.sources[index]
        if self.by_rows:
            rows = pl.ds(pl.multiple_of(plane * self.size, self.size), self.size)
            columns = source.shape[1] // 2
            part = source.at[rows, pl.ds(pl.multiple_of(other * columns, columns), columns)]
            offset = sum(item.shape[1] // 2 for item in self.sources[:index])
            target = self.quarter(plane).at[:, offset : offset + columns]
        else:
            start = pl.multiple_of(other * (source.shape[0] // 2) + plane * self.size, self.size)
            part = source.at[pl.ds(start, self.size)]
            target = self.quarter(plane)
        return self.wires.copy(self.base + SHARE_X, index, part, target, side)

    def local(self, index):
        mine = lax.axis_index("ty")
        source = self.held[index]
        if self.by_rows:
            columns = source.shape[1] // 2
            offset = sum(item.shape[1] // 2 for item in self.sources[:index])
            part = source.at[:, pl.ds(pl.multiple_of(mine * columns, columns), columns)]
            target = self.whole.at[: self.whole.shape[0] // 2, offset : offset + columns]
        else:
            half = source.shape[0] // 2
            part = source.at[pl.ds(pl.multiple_of(mine * half, half), half)]
            target = self.whole.at[:, : self.whole.shape[1] // 2]
        return pltpu.make_async_copy(part, target, self.local_sems.at[index])

    def piece_of(self, owner):
        place = self.quarter(owner)
        return place, place

    def over(self, near, index):
        beside, mirror = planes()
        plane = lax.axis_index("dp")
        other = 3 - plane
        if near:
            owner = (plane, other, other + 1 - 2 * lax.rem(other, 2))[index]
        else:
            owner = (plane, plane + 1 - 2 * lax.rem(plane, 2))[index]
        source, target = self.piece_of(owner) if index else self.own_piece()
        return self.wires.copy(
            self.base + (SHARE_NEAR if near else SHARE_MIDDLE),
            index,
            source,
            target,
            beside if near else mirror,
        )

    def own_piece(self):
        return self.piece_of(lax.axis_index("dp"))

    def start(self):
        for index in range(len(self.sources)):
            self.cross(index).start()
            self.local(index).start()

    def send_own(self):
        self.over(True, 0).start()

        @pl.when(inner())
        def _():
            self.over(False, 0).start()

    def middle(self):
        for index in range(len(self.sources)):
            self.cross(index).wait_recv()
        self.send_own()

    def late(self):
        @pl.when(inner())
        def _():
            self.over(True, 0).wait_recv()
            self.over(False, 1).start()
            self.over(False, 0).wait_recv()
            self.over(True, 1).start()

    def later(self):
        @pl.when(inner())
        def _():
            self.over(False, 1).wait_recv()
            self.over(True, 2).start()

    def close_planes(self):
        self.over(True, 0).wait_send()

        @pl.when(inner())
        def _():
            self.over(True, 1).wait_send()
            self.over(True, 2).wait_send()
            self.over(False, 0).wait_send()
            self.over(False, 1).wait_send()

        @pl.when(jnp.logical_not(inner()))
        def _():
            for index in range(3):
                self.over(True, index).wait_recv()

    def close(self):
        self.close_planes()
        for index in range(len(self.sources)):
            self.cross(index).wait_send()
            self.local(index).wait()


class Spread(Share):
    def __init__(self, wires, base, source, whole, local_sems, quarter):
        super().__init__(wires, base, (source,), whole, True, local_sems)
        self.piece = quarter

    def own_piece(self):
        return self.piece, self.quarter(lax.axis_index("dp"))

    def own(self):
        return pltpu.make_async_copy(
            self.piece, self.quarter(lax.axis_index("dp")), self.local_sems.at[1]
        )

    def start(self):
        self.send_own()
        self.local(0).start()
        self.own().start()

    def close(self):
        self.close_planes()
        self.local(0).wait()
        self.own().wait()


FOLD_END, FOLD_MIDDLE, FOLD_BACK, FOLD_X = 0, 2, 4, 5
FOLD_KINDS = 6


def side():
    return lax.div(lax.axis_index("dp"), 2)


def turn_shard(turn):
    return 3 * (1 - side()) + turn * (2 * side() - 1)


class Fold:
    def __init__(self, wires, base, tiles, bufs, mine, theirs, first=None):
        self.wires, self.base, self.tiles, self.mine, self.theirs = (
            wires,
            base,
            tiles,
            mine,
            theirs,
        )
        self.first = tiles if first is None else first
        (self.recv,) = bufs
        self.near, self.mirror = planes()

    def send(self, kind, half, slot, source, target, device):
        target = self.recv.at[2 * target + half]
        return self.wires.copy(self.base + kind, slot, source, target, device)

    def end(self, half, turn):
        source = self.first.at[4 * half + turn_shard(turn)]
        return self.send(FOLD_END + half, half, turn, source, turn, self.near)

    def across(self, half, turn):
        source = self.recv.at[2 * turn + half]
        return self.send(FOLD_MIDDLE + half, half, turn, source, 3 + turn, self.mirror)

    def back(self, half):
        return self.send(FOLD_BACK, half, half, self.recv.at[6 + half], 0, self.near)

    def cross(self):
        source = self.tiles.at[4 + lax.axis_index("dp")]
        return self.wires.copy(self.base + FOLD_X, 0, source, self.theirs, neighbours()[0])

    def add(self, slot, half, shard):
        self.recv[2 * slot + half] = (
            self.recv[2 * slot + half].astype(F32) + self.tiles[4 * half + shard].astype(F32)
        ).astype(B16)

    def begin(self, turn, half):
        @pl.when(jnp.logical_not(inner()))
        def _():
            self.end(half, turn).start()

    def start(self):
        for turn in range(3):
            for half in (1, 0):
                self.begin(turn, half)

    def pass_on(self, turn):
        @pl.when(inner())
        def _():
            for half in (1, 0):
                self.end(half, turn).wait_recv()
                self.add(turn, half, turn_shard(turn))
                self.across(half, turn).start()

    def step(self):
        self.pass_on(0)

    def middle(self):
        self.pass_on(1)

        @pl.when(inner())
        def _():
            for half in (1, 0):
                self.across(half, 0).wait_recv()
                self.add(3, half, 3 * side())
                self.back(half).start()

    def late(self):
        plane = lax.axis_index("dp")
        for half in (1, 0):

            @pl.when(inner())
            def _():
                self.end(half, 2).wait_recv()
                self.across(half, 1).wait_recv()
                self.add(2, half, plane)

            @pl.when(jnp.logical_not(inner()))
            def _():
                self.back(half).wait_recv()

            at = 4 * half + plane
            middle = inner().astype(jnp.int32)
            total = self.recv[4 * middle + half].astype(F32)
            other = jnp.where(
                inner(), self.recv[8 * middle + half].astype(F32), self.tiles[at].astype(F32)
            )
            total = total + other
            if half == 1:
                self.tiles[at] = total.astype(B16)
                self.cross().start()
            else:
                self.mine[...] = total

    def close(self):
        self.cross().wait_recv()

        @pl.when(inner())
        def _():
            for half in range(2):
                self.across(half, 0).wait_send()
                self.across(half, 1).wait_send()
                self.back(half).wait_send()

        @pl.when(jnp.logical_not(inner()))
        def _():
            for half in range(2):
                for turn in range(3):
                    self.end(half, turn).wait_send()

        self.cross().wait_send()


def fold_scratch(rows, columns):
    return [pltpu.VMEM((10, rows, columns), B16)]


def turn_tile(step):
    return 4 * (1 - lax.rem(step, 2)) + turn_shard(lax.div(step, 2))


def make_tiles(fold, make, low, high):
    @pl.loop(low, high)
    def _(step):
        make(step)

        @pl.when(step < 6)
        def _():
            half = 1 - lax.rem(step, 2)
            turn = lax.div(step, 2)
            for side_half in range(2):

                @pl.when(half == side_half)
                def _():
                    fold.begin(turn, side_half)


class Reduce:
    def __init__(self, wires, rows_ref, weight_ref, transposed, bufs):
        self.wires, self.rows_ref, self.weight_ref, self.transposed = (
            wires,
            rows_ref,
            weight_ref,
            transposed,
        )
        (
            self.sibling_send,
            self.sibling_recv,
            self.kept_ref,
            self.out,
            self.corner_recv,
            self.x_recv,
            self.y_recv,
        ) = bufs
        self.rows = rows_ref.shape[1]
        self.width = (weight_ref.shape[0] if transposed else weight_ref.shape[1]) // 2
        self.count = self.width // CHUNK

    def product(self, block, chunk, half):
        left = self.rows_ref[block : block + 2].reshape(2 * self.rows, self.rows_ref.shape[2])
        at = lanes(chunk, half, self.width)
        if self.transposed:
            return rows_dot(left, self.weight_ref[at, :])
        return jnp.dot(left, self.weight_ref[:, at], preferred_element_type=F32)

    def sibling(self, chunk, half):
        return self.wires.copy(
            SIBLING + half * (REDUCE_KINDS - 1),
            chunk,
            self.sibling_send.at[lax.rem(chunk, 2), half],
            self.sibling_recv.at[chunk, half],
            neighbours()[2],
        )

    def corner(self, chunk, device):
        return self.wires.copy(
            CORNER, chunk, self.out.at[2, chunk], self.corner_recv.at[chunk], device
        )

    def final_x(self, chunk):
        return self.wires.copy(
            FINAL_X, chunk, self.out.at[0, chunk], self.x_recv.at[chunk], neighbours()[0]
        )

    def final_y(self, chunk):
        return self.wires.copy(
            FINAL_Y, chunk, self.out.at[1, chunk], self.y_recv.at[chunk], neighbours()[1]
        )

    def give(self, chunk):
        @pl.loop(0, 2)
        def _(turn):
            half = 1 - turn
            self.sibling_send[lax.rem(chunk, 2), half] = self.product(2, chunk, half).astype(B16)
            self.sibling(chunk, half).start()

    def take(self, chunk):
        rows = self.rows
        even = lax.rem(chunk, 2) == 0
        side, across, _ = neighbours()

        @pl.loop(0, 2)
        def _(turn):
            half = 1 - turn
            own = self.product(0, chunk, half)
            self.sibling(chunk, half).wait_recv()
            total = own + self.sibling_recv[chunk, half].astype(F32)

            @pl.when(half == 1)
            def _():
                self.out[2, chunk] = total[rows:].astype(B16)
                self.out[0, chunk] = total[:rows].astype(B16)

                @pl.when(even)
                def _():
                    self.corner(chunk, side).start()
                    self.final_x(chunk).start()

                @pl.when(jnp.logical_not(even))
                def _():
                    self.corner(chunk, across).start()

            @pl.when(half == 0)
            def _():
                self.kept_ref[chunk] = total[:rows]
                self.out[1, chunk] = total[rows:].astype(B16)

                @pl.when(jnp.logical_not(even))
                def _():
                    self.final_y(chunk).start()

    def start(self, between=(lambda: None, lambda: None)):
        self.give(0)
        self.rest(between)

    def rest(self, between):
        self.take(0)
        self.give(1)
        self.take(1)
        between[0]()

        @pl.loop(2, self.count)
        def _(chunk):
            for half in range(2):
                self.sibling(chunk - 2, half).wait_send()
            self.give(chunk)
            self.take(chunk)
            self.middle(chunk - 2, chunk - 1)

        between[1]()

    def middle(self, low=None, high=None):
        @pl.loop(self.count - 2 if low is None else low, self.count if high is None else high)
        def _(chunk):
            even = lax.rem(chunk, 2) == 0
            self.corner(chunk, neighbours()[0]).wait_recv()
            came = self.corner_recv[chunk].astype(F32)

            @pl.when(even)
            def _():
                self.out[1, chunk] = (self.out[1, chunk].astype(F32) + came).astype(B16)
                self.final_y(chunk).start()

            @pl.when(jnp.logical_not(even))
            def _():
                self.out[0, chunk] = (self.out[0, chunk].astype(F32) + came).astype(B16)
                self.final_x(chunk).start()

    def total(self, chunk):
        self.final_x(chunk).wait_recv()
        self.final_y(chunk).wait_recv()
        return (
            self.kept_ref[chunk] + self.x_recv[chunk].astype(F32) + self.y_recv[chunk].astype(F32)
        )

    def close(self):
        @pl.loop(self.count - 2, self.count)
        def _(chunk):
            for half in range(2):
                self.sibling(chunk, half).wait_send()

        @pl.loop(0, self.count)
        def _(chunk):
            self.corner(chunk, neighbours()[0]).wait_send()
            self.final_x(chunk).wait_send()
            self.final_y(chunk).wait_send()


def reduce_scratch(rows, width):
    count = width // CHUNK
    return [
        pltpu.VMEM((2, 2, 2 * rows, CHUNK), B16),
        pltpu.VMEM((count, 2, 2 * rows, CHUNK), B16),
        pltpu.VMEM((count, rows, CHUNK), F32),
        pltpu.VMEM((3, count, rows, CHUNK), B16),
        pltpu.VMEM((count, rows, CHUNK), B16),
        pltpu.VMEM((count, rows, CHUNK), B16),
        pltpu.VMEM((count, rows, CHUNK), B16),
    ]


def gather_scratch(rows, width):
    count = width // CHUNK
    return [pltpu.VMEM((count, rows, CHUNK), B16), pltpu.SemaphoreType.DMA((count,))]


def wire_scratch(kinds, count):
    return [pltpu.SemaphoreType.DMA((kinds, count))] * 2


IN_VMEM = pl.BlockSpec(memory_space=pltpu.VMEM)
IN_ANY = pl.BlockSpec(memory_space=pl.ANY)
VMEM_MOST = 60 * 1024 * 1024


def remote_params(number):
    return pltpu.CompilerParams(
        collective_id=number, has_side_effects=True, vmem_limit_bytes=VMEM_MOST
    )


def cost(flops, size):
    return pl.CostEstimate(flops=flops, bytes_accessed=size, transcendentals=0)


def shape(dims, kind=B16):
    return jax.ShapeDtypeStruct(dims, kind)


def cut(own, block_ref):
    for chunk in range(own.shape[0]):
        own[chunk] = block_ref[:, chunk * CHUNK : (chunk + 1) * CHUNK]


def open_kernel(
    tokens_ref,
    query_ref,
    key_ref,
    value_ref,
    out_ref,
    attn_ref,
    mlp_ref,
    seg_ref,
    rate_ref,
    attn_all_ref,
    mlp_all_ref,
    starts_ref,
    cosine_ref,
    sine_ref,
    whole_ref,
    project_ref,
    branch_ref,
    *scratch,
):
    own, gather_sem, send_sems, recv_sems, project_sem, branch_sem = scratch[:6]
    attn_recv, mlp_recv, seg_recv, seg_all = scratch[6:]
    width = attn_ref.shape[1]
    length = seg_ref.shape[1]
    cut(own, tokens_ref)
    greet(neighbours() + planes())
    wires = Wires(send_sems, recv_sems)
    gather = Gather(wires, 0, whole_ref, own, gather_sem, 2)
    base = GATHER_KINDS + 2 * SHARE_KINDS
    side = neighbours()[0]
    small = [
        wires.copy(base, index, source, target, side)
        for index, (source, target) in enumerate(
            ((attn_ref, attn_recv), (mlp_ref, mlp_recv), (seg_ref, seg_recv))
        )
    ]
    shares = [
        Share(wires, GATHER_KINDS, (query_ref, key_ref, value_ref), project_ref, True, project_sem),
        Share(wires, GATHER_KINDS + SHARE_KINDS, (out_ref,), branch_ref, False, branch_sem),
    ]
    for copy in small:
        copy.start()
    shares[0].start()
    shares[1].start()

    @pl.loop(0, gather.count)
    def _(chunk):
        gather.send(chunk)

    for copy in small:
        copy.wait()
    attn_all_ref[:, :width] = attn_ref[...]
    attn_all_ref[:, width:] = attn_recv[...]
    mlp_all_ref[:, :width] = mlp_ref[...]
    mlp_all_ref[:, width:] = mlp_recv[...]
    mine = lax.rem(lax.axis_index("ty") + lax.div(lax.axis_index("tx"), 2), 2)
    seg_all[pl.ds(mine, 1)] = seg_ref[...].astype(F32)[None]
    seg_all[pl.ds(1 - mine, 1)] = seg_recv[...].astype(F32)[None]

    shares[0].middle()
    shares[1].middle()

    def between(seq, piece):
        @pl.when(seq == 0)
        def _():
            if piece == 4:
                gather.relay(0, 1)
            elif piece == 6:
                shares[0].late()
                shares[1].late()

        @pl.when(seq == 1)
        def _():
            if piece == 0:
                gather.relay(1, 2)
            elif piece == 2:
                shares[0].later()
                shares[1].later()
            elif piece == 3:
                gather.relay(2, 3)
            elif piece == 6:
                gather.relay(3, 4)

    @pl.loop(0, 2)
    def _(seq):
        for low in range(0, length, 128):
            between(seq, low // 128)
            here = stand(seg_all[seq, :, low : low + 128])
            before = jnp.zeros((128, 128), F32)
            for other in range(0, length, 128):
                before += (seg_all[seq, :, other : other + 128] < here).astype(F32)
            start = jnp.sum(before, axis=1, keepdims=True)
            at = slice(low, low + 128)
            starts_ref[seq, at, :] = start.astype(jnp.int32)
            row = lax.broadcasted_iota(jnp.int32, (128, 128), 0) + low
            lane = lax.broadcasted_iota(jnp.int32, (128, 128), 1)
            angle = (row.astype(F32) - start) * rate_ref[...]
            cosine_ref[seq, at, :] = jnp.cos(angle)
            sine = jnp.sin(angle)
            sine_ref[seq, at, :] = jnp.where(lane < 64, -sine, sine)

    gather.close()
    shares[0].close()
    shares[1].close()


def open_call(tokens, w_query, w_key, w_value, w_out, attn_gain, mlp_gain, seg_ids, rate, number):
    rows, width = tokens.shape
    columns = (w_query.shape[1] + w_key.shape[1] + w_value.shape[1]) // 2
    length = seg_ids.shape[1]
    return pl.pallas_call(
        open_kernel,
        out_shape=(
            shape((1, 2 * width), F32),
            shape((1, 2 * width), F32),
            shape((2, length, 1), jnp.int32),
            shape((2, length, 128), F32),
            shape((2, length, 128), F32),
            shape((4, rows, 2 * width)),
            shape((2 * width, columns)),
            shape((w_out.shape[0] // 2, 2 * width)),
        ),
        in_specs=[IN_VMEM] * 9,
        out_specs=(IN_VMEM,) * 5 + (IN_ANY,) * 3,
        scratch_shapes=gather_scratch(rows, width)
        + wire_scratch(GATHER_KINDS + 2 * SHARE_KINDS + 1, width // CHUNK)
        + [
            pltpu.SemaphoreType.DMA((3,)),
            pltpu.SemaphoreType.DMA((1,)),
            pltpu.VMEM((1, width), F32),
            pltpu.VMEM((1, width), F32),
            pltpu.VMEM((1, length), jnp.int32),
            pltpu.VMEM((2, 1, length), F32),
        ],
        compiler_params=remote_params(number),
        cost_estimate=cost(0, 32 * rows * width),
    )(tokens, w_query, w_key, w_value, w_out, attn_gain, mlp_gain, seg_ids, rate)


def front_kernel(
    most,
    whole_ref,
    project_ref,
    gain_ref,
    query_gain_ref,
    key_gain_ref,
    grad_ref,
    starts_in_ref,
    cosine_in_ref,
    sine_in_ref,
    down_in_ref,
    gate_in_ref,
    first_ref,
    projected_out_ref,
    scale_ref,
    mixed_ref,
    query_ref,
    key_ref,
    value_ref,
    log_ref,
    grad_whole_ref,
    back_ref,
    gate_ref,
    *scratch,
):
    own, gather_sem, send_sems, recv_sems, back_sem, tokens, firsts, tile_sem = scratch[:8]
    down_ref, starts_ref, cosine_ref, sine_ref = scratch[8:12]
    loads = Loads(
        (down_in_ref, starts_in_ref, cosine_in_ref, sine_in_ref), scratch[8:12], scratch[12]
    )
    projected_ref, projected_sem = scratch[13:]
    keep = pltpu.make_async_copy(projected_ref, projected_out_ref, projected_sem)
    core = lax.rem(lax.axis_index("tx"), 2)
    cut(own, grad_ref)
    rows = whole_ref.shape[1]

    def spot(ref, tile):
        at = pl.ds(pl.multiple_of(lax.rem(tile, rows // BLOCK) * BLOCK, BLOCK), BLOCK)
        return ref.at[lax.div(tile, rows // BLOCK), at, :]

    def fetch(tile):
        slot = lax.rem(tile, 2)
        return pltpu.make_async_copy(spot(whole_ref, tile), tokens.at[slot], tile_sem.at[0, slot])

    def store(tile):
        slot = lax.rem(tile, 2)
        return pltpu.make_async_copy(firsts.at[slot], spot(first_ref, tile), tile_sem.at[1, slot])

    fetch(0).start()
    loads.start()
    greet(neighbours() + planes())
    wires = Wires(send_sems, recv_sems)
    gather = Gather(wires, 0, grad_whole_ref, own, gather_sem, 0)
    back = Share(wires, GATHER_KINDS, (down_in_ref,), back_ref, False, back_sem, (down_ref,))
    size, columns = gate_ref.shape
    gate = wires.copy(
        GATHER_KINDS + SHARE_KINDS,
        0,
        gate_in_ref.at[
            pl.ds(pl.multiple_of(lax.axis_index("dp") * size, size), size),
            pl.ds(pl.multiple_of((1 - lax.axis_index("ty")) * columns, columns), columns),
        ],
        gate_ref,
        neighbours()[0],
    )
    back.cross(0).start()

    @pl.loop(0, gather.count)
    def _(chunk):
        gather.send(chunk)

    gate.start()

    loads.wait(0, 1)
    back.local(0).start()
    count = 4 * rows // BLOCK

    @pl.loop(0, count)
    def _(tile):
        slot = lax.rem(tile, 2)
        block = lax.div(tile, rows // BLOCK)
        at = pl.ds(pl.multiple_of(lax.rem(tile, rows // BLOCK) * BLOCK, BLOCK), BLOCK)

        @pl.when(tile < count - 1)
        def _():
            fetch(tile + 1).start()

        fetch(tile).wait()

        @pl.when(tile >= 2)
        def _():
            store(tile - 2).wait()

        value = tokens[slot].astype(F32)
        scale = lax.rsqrt(jnp.mean(value * value, axis=1, keepdims=True) + EPS)
        first = (value * scale * gain_ref[...]).astype(B16)
        firsts[slot] = first
        store(tile).start()
        projected_ref[block, at, :] = jnp.dot(
            first, project_ref[...], preferred_element_type=F32
        )

        @pl.when(block == 0)
        def _():
            scale_ref[at, :] = jnp.broadcast_to(scale, (BLOCK, 128))

        @pl.when(tile == count // 2)
        def _():
            back.middle()

    keep.start()
    loads.wait(1, 4)
    fixed_refs = (starts_ref, cosine_ref, sine_ref, query_gain_ref, key_gain_ref)
    saved_refs = (query_ref, key_ref, value_ref, log_ref)

    @pl.loop(0, 2)
    def _(seq):
        def between(turn):
            @pl.when(seq == 0)
            def _():
                if turn == 0:
                    gather.relay(0, 1)
                elif turn == 1:
                    back.late()
                elif turn == 2:
                    gather.relay(1, 2)
                else:
                    back.later()

            @pl.when(seq == 1)
            def _():
                if turn < 2:
                    gather.relay(turn + 2, turn + 3)

        attend_sequence(
            core, seq, most, projected_ref, fixed_refs, mixed_ref, saved_refs, between
        )

    for tile in range(count - 2, count):
        store(tile).wait()
    gather.close()
    back.close()
    gate.wait()
    keep.wait()


def front_call(whole, w_project, gain, fixed_args, most, cotangent, w_down, w_gate, number):
    starts, cosine, sine, query_gain, key_gain = fixed_args
    rows, width = cotangent.shape
    length = cosine.shape[1]
    depth = query_gain.shape[1]
    columns = w_project.shape[1]
    heads = columns // depth - 2
    outs = (
        shape((4, rows, 2 * width)),
        shape((4, rows, columns), F32),
        shape((rows, 128), F32),
        shape((4, rows, heads * depth)),
        shape((2, length, heads * depth)),
        shape((2, length, depth)),
        shape((2, length, depth)),
        shape((2, heads, length, 1), F32),
        shape((4, rows, 2 * width)),
        shape((w_down.shape[0] // 2, 2 * width)),
        shape((width // 4, w_gate.shape[1] // 2)),
    )
    return pl.pallas_call(
        lambda *refs: front_kernel(most, *refs),
        out_shape=outs,
        in_specs=[IN_ANY] + [IN_VMEM] * 5 + [IN_ANY] * 5,
        out_specs=[IN_ANY] * 2 + [IN_VMEM] * 6 + [IN_ANY] * 3,
        scratch_shapes=gather_scratch(rows, width)
        + wire_scratch(GATHER_KINDS + SHARE_KINDS + 1, width // CHUNK)
        + [
            pltpu.SemaphoreType.DMA((1,)),
            pltpu.VMEM((2, BLOCK, 2 * width), B16),
            pltpu.VMEM((2, BLOCK, 2 * width), B16),
            pltpu.SemaphoreType.DMA((2, 2)),
        ]
        + load_scratch((w_down, starts, cosine, sine))
        + [pltpu.VMEM((4, rows, columns), F32), pltpu.SemaphoreType.DMA],
        compiler_params=remote_params(number),
        cost_estimate=cost(16 * rows * width * columns, 64 * rows * width),
    )(whole, w_project, gain, query_gain, key_gain, cotangent, starts, cosine, sine, w_down, w_gate)


def branch_kernel(
    rows_in_ref,
    weight_in_ref,
    input_in_ref,
    up_in_ref,
    gate_in_ref,
    quarter_ref,
    residual_ref,
    whole_ref,
    up_ref,
    gate_ref,
    *scratch,
):
    bufs = scratch[:7]
    own, gather_sem, send_sems, recv_sems, up_sem = scratch[7:12]
    held, load_sem, gate_sem = scratch[12:17], scratch[17], scratch[18]
    rows_ref, weight_ref, input_ref, up_held, gate_held = held
    loads = Loads(
        (rows_in_ref, weight_in_ref, input_in_ref, up_in_ref, gate_in_ref), held, load_sem
    )
    loads.start()
    width = input_ref.shape[1]
    greet(neighbours() + planes())
    wires = Wires(send_sems, recv_sems)
    reduce = Reduce(wires, rows_ref, weight_ref, False, bufs)
    gather = Gather(wires, REDUCE_KINDS, whole_ref, own, gather_sem, 2)
    up = Share(
        wires, REDUCE_KINDS + GATHER_KINDS, (up_in_ref,), up_ref, True, up_sem, (up_held,)
    )
    gate = Spread(
        wires,
        REDUCE_KINDS + GATHER_KINDS + SHARE_KINDS,
        gate_held,
        gate_ref,
        gate_sem,
        quarter_ref,
    )
    loads.wait(0, 2)

    def between():
        loads.wait(2, 5)
        up.start()
        gate.start()

    reduce.start((between, gate.late))
    up.middle()
    reduce.middle()
    gate.later()

    @pl.loop(0, width // CHUNK)
    def _(chunk):
        at = lanes(chunk, 0, width)
        residual = input_ref[:, at].astype(F32) + reduce.total(chunk)
        residual_ref[:, at] = residual
        own[chunk] = residual.astype(B16)
        gather.send(chunk)

    up.late()
    gather.relay()
    up.later()
    gather.close()
    up.close()
    gate.close()
    reduce.close()


def branch_call(rows, weight, inputs, w_up, w_gate, quarter, number):
    height, width = inputs.shape
    count = width // CHUNK
    loaded = (rows, weight, inputs, w_up, w_gate)
    return pl.pallas_call(
        branch_kernel,
        out_shape=(
            shape((height, width), F32),
            shape((4, height, 2 * width)),
            shape((2 * width, w_up.shape[1] // 2)),
            shape((2 * width, w_gate.shape[1] // 2)),
        ),
        in_specs=[IN_ANY] * 6,
        out_specs=(IN_VMEM, IN_ANY, IN_ANY, IN_ANY),
        scratch_shapes=reduce_scratch(height, width)
        + gather_scratch(height, width)
        + wire_scratch(REDUCE_KINDS + GATHER_KINDS + 2 * SHARE_KINDS, count)
        + [pltpu.SemaphoreType.DMA((1,))]
        + load_scratch(loaded)
        + [pltpu.SemaphoreType.DMA((2,))],
        compiler_params=remote_params(number),
        cost_estimate=cost(16 * height * rows.shape[2] * width, 64 * height * width),
    )(*loaded, quarter)


def units_kernel(
    whole_ref, grad_ref, gates_ref, uppers_ref, back_ref, gain_ref, second_ref, hidden_ref, unit_ref, scale_ref, stats_ref
):
    units = hidden_ref.shape[1]
    value = whole_ref[...].astype(F32)
    scale = lax.rsqrt(jnp.mean(value * value, axis=1, keepdims=True) + EPS)
    second = (value * scale * gain_ref[...]).astype(B16)
    second_ref[...] = second
    scale_ref[...] = jnp.broadcast_to(scale, scale_ref.shape)
    total = jnp.zeros((value.shape[0], 1), F32)
    for low in range(0, units, CHUNK):
        at = slice(low, low + CHUNK)
        beside = slice(units + low, units + low + CHUNK)
        gate = jnp.dot(second, gates_ref[:, at], preferred_element_type=F32)
        upper = jnp.dot(second, uppers_ref[:, at], preferred_element_type=F32)
        hidden_grad = rows_dot(grad_ref[...], back_ref[at, :])
        sigma = jax.nn.sigmoid(gate)
        passed = gate * sigma
        hidden_ref[:, at] = (passed * upper).astype(B16)
        gate_grad = (hidden_grad * upper * (sigma + passed * (1.0 - sigma))).astype(B16)
        up_grad = (hidden_grad * passed).astype(B16)
        unit_ref[:, at] = gate_grad
        unit_ref[:, beside] = up_grad
        total += jnp.sum(
            gate_grad.astype(F32) * gate + up_grad.astype(F32) * upper, axis=1, keepdims=True
        )
    stats_ref[...] = jnp.zeros_like(stats_ref)
    for tile in range(stats_ref.shape[0]):
        put_stats(stats_ref, tile, total[tile * BLOCK : (tile + 1) * BLOCK])


def units_call(whole, grad, w_gates, w_uppers, w_back, gain):
    tokens, width = whole.shape
    units = w_back.shape[0]
    size = 2 * BLOCK
    tiles = tokens // size

    def tile(columns):
        return pl.BlockSpec((size, columns), lambda i: (i, 0))

    def all_of(item):
        return pl.BlockSpec(item.shape, lambda i: (0, 0))

    return pl.pallas_call(
        units_kernel,
        out_shape=(
            shape((tokens, width)),
            shape((tokens, units)),
            shape((tokens, 2 * units)),
            shape((tokens, 128), F32),
            shape((2 * tiles, 8, 128), F32),
        ),
        grid=(tiles,),
        in_specs=[tile(width), tile(width)]
        + [all_of(item) for item in (w_gates, w_uppers, w_back, gain)],
        out_specs=(
            tile(width),
            tile(units),
            tile(2 * units),
            tile(128),
            pl.BlockSpec((2, 8, 128), lambda i: (i, 0, 0)),
        ),
        compiler_params=pltpu.CompilerParams(vmem_limit_bytes=VMEM_MOST),
        cost_estimate=cost(6 * tokens * width * units, 20 * tokens * width // 2),
    )(whole, grad, w_gates, w_uppers, w_back, gain)


class Loads:
    def __init__(self, sources, targets, sems):
        self.copies = [
            pltpu.make_async_copy(source, target, sems.at[index])
            for index, (source, target) in enumerate(zip(sources, targets))
        ]

    def start(self):
        for copy in self.copies:
            copy.start()

    def wait(self, low, high):
        for copy in self.copies[low:high]:
            copy.wait()


def load_scratch(items):
    return [pltpu.VMEM(item.shape, item.dtype) for item in items] + [
        pltpu.SemaphoreType.DMA((len(items),))
    ]


class Stats:
    def __init__(self, wires, base, ref, recv):
        self.ref, self.recv = ref, recv
        side, across, core = neighbours()
        self.hops = (
            lambda: wires.copy(base, 0, ref.at[4:8], recv.at[0:4], core),
            lambda: wires.copy(base, 1, ref.at[2:4], recv.at[4:6], across),
            lambda: wires.copy(base, 2, ref.at[0:2], recv.at[6:8], side),
        )
        self.spans = ((4, 0), (2, 4), (2, 6))

    def start(self, hop):
        self.hops[hop]().start()

    def finish(self, hop):
        self.hops[hop]().wait()
        size, at = self.spans[hop]
        self.ref[0:size] = self.ref[0:size] + self.recv[at : at + size]

    def step(self, hop):
        self.finish(hop)
        self.start(hop + 1)


def pull_columns(stats_ref, scale_ref, column_ref, width):
    for part in range(scale_ref.shape[0] // 128):
        at = slice(part * 128, (part + 1) * 128)
        scale = scale_ref[at, :]
        column_ref[at, :] = (
            stand(stats_ref[part // 2, part % 2 : part % 2 + 1, :]) * scale * scale / (2 * width)
        )


def pulled(reduce, chunk, refs, column_ref):
    scale_ref, value_ref, gain_ref, base_ref = refs
    at = lanes(chunk, 0, value_ref.shape[1])
    upstream = reduce.total(chunk)
    value = value_ref[:, at].astype(F32)
    scale = scale_ref[:, 0:1]
    back = scale * gain_ref[:, at] * upstream - value * column_ref[:, 0:1]
    return at, base_ref[:, at].astype(F32) + back, upstream * value * scale


def tile_columns(tile):
    return pl.ds(pl.multiple_of(tile * BLOCK, BLOCK), BLOCK)


SPLIT = 512


def middle_kernel(
    rows_in_ref,
    gates_in_ref,
    uppers_in_ref,
    value_in_ref,
    base_in_ref,
    hidden_in_ref,
    scale_in_ref,
    stats_in_ref,
    gain_ref,
    grad_ref,
    second_ref,
    result_ref,
    gain_grad_ref,
    whole_ref,
    rest_ref,
    *refs,
):
    ends, scratch = refs[:4], refs[4:]
    bufs = scratch[:7]
    stats_ref, stats_recv, column_ref, send_sems, recv_sems, own, gather_sem = scratch[7:14]
    stream, stream_sem, stage, stage_sem = scratch[14:18]
    down_tiles, down_recv, made_tiles, made_recv = scratch[18:22]
    weight_ref, hidden_ref, rows_ref, value_ref, base_ref, scale_ref = scratch[22:28]
    load_sem = scratch[28]
    rows, width = value_ref.shape
    columns = rows_ref.shape[2]
    units = gates_in_ref.shape[1]
    loads = Loads(
        (
            hidden_in_ref,
            rows_in_ref,
            gates_in_ref,
            uppers_in_ref,
            scale_in_ref.at[pl.ds(0, rows)],
            value_in_ref,
            base_in_ref,
        ),
        (
            hidden_ref,
            rows_ref,
            weight_ref.at[:, :units],
            weight_ref.at[:, units:],
            scale_ref,
            value_ref,
            base_ref,
        ),
        load_sem,
    )

    def fetch(ref, step, tile):
        slot = lax.rem(step, 2)
        return pltpu.make_async_copy(
            ref.at[:, :, tile_columns(tile)], stream.at[slot], stream_sem.at[slot]
        )

    fetch(grad_ref, 0, turn_tile(0)).start()
    loads.start()
    stats_ref[...] = stats_in_ref[...]
    greet(neighbours() + planes())
    wires = Wires(send_sems, recv_sems)
    base = REDUCE_KINDS + 1 + GATHER_KINDS
    down = Fold(wires, base, down_tiles, (down_recv,), ends[0], ends[1])
    made = Fold(wires, base + FOLD_KINDS, made_tiles, (made_recv,), ends[2], ends[3])
    stats = Stats(wires, REDUCE_KINDS, stats_ref, stats_recv)
    def make_down(step):
        @pl.when(step < 7)
        def _():
            fetch(grad_ref, step + 1, turn_tile(step + 1)).start()

        fetch(grad_ref, step, turn_tile(step)).wait()
        left = stream[lax.rem(step, 2)].reshape(4 * rows, BLOCK)
        down_tiles[turn_tile(step)] = weight_grad(
            left, hidden_ref[...].reshape(4 * rows, units)
        ).astype(B16)

    stats.start(0)
    loads.wait(0, 1)
    make_tiles(down, make_down, 0, 2)
    reduce = Reduce(wires, rows_ref, weight_ref, True, bufs)
    loads.wait(1, 4)

    def first_part():
        stats.step(0)
        make_tiles(down, make_down, 2, 4)

    def second_part():
        down.step()
        stats.step(1)
        make_tiles(down, make_down, 4, 6)

    reduce.start((first_part, second_part))
    reduce.middle()

    def store(step):
        slot = lax.rem(step, 2)
        return pltpu.make_async_copy(
            stage.at[slot], rest_ref.at[turn_tile(step)], stage_sem.at[slot]
        )

    def make(step):
        slot = lax.rem(step, 2)

        @pl.when(step < 7)
        def _():
            fetch(second_ref, step + 1, turn_tile(step + 1)).start()

        fetch(second_ref, step, turn_tile(step)).wait()

        @pl.when(step >= 2)
        def _():
            store(step - 2).wait()

        left = stream[slot].reshape(4 * rows, BLOCK)
        flat = rows_ref[...].reshape(4 * rows, columns)
        made.tiles[turn_tile(step)] = weight_grad(left, flat[:, :SPLIT]).astype(B16)
        for low in range(SPLIT, columns, SPLIT):
            stage[slot, :, low - SPLIT : low] = weight_grad(
                left, flat[:, low : low + SPLIT]
            ).astype(B16)
        store(step).start()

    loads.wait(4, 7)
    stats.finish(2)
    pull_columns(stats_ref, scale_ref, column_ref, width)
    gather = Gather(wires, REDUCE_KINDS + 1, whole_ref, own, gather_sem, 2)

    def finish_chunks(low, high):
        @pl.loop(low, high)
        def _(chunk):
            at, result, share = pulled(
                reduce, chunk, (scale_ref, value_ref, gain_ref, base_ref), column_ref
            )
            result_ref[:, at] = result
            own[chunk] = result.astype(B16)
            gather.send(chunk)
            gain_grad_ref[:, at] = jnp.sum(share, axis=0, keepdims=True)

    finish_chunks(0, 2)
    make_tiles(down, make_down, 6, 8)
    fetch(second_ref, 0, turn_tile(0)).start()
    make_tiles(made, make, 0, 4)
    finish_chunks(2, width // CHUNK)
    down.middle()
    make_tiles(made, make, 4, 8)
    for step in (6, 7):
        store(step).wait()
    gather.relay(0, 3)
    down.late()
    made.step()
    gather.relay(3)
    made.middle()
    gather.close()
    made.late()
    down.close()
    made.close()
    reduce.close()


def middle_call(
    rows, w_gates, w_uppers, stats, scale, value, gain, base, hidden, grad, second, number
):
    height, width = value.shape
    count = width // CHUNK
    columns = rows.shape[2]
    quarter, units = width // 4, hidden.shape[2]
    sizes = (units, SPLIT)
    ends, tiles = [], []
    for size in sizes:
        ends += [shape((quarter, size), F32), shape((quarter, size))]
        tiles += [pltpu.VMEM((8, quarter, size), B16)] + fold_scratch(quarter, size)
    loaded = (rows, w_gates, w_uppers, value, base, hidden, scale)
    return pl.pallas_call(
        middle_kernel,
        out_shape=[
            shape((height, width), F32),
            shape((1, width), F32),
            shape((4, height, 2 * width)),
            shape((8, quarter, columns - SPLIT)),
        ]
        + ends,
        in_specs=[IN_ANY] * 7 + [IN_VMEM] * 2 + [IN_ANY] * 2,
        out_specs=[IN_VMEM] * 2 + [IN_ANY] * 2 + [IN_VMEM, IN_ANY] * 2,
        scratch_shapes=reduce_scratch(height, width)
        + [
            pltpu.VMEM((8, 8, 128), F32),
            pltpu.VMEM((8, 8, 128), F32),
            pltpu.VMEM((height, 128), F32),
        ]
        + wire_scratch(REDUCE_KINDS + 1 + GATHER_KINDS + 2 * FOLD_KINDS, count)
        + gather_scratch(height, width)
        + [
            pltpu.VMEM((2, 4, height, BLOCK), B16),
            pltpu.SemaphoreType.DMA((2,)),
            pltpu.VMEM((2, quarter, columns - SPLIT), B16),
            pltpu.SemaphoreType.DMA((2,)),
        ]
        + tiles
        + [pltpu.VMEM((2 * width, columns), B16)]
        + load_scratch((hidden, rows, value, base))[:-1]
        + [pltpu.VMEM((height, 128), F32)]
        + [pltpu.SemaphoreType.DMA((len(loaded),))],
        compiler_params=remote_params(number),
        cost_estimate=cost(48 * height * units * width, 64 * height * width),
    )(*loaded, stats, gain, grad, second)


def last_kernel(
    rows_in_ref,
    weight_in_ref,
    value_in_ref,
    base_in_ref,
    stats_in_ref,
    scale_ref,
    gain_ref,
    extra_ref,
    out_in_ref,
    project_in_ref,
    result_ref,
    totals_ref,
    out_mine_ref,
    out_theirs_ref,
    project_mine_ref,
    project_theirs_ref,
    *scratch,
):
    bufs = scratch[:7]
    stats_ref, stats_recv, column_ref, send_sems, recv_sems = scratch[7:12]
    out_ref, project_ref, sums_ref, sums_recv, load_sem = scratch[12:17]
    out_bufs, project_bufs = scratch[17:18], scratch[18:19]
    rows_ref, weight_ref, value_ref, base_ref = scratch[19:23]
    rows, width = value_ref.shape
    loads = Loads(
        (project_in_ref, weight_in_ref, rows_in_ref, value_in_ref, base_in_ref, out_in_ref),
        (project_ref, weight_ref, rows_ref, value_ref, base_ref, out_ref),
        load_sem,
    )
    loads.start()
    stats_ref[...] = stats_in_ref[...]
    sums_ref[...] = jnp.zeros_like(sums_ref)
    sums_ref[8] = extra_ref[0]
    sums_ref[9] = extra_ref[1]
    greet(neighbours() + planes())
    wires = Wires(send_sems, recv_sems)
    base = REDUCE_KINDS + 1
    out = Fold(wires, base, out_ref, out_bufs, out_mine_ref, out_theirs_ref, out_in_ref)
    project = Fold(
        wires,
        base + FOLD_KINDS,
        project_ref,
        project_bufs,
        project_mine_ref,
        project_theirs_ref,
        project_in_ref,
    )
    stats = Stats(wires, REDUCE_KINDS, stats_ref, stats_recv)
    stats.start(0)
    out.start()
    loads.wait(0, 2)

    @pl.loop(0, 8)
    def _(tile):
        share = jnp.sum(
            project_ref[tile].astype(F32) * weight_ref[tile_columns(tile), :].astype(F32),
            axis=1,
            keepdims=True,
        )
        sums_ref[tile, 0:1, :] = lie(share[:128])
        sums_ref[tile, 1:2, :] = lie(share[128:])

    side_device, across, core = neighbours()
    near, mirror = planes()

    def hop(index):
        slot, device = ((0, core), (1, across), (2, near), (3, mirror), (2, near))[index]
        kind, chunk = divmod(index, 4)
        return wires.copy(
            base + 2 * FOLD_KINDS + kind, chunk, sums_ref, sums_recv.at[slot], device
        )

    def add(slot):
        sums_ref[...] = sums_ref[...] + sums_recv[slot]

    reduce = Reduce(wires, rows_ref, weight_ref, True, bufs)
    loads.wait(2, 3)
    hop(0).start()
    reduce.give(0)
    hop(0).wait()
    add(0)
    hop(1).start()
    stats.step(0)

    def after_two():
        hop(1).wait()
        add(1)

        @pl.when(jnp.logical_not(inner()))
        def _():
            hop(2).start()

        project.start()
        stats.step(1)

    reduce.rest((after_two, lambda: None))
    loads.wait(3, 6)
    out.step()
    ends_line = jnp.logical_not(inner())

    @pl.when(inner())
    def _():
        hop(2).wait_recv()
        add(2)
        hop(3).start()

    out.middle()
    reduce.middle()
    stats.finish(2)
    pull_columns(stats_ref, scale_ref, column_ref, width)

    @pl.when(inner())
    def _():
        hop(3).wait()
        add(3)
        hop(4).start()

    project.step()
    project.middle()

    @pl.loop(0, width // CHUNK)
    def _(chunk):
        at, result, _ = pulled(
            reduce, chunk, (scale_ref, value_ref, gain_ref, base_ref), column_ref
        )
        result_ref[:, at] = result.astype(B16)

    @pl.when(inner())
    def _():
        hop(4).wait_send()

    @pl.when(ends_line)
    def _():
        hop(2).wait_send()
        hop(4).wait_recv()
        sums_ref[...] = sums_recv[2]

    move = wires.copy(base + 2 * FOLD_KINDS + 1, 1, sums_ref, sums_recv.at[4], side_device)
    move.start()
    out.late()
    project.late()
    move.wait()
    totals_ref[0:4] = sums_ref[0:4] + sums_recv[4, 4:8]
    totals_ref[4:8] = sums_ref[4:8] + sums_recv[4, 0:4]
    totals_ref[8] = sums_ref[8]
    totals_ref[9] = sums_recv[4, 8]
    totals_ref[10] = sums_ref[9] + sums_recv[4, 9]
    project.close()
    out.close()
    reduce.close()


def last_call(rows, weight, stats, scale, value, gain, base, extra, out, project, number):
    height, width = value.shape
    count = width // CHUNK
    quarter, branch = out.shape[1:]
    columns = rows.shape[2]
    return pl.pallas_call(
        last_kernel,
        out_shape=(
            shape((height, width)),
            shape((11, 8, 128), F32),
            shape((quarter, branch), F32),
            shape((quarter, branch)),
            shape((quarter, columns), F32),
            shape((quarter, columns)),
        ),
        in_specs=[IN_ANY] * 4 + [IN_VMEM] * 4 + [IN_ANY] * 2,
        out_specs=(IN_VMEM, IN_VMEM) + (IN_VMEM, IN_ANY) * 2,
        scratch_shapes=reduce_scratch(height, width)
        + [
            pltpu.VMEM((8, 8, 128), F32),
            pltpu.VMEM((8, 8, 128), F32),
            pltpu.VMEM((height, 128), F32),
        ]
        + wire_scratch(REDUCE_KINDS + 1 + 2 * FOLD_KINDS + 2, count)
        + [
            pltpu.VMEM((8, quarter, branch), B16),
            pltpu.VMEM((8, quarter, columns), B16),
            pltpu.VMEM((10, 8, 128), F32),
            pltpu.VMEM((5, 10, 8, 128), F32),
            pltpu.SemaphoreType.DMA((6,)),
        ]
        + fold_scratch(quarter, branch)
        + fold_scratch(quarter, columns)
        + load_scratch((rows, weight, value, base))[:4],
        compiler_params=remote_params(number),
        cost_estimate=cost(32 * height * columns * width, 64 * height * width),
    )(rows, weight, value, base, stats, scale, gain, extra, out, project)


def back_kernel(
    most,
    query_gain_ref,
    key_gain_ref,
    *refs,
):
    operands, refs = refs[:13], refs[13:]
    rest_ref, whole_ref, first_ref = refs[:3]
    output_ref, result_ref, stats_ref, gains_ref, out_ref, project_ref = refs[3:9]
    ends, scratch = refs[9:11], refs[11:]
    bufs = scratch[:7]
    key_acc, value_acc, send_sems, recv_sems, rest_sem = scratch[7:12]
    tiles, fold_recv = scratch[12:14]
    held, load_sem = scratch[14:27], scratch[27]
    upstream, acc, stream, stream_sem, stage, stage_sem = scratch[28:]
    hidden_ref, down_ref, branch_ref, mixed_ref, starts_ref, cosine_ref, sine_ref = held[:7]
    projected_ref, query_ref, key_ref, value_ref, log_ref, residual_ref = held[7:]
    attend_loads = Loads(operands, held, load_sem)
    attend_loads.start()
    width = residual_ref.shape[1]
    rows = residual_ref.shape[0]

    def fetch(ref, tile):
        slot = lax.rem(tile, 2)
        return pltpu.make_async_copy(
            ref.at[:, :, tile_columns(tile)], stream.at[slot], stream_sem.at[slot]
        )

    def each_tile(ref, target, right, work):
        columns = target.shape[2]

        def store(tile):
            slot = lax.rem(tile, 2)
            return pltpu.make_async_copy(
                stage.at[slot, :, :columns], target.at[tile], stage_sem.at[slot]
            )

        @pl.loop(0, 8)
        def _(tile):
            @pl.when(tile < 7)
            def _():
                fetch(ref, tile + 1).start()

            fetch(ref, tile).wait()

            @pl.when(tile >= 2)
            def _():
                store(tile - 2).wait()

            left = stream[lax.rem(tile, 2)].reshape(4 * rows, BLOCK)
            work(tile, left)
            stage[lax.rem(tile, 2), :, :columns] = weight_grad(
                left, right[...].reshape(4 * rows, columns)
            ).astype(B16)
            store(tile).start()

        for tile in (6, 7):
            store(tile).wait()

    fetch(whole_ref, 0).start()
    core = lax.rem(lax.axis_index("tx"), 2)
    load = pltpu.make_async_copy(rest_ref, tiles, rest_sem)
    load.start()
    greet(neighbours() + planes())
    wires = Wires(send_sems, recv_sems)
    fold = Fold(wires, REDUCE_KINDS, tiles, (fold_recv,), ends[0], ends[1], rest_ref)
    fold.start()
    reduce = Reduce(wires, hidden_ref, down_ref, False, bufs)
    attend_loads.wait(0, 2)
    reduce.start()
    attend_loads.wait(2, 13)
    load.wait()
    acc[...] = jnp.zeros_like(acc)

    def branch_work(tile, left):
        acc[...] += rows_dot(left, branch_ref[:, tile_columns(tile)])

    each_tile(whole_ref, out_ref, mixed_ref, branch_work)
    fetch(first_ref, 0).start()
    upstream[...] = acc[...].astype(B16).reshape(upstream.shape)
    fold.step()
    stats_ref[...] = jnp.zeros_like(stats_ref)
    fixed_refs = (starts_ref, cosine_ref, sine_ref, query_gain_ref, key_gain_ref)
    saved_refs = (query_ref, key_ref, value_ref, log_ref)

    @pl.loop(0, 2)
    def _(seq):
        attend_sequence_back(
            core,
            seq,
            most,
            projected_ref,
            upstream,
            fixed_refs,
            saved_refs,
            result_ref,
            stats_ref,
            gains_ref,
            (acc, key_acc, value_acc),
        )

        @pl.when(seq == 0)
        def _():
            reduce.middle()

    fold.middle()

    each_tile(first_ref, project_ref, result_ref, lambda tile, left: None)


    @pl.loop(0, width // CHUNK)
    def _(chunk):
        at = lanes(chunk, 0, width)
        output_ref[:, at] = (residual_ref[:, at] + reduce.total(chunk)).astype(B16)

    fold.late()
    fold.close()
    reduce.close()


def back_call(
    whole, first, w_branch, mixed, hidden, w_back, residual, fixed_args, projected, saved, rest, most, number
):
    height, width = residual.shape
    _, cosine, _, query_gain, _ = fixed_args
    depth = query_gain.shape[1]
    length = cosine.shape[1]
    columns = projected.shape[2]
    heads = columns // depth - 2
    quarter, columns_left = rest.shape[1:]
    loaded = (hidden, w_back, w_branch, mixed) + fixed_args[:3] + (projected,) + saved + (residual,)
    return pl.pallas_call(
        lambda *refs: back_kernel(most, *refs),
        out_shape=(
            shape((height, width)),
            shape((4, height, columns)),
            shape((8, 8, 128), F32),
            shape((2, 8, depth), F32),
            shape((8, quarter, heads * depth)),
            shape((8, quarter, columns)),
        )
        + (shape((quarter, columns_left), F32), shape((quarter, columns_left))),
        in_specs=[IN_VMEM] * 2 + [IN_ANY] * 16,
        out_specs=[IN_VMEM] * 4 + [IN_ANY] * 2 + [IN_VMEM, IN_ANY],
        scratch_shapes=reduce_scratch(height, width)
        + [
            pltpu.VMEM((length, depth), F32),
            pltpu.VMEM((length, depth), F32),
        ]
        + wire_scratch(REDUCE_KINDS + FOLD_KINDS, width // CHUNK)
        + [pltpu.SemaphoreType.DMA, pltpu.VMEM(rest.shape, B16)]
        + fold_scratch(quarter, columns_left)
        + load_scratch(loaded)
        + [
            pltpu.VMEM((4, height, heads * depth), B16),
            pltpu.VMEM((4 * height, heads * depth), F32),
            pltpu.VMEM((2, 4, height, BLOCK), B16),
            pltpu.SemaphoreType.DMA((2,)),
            pltpu.VMEM((2, quarter, columns), B16),
            pltpu.SemaphoreType.DMA((2,)),
        ],
        compiler_params=remote_params(number),
        cost_estimate=cost(16 * height * hidden.shape[2] * width, 64 * height * width),
    )(*fixed_args[3:], *loaded, rest, whole, first)


def finish_kernel(place_ref, *refs):
    downs, both, out, project = refs[0:2], refs[2:6], refs[6:8], refs[8:10]
    totals_ref, gain_ref = refs[10:12]
    moved, refs = refs[12:14], refs[14:]
    query_ref, key_ref, value_ref, out_ref, gate_ref, up_ref, down_ref = refs[:7]
    attn_ref, mlp_ref, query_gain_ref, key_gain_ref = refs[7:11]
    for source, target in zip(moved, refs[11:]):
        target[...] = source[...]
    query_gain_ref[...] = totals_ref[10, 0:1]
    key_gain_ref[...] = totals_ref[10, 1:2]
    first = place_ref[0] == 0

    def ordered(mine, theirs):
        theirs = theirs.astype(F32)
        return jnp.where(first, mine, theirs), jnp.where(first, theirs, mine)

    def put(target, at, mine, theirs):
        half = target.shape[1] // 2
        low, high = ordered(mine, theirs)
        target[:, at : at + mine.shape[1]] = low
        target[:, half + at : half + at + mine.shape[1]] = high

    def put_turned(target, at, mine, theirs):
        half = target.shape[0] // 2
        low, high = ordered(mine, theirs)
        target[at : at + mine.shape[1], :] = low.T
        target[half + at : half + at + mine.shape[1], :] = high.T

    put_turned(down_ref, 0, downs[0][...], downs[1][...])
    put_turned(out_ref, 0, out[0][...], out[1][...])
    at = 0
    for target in (query_ref, key_ref, value_ref):
        size = target.shape[1] // 2
        put(target, 0, project[0][:, at : at + size], project[1][:, at : at + size])
        at += size
    units = gate_ref.shape[1] // 2
    at = 0
    for index in (0, 2):
        low = 0
        while low < both[index].shape[1]:
            size = min(both[index].shape[1] - low, units - at % units)
            put(
                gate_ref if at < units else up_ref,
                at % units,
                both[index][:, low : low + size],
                both[index + 1][:, low : low + size],
            )
            low += size
            at += size
    mine = jnp.concatenate([totals_ref[tile, 0:2] for tile in range(4)], axis=0)
    theirs = jnp.concatenate([totals_ref[tile, 0:2] for tile in range(4, 8)], axis=0)
    low, high = ordered(mine / gain_ref[0:8], theirs / gain_ref[8:16])
    attn_ref[0:8], attn_ref[8:16] = low, high
    low, high = ordered(totals_ref[8], totals_ref[9])
    mlp_ref[0:8], mlp_ref[8:16] = low, high


def finish_call(place, parts, totals, gain, moved, sizes):
    quarter = parts[0].shape[0]
    queries, keys, branch, units = sizes
    return pl.pallas_call(
        finish_kernel,
        out_shape=(
            shape((quarter, queries), F32),
            shape((quarter, keys), F32),
            shape((quarter, keys), F32),
            shape((branch, quarter), F32),
            shape((quarter, units), F32),
            shape((quarter, units), F32),
            shape((units, quarter), F32),
            shape((16, 128), F32),
            shape((16, 128), F32),
            shape((1, 128), F32),
            shape((1, 128), F32),
        )
        + tuple(shape(item.shape, item.dtype) for item in moved),
        in_specs=[pl.BlockSpec(memory_space=pltpu.SMEM)] + [IN_VMEM] * (len(parts) + 4),
        out_specs=[IN_VMEM] * 13,
        compiler_params=pltpu.CompilerParams(vmem_limit_bytes=VMEM_MOST),
        cost_estimate=cost(0, 16 * 1024 * 1024),
    )(place, *parts, totals, gain, *moved)


def plane_device(
    tokens,
    seg_ids,
    w_query,
    w_key,
    w_value,
    w_out,
    w_gate,
    w_up,
    w_down,
    attn_gain,
    mlp_gain,
    query_gain,
    key_gain,
    cotangent,
):
    depth = query_gain.shape[0]
    most = seg_ids.shape[1] // 2
    rows, width = tokens.shape
    head_width = w_query.shape[1] // 2
    kv_width = w_key.shape[1] // 2
    units = w_gate.shape[1] // 2

    rate = np.float64(THETA) ** (-np.arange(depth // 2) * 2.0 / depth)
    rate = jnp.asarray(np.concatenate([rate, rate])[None].astype(np.float32))
    attn_row, mlp_row, starts, cosine, sine, token_whole, w_project, w_branch = open_call(
        tokens, w_query, w_key, w_value, w_out, attn_gain[None], mlp_gain[None], seg_ids, rate, 0
    )
    fixed_args = (starts, cosine, sine, query_gain[None], key_gain[None])
    (
        first,
        projected,
        first_scale,
        mixed,
        query,
        keys,
        values,
        logs,
        grad_whole,
        w_back,
        gate_quarter,
    ) = front_call(
        token_whole, w_project, attn_row, fixed_args, most, cotangent, w_down, w_gate, 1
    )
    residual, residual_whole, w_uppers, w_gates = branch_call(
        mixed, w_branch, tokens, w_up, w_gate, gate_quarter, 2
    )
    flat = (4 * rows, 2 * width)
    grad_flat = grad_whole.reshape(flat)
    second, hidden, unit_grads, second_scale, unit_stats = units_call(
        residual_whole.reshape(flat), grad_flat, w_gates, w_uppers, w_back, mlp_row
    )
    (
        residual_grad,
        mlp_gain_part,
        branch_whole,
        rest_tiles,
        *ends,
    ) = middle_call(
        unit_grads.reshape(4, rows, 2 * units),
        w_gates,
        w_uppers,
        unit_stats,
        second_scale,
        residual,
        mlp_gain[None],
        cotangent,
        hidden.reshape(4, rows, units),
        grad_whole,
        second.reshape(4, rows, 2 * width),
        3,
    )
    output, proj_grads, proj_stats, gain_parts, out_tiles, project_tiles, *rest_ends = back_call(
        branch_whole,
        first,
        w_branch,
        mixed,
        hidden.reshape(4, rows, units),
        w_back,
        residual,
        fixed_args,
        projected,
        (query, keys, values, logs),
        rest_tiles,
        most,
        4,
    )
    extra = jnp.stack(
        [
            mlp_gain_part.reshape(8, 128),
            jnp.pad(jnp.sum(gain_parts[:, :2], axis=0), ((0, 6), (0, 0))),
        ]
    )
    input_grad, totals, out_mine, out_theirs, project_mine, project_theirs = last_call(
        proj_grads,
        w_project,
        proj_stats,
        first_scale,
        tokens,
        attn_gain[None],
        residual_grad,
        extra,
        out_tiles,
        project_tiles,
        5,
    )
    place = lax.axis_index("ty").reshape(1).astype(jnp.int32)
    (
        query_share,
        key_share,
        value_share,
        out_share,
        gate_share,
        up_share,
        down_share,
        attn_total,
        mlp_total,
        query_total,
        key_total,
        output,
        input_grad,
    ) = finish_call(
        place,
        (*ends, *rest_ends, out_mine, out_theirs, project_mine, project_theirs),
        totals,
        attn_row.reshape(16, 128),
        (output, input_grad),
        (2 * head_width, 2 * kv_width, 2 * head_width, 2 * units),
    )
    attn_total, mlp_total = attn_total.reshape(-1), mlp_total.reshape(-1)
    query_total, key_total = query_total.reshape(-1), key_total.reshape(-1)
    return (
        output,
        input_grad,
        query_share,
        key_share,
        value_share,
        out_share,
        gate_share,
        up_share,
        down_share,
        attn_total,
        mlp_total,
        query_total,
        key_total,
    )


def solution(mesh):
    placed = (
        P(("dp", "tx"), "ty"),
        P(("dp", "ty"), None),
        P("ty", "tx"),
        P("ty", "tx"),
        P("ty", "tx"),
        P("tx", "ty"),
        P("ty", "tx"),
        P("ty", "tx"),
        P("tx", "ty"),
        P("ty"),
        P("ty"),
        P(),
        P(),
        P(("dp", "tx"), "ty"),
    )
    return jax.shard_map(
        plane_device if fits(mesh) else general_device,
        mesh=mesh,
        in_specs=placed,
        out_specs=(
            P(("dp", "tx"), "ty"),
            P(("dp", "tx"), "ty"),
            P(("ty", "dp"), "tx"),
            P(("ty", "dp"), "tx"),
            P(("ty", "dp"), "tx"),
            P("tx", ("ty", "dp")),
            P(("ty", "dp"), "tx"),
            P(("ty", "dp"), "tx"),
            P("tx", ("ty", "dp")),
            P(),
            P(),
            P(),
            P(),
        ),
        check_vma=False,
    )
```

```python
import jax
import jax.numpy as jnp
import numpy as np
from jax import lax
from jax.experimental import pallas as pl
from jax.experimental.pallas import tpu as pltpu
from jax.sharding import PartitionSpec as P

EPS = 1e-06
THETA = 1000000.0
NEG = -1e30
F32 = jnp.float32
B16 = jnp.bfloat16
MESH = pl.DeviceIdType.MESH


def width_sum(value):
    return lax.psum(value, "ty")


def token_gather(rows):
    return lax.all_gather(rows, "tx", axis=0, tiled=True)


def branch_gather(rows):
    return lax.all_gather(rows, "ty", axis=0, tiled=True)


def width_reduce(whole, apply):
    return lax.psum_scatter(apply(whole), "ty", scatter_dimension=0, tiled=True)


def head_reduce(whole, apply):
    return lax.psum_scatter(
        apply(whole).astype(jnp.bfloat16), "tx", scatter_dimension=0, tiled=True
    ).astype(jnp.float32)


def forward_with(weight):
    return lambda rows: jnp.dot(rows, weight, preferred_element_type=F32)


def backward_with(weight):
    return lambda rows: lax.dot_general(
        rows, weight, (((1,), (1,)), ((), ())), preferred_element_type=F32
    )


def weight_grad(left, right):
    return lax.dot_general(left, right, (((0,), (0,)), ((), ())), preferred_element_type=F32)


def norm_scale(rows):
    width = rows.shape[1] * lax.axis_size("ty")
    return lax.rsqrt(width_sum(jnp.sum(rows * rows, axis=1)) / width + EPS)


def norm_back(rows, scale, gain, upstream):
    width = rows.shape[1] * lax.axis_size("ty")
    inner = width_sum(jnp.sum(upstream * gain * rows, axis=1))
    back = scale[:, None] * gain * upstream - rows * (scale**3 * inner / width)[:, None]
    gain_part = jnp.sum(upstream * rows * scale[:, None], axis=0)
    return (back, gain_part)


def widen(part):
    whole = jnp.zeros((part.shape[0] * lax.axis_size("ty"),), F32)
    return lax.dynamic_update_slice_in_dim(whole, part, lax.axis_index("ty") * part.shape[0], 0)


def doc_positions(seg):
    count = seg.shape[-1]
    index = jnp.arange(count, dtype=jnp.int32)
    edge = jnp.concatenate([jnp.ones((1,), dtype=jnp.bool_), seg[1:] != seg[:-1]])
    first = lax.cummax(jnp.where(edge, index, jnp.zeros_like(index)), axis=0)
    return index - first


def rotary(positions, depth):
    half = depth // 2
    freq = THETA ** (-jnp.arange(half, dtype=F32) * 2.0 / depth)
    angle = positions.astype(F32)[..., None] * freq
    return (jnp.cos(angle), jnp.sin(angle))


def turn(value, gain, cosine, sine):
    normed = value * lax.rsqrt(jnp.mean(value * value, axis=-1, keepdims=True) + EPS) * gain
    half = value.shape[-1] // 2
    first = normed[..., :half]
    second = normed[..., half:]
    return jnp.concatenate(
        [first * cosine - second * sine, second * cosine + first * sine], axis=-1
    )


def block_scores(part, seq_keys, seq_ids, start, scale):
    block = part.shape[0]
    length = seq_ids.shape[0]
    index = jnp.arange(length, dtype=jnp.int32)
    rows = start + jnp.arange(block, dtype=jnp.int32)
    row_ids = lax.dynamic_slice_in_dim(seq_ids, start, block, 0)
    mask = (seq_ids[None, :] == row_ids[:, None]) & (index[None, :] <= rows[:, None])
    scores = jnp.einsum("qkgd,mkd->kgqm", part, seq_keys, preferred_element_type=F32) * scale
    return jnp.where(mask[None, None], scores, NEG)


def attend_forward(query, keys, values, seg, block):
    seqs, length, heads, depth = query.shape
    kv_heads = keys.shape[2]
    groups = heads // kv_heads
    scale = depth ** (-0.5)
    count = length // block
    starts = jnp.arange(count, dtype=jnp.int32) * block

    def one_sequence(operands):
        seq_query, seq_keys, seq_values, seq_ids = operands
        blocks = seq_query.reshape(count, block, kv_heads, groups, depth)

        def one_block(inputs):
            part, start = inputs
            scores = block_scores(part, seq_keys, seq_ids, start, scale)
            top = jnp.max(scores, axis=-1)
            weights = jnp.exp(scores - top[..., None])
            total = jnp.sum(weights, axis=-1)
            probs = (weights / total[..., None]).astype(B16)
            mixed = jnp.einsum("kgqm,mkd->qkgd", probs, seq_values, preferred_element_type=F32)
            return (mixed, top + jnp.log(total))

        mixed, logs = lax.map(one_block, (blocks, starts))
        return (mixed.reshape(length, heads * depth), logs)

    return lax.map(one_sequence, (query, keys, values, seg))


def attend_backward(query, keys, values, seg, logs, grad_out, block):
    seqs, length, heads, depth = query.shape
    kv_heads = keys.shape[2]
    groups = heads // kv_heads
    scale = depth ** (-0.5)
    count = length // block
    starts = jnp.arange(count, dtype=jnp.int32) * block

    def one_sequence(operands):
        seq_query, seq_keys, seq_values, seq_ids, seq_logs, seq_grad = operands
        blocks = seq_query.reshape(count, block, kv_heads, groups, depth)
        grads = seq_grad.reshape(count, block, kv_heads, groups, depth)

        def one_block(carry, inputs):
            key_acc, value_acc = carry
            part, grad_part, log_part, start = inputs
            scores = block_scores(part, seq_keys, seq_ids, start, scale)
            probs = jnp.exp(scores - log_part[..., None])
            value_acc = value_acc + jnp.einsum(
                "kgqm,qkgd->mkd", probs.astype(B16), grad_part, preferred_element_type=F32
            )
            prob_grad = jnp.einsum(
                "qkgd,mkd->kgqm", grad_part, seq_values, preferred_element_type=F32
            )
            delta = jnp.sum(probs * prob_grad, axis=-1, keepdims=True)
            score_grad = (probs * (prob_grad - delta)).astype(B16)
            query_grad = (
                jnp.einsum("kgqm,mkd->qkgd", score_grad, seq_keys, preferred_element_type=F32)
                * scale
            )
            key_acc = (
                key_acc
                + jnp.einsum("kgqm,qkgd->mkd", score_grad, part, preferred_element_type=F32) * scale
            )
            return ((key_acc, value_acc), query_grad)

        zeros = jnp.zeros((length, kv_heads, depth), F32)
        (key_grad, value_grad), query_grad = lax.scan(
            one_block, (zeros, zeros), (blocks, grads, seq_logs, starts)
        )
        return (query_grad.reshape(length, heads, depth), key_grad, value_grad)

    return lax.map(one_sequence, (query, keys, values, seg, logs, grad_out))


def general_device(
    tokens,
    seg_ids,
    w_query,
    w_key,
    w_value,
    w_out,
    w_gate,
    w_up,
    w_down,
    attn_gain,
    mlp_gain,
    query_gain,
    key_gain,
    cotangent,
):
    seqs, length = seg_ids.shape
    depth = query_gain.shape[0]
    query_width = w_query.shape[1]
    key_width = w_key.shape[1]
    units = w_gate.shape[1]
    block = min(512, length)
    inputs = tokens.astype(F32)
    first_scale = norm_scale(inputs)
    first_normed = (inputs * first_scale[:, None] * attn_gain).astype(B16)
    first_whole = token_gather(first_normed)
    w_project = jnp.concatenate([w_query, w_key, w_value], axis=1)
    projected = width_reduce(first_whole, forward_with(w_project))
    query_proj = projected[:, :query_width].reshape(seqs, length, -1, depth)
    key_proj = projected[:, query_width : query_width + key_width].reshape(seqs, length, -1, depth)
    values = projected[:, query_width + key_width :].astype(B16).reshape(seqs, length, -1, depth)
    positions = jax.vmap(doc_positions)(seg_ids)
    cosine, sine = rotary(positions, depth)
    cosine = cosine[:, :, None, :]
    sine = sine[:, :, None, :]
    query = turn(query_proj, query_gain, cosine, sine).astype(B16)
    keys = turn(key_proj, key_gain, cosine, sine).astype(B16)
    mixed, logs = attend_forward(query, keys, values, seg_ids, block)
    attended = mixed.reshape(seqs * length, -1).astype(B16)
    attended_whole = branch_gather(attended)
    residual = inputs + head_reduce(attended_whole, forward_with(w_out))
    second_scale = norm_scale(residual)
    second_normed = (residual * second_scale[:, None] * mlp_gain).astype(B16)
    second_whole = token_gather(second_normed)
    w_both = jnp.concatenate([w_gate, w_up], axis=1)
    gate_up = width_reduce(second_whole, forward_with(w_both))
    gate = gate_up[:, :units]
    upper = gate_up[:, units:]
    hidden = (jax.nn.silu(gate) * upper).astype(B16)
    hidden_whole = branch_gather(hidden)
    output = residual + head_reduce(hidden_whole, forward_with(w_down))
    grad_whole = token_gather(cotangent)
    hidden_grad = width_reduce(grad_whole, backward_with(w_down))
    down_grad = weight_grad(hidden_whole, grad_whole)
    gate_grad, up_grad = jax.vjp(lambda left, right: jax.nn.silu(left) * right, gate, upper)[1](
        hidden_grad
    )
    unit_grads = jnp.concatenate([gate_grad, up_grad], axis=1).astype(B16)
    unit_whole = branch_gather(unit_grads)
    second_grad = head_reduce(unit_whole, backward_with(w_both))
    both_grad = weight_grad(second_whole, unit_whole)
    gate_weight = both_grad[:, :units]
    up_weight = both_grad[:, units:]
    resid_norm_grad, mlp_gain_part = norm_back(residual, second_scale, mlp_gain, second_grad)
    residual_grad = cotangent.astype(F32) + resid_norm_grad
    residual_whole = token_gather(residual_grad.astype(B16))
    mixed_grad = width_reduce(residual_whole, backward_with(w_out)).astype(B16)
    out_grad = weight_grad(attended_whole, residual_whole)
    query_grad, key_grad, value_grad = attend_backward(
        query, keys, values, seg_ids, logs, mixed_grad.reshape(seqs, length, -1), block
    )
    query_proj_grad, query_gain_grad = jax.vjp(
        lambda value, gain: turn(value, gain, cosine, sine), query_proj, query_gain
    )[1](query_grad)
    key_proj_grad, key_gain_grad = jax.vjp(
        lambda value, gain: turn(value, gain, cosine, sine), key_proj, key_gain
    )[1](key_grad)
    rows = seqs * length
    proj_grad = jnp.concatenate(
        [
            query_proj_grad.reshape(rows, -1),
            key_proj_grad.reshape(rows, -1),
            value_grad.reshape(rows, -1),
        ],
        axis=1,
    ).astype(B16)
    proj_whole = branch_gather(proj_grad)
    first_grad = head_reduce(proj_whole, backward_with(w_project))
    project_grad = weight_grad(first_whole, proj_whole)
    query_weight = project_grad[:, :query_width]
    key_weight = project_grad[:, query_width : query_width + key_width]
    value_weight = project_grad[:, query_width + key_width :]
    input_norm_grad, attn_gain_part = norm_back(inputs, first_scale, attn_gain, first_grad)
    input_grad = (residual_grad + input_norm_grad).astype(B16)
    attn_total, mlp_total, query_total, key_total = lax.psum(
        (widen(attn_gain_part), widen(mlp_gain_part), query_gain_grad, key_gain_grad),
        ("dp", "tx", "ty"),
    )
    query_share, key_share, value_share, gate_share, up_share = (
        lax.psum_scatter(
            query_weight.astype(jnp.bfloat16), "dp", scatter_dimension=0, tiled=True
        ).astype(jnp.float32),
        lax.psum_scatter(
            key_weight.astype(jnp.bfloat16), "dp", scatter_dimension=0, tiled=True
        ).astype(jnp.float32),
        lax.psum_scatter(
            value_weight.astype(jnp.bfloat16), "dp", scatter_dimension=0, tiled=True
        ).astype(jnp.float32),
        lax.psum_scatter(
            gate_weight.astype(jnp.bfloat16), "dp", scatter_dimension=0, tiled=True
        ).astype(jnp.float32),
        lax.psum_scatter(
            up_weight.astype(jnp.bfloat16), "dp", scatter_dimension=0, tiled=True
        ).astype(jnp.float32),
    )
    out_share, down_share = (
        lax.psum_scatter(
            out_grad.astype(jnp.bfloat16), "dp", scatter_dimension=1, tiled=True
        ).astype(jnp.float32),
        lax.psum_scatter(
            down_grad.astype(jnp.bfloat16), "dp", scatter_dimension=1, tiled=True
        ).astype(jnp.float32),
    )
    return (
        output.astype(B16),
        input_grad,
        query_share,
        key_share,
        value_share,
        out_share,
        gate_share,
        up_share,
        down_share,
        attn_total,
        mlp_total,
        query_total,
        key_total,
    )


def fits(mesh):
    return mesh.shape["tx"] == 4 and mesh.shape["ty"] == 2 and mesh.shape["dp"] == 4


def swap_x(value):
    return lax.ppermute(value, "ty", [(0, 1), (1, 0)])


def in_order(mine, theirs, axis):
    first = lax.axis_index("ty") == 0
    return jnp.concatenate(
        [jnp.where(first, mine, theirs), jnp.where(first, theirs, mine)], axis=axis
    )


def spin(value, cosine, sine):
    return value * cosine + pltpu.roll(value, value.shape[1] // 2, 1) * sine


def spin_back(value, cosine, sine):
    return value * cosine + pltpu.roll(value * sine, value.shape[1] // 2, 1)


def head_scale(value):
    return lax.rsqrt(jnp.mean(value * value, axis=1, keepdims=True) + EPS)


def window(first, block, most):
    return max(0, first - most), first + block


def kept(first, block, low, high, starts):
    shape = (block, high - low)
    column = low + lax.broadcasted_iota(jnp.int32, shape, 1)
    row = first + lax.broadcasted_iota(jnp.int32, shape, 0)
    return (column >= starts) & (column <= row)


def rows_dot(left, right):
    return lax.dot_general(left, right, (((1,), (1,)), ((), ())), preferred_element_type=F32)


def stand(row):
    return jnp.transpose(jnp.broadcast_to(row, (row.shape[1], row.shape[1])))


def lie(column):
    return jnp.transpose(jnp.broadcast_to(column, (column.shape[0], column.shape[0])))[0:1]


def put_stats(stats_ref, tile, column):
    stats_ref[tile, 0:1, :] = lie(column[:128])
    stats_ref[tile, 1:2, :] = lie(column[128:])


BLOCK = 256


def attend_sequence(core, seq, most, projected, fixed_refs, mixed, saved_refs, between):
    starts_ref, cosine_ref, sine_ref, query_gain_ref, key_gain_ref = fixed_refs
    query_ref, key_ref, value_ref, log_ref = saved_refs
    rows = projected.shape[1]
    length = query_ref.shape[1]
    depth = key_ref.shape[2]
    heads = query_ref.shape[2] // depth
    scale = depth ** (-0.5)
    for half in range(2):
        place = 2 * lax.rem(core + half, 2) + seq
        for at in range(half * rows, (half + 1) * rows, BLOCK):
            inner = at - half * rows
            cosine = cosine_ref[seq, at : at + BLOCK, :]
            sine = sine_ref[seq, at : at + BLOCK, :]
            for head in range(heads + 2):
                lane = slice(head * depth, (head + 1) * depth)
                value = projected[place, inner : inner + BLOCK, lane]
                if head < heads:
                    normed = value * head_scale(value) * query_gain_ref[...]
                    query_ref[seq, at : at + BLOCK, lane] = spin(normed, cosine, sine).astype(B16)
                elif head == heads:
                    normed = value * head_scale(value) * key_gain_ref[...]
                    key_ref[seq, at : at + BLOCK, :] = spin(normed, cosine, sine).astype(B16)
                else:
                    value_ref[seq, at : at + BLOCK, :] = value.astype(B16)
    for first in range(0, length, BLOCK):
        between(first // BLOCK)
        low, high = window(first, BLOCK, most)
        mask = kept(first, BLOCK, low, high, starts_ref[seq, first : first + BLOCK, :])
        half, inner = divmod(first, rows)
        place = 2 * lax.rem(core + half, 2) + seq
        for head in range(heads):
            lane = slice(head * depth, (head + 1) * depth)
            query = query_ref[seq, first : first + BLOCK, lane]
            scores = rows_dot(query, key_ref[seq, low:high, :]) * scale
            scores = jnp.where(mask, scores, NEG)
            top = jnp.max(scores, axis=1, keepdims=True)
            weights = jnp.exp(scores - top)
            total = jnp.sum(weights, axis=1, keepdims=True)
            probs = (weights * (1.0 / total)).astype(B16)
            out = jnp.dot(probs, value_ref[seq, low:high, :], preferred_element_type=F32)
            mixed[place, inner : inner + BLOCK, lane] = out.astype(B16)
            log_ref[seq, head, first : first + BLOCK, :] = top + jnp.log(total)


def attend_sequence_back(
    core, seq, most, projected, upstream, fixed_refs, saved_refs, result, stats, gains, accs
):
    starts_ref, cosine_ref, sine_ref, query_gain_ref, key_gain_ref = fixed_refs
    query_ref, key_ref, value_ref, log_ref = saved_refs
    query_acc, key_acc, value_acc = accs
    rows = projected.shape[1]
    length = query_ref.shape[1]
    depth = key_ref.shape[2]
    heads = query_ref.shape[2] // depth
    scale = depth ** (-0.5)
    key_acc[...] = jnp.zeros_like(key_acc)
    value_acc[...] = jnp.zeros_like(value_acc)
    for first in range(0, length, BLOCK):
        low, high = window(first, BLOCK, most)
        mask = kept(first, BLOCK, low, high, starts_ref[seq, first : first + BLOCK, :])
        half, inner = divmod(first, rows)
        place = 2 * lax.rem(core + half, 2) + seq
        keys = key_ref[seq, low:high, :]
        values = value_ref[seq, low:high, :]
        for head in range(heads):
            lane = slice(head * depth, (head + 1) * depth)
            query = query_ref[seq, first : first + BLOCK, lane]
            grad = upstream[place, inner : inner + BLOCK, lane]
            scores = rows_dot(query, keys) * scale - log_ref[seq, head, first : first + BLOCK, :]
            probs = jnp.exp(jnp.where(mask, scores, NEG))
            prob_grad = rows_dot(grad, values)
            delta = jnp.sum(probs * prob_grad, axis=1, keepdims=True)
            score_grad = (probs * (prob_grad - delta)).astype(B16)
            query_acc[first : first + BLOCK, lane] = (
                jnp.dot(score_grad, keys, preferred_element_type=F32) * scale
            )
            key_acc[low:high, :] += weight_grad(score_grad, query) * scale
            value_acc[low:high, :] += weight_grad(probs.astype(B16), grad)
    query_total = jnp.zeros((1, depth), F32)
    key_total = jnp.zeros((1, depth), F32)
    for half in range(2):
        block = 2 * lax.rem(core + half, 2) + seq
        for at in range(half * rows, (half + 1) * rows, BLOCK):
            inner = at - half * rows
            cosine = cosine_ref[seq, at : at + BLOCK, :]
            sine = sine_ref[seq, at : at + BLOCK, :]
            total = jnp.zeros((BLOCK, 1), F32)
            for head in range(heads + 2):
                lane = slice(head * depth, (head + 1) * depth)
                value = projected[block, inner : inner + BLOCK, lane]
                if head == heads + 1:
                    back = value_acc[at : at + BLOCK, :].astype(B16)
                else:
                    if head < heads:
                        grad = query_acc[at : at + BLOCK, lane]
                        gain = query_gain_ref[...]
                    else:
                        grad = key_acc[at : at + BLOCK, :]
                        gain = key_gain_ref[...]
                    grad = spin_back(grad, cosine, sine)
                    rate = head_scale(value)
                    scaled = value * rate
                    share = jnp.sum(grad * scaled, axis=0, keepdims=True)
                    if head < heads:
                        query_total += share
                    else:
                        key_total += share
                    middle = jnp.mean(gain * grad * scaled, axis=1, keepdims=True)
                    back = (rate * (gain * grad - scaled * middle)).astype(B16)
                result[block, inner : inner + BLOCK, lane] = back
                total += jnp.sum(back.astype(F32) * value, axis=1, keepdims=True)
            put_stats(stats, 2 * block + inner // BLOCK, total)
    gains[seq, 0:1, :] = query_total
    gains[seq, 1:2, :] = key_total


def neighbours():
    spot = lax.axis_index("tx")
    core = lax.rem(spot, 2)
    return (
        {"ty": 1 - lax.axis_index("ty")},
        {"tx": lax.rem(spot + 2, 4)},
        {"tx": spot + 1 - 2 * core},
    )


def planes():
    plane = lax.axis_index("dp")
    return {"dp": plane + 1 - 2 * lax.rem(plane, 2)}, {"dp": 3 - plane}


def inner():
    plane = lax.axis_index("dp")
    return (plane == 1) | (plane == 2)


def greet(targets):
    barrier = pltpu.get_barrier_semaphore()
    for target in targets:
        pl.semaphore_signal(barrier, inc=1, device_id=target, device_id_type=MESH)
    pl.semaphore_wait(barrier, len(targets))


class Wires:
    def __init__(self, send_sems, recv_sems):
        self.send_sems = send_sems
        self.recv_sems = recv_sems

    def copy(self, kind, chunk, source, target, device):
        return pltpu.make_async_remote_copy(
            src_ref=source,
            dst_ref=target,
            send_sem=self.send_sems.at[kind, chunk],
            recv_sem=self.recv_sems.at[kind, chunk],
            device_id=device,
            device_id_type=MESH,
        )


CHUNK = 256
SIBLING, CORNER, FINAL_X, FINAL_Y = 0, 1, 2, 3
REDUCE_KINDS = 5
OUT_X, OUT_Y, OUT_CORNER, CORE_OWN, CORE_X, CORE_Y, CORE_CORNER = range(7)
GATHER_KINDS = 7
SHARE_X, SHARE_NEAR, SHARE_MIDDLE = 0, 1, 2
SHARE_KINDS = 3


def lanes(chunk, half, width):
    return pl.ds(pl.multiple_of(half * width + chunk * CHUNK, CHUNK), CHUNK)


class Gather:
    def __init__(self, wires, base, whole, own, local_sem, most=4):
        self.wires, self.base, self.whole, self.own, self.local_sem = (
            wires,
            base,
            whole,
            own,
            local_sem,
        )
        self.most = most
        self.width = whole.shape[2] // 2
        self.count = self.width // CHUNK

    def place(self, block, chunk, half):
        return self.whole.at[block, :, lanes(chunk, half, self.width)]

    def copy(self, name, chunk):
        side, across, core = neighbours()
        at = self.place
        own = self.own.at[chunk]
        if name == "local":
            return pltpu.make_async_copy(own, at(0, chunk, 0), self.local_sem.at[chunk])
        kind, source, target, device = {
            "x": (OUT_X, own, at(0, chunk, 1), side),
            "y": (OUT_Y, own, at(1, chunk, 0), across),
            "core": (CORE_OWN, own, at(2, chunk, 0), core),
            "even": (OUT_CORNER, at(0, chunk, 1), at(1, chunk, 1), across),
            "odd": (OUT_CORNER, at(1, chunk, 0), at(1, chunk, 1), side),
            "core_x": (CORE_X, at(0, chunk, 1), at(2, chunk, 1), core),
            "core_y": (CORE_Y, at(1, chunk, 0), at(3, chunk, 0), core),
            "core_corner": (CORE_CORNER, at(1, chunk, 1), at(3, chunk, 1), core),
        }[name]
        return self.wires.copy(self.base + kind, chunk, source, target, device)

    def send(self, chunk):
        for name in ("x", "y", "core", "local"):
            self.copy(name, chunk).start()

    def relay(self, low=0, high=None):
        @pl.loop(low, self.count if high is None else high)
        def _(chunk):
            even = (lax.rem(chunk, 2) == 0) | (chunk >= self.most)
            self.copy("x", chunk).wait_recv()

            @pl.when(even)
            def _():
                self.copy("even", chunk).start()

            self.copy("core_x", chunk).start()
            self.copy("y", chunk).wait_recv()

            @pl.when(jnp.logical_not(even))
            def _():
                self.copy("odd", chunk).start()

            self.copy("core_y", chunk).start()

    def close(self):
        @pl.loop(0, self.count)
        def _(chunk):
            self.copy("even", chunk).wait_recv()
            self.copy("core_corner", chunk).start()

        @pl.loop(0, self.count)
        def _(chunk):
            for name in ("core", "core_x", "core_y", "core_corner"):
                self.copy(name, chunk).wait_recv()
            for name in ("x", "y", "core", "even", "core_x", "core_y", "core_corner"):
                self.copy(name, chunk).wait_send()
            self.copy("local", chunk).wait()


class Share:
    def __init__(self, wires, base, sources, whole, by_rows, local_sems, held=None):
        self.wires, self.base, self.sources, self.whole, self.by_rows, self.local_sems = (
            wires,
            base,
            sources,
            whole,
            by_rows,
            local_sems,
        )
        self.held = held or sources
        self.size = (whole.shape[0] // 2 if by_rows else whole.shape[0]) // 4

    def quarter(self, plane):
        start = plane * self.size
        if self.by_rows:
            rows = pl.ds(pl.multiple_of(self.whole.shape[0] // 2 + start, self.size), self.size)
            return self.whole.at[rows]
        width = self.whole.shape[1] // 2
        return self.whole.at[pl.ds(pl.multiple_of(start, self.size), self.size), width:]

    def cross(self, index):
        side, _, _ = neighbours()
        plane = lax.axis_index("dp")
        other = 1 - lax.axis_index("ty")
        source = self.sources[index]
        if self.by_rows:
            rows = pl.ds(pl.multiple_of(plane * self.size, self.size), self.size)
            columns = source.shape[1] // 2
            part = source.at[rows, pl.ds(pl.multiple_of(other * columns, columns), columns)]
            offset = sum(item.shape[1] // 2 for item in self.sources[:index])
            target = self.quarter(plane).at[:, offset : offset + columns]
        else:
            start = pl.multiple_of(other * (source.shape[0] // 2) + plane * self.size, self.size)
            part = source.at[pl.ds(start, self.size)]
            target = self.quarter(plane)
        return self.wires.copy(self.base + SHARE_X, index, part, target, side)

    def local(self, index):
        mine = lax.axis_index("ty")
        source = self.held[index]
        if self.by_rows:
            columns = source.shape[1] // 2
            offset = sum(item.shape[1] // 2 for item in self.sources[:index])
            part = source.at[:, pl.ds(pl.multiple_of(mine * columns, columns), columns)]
            target = self.whole.at[: self.whole.shape[0] // 2, offset : offset + columns]
        else:
            half = source.shape[0] // 2
            part = source.at[pl.ds(pl.multiple_of(mine * half, half), half)]
            target = self.whole.at[:, : self.whole.shape[1] // 2]
        return pltpu.make_async_copy(part, target, self.local_sems.at[index])

    def piece_of(self, owner):
        place = self.quarter(owner)
        return place, place

    def over(self, near, index):
        beside, mirror = planes()
        plane = lax.axis_index("dp")
        other = 3 - plane
        if near:
            owner = (plane, other, other + 1 - 2 * lax.rem(other, 2))[index]
        else:
            owner = (plane, plane + 1 - 2 * lax.rem(plane, 2))[index]
        source, target = self.piece_of(owner) if index else self.own_piece()
        return self.wires.copy(
            self.base + (SHARE_NEAR if near else SHARE_MIDDLE),
            index,
            source,
            target,
            beside if near else mirror,
        )

    def own_piece(self):
        return self.piece_of(lax.axis_index("dp"))

    def start(self):
        for index in range(len(self.sources)):
            self.cross(index).start()
            self.local(index).start()

    def send_own(self):
        self.over(True, 0).start()

        @pl.when(inner())
        def _():
            self.over(False, 0).start()

    def middle(self):
        for index in range(len(self.sources)):
            self.cross(index).wait_recv()
        self.send_own()

    def late(self):
        @pl.when(inner())
        def _():
            self.over(True, 0).wait_recv()
            self.over(False, 1).start()
            self.over(False, 0).wait_recv()
            self.over(True, 1).start()

    def later(self):
        @pl.when(inner())
        def _():
            self.over(False, 1).wait_recv()
            self.over(True, 2).start()

    def close_planes(self):
        self.over(True, 0).wait_send()

        @pl.when(inner())
        def _():
            self.over(True, 1).wait_send()
            self.over(True, 2).wait_send()
            self.over(False, 0).wait_send()
            self.over(False, 1).wait_send()

        @pl.when(jnp.logical_not(inner()))
        def _():
            for index in range(3):
                self.over(True, index).wait_recv()

    def close(self):
        self.close_planes()
        for index in range(len(self.sources)):
            self.cross(index).wait_send()
            self.local(index).wait()


class Spread(Share):
    def __init__(self, wires, base, source, whole, local_sems, quarter):
        super().__init__(wires, base, (source,), whole, True, local_sems)
        self.piece = quarter

    def own_piece(self):
        return self.piece, self.quarter(lax.axis_index("dp"))

    def own(self):
        return pltpu.make_async_copy(
            self.piece, self.quarter(lax.axis_index("dp")), self.local_sems.at[1]
        )

    def start(self):
        self.send_own()
        self.local(0).start()
        self.own().start()

    def close(self):
        self.close_planes()
        self.local(0).wait()
        self.own().wait()


FOLD_END, FOLD_MIDDLE, FOLD_BACK, FOLD_X = 0, 2, 4, 5
FOLD_KINDS = 6


def side():
    return lax.div(lax.axis_index("dp"), 2)


def turn_shard(turn):
    return 3 * (1 - side()) + turn * (2 * side() - 1)


class Fold:
    def __init__(self, wires, base, tiles, bufs, mine, theirs, first=None):
        self.wires, self.base, self.tiles, self.mine, self.theirs = (
            wires,
            base,
            tiles,
            mine,
            theirs,
        )
        self.first = tiles if first is None else first
        (self.recv,) = bufs
        self.near, self.mirror = planes()

    def send(self, kind, half, slot, source, target, device):
        target = self.recv.at[2 * target + half]
        return self.wires.copy(self.base + kind, slot, source, target, device)

    def end(self, half, turn):
        source = self.first.at[4 * half + turn_shard(turn)]
        return self.send(FOLD_END + half, half, turn, source, turn, self.near)

    def across(self, half, turn):
        source = self.recv.at[2 * turn + half]
        return self.send(FOLD_MIDDLE + half, half, turn, source, 3 + turn, self.mirror)

    def back(self, half):
        return self.send(FOLD_BACK, half, half, self.recv.at[6 + half], 0, self.near)

    def cross(self):
        source = self.tiles.at[4 + lax.axis_index("dp")]
        return self.wires.copy(self.base + FOLD_X, 0, source, self.theirs, neighbours()[0])

    def add(self, slot, half, shard):
        self.recv[2 * slot + half] = (
            self.recv[2 * slot + half].astype(F32) + self.tiles[4 * half + shard].astype(F32)
        ).astype(B16)

    def begin(self, turn, half):
        @pl.when(jnp.logical_not(inner()))
        def _():
            self.end(half, turn).start()

    def start(self):
        for turn in range(3):
            for half in (1, 0):
                self.begin(turn, half)

    def pass_on(self, turn):
        @pl.when(inner())
        def _():
            for half in (1, 0):
                self.end(half, turn).wait_recv()
                self.add(turn, half, turn_shard(turn))
                self.across(half, turn).start()

    def step(self):
        self.pass_on(0)

    def middle(self):
        self.pass_on(1)

        @pl.when(inner())
        def _():
            for half in (1, 0):
                self.across(half, 0).wait_recv()
                self.add(3, half, 3 * side())
                self.back(half).start()

    def late(self):
        plane = lax.axis_index("dp")
        for half in (1, 0):

            @pl.when(inner())
            def _():
                self.end(half, 2).wait_recv()
                self.across(half, 1).wait_recv()
                self.add(2, half, plane)

            @pl.when(jnp.logical_not(inner()))
            def _():
                self.back(half).wait_recv()

            at = 4 * half + plane
            middle = inner().astype(jnp.int32)
            total = self.recv[4 * middle + half].astype(F32)
            other = jnp.where(
                inner(), self.recv[8 * middle + half].astype(F32), self.tiles[at].astype(F32)
            )
            total = total + other
            if half == 1:
                self.tiles[at] = total.astype(B16)
                self.cross().start()
            else:
                self.mine[...] = total

    def close(self):
        self.cross().wait_recv()

        @pl.when(inner())
        def _():
            for half in range(2):
                self.across(half, 0).wait_send()
                self.across(half, 1).wait_send()
                self.back(half).wait_send()

        @pl.when(jnp.logical_not(inner()))
        def _():
            for half in range(2):
                for turn in range(3):
                    self.end(half, turn).wait_send()

        self.cross().wait_send()


def fold_scratch(rows, columns):
    return [pltpu.VMEM((10, rows, columns), B16)]


def turn_tile(step):
    return 4 * (1 - lax.rem(step, 2)) + turn_shard(lax.div(step, 2))


def make_tiles(fold, make, low, high):
    @pl.loop(low, high)
    def _(step):
        make(step)

        @pl.when(step < 6)
        def _():
            half = 1 - lax.rem(step, 2)
            turn = lax.div(step, 2)
            for side_half in range(2):

                @pl.when(half == side_half)
                def _():
                    fold.begin(turn, side_half)


class Reduce:
    def __init__(self, wires, rows_ref, weight_ref, transposed, bufs):
        self.wires, self.rows_ref, self.weight_ref, self.transposed = (
            wires,
            rows_ref,
            weight_ref,
            transposed,
        )
        (
            self.sibling_send,
            self.sibling_recv,
            self.kept_ref,
            self.out,
            self.corner_recv,
            self.x_recv,
            self.y_recv,
        ) = bufs
        self.rows = rows_ref.shape[1]
        self.width = (weight_ref.shape[0] if transposed else weight_ref.shape[1]) // 2
        self.count = self.width // CHUNK

    def product(self, block, chunk, half):
        left = self.rows_ref[block : block + 2].reshape(2 * self.rows, self.rows_ref.shape[2])
        at = lanes(chunk, half, self.width)
        if self.transposed:
            return rows_dot(left, self.weight_ref[at, :])
        return jnp.dot(left, self.weight_ref[:, at], preferred_element_type=F32)

    def sibling(self, chunk, half):
        return self.wires.copy(
            SIBLING + half * (REDUCE_KINDS - 1),
            chunk,
            self.sibling_send.at[lax.rem(chunk, 2), half],
            self.sibling_recv.at[chunk, half],
            neighbours()[2],
        )

    def corner(self, chunk, device):
        return self.wires.copy(
            CORNER, chunk, self.out.at[2, chunk], self.corner_recv.at[chunk], device
        )

    def final_x(self, chunk):
        return self.wires.copy(
            FINAL_X, chunk, self.out.at[0, chunk], self.x_recv.at[chunk], neighbours()[0]
        )

    def final_y(self, chunk):
        return self.wires.copy(
            FINAL_Y, chunk, self.out.at[1, chunk], self.y_recv.at[chunk], neighbours()[1]
        )

    def give(self, chunk):
        @pl.loop(0, 2)
        def _(turn):
            half = 1 - turn
            self.sibling_send[lax.rem(chunk, 2), half] = self.product(2, chunk, half).astype(B16)
            self.sibling(chunk, half).start()

    def take(self, chunk):
        rows = self.rows
        even = lax.rem(chunk, 2) == 0
        side, across, _ = neighbours()

        @pl.loop(0, 2)
        def _(turn):
            half = 1 - turn
            own = self.product(0, chunk, half)
            self.sibling(chunk, half).wait_recv()
            total = own + self.sibling_recv[chunk, half].astype(F32)

            @pl.when(half == 1)
            def _():
                self.out[2, chunk] = total[rows:].astype(B16)
                self.out[0, chunk] = total[:rows].astype(B16)

                @pl.when(even)
                def _():
                    self.corner(chunk, side).start()
                    self.final_x(chunk).start()

                @pl.when(jnp.logical_not(even))
                def _():
                    self.corner(chunk, across).start()

            @pl.when(half == 0)
            def _():
                self.kept_ref[chunk] = total[:rows]
                self.out[1, chunk] = total[rows:].astype(B16)

                @pl.when(jnp.logical_not(even))
                def _():
                    self.final_y(chunk).start()

    def start(self, between=(lambda: None, lambda: None)):
        self.give(0)
        self.rest(between)

    def rest(self, between):
        self.take(0)
        self.give(1)
        self.take(1)
        between[0]()

        @pl.loop(2, self.count)
        def _(chunk):
            for half in range(2):
                self.sibling(chunk - 2, half).wait_send()
            self.give(chunk)
            self.take(chunk)
            self.middle(chunk - 2, chunk - 1)

        between[1]()

    def middle(self, low=None, high=None):
        @pl.loop(self.count - 2 if low is None else low, self.count if high is None else high)
        def _(chunk):
            even = lax.rem(chunk, 2) == 0
            self.corner(chunk, neighbours()[0]).wait_recv()
            came = self.corner_recv[chunk].astype(F32)

            @pl.when(even)
            def _():
                self.out[1, chunk] = (self.out[1, chunk].astype(F32) + came).astype(B16)
                self.final_y(chunk).start()

            @pl.when(jnp.logical_not(even))
            def _():
                self.out[0, chunk] = (self.out[0, chunk].astype(F32) + came).astype(B16)
                self.final_x(chunk).start()

    def total(self, chunk):
        self.final_x(chunk).wait_recv()
        self.final_y(chunk).wait_recv()
        return (
            self.kept_ref[chunk] + self.x_recv[chunk].astype(F32) + self.y_recv[chunk].astype(F32)
        )

    def close(self):
        @pl.loop(self.count - 2, self.count)
        def _(chunk):
            for half in range(2):
                self.sibling(chunk, half).wait_send()

        @pl.loop(0, self.count)
        def _(chunk):
            self.corner(chunk, neighbours()[0]).wait_send()
            self.final_x(chunk).wait_send()
            self.final_y(chunk).wait_send()


def reduce_scratch(rows, width):
    count = width // CHUNK
    return [
        pltpu.VMEM((2, 2, 2 * rows, CHUNK), B16),
        pltpu.VMEM((count, 2, 2 * rows, CHUNK), B16),
        pltpu.VMEM((count, rows, CHUNK), F32),
        pltpu.VMEM((3, count, rows, CHUNK), B16),
        pltpu.VMEM((count, rows, CHUNK), B16),
        pltpu.VMEM((count, rows, CHUNK), B16),
        pltpu.VMEM((count, rows, CHUNK), B16),
    ]


def gather_scratch(rows, width):
    count = width // CHUNK
    return [pltpu.VMEM((count, rows, CHUNK), B16), pltpu.SemaphoreType.DMA((count,))]


def wire_scratch(kinds, count):
    return [pltpu.SemaphoreType.DMA((kinds, count))] * 2


IN_VMEM = pl.BlockSpec(memory_space=pltpu.VMEM)
IN_ANY = pl.BlockSpec(memory_space=pl.ANY)
VMEM_MOST = 60 * 1024 * 1024


def remote_params(number):
    return pltpu.CompilerParams(
        collective_id=number, has_side_effects=True, vmem_limit_bytes=VMEM_MOST
    )


def cost(flops, size):
    return pl.CostEstimate(flops=flops, bytes_accessed=size, transcendentals=0)


def shape(dims, kind=B16):
    return jax.ShapeDtypeStruct(dims, kind)


def cut(own, block_ref):
    for chunk in range(own.shape[0]):
        own[chunk] = block_ref[:, chunk * CHUNK : (chunk + 1) * CHUNK]


def open_kernel(
    tokens_ref,
    query_ref,
    key_ref,
    value_ref,
    out_ref,
    attn_ref,
    mlp_ref,
    seg_ref,
    rate_ref,
    attn_all_ref,
    mlp_all_ref,
    starts_ref,
    cosine_ref,
    sine_ref,
    whole_ref,
    project_ref,
    branch_ref,
    *scratch,
):
    own, gather_sem, send_sems, recv_sems, project_sem, branch_sem = scratch[:6]
    attn_recv, mlp_recv, seg_recv, seg_all = scratch[6:]
    width = attn_ref.shape[1]
    length = seg_ref.shape[1]
    cut(own, tokens_ref)
    greet(neighbours() + planes())
    wires = Wires(send_sems, recv_sems)
    gather = Gather(wires, 0, whole_ref, own, gather_sem, 2)
    base = GATHER_KINDS + 2 * SHARE_KINDS
    side = neighbours()[0]
    small = [
        wires.copy(base, index, source, target, side)
        for index, (source, target) in enumerate(
            ((attn_ref, attn_recv), (mlp_ref, mlp_recv), (seg_ref, seg_recv))
        )
    ]
    shares = [
        Share(wires, GATHER_KINDS, (query_ref, key_ref, value_ref), project_ref, True, project_sem),
        Share(wires, GATHER_KINDS + SHARE_KINDS, (out_ref,), branch_ref, False, branch_sem),
    ]
    for copy in small:
        copy.start()
    shares[0].start()
    shares[1].start()

    @pl.loop(0, gather.count)
    def _(chunk):
        gather.send(chunk)

    for copy in small:
        copy.wait()
    attn_all_ref[:, :width] = attn_ref[...]
    attn_all_ref[:, width:] = attn_recv[...]
    mlp_all_ref[:, :width] = mlp_ref[...]
    mlp_all_ref[:, width:] = mlp_recv[...]
    mine = lax.rem(lax.axis_index("ty") + lax.div(lax.axis_index("tx"), 2), 2)
    seg_all[pl.ds(mine, 1)] = seg_ref[...].astype(F32)[None]
    seg_all[pl.ds(1 - mine, 1)] = seg_recv[...].astype(F32)[None]

    shares[0].middle()
    shares[1].middle()

    def between(seq, piece):
        @pl.when(seq == 0)
        def _():
            if piece == 4:
                gather.relay(0, 1)
            elif piece == 6:
                shares[0].late()
                shares[1].late()

        @pl.when(seq == 1)
        def _():
            if piece == 0:
                gather.relay(1, 2)
            elif piece == 2:
                shares[0].later()
                shares[1].later()
            elif piece == 3:
                gather.relay(2, 3)
            elif piece == 6:
                gather.relay(3, 4)

    @pl.loop(0, 2)
    def _(seq):
        for low in range(0, length, 128):
            between(seq, low // 128)
            here = stand(seg_all[seq, :, low : low + 128])
            before = jnp.zeros((128, 128), F32)
            for other in range(0, length, 128):
                before += (seg_all[seq, :, other : other + 128] < here).astype(F32)
            start = jnp.sum(before, axis=1, keepdims=True)
            at = slice(low, low + 128)
            starts_ref[seq, at, :] = start.astype(jnp.int32)
            row = lax.broadcasted_iota(jnp.int32, (128, 128), 0) + low
            lane = lax.broadcasted_iota(jnp.int32, (128, 128), 1)
            angle = (row.astype(F32) - start) * rate_ref[...]
            cosine_ref[seq, at, :] = jnp.cos(angle)
            sine = jnp.sin(angle)
            sine_ref[seq, at, :] = jnp.where(lane < 64, -sine, sine)

    gather.close()
    shares[0].close()
    shares[1].close()


def open_call(tokens, w_query, w_key, w_value, w_out, attn_gain, mlp_gain, seg_ids, rate, number):
    rows, width = tokens.shape
    columns = (w_query.shape[1] + w_key.shape[1] + w_value.shape[1]) // 2
    length = seg_ids.shape[1]
    return pl.pallas_call(
        open_kernel,
        out_shape=(
            shape((1, 2 * width), F32),
            shape((1, 2 * width), F32),
            shape((2, length, 1), jnp.int32),
            shape((2, length, 128), F32),
            shape((2, length, 128), F32),
            shape((4, rows, 2 * width)),
            shape((2 * width, columns)),
            shape((w_out.shape[0] // 2, 2 * width)),
        ),
        in_specs=[IN_VMEM] * 9,
        out_specs=(IN_VMEM,) * 5 + (IN_ANY,) * 3,
        scratch_shapes=gather_scratch(rows, width)
        + wire_scratch(GATHER_KINDS + 2 * SHARE_KINDS + 1, width // CHUNK)
        + [
            pltpu.SemaphoreType.DMA((3,)),
            pltpu.SemaphoreType.DMA((1,)),
            pltpu.VMEM((1, width), F32),
            pltpu.VMEM((1, width), F32),
            pltpu.VMEM((1, length), jnp.int32),
            pltpu.VMEM((2, 1, length), F32),
        ],
        compiler_params=remote_params(number),
        cost_estimate=cost(0, 32 * rows * width),
    )(tokens, w_query, w_key, w_value, w_out, attn_gain, mlp_gain, seg_ids, rate)


def front_kernel(
    most,
    whole_ref,
    project_ref,
    gain_ref,
    query_gain_ref,
    key_gain_ref,
    grad_ref,
    starts_in_ref,
    cosine_in_ref,
    sine_in_ref,
    down_in_ref,
    gate_in_ref,
    first_ref,
    projected_out_ref,
    scale_ref,
    mixed_ref,
    query_ref,
    key_ref,
    value_ref,
    log_ref,
    grad_whole_ref,
    back_ref,
    gate_ref,
    *scratch,
):
    own, gather_sem, send_sems, recv_sems, back_sem, tokens, firsts, tile_sem = scratch[:8]
    down_ref, starts_ref, cosine_ref, sine_ref = scratch[8:12]
    loads = Loads(
        (down_in_ref, starts_in_ref, cosine_in_ref, sine_in_ref), scratch[8:12], scratch[12]
    )
    projected_ref, projected_sem = scratch[13:]
    keep = pltpu.make_async_copy(projected_ref, projected_out_ref, projected_sem)
    core = lax.rem(lax.axis_index("tx"), 2)
    cut(own, grad_ref)
    rows = whole_ref.shape[1]

    def spot(ref, tile):
        at = pl.ds(pl.multiple_of(lax.rem(tile, rows // BLOCK) * BLOCK, BLOCK), BLOCK)
        return ref.at[lax.div(tile, rows // BLOCK), at, :]

    def fetch(tile):
        slot = lax.rem(tile, 2)
        return pltpu.make_async_copy(spot(whole_ref, tile), tokens.at[slot], tile_sem.at[0, slot])

    def store(tile):
        slot = lax.rem(tile, 2)
        return pltpu.make_async_copy(firsts.at[slot], spot(first_ref, tile), tile_sem.at[1, slot])

    fetch(0).start()
    loads.start()
    greet(neighbours() + planes())
    wires = Wires(send_sems, recv_sems)
    gather = Gather(wires, 0, grad_whole_ref, own, gather_sem, 0)
    back = Share(wires, GATHER_KINDS, (down_in_ref,), back_ref, False, back_sem, (down_ref,))
    size, columns = gate_ref.shape
    gate = wires.copy(
        GATHER_KINDS + SHARE_KINDS,
        0,
        gate_in_ref.at[
            pl.ds(pl.multiple_of(lax.axis_index("dp") * size, size), size),
            pl.ds(pl.multiple_of((1 - lax.axis_index("ty")) * columns, columns), columns),
        ],
        gate_ref,
        neighbours()[0],
    )
    back.cross(0).start()

    @pl.loop(0, gather.count)
    def _(chunk):
        gather.send(chunk)

    gate.start()

    loads.wait(0, 1)
    back.local(0).start()
    count = 4 * rows // BLOCK

    @pl.loop(0, count)
    def _(tile):
        slot = lax.rem(tile, 2)
        block = lax.div(tile, rows // BLOCK)
        at = pl.ds(pl.multiple_of(lax.rem(tile, rows // BLOCK) * BLOCK, BLOCK), BLOCK)

        @pl.when(tile < count - 1)
        def _():
            fetch(tile + 1).start()

        fetch(tile).wait()

        @pl.when(tile >= 2)
        def _():
            store(tile - 2).wait()

        value = tokens[slot].astype(F32)
        scale = lax.rsqrt(jnp.mean(value * value, axis=1, keepdims=True) + EPS)
        first = (value * scale * gain_ref[...]).astype(B16)
        firsts[slot] = first
        store(tile).start()
        projected_ref[block, at, :] = jnp.dot(
            first, project_ref[...], preferred_element_type=F32
        )

        @pl.when(block == 0)
        def _():
            scale_ref[at, :] = jnp.broadcast_to(scale, (BLOCK, 128))

        @pl.when(tile == count // 2)
        def _():
            back.middle()

    keep.start()
    loads.wait(1, 4)
    fixed_refs = (starts_ref, cosine_ref, sine_ref, query_gain_ref, key_gain_ref)
    saved_refs = (query_ref, key_ref, value_ref, log_ref)

    @pl.loop(0, 2)
    def _(seq):
        def between(turn):
            @pl.when(seq == 0)
            def _():
                if turn == 0:
                    gather.relay(0, 1)
                elif turn == 1:
                    back.late()
                elif turn == 2:
                    gather.relay(1, 2)
                else:
                    back.later()

            @pl.when(seq == 1)
            def _():
                if turn < 2:
                    gather.relay(turn + 2, turn + 3)

        attend_sequence(
            core, seq, most, projected_ref, fixed_refs, mixed_ref, saved_refs, between
        )

    for tile in range(count - 2, count):
        store(tile).wait()
    gather.close()
    back.close()
    gate.wait()
    keep.wait()


def front_call(whole, w_project, gain, fixed_args, most, cotangent, w_down, w_gate, number):
    starts, cosine, sine, query_gain, key_gain = fixed_args
    rows, width = cotangent.shape
    length = cosine.shape[1]
    depth = query_gain.shape[1]
    columns = w_project.shape[1]
    heads = columns // depth - 2
    outs = (
        shape((4, rows, 2 * width)),
        shape((4, rows, columns), F32),
        shape((rows, 128), F32),
        shape((4, rows, heads * depth)),
        shape((2, length, heads * depth)),
        shape((2, length, depth)),
        shape((2, length, depth)),
        shape((2, heads, length, 1), F32),
        shape((4, rows, 2 * width)),
        shape((w_down.shape[0] // 2, 2 * width)),
        shape((width // 4, w_gate.shape[1] // 2)),
    )
    return pl.pallas_call(
        lambda *refs: front_kernel(most, *refs),
        out_shape=outs,
        in_specs=[IN_ANY] + [IN_VMEM] * 5 + [IN_ANY] * 5,
        out_specs=[IN_ANY] * 2 + [IN_VMEM] * 6 + [IN_ANY] * 3,
        scratch_shapes=gather_scratch(rows, width)
        + wire_scratch(GATHER_KINDS + SHARE_KINDS + 1, width // CHUNK)
        + [
            pltpu.SemaphoreType.DMA((1,)),
            pltpu.VMEM((2, BLOCK, 2 * width), B16),
            pltpu.VMEM((2, BLOCK, 2 * width), B16),
            pltpu.SemaphoreType.DMA((2, 2)),
        ]
        + load_scratch((w_down, starts, cosine, sine))
        + [pltpu.VMEM((4, rows, columns), F32), pltpu.SemaphoreType.DMA],
        compiler_params=remote_params(number),
        cost_estimate=cost(16 * rows * width * columns, 64 * rows * width),
    )(whole, w_project, gain, query_gain, key_gain, cotangent, starts, cosine, sine, w_down, w_gate)


def branch_kernel(
    rows_in_ref,
    weight_in_ref,
    input_in_ref,
    up_in_ref,
    gate_in_ref,
    quarter_ref,
    residual_ref,
    whole_ref,
    up_ref,
    gate_ref,
    *scratch,
):
    bufs = scratch[:7]
    own, gather_sem, send_sems, recv_sems, up_sem = scratch[7:12]
    held, load_sem, gate_sem = scratch[12:17], scratch[17], scratch[18]
    rows_ref, weight_ref, input_ref, up_held, gate_held = held
    loads = Loads(
        (rows_in_ref, weight_in_ref, input_in_ref, up_in_ref, gate_in_ref), held, load_sem
    )
    loads.start()
    width = input_ref.shape[1]
    greet(neighbours() + planes())
    wires = Wires(send_sems, recv_sems)
    reduce = Reduce(wires, rows_ref, weight_ref, False, bufs)
    gather = Gather(wires, REDUCE_KINDS, whole_ref, own, gather_sem, 2)
    up = Share(
        wires, REDUCE_KINDS + GATHER_KINDS, (up_in_ref,), up_ref, True, up_sem, (up_held,)
    )
    gate = Spread(
        wires,
        REDUCE_KINDS + GATHER_KINDS + SHARE_KINDS,
        gate_held,
        gate_ref,
        gate_sem,
        quarter_ref,
    )
    loads.wait(0, 2)

    def between():
        loads.wait(2, 5)
        up.start()
        gate.start()

    reduce.start((between, gate.late))
    up.middle()
    reduce.middle()
    gate.later()

    @pl.loop(0, width // CHUNK)
    def _(chunk):
        at = lanes(chunk, 0, width)
        residual = input_ref[:, at].astype(F32) + reduce.total(chunk)
        residual_ref[:, at] = residual
        own[chunk] = residual.astype(B16)
        gather.send(chunk)

    up.late()
    gather.relay()
    up.later()
    gather.close()
    up.close()
    gate.close()
    reduce.close()


def branch_call(rows, weight, inputs, w_up, w_gate, quarter, number):
    height, width = inputs.shape
    count = width // CHUNK
    loaded = (rows, weight, inputs, w_up, w_gate)
    return pl.pallas_call(
        branch_kernel,
        out_shape=(
            shape((height, width), F32),
            shape((4, height, 2 * width)),
            shape((2 * width, w_up.shape[1] // 2)),
            shape((2 * width, w_gate.shape[1] // 2)),
        ),
        in_specs=[IN_ANY] * 6,
        out_specs=(IN_VMEM, IN_ANY, IN_ANY, IN_ANY),
        scratch_shapes=reduce_scratch(height, width)
        + gather_scratch(height, width)
        + wire_scratch(REDUCE_KINDS + GATHER_KINDS + 2 * SHARE_KINDS, count)
        + [pltpu.SemaphoreType.DMA((1,))]
        + load_scratch(loaded)
        + [pltpu.SemaphoreType.DMA((2,))],
        compiler_params=remote_params(number),
        cost_estimate=cost(16 * height * rows.shape[2] * width, 64 * height * width),
    )(*loaded, quarter)


def units_kernel(
    whole_ref, grad_ref, gates_ref, uppers_ref, back_ref, gain_ref, second_ref, hidden_ref, unit_ref, scale_ref, stats_ref
):
    units = hidden_ref.shape[1]
    value = whole_ref[...].astype(F32)
    scale = lax.rsqrt(jnp.mean(value * value, axis=1, keepdims=True) + EPS)
    second = (value * scale * gain_ref[...]).astype(B16)
    second_ref[...] = second
    scale_ref[...] = jnp.broadcast_to(scale, scale_ref.shape)
    total = jnp.zeros((value.shape[0], 1), F32)
    for low in range(0, units, CHUNK):
        at = slice(low, low + CHUNK)
        beside = slice(units + low, units + low + CHUNK)
        gate = jnp.dot(second, gates_ref[:, at], preferred_element_type=F32)
        upper = jnp.dot(second, uppers_ref[:, at], preferred_element_type=F32)
        hidden_grad = rows_dot(grad_ref[...], back_ref[at, :])
        sigma = jax.nn.sigmoid(gate)
        passed = gate * sigma
        hidden_ref[:, at] = (passed * upper).astype(B16)
        gate_grad = (hidden_grad * upper * (sigma + passed * (1.0 - sigma))).astype(B16)
        up_grad = (hidden_grad * passed).astype(B16)
        unit_ref[:, at] = gate_grad
        unit_ref[:, beside] = up_grad
        total += jnp.sum(
            gate_grad.astype(F32) * gate + up_grad.astype(F32) * upper, axis=1, keepdims=True
        )
    stats_ref[...] = jnp.zeros_like(stats_ref)
    for tile in range(stats_ref.shape[0]):
        put_stats(stats_ref, tile, total[tile * BLOCK : (tile + 1) * BLOCK])


def units_call(whole, grad, w_gates, w_uppers, w_back, gain):
    tokens, width = whole.shape
    units = w_back.shape[0]
    size = 2 * BLOCK
    tiles = tokens // size

    def tile(columns):
        return pl.BlockSpec((size, columns), lambda i: (i, 0))

    def all_of(item):
        return pl.BlockSpec(item.shape, lambda i: (0, 0))

    return pl.pallas_call(
        units_kernel,
        out_shape=(
            shape((tokens, width)),
            shape((tokens, units)),
            shape((tokens, 2 * units)),
            shape((tokens, 128), F32),
            shape((2 * tiles, 8, 128), F32),
        ),
        grid=(tiles,),
        in_specs=[tile(width), tile(width)]
        + [all_of(item) for item in (w_gates, w_uppers, w_back, gain)],
        out_specs=(
            tile(width),
            tile(units),
            tile(2 * units),
            tile(128),
            pl.BlockSpec((2, 8, 128), lambda i: (i, 0, 0)),
        ),
        compiler_params=pltpu.CompilerParams(vmem_limit_bytes=VMEM_MOST),
        cost_estimate=cost(6 * tokens * width * units, 20 * tokens * width // 2),
    )(whole, grad, w_gates, w_uppers, w_back, gain)


class Loads:
    def __init__(self, sources, targets, sems):
        self.copies = [
            pltpu.make_async_copy(source, target, sems.at[index])
            for index, (source, target) in enumerate(zip(sources, targets))
        ]

    def start(self):
        for copy in self.copies:
            copy.start()

    def wait(self, low, high):
        for copy in self.copies[low:high]:
            copy.wait()


def load_scratch(items):
    return [pltpu.VMEM(item.shape, item.dtype) for item in items] + [
        pltpu.SemaphoreType.DMA((len(items),))
    ]


class Stats:
    def __init__(self, wires, base, ref, recv):
        self.ref, self.recv = ref, recv
        side, across, core = neighbours()
        self.hops = (
            lambda: wires.copy(base, 0, ref.at[4:8], recv.at[0:4], core),
            lambda: wires.copy(base, 1, ref.at[2:4], recv.at[4:6], across),
            lambda: wires.copy(base, 2, ref.at[0:2], recv.at[6:8], side),
        )
        self.spans = ((4, 0), (2, 4), (2, 6))

    def start(self, hop):
        self.hops[hop]().start()

    def finish(self, hop):
        self.hops[hop]().wait()
        size, at = self.spans[hop]
        self.ref[0:size] = self.ref[0:size] + self.recv[at : at + size]

    def step(self, hop):
        self.finish(hop)
        self.start(hop + 1)


def pull_columns(stats_ref, scale_ref, column_ref, width):
    for part in range(scale_ref.shape[0] // 128):
        at = slice(part * 128, (part + 1) * 128)
        scale = scale_ref[at, :]
        column_ref[at, :] = (
            stand(stats_ref[part // 2, part % 2 : part % 2 + 1, :]) * scale * scale / (2 * width)
        )


def pulled(reduce, chunk, refs, column_ref):
    scale_ref, value_ref, gain_ref, base_ref = refs
    at = lanes(chunk, 0, value_ref.shape[1])
    upstream = reduce.total(chunk)
    value = value_ref[:, at].astype(F32)
    scale = scale_ref[:, 0:1]
    back = scale * gain_ref[:, at] * upstream - value * column_ref[:, 0:1]
    return at, base_ref[:, at].astype(F32) + back, upstream * value * scale


def tile_columns(tile):
    return pl.ds(pl.multiple_of(tile * BLOCK, BLOCK), BLOCK)


SPLIT = 512


def middle_kernel(
    rows_in_ref,
    gates_in_ref,
    uppers_in_ref,
    value_in_ref,
    base_in_ref,
    hidden_in_ref,
    scale_in_ref,
    stats_in_ref,
    gain_ref,
    grad_ref,
    second_ref,
    result_ref,
    gain_grad_ref,
    whole_ref,
    rest_ref,
    *refs,
):
    ends, scratch = refs[:4], refs[4:]
    bufs = scratch[:7]
    stats_ref, stats_recv, column_ref, send_sems, recv_sems, own, gather_sem = scratch[7:14]
    stream, stream_sem, stage, stage_sem = scratch[14:18]
    down_tiles, down_recv, made_tiles, made_recv = scratch[18:22]
    weight_ref, hidden_ref, rows_ref, value_ref, base_ref, scale_ref = scratch[22:28]
    load_sem = scratch[28]
    rows, width = value_ref.shape
    columns = rows_ref.shape[2]
    units = gates_in_ref.shape[1]
    loads = Loads(
        (
            hidden_in_ref,
            rows_in_ref,
            gates_in_ref,
            uppers_in_ref,
            scale_in_ref.at[pl.ds(0, rows)],
            value_in_ref,
            base_in_ref,
        ),
        (
            hidden_ref,
            rows_ref,
            weight_ref.at[:, :units],
            weight_ref.at[:, units:],
            scale_ref,
            value_ref,
            base_ref,
        ),
        load_sem,
    )

    def fetch(ref, step, tile):
        slot = lax.rem(step, 2)
        return pltpu.make_async_copy(
            ref.at[:, :, tile_columns(tile)], stream.at[slot], stream_sem.at[slot]
        )

    fetch(grad_ref, 0, turn_tile(0)).start()
    loads.start()
    stats_ref[...] = stats_in_ref[...]
    greet(neighbours() + planes())
    wires = Wires(send_sems, recv_sems)
    base = REDUCE_KINDS + 1 + GATHER_KINDS
    down = Fold(wires, base, down_tiles, (down_recv,), ends[0], ends[1])
    made = Fold(wires, base + FOLD_KINDS, made_tiles, (made_recv,), ends[2], ends[3])
    stats = Stats(wires, REDUCE_KINDS, stats_ref, stats_recv)
    def make_down(step):
        @pl.when(step < 7)
        def _():
            fetch(grad_ref, step + 1, turn_tile(step + 1)).start()

        fetch(grad_ref, step, turn_tile(step)).wait()
        left = stream[lax.rem(step, 2)].reshape(4 * rows, BLOCK)
        down_tiles[turn_tile(step)] = weight_grad(
            left, hidden_ref[...].reshape(4 * rows, units)
        ).astype(B16)

    stats.start(0)
    loads.wait(0, 1)
    make_tiles(down, make_down, 0, 2)
    reduce = Reduce(wires, rows_ref, weight_ref, True, bufs)
    loads.wait(1, 4)

    def first_part():
        stats.step(0)
        make_tiles(down, make_down, 2, 4)

    def second_part():
        down.step()
        stats.step(1)
        make_tiles(down, make_down, 4, 6)

    reduce.start((first_part, second_part))
    reduce.middle()

    def store(step):
        slot = lax.rem(step, 2)
        return pltpu.make_async_copy(
            stage.at[slot], rest_ref.at[turn_tile(step)], stage_sem.at[slot]
        )

    def make(step):
        slot = lax.rem(step, 2)

        @pl.when(step < 7)
        def _():
            fetch(second_ref, step + 1, turn_tile(step + 1)).start()

        fetch(second_ref, step, turn_tile(step)).wait()

        @pl.when(step >= 2)
        def _():
            store(step - 2).wait()

        left = stream[slot].reshape(4 * rows, BLOCK)
        flat = rows_ref[...].reshape(4 * rows, columns)
        made.tiles[turn_tile(step)] = weight_grad(left, flat[:, :SPLIT]).astype(B16)
        stage[slot] = weight_grad(left, flat[:, SPLIT:]).astype(B16)
        store(step).start()

    loads.wait(4, 7)
    stats.finish(2)
    pull_columns(stats_ref, scale_ref, column_ref, width)
    gather = Gather(wires, REDUCE_KINDS + 1, whole_ref, own, gather_sem, 2)

    def finish_chunks(low, high):
        @pl.loop(low, high)
        def _(chunk):
            at, result, share = pulled(
                reduce, chunk, (scale_ref, value_ref, gain_ref, base_ref), column_ref
            )
            result_ref[:, at] = result
            own[chunk] = result.astype(B16)
            gather.send(chunk)
            gain_grad_ref[:, at] = jnp.sum(share, axis=0, keepdims=True)

    finish_chunks(0, 2)
    make_tiles(down, make_down, 6, 8)
    fetch(second_ref, 0, turn_tile(0)).start()
    make_tiles(made, make, 0, 4)
    finish_chunks(2, width // CHUNK)
    down.middle()
    make_tiles(made, make, 4, 8)
    for step in (6, 7):
        store(step).wait()
    gather.relay(0, 3)
    down.late()
    made.step()
    gather.relay(3)
    made.middle()
    gather.close()
    made.late()
    down.close()
    made.close()
    reduce.close()


def middle_call(
    rows, w_gates, w_uppers, stats, scale, value, gain, base, hidden, grad, second, number
):
    height, width = value.shape
    count = width // CHUNK
    columns = rows.shape[2]
    quarter, units = width // 4, hidden.shape[2]
    sizes = (units, SPLIT)
    ends, tiles = [], []
    for size in sizes:
        ends += [shape((quarter, size), F32), shape((quarter, size))]
        tiles += [pltpu.VMEM((8, quarter, size), B16)] + fold_scratch(quarter, size)
    loaded = (rows, w_gates, w_uppers, value, base, hidden, scale)
    return pl.pallas_call(
        middle_kernel,
        out_shape=[
            shape((height, width), F32),
            shape((1, width), F32),
            shape((4, height, 2 * width)),
            shape((8, quarter, columns - SPLIT)),
        ]
        + ends,
        in_specs=[IN_ANY] * 7 + [IN_VMEM] * 2 + [IN_ANY] * 2,
        out_specs=[IN_VMEM] * 2 + [IN_ANY] * 2 + [IN_VMEM, IN_ANY] * 2,
        scratch_shapes=reduce_scratch(height, width)
        + [
            pltpu.VMEM((8, 8, 128), F32),
            pltpu.VMEM((8, 8, 128), F32),
            pltpu.VMEM((height, 128), F32),
        ]
        + wire_scratch(REDUCE_KINDS + 1 + GATHER_KINDS + 2 * FOLD_KINDS, count)
        + gather_scratch(height, width)
        + [
            pltpu.VMEM((2, 4, height, BLOCK), B16),
            pltpu.SemaphoreType.DMA((2,)),
            pltpu.VMEM((2, quarter, columns - SPLIT), B16),
            pltpu.SemaphoreType.DMA((2,)),
        ]
        + tiles
        + [pltpu.VMEM((2 * width, columns), B16)]
        + load_scratch((hidden, rows, value, base))[:-1]
        + [pltpu.VMEM((height, 128), F32)]
        + [pltpu.SemaphoreType.DMA((len(loaded),))],
        compiler_params=remote_params(number),
        cost_estimate=cost(48 * height * units * width, 64 * height * width),
    )(*loaded, stats, gain, grad, second)


def last_kernel(
    rows_in_ref,
    weight_in_ref,
    value_in_ref,
    base_in_ref,
    stats_in_ref,
    scale_ref,
    gain_ref,
    mlp_ref,
    heads_ref,
    out_in_ref,
    project_in_ref,
    result_ref,
    totals_ref,
    out_mine_ref,
    out_theirs_ref,
    project_mine_ref,
    project_theirs_ref,
    *scratch,
):
    bufs = scratch[:7]
    stats_ref, stats_recv, column_ref, send_sems, recv_sems = scratch[7:12]
    out_ref, project_ref, sums_ref, sums_recv, load_sem = scratch[12:17]
    out_bufs, project_bufs = scratch[17:18], scratch[18:19]
    rows_ref, weight_ref, value_ref, base_ref = scratch[19:23]
    rows, width = value_ref.shape
    loads = Loads(
        (project_in_ref, weight_in_ref, rows_in_ref, value_in_ref, base_in_ref, out_in_ref),
        (project_ref, weight_ref, rows_ref, value_ref, base_ref, out_ref),
        load_sem,
    )
    loads.start()
    stats_ref[...] = stats_in_ref[...]
    sums_ref[...] = jnp.zeros_like(sums_ref)
    for row in range(8):
        sums_ref[8, row : row + 1, :] = mlp_ref[:, row * 128 : (row + 1) * 128]
    sums_ref[9, 0:2, :] = heads_ref[0, 0:2, :] + heads_ref[1, 0:2, :]
    greet(neighbours() + planes())
    wires = Wires(send_sems, recv_sems)
    base = REDUCE_KINDS + 1
    out = Fold(wires, base, out_ref, out_bufs, out_mine_ref, out_theirs_ref, out_in_ref)
    project = Fold(
        wires,
        base + FOLD_KINDS,
        project_ref,
        project_bufs,
        project_mine_ref,
        project_theirs_ref,
        project_in_ref,
    )
    stats = Stats(wires, REDUCE_KINDS, stats_ref, stats_recv)
    stats.start(0)
    out.start()
    loads.wait(0, 2)

    @pl.loop(0, 8)
    def _(tile):
        share = jnp.sum(
            project_ref[tile].astype(F32) * weight_ref[tile_columns(tile), :].astype(F32),
            axis=1,
            keepdims=True,
        )
        sums_ref[tile, 0:1, :] = lie(share[:128])
        sums_ref[tile, 1:2, :] = lie(share[128:])

    side_device, across, core = neighbours()
    near, mirror = planes()

    def hop(index):
        slot, device = ((0, core), (1, across), (2, near), (3, mirror), (2, near))[index]
        kind, chunk = divmod(index, 4)
        return wires.copy(
            base + 2 * FOLD_KINDS + kind, chunk, sums_ref, sums_recv.at[slot], device
        )

    def add(slot):
        sums_ref[...] = sums_ref[...] + sums_recv[slot]

    reduce = Reduce(wires, rows_ref, weight_ref, True, bufs)
    loads.wait(2, 3)
    hop(0).start()
    reduce.give(0)
    hop(0).wait()
    add(0)
    hop(1).start()
    stats.step(0)

    def after_two():
        hop(1).wait()
        add(1)

        @pl.when(jnp.logical_not(inner()))
        def _():
            hop(2).start()

        project.start()
        stats.step(1)

    reduce.rest((after_two, lambda: None))
    loads.wait(3, 6)
    out.step()
    ends_line = jnp.logical_not(inner())

    @pl.when(inner())
    def _():
        hop(2).wait_recv()
        add(2)
        hop(3).start()

    out.middle()
    reduce.middle()
    stats.finish(2)
    pull_columns(stats_ref, scale_ref, column_ref, width)

    @pl.when(inner())
    def _():
        hop(3).wait()
        add(3)
        hop(4).start()

    project.step()
    project.middle()

    @pl.loop(0, width // CHUNK)
    def _(chunk):
        at, result, _ = pulled(
            reduce, chunk, (scale_ref, value_ref, gain_ref, base_ref), column_ref
        )
        result_ref[:, at] = result.astype(B16)

    @pl.when(inner())
    def _():
        hop(4).wait_send()

    @pl.when(ends_line)
    def _():
        hop(2).wait_send()
        hop(4).wait_recv()
        sums_ref[...] = sums_recv[2]

    move = wires.copy(base + 2 * FOLD_KINDS + 1, 1, sums_ref, sums_recv.at[4], side_device)
    move.start()
    out.late()
    project.late()
    move.wait()
    totals_ref[0:4] = sums_ref[0:4] + sums_recv[4, 4:8]
    totals_ref[4:8] = sums_ref[4:8] + sums_recv[4, 0:4]
    totals_ref[8] = sums_ref[8]
    totals_ref[9] = sums_recv[4, 8]
    totals_ref[10] = sums_ref[9] + sums_recv[4, 9]
    project.close()
    out.close()
    reduce.close()


def last_call(
    rows, weight, stats, scale, value, gain, base, mlp_part, head_parts, out, project, number
):
    height, width = value.shape
    count = width // CHUNK
    quarter, branch = out.shape[1:]
    columns = rows.shape[2]
    return pl.pallas_call(
        last_kernel,
        out_shape=(
            shape((height, width)),
            shape((11, 8, 128), F32),
            shape((quarter, branch), F32),
            shape((quarter, branch)),
            shape((quarter, columns), F32),
            shape((quarter, columns)),
        ),
        in_specs=[IN_ANY] * 4 + [IN_VMEM] * 5 + [IN_ANY] * 2,
        out_specs=(IN_VMEM, IN_VMEM) + (IN_VMEM, IN_ANY) * 2,
        scratch_shapes=reduce_scratch(height, width)
        + [
            pltpu.VMEM((8, 8, 128), F32),
            pltpu.VMEM((8, 8, 128), F32),
            pltpu.VMEM((height, 128), F32),
        ]
        + wire_scratch(REDUCE_KINDS + 1 + 2 * FOLD_KINDS + 2, count)
        + [
            pltpu.VMEM((8, quarter, branch), B16),
            pltpu.VMEM((8, quarter, columns), B16),
            pltpu.VMEM((10, 8, 128), F32),
            pltpu.VMEM((5, 10, 8, 128), F32),
            pltpu.SemaphoreType.DMA((6,)),
        ]
        + fold_scratch(quarter, branch)
        + fold_scratch(quarter, columns)
        + load_scratch((rows, weight, value, base))[:4],
        compiler_params=remote_params(number),
        cost_estimate=cost(32 * height * columns * width, 64 * height * width),
    )(rows, weight, value, base, stats, scale, gain, mlp_part, head_parts, out, project)


def back_kernel(
    most,
    query_gain_ref,
    key_gain_ref,
    *refs,
):
    operands, refs = refs[:13], refs[13:]
    rest_ref, whole_ref, first_ref = refs[:3]
    output_ref, result_ref, stats_ref, gains_ref, out_ref, project_ref = refs[3:9]
    ends, scratch = refs[9:11], refs[11:]
    bufs = scratch[:7]
    key_acc, value_acc, send_sems, recv_sems, rest_sem = scratch[7:12]
    tiles, fold_recv = scratch[12:14]
    held, load_sem = scratch[14:27], scratch[27]
    upstream, acc, stream, stream_sem, stage, stage_sem = scratch[28:]
    hidden_ref, down_ref, branch_ref, mixed_ref, starts_ref, cosine_ref, sine_ref = held[:7]
    projected_ref, query_ref, key_ref, value_ref, log_ref, residual_ref = held[7:]
    attend_loads = Loads(operands, held, load_sem)
    attend_loads.start()
    width = residual_ref.shape[1]
    rows = residual_ref.shape[0]

    def fetch(ref, tile):
        slot = lax.rem(tile, 2)
        return pltpu.make_async_copy(
            ref.at[:, :, tile_columns(tile)], stream.at[slot], stream_sem.at[slot]
        )

    def each_tile(ref, target, right, work):
        columns = target.shape[2]

        def store(tile):
            slot = lax.rem(tile, 2)
            return pltpu.make_async_copy(
                stage.at[slot, :, :columns], target.at[tile], stage_sem.at[slot]
            )

        @pl.loop(0, 8)
        def _(tile):
            @pl.when(tile < 7)
            def _():
                fetch(ref, tile + 1).start()

            fetch(ref, tile).wait()

            @pl.when(tile >= 2)
            def _():
                store(tile - 2).wait()

            left = stream[lax.rem(tile, 2)].reshape(4 * rows, BLOCK)
            work(tile, left)
            stage[lax.rem(tile, 2), :, :columns] = weight_grad(
                left, right[...].reshape(4 * rows, columns)
            ).astype(B16)
            store(tile).start()

        for tile in (6, 7):
            store(tile).wait()

    fetch(whole_ref, 0).start()
    core = lax.rem(lax.axis_index("tx"), 2)
    load = pltpu.make_async_copy(rest_ref, tiles, rest_sem)
    load.start()
    greet(neighbours() + planes())
    wires = Wires(send_sems, recv_sems)
    fold = Fold(wires, REDUCE_KINDS, tiles, (fold_recv,), ends[0], ends[1], rest_ref)
    fold.start()
    reduce = Reduce(wires, hidden_ref, down_ref, False, bufs)
    attend_loads.wait(0, 2)
    reduce.start()
    attend_loads.wait(2, 13)
    load.wait()
    acc[...] = jnp.zeros_like(acc)

    def branch_work(tile, left):
        acc[...] += rows_dot(left, branch_ref[:, tile_columns(tile)])

    each_tile(whole_ref, out_ref, mixed_ref, branch_work)
    fetch(first_ref, 0).start()
    upstream[...] = acc[...].astype(B16).reshape(upstream.shape)
    fold.step()
    stats_ref[...] = jnp.zeros_like(stats_ref)
    fixed_refs = (starts_ref, cosine_ref, sine_ref, query_gain_ref, key_gain_ref)
    saved_refs = (query_ref, key_ref, value_ref, log_ref)

    @pl.loop(0, 2)
    def _(seq):
        attend_sequence_back(
            core,
            seq,
            most,
            projected_ref,
            upstream,
            fixed_refs,
            saved_refs,
            result_ref,
            stats_ref,
            gains_ref,
            (acc, key_acc, value_acc),
        )

        @pl.when(seq == 0)
        def _():
            reduce.middle()

    fold.middle()

    each_tile(first_ref, project_ref, result_ref, lambda tile, left: None)


    @pl.loop(0, width // CHUNK)
    def _(chunk):
        at = lanes(chunk, 0, width)
        output_ref[:, at] = (residual_ref[:, at] + reduce.total(chunk)).astype(B16)

    fold.late()
    fold.close()
    reduce.close()


def back_call(
    whole, first, w_branch, mixed, hidden, w_back, residual, fixed_args, projected, saved, rest, most, number
):
    height, width = residual.shape
    _, cosine, _, query_gain, _ = fixed_args
    depth = query_gain.shape[1]
    length = cosine.shape[1]
    columns = projected.shape[2]
    heads = columns // depth - 2
    quarter, columns_left = rest.shape[1:]
    loaded = (hidden, w_back, w_branch, mixed) + fixed_args[:3] + (projected,) + saved + (residual,)
    return pl.pallas_call(
        lambda *refs: back_kernel(most, *refs),
        out_shape=(
            shape((height, width)),
            shape((4, height, columns)),
            shape((8, 8, 128), F32),
            shape((2, 8, depth), F32),
            shape((8, quarter, heads * depth)),
            shape((8, quarter, columns)),
        )
        + (shape((quarter, columns_left), F32), shape((quarter, columns_left))),
        in_specs=[IN_VMEM] * 2 + [IN_ANY] * 16,
        out_specs=[IN_VMEM] * 4 + [IN_ANY] * 2 + [IN_VMEM, IN_ANY],
        scratch_shapes=reduce_scratch(height, width)
        + [
            pltpu.VMEM((length, depth), F32),
            pltpu.VMEM((length, depth), F32),
        ]
        + wire_scratch(REDUCE_KINDS + FOLD_KINDS, width // CHUNK)
        + [pltpu.SemaphoreType.DMA, pltpu.VMEM(rest.shape, B16)]
        + fold_scratch(quarter, columns_left)
        + load_scratch(loaded)
        + [
            pltpu.VMEM((4, height, heads * depth), B16),
            pltpu.VMEM((4 * height, heads * depth), F32),
            pltpu.VMEM((2, 4, height, BLOCK), B16),
            pltpu.SemaphoreType.DMA((2,)),
            pltpu.VMEM((2, quarter, columns), B16),
            pltpu.SemaphoreType.DMA((2,)),
        ],
        compiler_params=remote_params(number),
        cost_estimate=cost(16 * height * hidden.shape[2] * width, 64 * height * width),
    )(*fixed_args[3:], *loaded, rest, whole, first)


def finish_kernel(place_ref, *refs):
    downs, both, out, project = refs[0:2], refs[2:6], refs[6:8], refs[8:10]
    totals_ref, gain_ref = refs[10:12]
    moved, refs = refs[12:14], refs[14:]
    query_ref, key_ref, value_ref, out_ref, gate_ref, up_ref, down_ref = refs[:7]
    attn_ref, mlp_ref, query_gain_ref, key_gain_ref = refs[7:11]
    for source, target in zip(moved, refs[11:]):
        target[...] = source[...]
    query_gain_ref[...] = totals_ref[10, 0:1]
    key_gain_ref[...] = totals_ref[10, 1:2]
    first = place_ref[0] == 0

    def ordered(mine, theirs):
        theirs = theirs.astype(F32)
        return jnp.where(first, mine, theirs), jnp.where(first, theirs, mine)

    def put(target, at, mine, theirs):
        half = target.shape[1] // 2
        low, high = ordered(mine, theirs)
        target[:, at : at + mine.shape[1]] = low
        target[:, half + at : half + at + mine.shape[1]] = high

    def put_turned(target, at, mine, theirs):
        half = target.shape[0] // 2
        low, high = ordered(mine, theirs)
        target[at : at + mine.shape[1], :] = low.T
        target[half + at : half + at + mine.shape[1], :] = high.T

    put_turned(down_ref, 0, downs[0][...], downs[1][...])
    put_turned(out_ref, 0, out[0][...], out[1][...])
    at = 0
    for target in (query_ref, key_ref, value_ref):
        size = target.shape[1] // 2
        put(target, 0, project[0][:, at : at + size], project[1][:, at : at + size])
        at += size
    units = gate_ref.shape[1] // 2
    at = 0
    for index in (0, 2):
        low = 0
        while low < both[index].shape[1]:
            size = min(both[index].shape[1] - low, units - at % units)
            put(
                gate_ref if at < units else up_ref,
                at % units,
                both[index][:, low : low + size],
                both[index + 1][:, low : low + size],
            )
            low += size
            at += size
    mine = jnp.concatenate([totals_ref[tile, 0:2] for tile in range(4)], axis=0)
    theirs = jnp.concatenate([totals_ref[tile, 0:2] for tile in range(4, 8)], axis=0)
    low, high = ordered(mine / gain_ref[0:8], theirs / gain_ref[8:16])
    attn_ref[0:8], attn_ref[8:16] = low, high
    low, high = ordered(totals_ref[8], totals_ref[9])
    mlp_ref[0:8], mlp_ref[8:16] = low, high


def finish_call(place, parts, totals, gain, moved, sizes):
    quarter = parts[0].shape[0]
    queries, keys, branch, units = sizes
    return pl.pallas_call(
        finish_kernel,
        out_shape=(
            shape((quarter, queries), F32),
            shape((quarter, keys), F32),
            shape((quarter, keys), F32),
            shape((branch, quarter), F32),
            shape((quarter, units), F32),
            shape((quarter, units), F32),
            shape((units, quarter), F32),
            shape((16, 128), F32),
            shape((16, 128), F32),
            shape((1, 128), F32),
            shape((1, 128), F32),
        )
        + tuple(shape(item.shape, item.dtype) for item in moved),
        in_specs=[pl.BlockSpec(memory_space=pltpu.SMEM)] + [IN_VMEM] * (len(parts) + 4),
        out_specs=[IN_VMEM] * 13,
        compiler_params=pltpu.CompilerParams(vmem_limit_bytes=VMEM_MOST),
        cost_estimate=cost(0, 16 * 1024 * 1024),
    )(place, *parts, totals, gain, *moved)


def plane_device(
    tokens,
    seg_ids,
    w_query,
    w_key,
    w_value,
    w_out,
    w_gate,
    w_up,
    w_down,
    attn_gain,
    mlp_gain,
    query_gain,
    key_gain,
    cotangent,
):
    depth = query_gain.shape[0]
    most = seg_ids.shape[1] // 2
    rows, width = tokens.shape
    head_width = w_query.shape[1] // 2
    kv_width = w_key.shape[1] // 2
    units = w_gate.shape[1] // 2

    rate = np.float64(THETA) ** (-np.arange(depth // 2) * 2.0 / depth)
    rate = jnp.asarray(np.concatenate([rate, rate])[None].astype(np.float32))
    attn_row, mlp_row, starts, cosine, sine, token_whole, w_project, w_branch = open_call(
        tokens, w_query, w_key, w_value, w_out, attn_gain[None], mlp_gain[None], seg_ids, rate, 0
    )
    fixed_args = (starts, cosine, sine, query_gain[None], key_gain[None])
    (
        first,
        projected,
        first_scale,
        mixed,
        query,
        keys,
        values,
        logs,
        grad_whole,
        w_back,
        gate_quarter,
    ) = front_call(
        token_whole, w_project, attn_row, fixed_args, most, cotangent, w_down, w_gate, 1
    )
    residual, residual_whole, w_uppers, w_gates = branch_call(
        mixed, w_branch, tokens, w_up, w_gate, gate_quarter, 2
    )
    flat = (4 * rows, 2 * width)
    grad_flat = grad_whole.reshape(flat)
    second, hidden, unit_grads, second_scale, unit_stats = units_call(
        residual_whole.reshape(flat), grad_flat, w_gates, w_uppers, w_back, mlp_row
    )
    (
        residual_grad,
        mlp_gain_part,
        branch_whole,
        rest_tiles,
        *ends,
    ) = middle_call(
        unit_grads.reshape(4, rows, 2 * units),
        w_gates,
        w_uppers,
        unit_stats,
        second_scale,
        residual,
        mlp_gain[None],
        cotangent,
        hidden.reshape(4, rows, units),
        grad_whole,
        second.reshape(4, rows, 2 * width),
        3,
    )
    output, proj_grads, proj_stats, gain_parts, out_tiles, project_tiles, *rest_ends = back_call(
        branch_whole,
        first,
        w_branch,
        mixed,
        hidden.reshape(4, rows, units),
        w_back,
        residual,
        fixed_args,
        projected,
        (query, keys, values, logs),
        rest_tiles,
        most,
        4,
    )
    input_grad, totals, out_mine, out_theirs, project_mine, project_theirs = last_call(
        proj_grads,
        w_project,
        proj_stats,
        first_scale,
        tokens,
        attn_gain[None],
        residual_grad,
        mlp_gain_part,
        gain_parts,
        out_tiles,
        project_tiles,
        5,
    )
    place = lax.axis_index("ty").reshape(1).astype(jnp.int32)
    (
        query_share,
        key_share,
        value_share,
        out_share,
        gate_share,
        up_share,
        down_share,
        attn_total,
        mlp_total,
        query_total,
        key_total,
        output,
        input_grad,
    ) = finish_call(
        place,
        (*ends, *rest_ends, out_mine, out_theirs, project_mine, project_theirs),
        totals,
        attn_row.reshape(16, 128),
        (output, input_grad),
        (2 * head_width, 2 * kv_width, 2 * head_width, 2 * units),
    )
    attn_total, mlp_total = attn_total.reshape(-1), mlp_total.reshape(-1)
    query_total, key_total = query_total.reshape(-1), key_total.reshape(-1)
    return (
        output,
        input_grad,
        query_share,
        key_share,
        value_share,
        out_share,
        gate_share,
        up_share,
        down_share,
        attn_total,
        mlp_total,
        query_total,
        key_total,
    )


def solution(mesh):
    placed = (
        P(("dp", "tx"), "ty"),
        P(("dp", "ty"), None),
        P("ty", "tx"),
        P("ty", "tx"),
        P("ty", "tx"),
        P("tx", "ty"),
        P("ty", "tx"),
        P("ty", "tx"),
        P("tx", "ty"),
        P("ty"),
        P("ty"),
        P(),
        P(),
        P(("dp", "tx"), "ty"),
    )
    return jax.shard_map(
        plane_device if fits(mesh) else general_device,
        mesh=mesh,
        in_specs=placed,
        out_specs=(
            P(("dp", "tx"), "ty"),
            P(("dp", "tx"), "ty"),
            P(("ty", "dp"), "tx"),
            P(("ty", "dp"), "tx"),
            P(("ty", "dp"), "tx"),
            P("tx", ("ty", "dp")),
            P(("ty", "dp"), "tx"),
            P(("ty", "dp"), "tx"),
            P("tx", ("ty", "dp")),
            P(),
            P(),
            P(),
            P(),
        ),
        check_vma=False,
    )
```

```python
import jax
import jax.numpy as jnp
import numpy as np
from jax import lax
from jax.experimental import pallas as pl
from jax.experimental.pallas import tpu as pltpu
from jax.sharding import PartitionSpec as P

EPS = 1e-06
THETA = 1000000.0
NEG = -1e30
F32 = jnp.float32
B16 = jnp.bfloat16
MESH = pl.DeviceIdType.MESH


def width_sum(value):
    return lax.psum(value, "ty")


def token_gather(rows):
    return lax.all_gather(rows, "tx", axis=0, tiled=True)


def branch_gather(rows):
    return lax.all_gather(rows, "ty", axis=0, tiled=True)


def width_reduce(whole, apply):
    return lax.psum_scatter(apply(whole), "ty", scatter_dimension=0, tiled=True)


def head_reduce(whole, apply):
    return lax.psum_scatter(
        apply(whole).astype(jnp.bfloat16), "tx", scatter_dimension=0, tiled=True
    ).astype(jnp.float32)


def forward_with(weight):
    return lambda rows: jnp.dot(rows, weight, preferred_element_type=F32)


def backward_with(weight):
    return lambda rows: lax.dot_general(
        rows, weight, (((1,), (1,)), ((), ())), preferred_element_type=F32
    )


def weight_grad(left, right):
    return lax.dot_general(left, right, (((0,), (0,)), ((), ())), preferred_element_type=F32)


def norm_scale(rows):
    width = rows.shape[1] * lax.axis_size("ty")
    return lax.rsqrt(width_sum(jnp.sum(rows * rows, axis=1)) / width + EPS)


def norm_back(rows, scale, gain, upstream):
    width = rows.shape[1] * lax.axis_size("ty")
    inner = width_sum(jnp.sum(upstream * gain * rows, axis=1))
    back = scale[:, None] * gain * upstream - rows * (scale**3 * inner / width)[:, None]
    gain_part = jnp.sum(upstream * rows * scale[:, None], axis=0)
    return (back, gain_part)


def widen(part):
    whole = jnp.zeros((part.shape[0] * lax.axis_size("ty"),), F32)
    return lax.dynamic_update_slice_in_dim(whole, part, lax.axis_index("ty") * part.shape[0], 0)


def doc_positions(seg):
    count = seg.shape[-1]
    index = jnp.arange(count, dtype=jnp.int32)
    edge = jnp.concatenate([jnp.ones((1,), dtype=jnp.bool_), seg[1:] != seg[:-1]])
    first = lax.cummax(jnp.where(edge, index, jnp.zeros_like(index)), axis=0)
    return index - first


def rotary(positions, depth):
    half = depth // 2
    freq = THETA ** (-jnp.arange(half, dtype=F32) * 2.0 / depth)
    angle = positions.astype(F32)[..., None] * freq
    return (jnp.cos(angle), jnp.sin(angle))


def turn(value, gain, cosine, sine):
    normed = value * lax.rsqrt(jnp.mean(value * value, axis=-1, keepdims=True) + EPS) * gain
    half = value.shape[-1] // 2
    first = normed[..., :half]
    second = normed[..., half:]
    return jnp.concatenate(
        [first * cosine - second * sine, second * cosine + first * sine], axis=-1
    )


def block_scores(part, seq_keys, seq_ids, start, scale):
    block = part.shape[0]
    length = seq_ids.shape[0]
    index = jnp.arange(length, dtype=jnp.int32)
    rows = start + jnp.arange(block, dtype=jnp.int32)
    row_ids = lax.dynamic_slice_in_dim(seq_ids, start, block, 0)
    mask = (seq_ids[None, :] == row_ids[:, None]) & (index[None, :] <= rows[:, None])
    scores = jnp.einsum("qkgd,mkd->kgqm", part, seq_keys, preferred_element_type=F32) * scale
    return jnp.where(mask[None, None], scores, NEG)


def attend_forward(query, keys, values, seg, block):
    seqs, length, heads, depth = query.shape
    kv_heads = keys.shape[2]
    groups = heads // kv_heads
    scale = depth ** (-0.5)
    count = length // block
    starts = jnp.arange(count, dtype=jnp.int32) * block

    def one_sequence(operands):
        seq_query, seq_keys, seq_values, seq_ids = operands
        blocks = seq_query.reshape(count, block, kv_heads, groups, depth)

        def one_block(inputs):
            part, start = inputs
            scores = block_scores(part, seq_keys, seq_ids, start, scale)
            top = jnp.max(scores, axis=-1)
            weights = jnp.exp(scores - top[..., None])
            total = jnp.sum(weights, axis=-1)
            probs = (weights / total[..., None]).astype(B16)
            mixed = jnp.einsum("kgqm,mkd->qkgd", probs, seq_values, preferred_element_type=F32)
            return (mixed, top + jnp.log(total))

        mixed, logs = lax.map(one_block, (blocks, starts))
        return (mixed.reshape(length, heads * depth), logs)

    return lax.map(one_sequence, (query, keys, values, seg))


def attend_backward(query, keys, values, seg, logs, grad_out, block):
    seqs, length, heads, depth = query.shape
    kv_heads = keys.shape[2]
    groups = heads // kv_heads
    scale = depth ** (-0.5)
    count = length // block
    starts = jnp.arange(count, dtype=jnp.int32) * block

    def one_sequence(operands):
        seq_query, seq_keys, seq_values, seq_ids, seq_logs, seq_grad = operands
        blocks = seq_query.reshape(count, block, kv_heads, groups, depth)
        grads = seq_grad.reshape(count, block, kv_heads, groups, depth)

        def one_block(carry, inputs):
            key_acc, value_acc = carry
            part, grad_part, log_part, start = inputs
            scores = block_scores(part, seq_keys, seq_ids, start, scale)
            probs = jnp.exp(scores - log_part[..., None])
            value_acc = value_acc + jnp.einsum(
                "kgqm,qkgd->mkd", probs.astype(B16), grad_part, preferred_element_type=F32
            )
            prob_grad = jnp.einsum(
                "qkgd,mkd->kgqm", grad_part, seq_values, preferred_element_type=F32
            )
            delta = jnp.sum(probs * prob_grad, axis=-1, keepdims=True)
            score_grad = (probs * (prob_grad - delta)).astype(B16)
            query_grad = (
                jnp.einsum("kgqm,mkd->qkgd", score_grad, seq_keys, preferred_element_type=F32)
                * scale
            )
            key_acc = (
                key_acc
                + jnp.einsum("kgqm,qkgd->mkd", score_grad, part, preferred_element_type=F32) * scale
            )
            return ((key_acc, value_acc), query_grad)

        zeros = jnp.zeros((length, kv_heads, depth), F32)
        (key_grad, value_grad), query_grad = lax.scan(
            one_block, (zeros, zeros), (blocks, grads, seq_logs, starts)
        )
        return (query_grad.reshape(length, heads, depth), key_grad, value_grad)

    return lax.map(one_sequence, (query, keys, values, seg, logs, grad_out))


def general_device(
    tokens,
    seg_ids,
    w_query,
    w_key,
    w_value,
    w_out,
    w_gate,
    w_up,
    w_down,
    attn_gain,
    mlp_gain,
    query_gain,
    key_gain,
    cotangent,
):
    seqs, length = seg_ids.shape
    depth = query_gain.shape[0]
    query_width = w_query.shape[1]
    key_width = w_key.shape[1]
    units = w_gate.shape[1]
    block = min(512, length)
    inputs = tokens.astype(F32)
    first_scale = norm_scale(inputs)
    first_normed = (inputs * first_scale[:, None] * attn_gain).astype(B16)
    first_whole = token_gather(first_normed)
    w_project = jnp.concatenate([w_query, w_key, w_value], axis=1)
    projected = width_reduce(first_whole, forward_with(w_project))
    query_proj = projected[:, :query_width].reshape(seqs, length, -1, depth)
    key_proj = projected[:, query_width : query_width + key_width].reshape(seqs, length, -1, depth)
    values = projected[:, query_width + key_width :].astype(B16).reshape(seqs, length, -1, depth)
    positions = jax.vmap(doc_positions)(seg_ids)
    cosine, sine = rotary(positions, depth)
    cosine = cosine[:, :, None, :]
    sine = sine[:, :, None, :]
    query = turn(query_proj, query_gain, cosine, sine).astype(B16)
    keys = turn(key_proj, key_gain, cosine, sine).astype(B16)
    mixed, logs = attend_forward(query, keys, values, seg_ids, block)
    attended = mixed.reshape(seqs * length, -1).astype(B16)
    attended_whole = branch_gather(attended)
    residual = inputs + head_reduce(attended_whole, forward_with(w_out))
    second_scale = norm_scale(residual)
    second_normed = (residual * second_scale[:, None] * mlp_gain).astype(B16)
    second_whole = token_gather(second_normed)
    w_both = jnp.concatenate([w_gate, w_up], axis=1)
    gate_up = width_reduce(second_whole, forward_with(w_both))
    gate = gate_up[:, :units]
    upper = gate_up[:, units:]
    hidden = (jax.nn.silu(gate) * upper).astype(B16)
    hidden_whole = branch_gather(hidden)
    output = residual + head_reduce(hidden_whole, forward_with(w_down))
    grad_whole = token_gather(cotangent)
    hidden_grad = width_reduce(grad_whole, backward_with(w_down))
    down_grad = weight_grad(hidden_whole, grad_whole)
    gate_grad, up_grad = jax.vjp(lambda left, right: jax.nn.silu(left) * right, gate, upper)[1](
        hidden_grad
    )
    unit_grads = jnp.concatenate([gate_grad, up_grad], axis=1).astype(B16)
    unit_whole = branch_gather(unit_grads)
    second_grad = head_reduce(unit_whole, backward_with(w_both))
    both_grad = weight_grad(second_whole, unit_whole)
    gate_weight = both_grad[:, :units]
    up_weight = both_grad[:, units:]
    resid_norm_grad, mlp_gain_part = norm_back(residual, second_scale, mlp_gain, second_grad)
    residual_grad = cotangent.astype(F32) + resid_norm_grad
    residual_whole = token_gather(residual_grad.astype(B16))
    mixed_grad = width_reduce(residual_whole, backward_with(w_out)).astype(B16)
    out_grad = weight_grad(attended_whole, residual_whole)
    query_grad, key_grad, value_grad = attend_backward(
        query, keys, values, seg_ids, logs, mixed_grad.reshape(seqs, length, -1), block
    )
    query_proj_grad, query_gain_grad = jax.vjp(
        lambda value, gain: turn(value, gain, cosine, sine), query_proj, query_gain
    )[1](query_grad)
    key_proj_grad, key_gain_grad = jax.vjp(
        lambda value, gain: turn(value, gain, cosine, sine), key_proj, key_gain
    )[1](key_grad)
    rows = seqs * length
    proj_grad = jnp.concatenate(
        [
            query_proj_grad.reshape(rows, -1),
            key_proj_grad.reshape(rows, -1),
            value_grad.reshape(rows, -1),
        ],
        axis=1,
    ).astype(B16)
    proj_whole = branch_gather(proj_grad)
    first_grad = head_reduce(proj_whole, backward_with(w_project))
    project_grad = weight_grad(first_whole, proj_whole)
    query_weight = project_grad[:, :query_width]
    key_weight = project_grad[:, query_width : query_width + key_width]
    value_weight = project_grad[:, query_width + key_width :]
    input_norm_grad, attn_gain_part = norm_back(inputs, first_scale, attn_gain, first_grad)
    input_grad = (residual_grad + input_norm_grad).astype(B16)
    attn_total, mlp_total, query_total, key_total = lax.psum(
        (widen(attn_gain_part), widen(mlp_gain_part), query_gain_grad, key_gain_grad),
        ("dp", "tx", "ty"),
    )
    query_share, key_share, value_share, gate_share, up_share = (
        lax.psum_scatter(
            query_weight.astype(jnp.bfloat16), "dp", scatter_dimension=0, tiled=True
        ).astype(jnp.float32),
        lax.psum_scatter(
            key_weight.astype(jnp.bfloat16), "dp", scatter_dimension=0, tiled=True
        ).astype(jnp.float32),
        lax.psum_scatter(
            value_weight.astype(jnp.bfloat16), "dp", scatter_dimension=0, tiled=True
        ).astype(jnp.float32),
        lax.psum_scatter(
            gate_weight.astype(jnp.bfloat16), "dp", scatter_dimension=0, tiled=True
        ).astype(jnp.float32),
        lax.psum_scatter(
            up_weight.astype(jnp.bfloat16), "dp", scatter_dimension=0, tiled=True
        ).astype(jnp.float32),
    )
    out_share, down_share = (
        lax.psum_scatter(
            out_grad.astype(jnp.bfloat16), "dp", scatter_dimension=1, tiled=True
        ).astype(jnp.float32),
        lax.psum_scatter(
            down_grad.astype(jnp.bfloat16), "dp", scatter_dimension=1, tiled=True
        ).astype(jnp.float32),
    )
    return (
        output.astype(B16),
        input_grad,
        query_share,
        key_share,
        value_share,
        out_share,
        gate_share,
        up_share,
        down_share,
        attn_total,
        mlp_total,
        query_total,
        key_total,
    )


def fits(mesh):
    return mesh.shape["tx"] == 4 and mesh.shape["ty"] == 2 and mesh.shape["dp"] == 4


def swap_x(value):
    return lax.ppermute(value, "ty", [(0, 1), (1, 0)])


def in_order(mine, theirs, axis):
    first = lax.axis_index("ty") == 0
    return jnp.concatenate(
        [jnp.where(first, mine, theirs), jnp.where(first, theirs, mine)], axis=axis
    )


def spin(value, cosine, sine):
    return value * cosine + pltpu.roll(value, value.shape[1] // 2, 1) * sine


def spin_back(value, cosine, sine):
    return value * cosine + pltpu.roll(value * sine, value.shape[1] // 2, 1)


def head_scale(value):
    return lax.rsqrt(jnp.mean(value * value, axis=1, keepdims=True) + EPS)


def window(first, block, most):
    return max(0, first - most), first + block


def kept(first, block, low, high, starts):
    shape = (block, high - low)
    column = low + lax.broadcasted_iota(jnp.int32, shape, 1)
    row = first + lax.broadcasted_iota(jnp.int32, shape, 0)
    return (column >= starts) & (column <= row)


def rows_dot(left, right):
    return lax.dot_general(left, right, (((1,), (1,)), ((), ())), preferred_element_type=F32)


def stand(row):
    return jnp.transpose(jnp.broadcast_to(row, (row.shape[1], row.shape[1])))


def lie(column):
    return jnp.transpose(jnp.broadcast_to(column, (column.shape[0], column.shape[0])))[0:1]


def put_stats(stats_ref, tile, column):
    stats_ref[tile, 0:1, :] = lie(column[:128])
    stats_ref[tile, 1:2, :] = lie(column[128:])


BLOCK = 256


def attend_sequence(core, seq, most, projected, fixed_refs, mixed, saved_refs, between):
    starts_ref, cosine_ref, sine_ref, query_gain_ref, key_gain_ref = fixed_refs
    query_ref, key_ref, value_ref, log_ref = saved_refs
    rows = projected.shape[1]
    length = query_ref.shape[1]
    depth = key_ref.shape[2]
    heads = query_ref.shape[2] // depth
    scale = depth ** (-0.5)
    for half in range(2):
        place = 2 * lax.rem(core + half, 2) + seq
        for at in range(half * rows, (half + 1) * rows, BLOCK):
            inner = at - half * rows
            cosine = cosine_ref[seq, at : at + BLOCK, :]
            sine = sine_ref[seq, at : at + BLOCK, :]
            for head in range(heads + 2):
                lane = slice(head * depth, (head + 1) * depth)
                value = projected[place, inner : inner + BLOCK, lane]
                if head < heads:
                    normed = value * head_scale(value) * query_gain_ref[...]
                    query_ref[seq, at : at + BLOCK, lane] = spin(normed, cosine, sine).astype(B16)
                elif head == heads:
                    normed = value * head_scale(value) * key_gain_ref[...]
                    key_ref[seq, at : at + BLOCK, :] = spin(normed, cosine, sine).astype(B16)
                else:
                    value_ref[seq, at : at + BLOCK, :] = value.astype(B16)
    for first in range(0, length, BLOCK):
        between(first // BLOCK)
        low, high = window(first, BLOCK, most)
        mask = kept(first, BLOCK, low, high, starts_ref[seq, first : first + BLOCK, :])
        half, inner = divmod(first, rows)
        place = 2 * lax.rem(core + half, 2) + seq
        for head in range(heads):
            lane = slice(head * depth, (head + 1) * depth)
            query = query_ref[seq, first : first + BLOCK, lane]
            scores = rows_dot(query, key_ref[seq, low:high, :]) * scale
            scores = jnp.where(mask, scores, NEG)
            top = jnp.max(scores, axis=1, keepdims=True)
            weights = jnp.exp(scores - top)
            total = jnp.sum(weights, axis=1, keepdims=True)
            probs = (weights * (1.0 / total)).astype(B16)
            out = jnp.dot(probs, value_ref[seq, low:high, :], preferred_element_type=F32)
            mixed[place, inner : inner + BLOCK, lane] = out.astype(B16)
            log_ref[seq, head, first : first + BLOCK, :] = top + jnp.log(total)


def attend_sequence_back(
    core, seq, most, projected, upstream, fixed_refs, saved_refs, result, stats, gains, accs
):
    starts_ref, cosine_ref, sine_ref, query_gain_ref, key_gain_ref = fixed_refs
    query_ref, key_ref, value_ref, log_ref = saved_refs
    query_acc, key_acc, value_acc = accs
    rows = projected.shape[1]
    length = query_ref.shape[1]
    depth = key_ref.shape[2]
    heads = query_ref.shape[2] // depth
    scale = depth ** (-0.5)
    key_acc[...] = jnp.zeros_like(key_acc)
    value_acc[...] = jnp.zeros_like(value_acc)
    for first in range(0, length, BLOCK):
        low, high = window(first, BLOCK, most)
        mask = kept(first, BLOCK, low, high, starts_ref[seq, first : first + BLOCK, :])
        half, inner = divmod(first, rows)
        place = 2 * lax.rem(core + half, 2) + seq
        keys = key_ref[seq, low:high, :]
        values = value_ref[seq, low:high, :]
        for head in range(heads):
            lane = slice(head * depth, (head + 1) * depth)
            query = query_ref[seq, first : first + BLOCK, lane]
            grad = upstream[place, inner : inner + BLOCK, lane]
            scores = rows_dot(query, keys) * scale - log_ref[seq, head, first : first + BLOCK, :]
            probs = jnp.exp(jnp.where(mask, scores, NEG))
            prob_grad = rows_dot(grad, values)
            delta = jnp.sum(probs * prob_grad, axis=1, keepdims=True)
            score_grad = (probs * (prob_grad - delta)).astype(B16)
            query_acc[first : first + BLOCK, lane] = (
                jnp.dot(score_grad, keys, preferred_element_type=F32) * scale
            )
            key_acc[low:high, :] += weight_grad(score_grad, query) * scale
            value_acc[low:high, :] += weight_grad(probs.astype(B16), grad)
    query_total = jnp.zeros((1, depth), F32)
    key_total = jnp.zeros((1, depth), F32)
    for half in range(2):
        block = 2 * lax.rem(core + half, 2) + seq
        for at in range(half * rows, (half + 1) * rows, BLOCK):
            inner = at - half * rows
            cosine = cosine_ref[seq, at : at + BLOCK, :]
            sine = sine_ref[seq, at : at + BLOCK, :]
            total = jnp.zeros((BLOCK, 1), F32)
            for head in range(heads + 2):
                lane = slice(head * depth, (head + 1) * depth)
                value = projected[block, inner : inner + BLOCK, lane]
                if head == heads + 1:
                    back = value_acc[at : at + BLOCK, :].astype(B16)
                else:
                    if head < heads:
                        grad = query_acc[at : at + BLOCK, lane]
                        gain = query_gain_ref[...]
                    else:
                        grad = key_acc[at : at + BLOCK, :]
                        gain = key_gain_ref[...]
                    grad = spin_back(grad, cosine, sine)
                    rate = head_scale(value)
                    scaled = value * rate
                    share = jnp.sum(grad * scaled, axis=0, keepdims=True)
                    if head < heads:
                        query_total += share
                    else:
                        key_total += share
                    middle = jnp.mean(gain * grad * scaled, axis=1, keepdims=True)
                    back = (rate * (gain * grad - scaled * middle)).astype(B16)
                result[block, inner : inner + BLOCK, lane] = back
                total += jnp.sum(back.astype(F32) * value, axis=1, keepdims=True)
            put_stats(stats, 2 * block + inner // BLOCK, total)
    gains[seq, 0:1, :] = query_total
    gains[seq, 1:2, :] = key_total


def neighbours():
    spot = lax.axis_index("tx")
    core = lax.rem(spot, 2)
    return (
        {"ty": 1 - lax.axis_index("ty")},
        {"tx": lax.rem(spot + 2, 4)},
        {"tx": spot + 1 - 2 * core},
    )


def planes():
    plane = lax.axis_index("dp")
    return {"dp": plane + 1 - 2 * lax.rem(plane, 2)}, {"dp": 3 - plane}


def inner():
    plane = lax.axis_index("dp")
    return (plane == 1) | (plane == 2)


def greet(targets):
    barrier = pltpu.get_barrier_semaphore()
    for target in targets:
        pl.semaphore_signal(barrier, inc=1, device_id=target, device_id_type=MESH)
    pl.semaphore_wait(barrier, len(targets))


class Wires:
    def __init__(self, send_sems, recv_sems):
        self.send_sems = send_sems
        self.recv_sems = recv_sems

    def copy(self, kind, chunk, source, target, device):
        return pltpu.make_async_remote_copy(
            src_ref=source,
            dst_ref=target,
            send_sem=self.send_sems.at[kind, chunk],
            recv_sem=self.recv_sems.at[kind, chunk],
            device_id=device,
            device_id_type=MESH,
        )


CHUNK = 256
SIBLING, CORNER, FINAL_X, FINAL_Y = 0, 1, 2, 3
REDUCE_KINDS = 5
OUT_X, OUT_Y, OUT_CORNER, CORE_OWN, CORE_X, CORE_Y, CORE_CORNER = range(7)
GATHER_KINDS = 7
SHARE_X, SHARE_NEAR, SHARE_MIDDLE = 0, 1, 2
SHARE_KINDS = 3


def lanes(chunk, half, width):
    return pl.ds(pl.multiple_of(half * width + chunk * CHUNK, CHUNK), CHUNK)


class Gather:
    def __init__(self, wires, base, whole, own, local_sem, most=4):
        self.wires, self.base, self.whole, self.own, self.local_sem = (
            wires,
            base,
            whole,
            own,
            local_sem,
        )
        self.most = most
        self.width = whole.shape[2] // 2
        self.count = self.width // CHUNK

    def place(self, block, chunk, half):
        return self.whole.at[block, :, lanes(chunk, half, self.width)]

    def copy(self, name, chunk):
        side, across, core = neighbours()
        at = self.place
        own = self.own.at[chunk]
        if name == "local":
            return pltpu.make_async_copy(own, at(0, chunk, 0), self.local_sem.at[chunk])
        kind, source, target, device = {
            "x": (OUT_X, own, at(0, chunk, 1), side),
            "y": (OUT_Y, own, at(1, chunk, 0), across),
            "core": (CORE_OWN, own, at(2, chunk, 0), core),
            "even": (OUT_CORNER, at(0, chunk, 1), at(1, chunk, 1), across),
            "odd": (OUT_CORNER, at(1, chunk, 0), at(1, chunk, 1), side),
            "core_x": (CORE_X, at(0, chunk, 1), at(2, chunk, 1), core),
            "core_y": (CORE_Y, at(1, chunk, 0), at(3, chunk, 0), core),
            "core_corner": (CORE_CORNER, at(1, chunk, 1), at(3, chunk, 1), core),
        }[name]
        return self.wires.copy(self.base + kind, chunk, source, target, device)

    def send(self, chunk):
        for name in ("x", "y", "core", "local"):
            self.copy(name, chunk).start()

    def relay(self, low=0, high=None):
        @pl.loop(low, self.count if high is None else high)
        def _(chunk):
            even = (lax.rem(chunk, 2) == 0) | (chunk >= self.most)
            self.copy("x", chunk).wait_recv()

            @pl.when(even)
            def _():
                self.copy("even", chunk).start()

            self.copy("core_x", chunk).start()
            self.copy("y", chunk).wait_recv()

            @pl.when(jnp.logical_not(even))
            def _():
                self.copy("odd", chunk).start()

            self.copy("core_y", chunk).start()

    def close(self):
        @pl.loop(0, self.count)
        def _(chunk):
            self.copy("even", chunk).wait_recv()
            self.copy("core_corner", chunk).start()

        @pl.loop(0, self.count)
        def _(chunk):
            for name in ("core", "core_x", "core_y", "core_corner"):
                self.copy(name, chunk).wait_recv()
            for name in ("x", "y", "core", "even", "core_x", "core_y", "core_corner"):
                self.copy(name, chunk).wait_send()
            self.copy("local", chunk).wait()


class Share:
    def __init__(self, wires, base, sources, whole, by_rows, local_sems, held=None):
        self.wires, self.base, self.sources, self.whole, self.by_rows, self.local_sems = (
            wires,
            base,
            sources,
            whole,
            by_rows,
            local_sems,
        )
        self.held = held or sources
        self.size = (whole.shape[0] // 2 if by_rows else whole.shape[0]) // 4

    def quarter(self, plane):
        start = plane * self.size
        if self.by_rows:
            rows = pl.ds(pl.multiple_of(self.whole.shape[0] // 2 + start, self.size), self.size)
            return self.whole.at[rows]
        width = self.whole.shape[1] // 2
        return self.whole.at[pl.ds(pl.multiple_of(start, self.size), self.size), width:]

    def cross(self, index):
        side, _, _ = neighbours()
        plane = lax.axis_index("dp")
        other = 1 - lax.axis_index("ty")
        source = self.sources[index]
        if self.by_rows:
            rows = pl.ds(pl.multiple_of(plane * self.size, self.size), self.size)
            columns = source.shape[1] // 2
            part = source.at[rows, pl.ds(pl.multiple_of(other * columns, columns), columns)]
            offset = sum(item.shape[1] // 2 for item in self.sources[:index])
            target = self.quarter(plane).at[:, offset : offset + columns]
        else:
            start = pl.multiple_of(other * (source.shape[0] // 2) + plane * self.size, self.size)
            part = source.at[pl.ds(start, self.size)]
            target = self.quarter(plane)
        return self.wires.copy(self.base + SHARE_X, index, part, target, side)

    def local(self, index):
        mine = lax.axis_index("ty")
        source = self.held[index]
        if self.by_rows:
            columns = source.shape[1] // 2
            offset = sum(item.shape[1] // 2 for item in self.sources[:index])
            part = source.at[:, pl.ds(pl.multiple_of(mine * columns, columns), columns)]
            target = self.whole.at[: self.whole.shape[0] // 2, offset : offset + columns]
        else:
            half = source.shape[0] // 2
            part = source.at[pl.ds(pl.multiple_of(mine * half, half), half)]
            target = self.whole.at[:, : self.whole.shape[1] // 2]
        return pltpu.make_async_copy(part, target, self.local_sems.at[index])

    def piece_of(self, owner):
        place = self.quarter(owner)
        return place, place

    def over(self, near, index):
        beside, mirror = planes()
        plane = lax.axis_index("dp")
        other = 3 - plane
        if near:
            owner = (plane, other, other + 1 - 2 * lax.rem(other, 2))[index]
        else:
            owner = (plane, plane + 1 - 2 * lax.rem(plane, 2))[index]
        source, target = self.piece_of(owner) if index else self.own_piece()
        return self.wires.copy(
            self.base + (SHARE_NEAR if near else SHARE_MIDDLE),
            index,
            source,
            target,
            beside if near else mirror,
        )

    def own_piece(self):
        return self.piece_of(lax.axis_index("dp"))

    def start(self):
        for index in range(len(self.sources)):
            self.cross(index).start()
            self.local(index).start()

    def send_own(self):
        self.over(True, 0).start()

        @pl.when(inner())
        def _():
            self.over(False, 0).start()

    def middle(self):
        for index in range(len(self.sources)):
            self.cross(index).wait_recv()
        self.send_own()

    def late(self):
        @pl.when(inner())
        def _():
            self.over(True, 0).wait_recv()
            self.over(False, 1).start()
            self.over(False, 0).wait_recv()
            self.over(True, 1).start()

    def later(self):
        @pl.when(inner())
        def _():
            self.over(False, 1).wait_recv()
            self.over(True, 2).start()

    def close_planes(self):
        self.over(True, 0).wait_send()

        @pl.when(inner())
        def _():
            self.over(True, 1).wait_send()
            self.over(True, 2).wait_send()
            self.over(False, 0).wait_send()
            self.over(False, 1).wait_send()

        @pl.when(jnp.logical_not(inner()))
        def _():
            for index in range(3):
                self.over(True, index).wait_recv()

    def close(self):
        self.close_planes()
        for index in range(len(self.sources)):
            self.cross(index).wait_send()
            self.local(index).wait()


class Spread(Share):
    def __init__(self, wires, base, source, whole, local_sems, quarter):
        super().__init__(wires, base, (source,), whole, True, local_sems)
        self.piece = quarter

    def own_piece(self):
        return self.piece, self.quarter(lax.axis_index("dp"))

    def own(self):
        return pltpu.make_async_copy(
            self.piece, self.quarter(lax.axis_index("dp")), self.local_sems.at[1]
        )

    def start(self):
        self.send_own()
        self.local(0).start()
        self.own().start()

    def close(self):
        self.close_planes()
        self.local(0).wait()
        self.own().wait()


FOLD_END, FOLD_MIDDLE, FOLD_BACK, FOLD_X = 0, 2, 4, 5
FOLD_KINDS = 6


def side():
    return lax.div(lax.axis_index("dp"), 2)


def turn_shard(turn):
    return 3 * (1 - side()) + turn * (2 * side() - 1)


class Fold:
    def __init__(self, wires, base, tiles, bufs, mine, theirs, first=None):
        self.wires, self.base, self.tiles, self.mine, self.theirs = (
            wires,
            base,
            tiles,
            mine,
            theirs,
        )
        self.first = tiles if first is None else first
        (self.recv,) = bufs
        self.near, self.mirror = planes()

    def send(self, kind, half, slot, source, target, device):
        target = self.recv.at[2 * target + half]
        return self.wires.copy(self.base + kind, slot, source, target, device)

    def end(self, half, turn):
        source = self.first.at[4 * half + turn_shard(turn)]
        return self.send(FOLD_END + half, half, turn, source, turn, self.near)

    def across(self, half, turn):
        source = self.recv.at[2 * turn + half]
        return self.send(FOLD_MIDDLE + half, half, turn, source, 3 + turn, self.mirror)

    def back(self, half):
        return self.send(FOLD_BACK, half, half, self.recv.at[6 + half], 0, self.near)

    def cross(self):
        source = self.tiles.at[4 + lax.axis_index("dp")]
        return self.wires.copy(self.base + FOLD_X, 0, source, self.theirs, neighbours()[0])

    def add(self, slot, half, shard):
        self.recv[2 * slot + half] = (
            self.recv[2 * slot + half].astype(F32) + self.tiles[4 * half + shard].astype(F32)
        ).astype(B16)

    def begin(self, turn, half):
        @pl.when(jnp.logical_not(inner()))
        def _():
            self.end(half, turn).start()

    def start(self):
        for turn in range(3):
            for half in (1, 0):
                self.begin(turn, half)

    def pass_on(self, turn):
        @pl.when(inner())
        def _():
            for half in (1, 0):
                self.end(half, turn).wait_recv()
                self.add(turn, half, turn_shard(turn))
                self.across(half, turn).start()

    def step(self):
        self.pass_on(0)

    def middle(self):
        self.pass_on(1)

        @pl.when(inner())
        def _():
            for half in (1, 0):
                self.across(half, 0).wait_recv()
                self.add(3, half, 3 * side())
                self.back(half).start()

    def late(self):
        plane = lax.axis_index("dp")
        for half in (1, 0):

            @pl.when(inner())
            def _():
                self.end(half, 2).wait_recv()
                self.across(half, 1).wait_recv()
                self.add(2, half, plane)

            @pl.when(jnp.logical_not(inner()))
            def _():
                self.back(half).wait_recv()

            at = 4 * half + plane
            middle = inner().astype(jnp.int32)
            total = self.recv[4 * middle + half].astype(F32)
            other = jnp.where(
                inner(), self.recv[8 * middle + half].astype(F32), self.tiles[at].astype(F32)
            )
            total = total + other
            if half == 1:
                self.tiles[at] = total.astype(B16)
                self.cross().start()
            else:
                self.mine[...] = total

    def close(self):
        self.cross().wait_recv()

        @pl.when(inner())
        def _():
            for half in range(2):
                self.across(half, 0).wait_send()
                self.across(half, 1).wait_send()
                self.back(half).wait_send()

        @pl.when(jnp.logical_not(inner()))
        def _():
            for half in range(2):
                for turn in range(3):
                    self.end(half, turn).wait_send()

        self.cross().wait_send()


def fold_scratch(rows, columns):
    return [pltpu.VMEM((10, rows, columns), B16)]


def turn_tile(step):
    return 4 * (1 - lax.rem(step, 2)) + turn_shard(lax.div(step, 2))


def make_tiles(fold, make, low, high):
    @pl.loop(low, high)
    def _(step):
        make(step)

        @pl.when(step < 6)
        def _():
            half = 1 - lax.rem(step, 2)
            turn = lax.div(step, 2)
            for side_half in range(2):

                @pl.when(half == side_half)
                def _():
                    fold.begin(turn, side_half)


class Reduce:
    def __init__(self, wires, rows_ref, weight_ref, transposed, bufs):
        self.wires, self.rows_ref, self.weight_ref, self.transposed = (
            wires,
            rows_ref,
            weight_ref,
            transposed,
        )
        (
            self.sibling_send,
            self.sibling_recv,
            self.kept_ref,
            self.out,
            self.corner_recv,
            self.x_recv,
            self.y_recv,
        ) = bufs
        self.rows = rows_ref.shape[1]
        self.width = (weight_ref.shape[0] if transposed else weight_ref.shape[1]) // 2
        self.count = self.width // CHUNK

    def product(self, block, chunk, half):
        left = self.rows_ref[block : block + 2].reshape(2 * self.rows, self.rows_ref.shape[2])
        at = lanes(chunk, half, self.width)
        if self.transposed:
            return rows_dot(left, self.weight_ref[at, :])
        return jnp.dot(left, self.weight_ref[:, at], preferred_element_type=F32)

    def sibling(self, chunk, half):
        return self.wires.copy(
            SIBLING + half * (REDUCE_KINDS - 1),
            chunk,
            self.sibling_send.at[lax.rem(chunk, 2), half],
            self.sibling_recv.at[chunk, half],
            neighbours()[2],
        )

    def corner(self, chunk, device):
        return self.wires.copy(
            CORNER, chunk, self.out.at[2, chunk], self.corner_recv.at[chunk], device
        )

    def final_x(self, chunk):
        return self.wires.copy(
            FINAL_X, chunk, self.out.at[0, chunk], self.x_recv.at[chunk], neighbours()[0]
        )

    def final_y(self, chunk):
        return self.wires.copy(
            FINAL_Y, chunk, self.out.at[1, chunk], self.y_recv.at[chunk], neighbours()[1]
        )

    def give(self, chunk):
        @pl.loop(0, 2)
        def _(turn):
            half = 1 - turn
            self.sibling_send[lax.rem(chunk, 2), half] = self.product(2, chunk, half).astype(B16)
            self.sibling(chunk, half).start()

    def take(self, chunk):
        rows = self.rows
        even = lax.rem(chunk, 2) == 0
        side, across, _ = neighbours()

        @pl.loop(0, 2)
        def _(turn):
            half = 1 - turn
            own = self.product(0, chunk, half)
            self.sibling(chunk, half).wait_recv()
            total = own + self.sibling_recv[chunk, half].astype(F32)

            @pl.when(half == 1)
            def _():
                self.out[2, chunk] = total[rows:].astype(B16)
                self.out[0, chunk] = total[:rows].astype(B16)

                @pl.when(even)
                def _():
                    self.corner(chunk, side).start()
                    self.final_x(chunk).start()

                @pl.when(jnp.logical_not(even))
                def _():
                    self.corner(chunk, across).start()

            @pl.when(half == 0)
            def _():
                self.kept_ref[chunk] = total[:rows]
                self.out[1, chunk] = total[rows:].astype(B16)

                @pl.when(jnp.logical_not(even))
                def _():
                    self.final_y(chunk).start()

    def start(self, between=(lambda: None, lambda: None)):
        self.give(0)
        self.rest(between)

    def rest(self, between):
        self.take(0)
        self.give(1)
        self.take(1)
        between[0]()

        @pl.loop(2, self.count)
        def _(chunk):
            for half in range(2):
                self.sibling(chunk - 2, half).wait_send()
            self.give(chunk)
            self.take(chunk)
            self.middle(chunk - 2, chunk - 1)

        between[1]()

    def middle(self, low=None, high=None):
        @pl.loop(self.count - 2 if low is None else low, self.count if high is None else high)
        def _(chunk):
            even = lax.rem(chunk, 2) == 0
            self.corner(chunk, neighbours()[0]).wait_recv()
            came = self.corner_recv[chunk].astype(F32)

            @pl.when(even)
            def _():
                self.out[1, chunk] = (self.out[1, chunk].astype(F32) + came).astype(B16)
                self.final_y(chunk).start()

            @pl.when(jnp.logical_not(even))
            def _():
                self.out[0, chunk] = (self.out[0, chunk].astype(F32) + came).astype(B16)
                self.final_x(chunk).start()

    def total(self, chunk):
        self.final_x(chunk).wait_recv()
        self.final_y(chunk).wait_recv()
        return (
            self.kept_ref[chunk] + self.x_recv[chunk].astype(F32) + self.y_recv[chunk].astype(F32)
        )

    def close(self):
        @pl.loop(self.count - 2, self.count)
        def _(chunk):
            for half in range(2):
                self.sibling(chunk, half).wait_send()

        @pl.loop(0, self.count)
        def _(chunk):
            self.corner(chunk, neighbours()[0]).wait_send()
            self.final_x(chunk).wait_send()
            self.final_y(chunk).wait_send()


def reduce_scratch(rows, width):
    count = width // CHUNK
    return [
        pltpu.VMEM((2, 2, 2 * rows, CHUNK), B16),
        pltpu.VMEM((count, 2, 2 * rows, CHUNK), B16),
        pltpu.VMEM((count, rows, CHUNK), F32),
        pltpu.VMEM((3, count, rows, CHUNK), B16),
        pltpu.VMEM((count, rows, CHUNK), B16),
        pltpu.VMEM((count, rows, CHUNK), B16),
        pltpu.VMEM((count, rows, CHUNK), B16),
    ]


def gather_scratch(rows, width):
    count = width // CHUNK
    return [pltpu.VMEM((count, rows, CHUNK), B16), pltpu.SemaphoreType.DMA((count,))]


def wire_scratch(kinds, count):
    return [pltpu.SemaphoreType.DMA((kinds, count))] * 2


IN_VMEM = pl.BlockSpec(memory_space=pltpu.VMEM)
IN_ANY = pl.BlockSpec(memory_space=pl.ANY)
VMEM_MOST = 60 * 1024 * 1024


def remote_params(number):
    return pltpu.CompilerParams(
        collective_id=number, has_side_effects=True, vmem_limit_bytes=VMEM_MOST
    )


def cost(flops, size):
    return pl.CostEstimate(flops=flops, bytes_accessed=size, transcendentals=0)


def shape(dims, kind=B16):
    return jax.ShapeDtypeStruct(dims, kind)


def cut(own, block_ref):
    for chunk in range(own.shape[0]):
        own[chunk] = block_ref[:, chunk * CHUNK : (chunk + 1) * CHUNK]


def open_kernel(
    tokens_ref,
    query_ref,
    key_ref,
    value_ref,
    out_ref,
    attn_ref,
    mlp_ref,
    seg_ref,
    rate_ref,
    attn_all_ref,
    mlp_all_ref,
    starts_ref,
    cosine_ref,
    sine_ref,
    whole_ref,
    project_ref,
    branch_ref,
    *scratch,
):
    own, gather_sem, send_sems, recv_sems, project_sem, branch_sem = scratch[:6]
    attn_recv, mlp_recv, seg_recv, seg_all = scratch[6:]
    width = attn_ref.shape[1]
    length = seg_ref.shape[1]
    cut(own, tokens_ref)
    greet(neighbours() + planes())
    wires = Wires(send_sems, recv_sems)
    gather = Gather(wires, 0, whole_ref, own, gather_sem, 2)
    base = GATHER_KINDS + 2 * SHARE_KINDS
    side = neighbours()[0]
    small = [
        wires.copy(base, index, source, target, side)
        for index, (source, target) in enumerate(
            ((attn_ref, attn_recv), (mlp_ref, mlp_recv), (seg_ref, seg_recv))
        )
    ]
    shares = [
        Share(wires, GATHER_KINDS, (query_ref, key_ref, value_ref), project_ref, True, project_sem),
        Share(wires, GATHER_KINDS + SHARE_KINDS, (out_ref,), branch_ref, False, branch_sem),
    ]
    for copy in small:
        copy.start()
    shares[0].start()
    shares[1].start()

    @pl.loop(0, gather.count)
    def _(chunk):
        gather.send(chunk)

    for copy in small:
        copy.wait()
    attn_all_ref[:, :width] = attn_ref[...]
    attn_all_ref[:, width:] = attn_recv[...]
    mlp_all_ref[:, :width] = mlp_ref[...]
    mlp_all_ref[:, width:] = mlp_recv[...]
    mine = lax.rem(lax.axis_index("ty") + lax.div(lax.axis_index("tx"), 2), 2)
    seg_all[pl.ds(mine, 1)] = seg_ref[...].astype(F32)[None]
    seg_all[pl.ds(1 - mine, 1)] = seg_recv[...].astype(F32)[None]

    shares[0].middle()
    shares[1].middle()

    def between(seq, piece):
        @pl.when(seq == 0)
        def _():
            if piece == 4:
                gather.relay(0, 1)
            elif piece == 6:
                shares[0].late()
                shares[1].late()

        @pl.when(seq == 1)
        def _():
            if piece == 0:
                gather.relay(1, 2)
            elif piece == 2:
                shares[0].later()
                shares[1].later()
            elif piece == 3:
                gather.relay(2, 3)
            elif piece == 6:
                gather.relay(3, 4)

    @pl.loop(0, 2)
    def _(seq):
        for low in range(0, length, 128):
            between(seq, low // 128)
            here = stand(seg_all[seq, :, low : low + 128])
            before = jnp.zeros((128, 128), F32)
            for other in range(0, length, 128):
                before += (seg_all[seq, :, other : other + 128] < here).astype(F32)
            start = jnp.sum(before, axis=1, keepdims=True)
            at = slice(low, low + 128)
            starts_ref[seq, at, :] = start.astype(jnp.int32)
            row = lax.broadcasted_iota(jnp.int32, (128, 128), 0) + low
            lane = lax.broadcasted_iota(jnp.int32, (128, 128), 1)
            angle = (row.astype(F32) - start) * rate_ref[...]
            cosine_ref[seq, at, :] = jnp.cos(angle)
            sine = jnp.sin(angle)
            sine_ref[seq, at, :] = jnp.where(lane < 64, -sine, sine)

    gather.close()
    shares[0].close()
    shares[1].close()


def open_call(tokens, w_query, w_key, w_value, w_out, attn_gain, mlp_gain, seg_ids, rate, number):
    rows, width = tokens.shape
    columns = (w_query.shape[1] + w_key.shape[1] + w_value.shape[1]) // 2
    length = seg_ids.shape[1]
    return pl.pallas_call(
        open_kernel,
        out_shape=(
            shape((1, 2 * width), F32),
            shape((1, 2 * width), F32),
            shape((2, length, 1), jnp.int32),
            shape((2, length, 128), F32),
            shape((2, length, 128), F32),
            shape((4, rows, 2 * width)),
            shape((2 * width, columns)),
            shape((w_out.shape[0] // 2, 2 * width)),
        ),
        in_specs=[IN_VMEM] * 9,
        out_specs=(IN_VMEM,) * 5 + (IN_ANY,) * 3,
        scratch_shapes=gather_scratch(rows, width)
        + wire_scratch(GATHER_KINDS + 2 * SHARE_KINDS + 1, width // CHUNK)
        + [
            pltpu.SemaphoreType.DMA((3,)),
            pltpu.SemaphoreType.DMA((1,)),
            pltpu.VMEM((1, width), F32),
            pltpu.VMEM((1, width), F32),
            pltpu.VMEM((1, length), jnp.int32),
            pltpu.VMEM((2, 1, length), F32),
        ],
        compiler_params=remote_params(number),
        cost_estimate=cost(0, 32 * rows * width),
    )(tokens, w_query, w_key, w_value, w_out, attn_gain, mlp_gain, seg_ids, rate)


def front_kernel(
    most,
    whole_ref,
    project_ref,
    gain_ref,
    query_gain_ref,
    key_gain_ref,
    grad_ref,
    starts_in_ref,
    cosine_in_ref,
    sine_in_ref,
    down_in_ref,
    gate_in_ref,
    first_ref,
    projected_out_ref,
    scale_ref,
    mixed_ref,
    query_ref,
    key_ref,
    value_ref,
    log_ref,
    grad_whole_ref,
    back_ref,
    gate_ref,
    *scratch,
):
    own, gather_sem, send_sems, recv_sems, back_sem, tokens, firsts, tile_sem = scratch[:8]
    down_ref, starts_ref, cosine_ref, sine_ref = scratch[8:12]
    loads = Loads(
        (down_in_ref, starts_in_ref, cosine_in_ref, sine_in_ref), scratch[8:12], scratch[12]
    )
    projected_ref, projected_sem = scratch[13:]
    keep = pltpu.make_async_copy(projected_ref, projected_out_ref, projected_sem)
    core = lax.rem(lax.axis_index("tx"), 2)
    cut(own, grad_ref)
    rows = whole_ref.shape[1]

    def spot(ref, tile):
        at = pl.ds(pl.multiple_of(lax.rem(tile, rows // BLOCK) * BLOCK, BLOCK), BLOCK)
        return ref.at[lax.div(tile, rows // BLOCK), at, :]

    def fetch(tile):
        slot = lax.rem(tile, 2)
        return pltpu.make_async_copy(spot(whole_ref, tile), tokens.at[slot], tile_sem.at[0, slot])

    def store(tile):
        slot = lax.rem(tile, 2)
        return pltpu.make_async_copy(firsts.at[slot], spot(first_ref, tile), tile_sem.at[1, slot])

    fetch(0).start()
    loads.start()
    greet(neighbours() + planes())
    wires = Wires(send_sems, recv_sems)
    gather = Gather(wires, 0, grad_whole_ref, own, gather_sem, 0)
    back = Share(wires, GATHER_KINDS, (down_in_ref,), back_ref, False, back_sem, (down_ref,))
    size, columns = gate_ref.shape
    gate = wires.copy(
        GATHER_KINDS + SHARE_KINDS,
        0,
        gate_in_ref.at[
            pl.ds(pl.multiple_of(lax.axis_index("dp") * size, size), size),
            pl.ds(pl.multiple_of((1 - lax.axis_index("ty")) * columns, columns), columns),
        ],
        gate_ref,
        neighbours()[0],
    )
    back.cross(0).start()

    @pl.loop(0, gather.count)
    def _(chunk):
        gather.send(chunk)

    gate.start()

    loads.wait(0, 1)
    back.local(0).start()
    count = 4 * rows // BLOCK

    @pl.loop(0, count)
    def _(tile):
        slot = lax.rem(tile, 2)
        block = lax.div(tile, rows // BLOCK)
        at = pl.ds(pl.multiple_of(lax.rem(tile, rows // BLOCK) * BLOCK, BLOCK), BLOCK)

        @pl.when(tile < count - 1)
        def _():
            fetch(tile + 1).start()

        fetch(tile).wait()

        @pl.when(tile >= 2)
        def _():
            store(tile - 2).wait()

        value = tokens[slot].astype(F32)
        scale = lax.rsqrt(jnp.mean(value * value, axis=1, keepdims=True) + EPS)
        first = (value * scale * gain_ref[...]).astype(B16)
        firsts[slot] = first
        store(tile).start()
        projected_ref[block, at, :] = jnp.dot(
            first, project_ref[...], preferred_element_type=F32
        )

        @pl.when(block == 0)
        def _():
            scale_ref[at, :] = jnp.broadcast_to(scale, (BLOCK, 128))

        @pl.when(tile == count // 2)
        def _():
            back.middle()

    keep.start()
    loads.wait(1, 4)
    fixed_refs = (starts_ref, cosine_ref, sine_ref, query_gain_ref, key_gain_ref)
    saved_refs = (query_ref, key_ref, value_ref, log_ref)

    @pl.loop(0, 2)
    def _(seq):
        def between(turn):
            @pl.when(seq == 0)
            def _():
                if turn == 0:
                    gather.relay(0, 1)
                elif turn == 1:
                    back.late()
                elif turn == 2:
                    gather.relay(1, 2)
                else:
                    back.later()

            @pl.when(seq == 1)
            def _():
                if turn < 2:
                    gather.relay(turn + 2, turn + 3)

        attend_sequence(
            core, seq, most, projected_ref, fixed_refs, mixed_ref, saved_refs, between
        )

    for tile in range(count - 2, count):
        store(tile).wait()
    gather.close()
    back.close()
    gate.wait()
    keep.wait()


def front_call(whole, w_project, gain, fixed_args, most, cotangent, w_down, w_gate, number):
    starts, cosine, sine, query_gain, key_gain = fixed_args
    rows, width = cotangent.shape
    length = cosine.shape[1]
    depth = query_gain.shape[1]
    columns = w_project.shape[1]
    heads = columns // depth - 2
    outs = (
        shape((4, rows, 2 * width)),
        shape((4, rows, columns), F32),
        shape((rows, 128), F32),
        shape((4, rows, heads * depth)),
        shape((2, length, heads * depth)),
        shape((2, length, depth)),
        shape((2, length, depth)),
        shape((2, heads, length, 1), F32),
        shape((4, rows, 2 * width)),
        shape((w_down.shape[0] // 2, 2 * width)),
        shape((width // 4, w_gate.shape[1] // 2)),
    )
    return pl.pallas_call(
        lambda *refs: front_kernel(most, *refs),
        out_shape=outs,
        in_specs=[IN_ANY] + [IN_VMEM] * 5 + [IN_ANY] * 5,
        out_specs=[IN_ANY] * 2 + [IN_VMEM] * 6 + [IN_ANY] * 3,
        scratch_shapes=gather_scratch(rows, width)
        + wire_scratch(GATHER_KINDS + SHARE_KINDS + 1, width // CHUNK)
        + [
            pltpu.SemaphoreType.DMA((1,)),
            pltpu.VMEM((2, BLOCK, 2 * width), B16),
            pltpu.VMEM((2, BLOCK, 2 * width), B16),
            pltpu.SemaphoreType.DMA((2, 2)),
        ]
        + load_scratch((w_down, starts, cosine, sine))
        + [pltpu.VMEM((4, rows, columns), F32), pltpu.SemaphoreType.DMA],
        compiler_params=remote_params(number),
        cost_estimate=cost(16 * rows * width * columns, 64 * rows * width),
    )(whole, w_project, gain, query_gain, key_gain, cotangent, starts, cosine, sine, w_down, w_gate)


def branch_kernel(
    rows_in_ref,
    weight_in_ref,
    input_in_ref,
    up_in_ref,
    gate_in_ref,
    quarter_ref,
    residual_ref,
    whole_ref,
    up_ref,
    gate_ref,
    *scratch,
):
    bufs = scratch[:7]
    own, gather_sem, send_sems, recv_sems, up_sem = scratch[7:12]
    held, load_sem, gate_sem = scratch[12:17], scratch[17], scratch[18]
    rows_ref, weight_ref, input_ref, up_held, gate_held = held
    loads = Loads(
        (rows_in_ref, weight_in_ref, input_in_ref, up_in_ref, gate_in_ref), held, load_sem
    )
    loads.start()
    width = input_ref.shape[1]
    greet(neighbours() + planes())
    wires = Wires(send_sems, recv_sems)
    reduce = Reduce(wires, rows_ref, weight_ref, False, bufs)
    gather = Gather(wires, REDUCE_KINDS, whole_ref, own, gather_sem, 2)
    up = Share(
        wires, REDUCE_KINDS + GATHER_KINDS, (up_in_ref,), up_ref, True, up_sem, (up_held,)
    )
    gate = Spread(
        wires,
        REDUCE_KINDS + GATHER_KINDS + SHARE_KINDS,
        gate_held,
        gate_ref,
        gate_sem,
        quarter_ref,
    )
    loads.wait(0, 2)

    def between():
        loads.wait(2, 5)
        up.start()
        gate.start()

    reduce.start((between, gate.late))
    up.middle()
    reduce.middle()
    gate.later()

    @pl.loop(0, width // CHUNK)
    def _(chunk):
        at = lanes(chunk, 0, width)
        residual = input_ref[:, at].astype(F32) + reduce.total(chunk)
        residual_ref[:, at] = residual
        own[chunk] = residual.astype(B16)
        gather.send(chunk)

    up.late()
    gather.relay()
    up.later()
    gather.close()
    up.close()
    gate.close()
    reduce.close()


def branch_call(rows, weight, inputs, w_up, w_gate, quarter, number):
    height, width = inputs.shape
    count = width // CHUNK
    loaded = (rows, weight, inputs, w_up, w_gate)
    return pl.pallas_call(
        branch_kernel,
        out_shape=(
            shape((height, width), F32),
            shape((4, height, 2 * width)),
            shape((2 * width, w_up.shape[1] // 2)),
            shape((2 * width, w_gate.shape[1] // 2)),
        ),
        in_specs=[IN_ANY] * 6,
        out_specs=(IN_VMEM, IN_ANY, IN_ANY, IN_ANY),
        scratch_shapes=reduce_scratch(height, width)
        + gather_scratch(height, width)
        + wire_scratch(REDUCE_KINDS + GATHER_KINDS + 2 * SHARE_KINDS, count)
        + [pltpu.SemaphoreType.DMA((1,))]
        + load_scratch(loaded)
        + [pltpu.SemaphoreType.DMA((2,))],
        compiler_params=remote_params(number),
        cost_estimate=cost(16 * height * rows.shape[2] * width, 64 * height * width),
    )(*loaded, quarter)


def units_kernel(
    whole_ref, grad_ref, gates_ref, uppers_ref, back_ref, gain_ref, second_ref, hidden_ref, unit_ref, scale_ref, stats_ref
):
    units = hidden_ref.shape[1]
    value = whole_ref[...].astype(F32)
    scale = lax.rsqrt(jnp.mean(value * value, axis=1, keepdims=True) + EPS)
    second = (value * scale * gain_ref[...]).astype(B16)
    second_ref[...] = second
    scale_ref[...] = jnp.broadcast_to(scale, scale_ref.shape)
    total = jnp.zeros((value.shape[0], 1), F32)
    for low in range(0, units, CHUNK):
        at = slice(low, low + CHUNK)
        beside = slice(units + low, units + low + CHUNK)
        gate = jnp.dot(second, gates_ref[:, at], preferred_element_type=F32)
        upper = jnp.dot(second, uppers_ref[:, at], preferred_element_type=F32)
        hidden_grad = rows_dot(grad_ref[...], back_ref[at, :])
        sigma = jax.nn.sigmoid(gate)
        passed = gate * sigma
        hidden_ref[:, at] = (passed * upper).astype(B16)
        gate_grad = (hidden_grad * upper * (sigma + passed * (1.0 - sigma))).astype(B16)
        up_grad = (hidden_grad * passed).astype(B16)
        unit_ref[:, at] = gate_grad
        unit_ref[:, beside] = up_grad
        total += jnp.sum(
            gate_grad.astype(F32) * gate + up_grad.astype(F32) * upper, axis=1, keepdims=True
        )
    stats_ref[...] = jnp.zeros_like(stats_ref)
    for tile in range(stats_ref.shape[0]):
        put_stats(stats_ref, tile, total[tile * BLOCK : (tile + 1) * BLOCK])


def units_call(whole, grad, w_gates, w_uppers, w_back, gain):
    tokens, width = whole.shape
    units = w_back.shape[0]
    size = 2 * BLOCK
    tiles = tokens // size

    def tile(columns):
        return pl.BlockSpec((size, columns), lambda i: (i, 0))

    def all_of(item):
        return pl.BlockSpec(item.shape, lambda i: (0, 0))

    return pl.pallas_call(
        units_kernel,
        out_shape=(
            shape((tokens, width)),
            shape((tokens, units)),
            shape((tokens, 2 * units)),
            shape((tokens, 128), F32),
            shape((2 * tiles, 8, 128), F32),
        ),
        grid=(tiles,),
        in_specs=[tile(width), tile(width)]
        + [all_of(item) for item in (w_gates, w_uppers, w_back, gain)],
        out_specs=(
            tile(width),
            tile(units),
            tile(2 * units),
            tile(128),
            pl.BlockSpec((2, 8, 128), lambda i: (i, 0, 0)),
        ),
        compiler_params=pltpu.CompilerParams(vmem_limit_bytes=VMEM_MOST),
        cost_estimate=cost(6 * tokens * width * units, 20 * tokens * width // 2),
    )(whole, grad, w_gates, w_uppers, w_back, gain)


class Loads:
    def __init__(self, sources, targets, sems):
        self.copies = [
            pltpu.make_async_copy(source, target, sems.at[index])
            for index, (source, target) in enumerate(zip(sources, targets))
        ]

    def start(self):
        for copy in self.copies:
            copy.start()

    def wait(self, low, high):
        for copy in self.copies[low:high]:
            copy.wait()


def load_scratch(items):
    return [pltpu.VMEM(item.shape, item.dtype) for item in items] + [
        pltpu.SemaphoreType.DMA((len(items),))
    ]


class Stats:
    def __init__(self, wires, base, ref, recv):
        self.ref, self.recv = ref, recv
        side, across, core = neighbours()
        self.hops = (
            lambda: wires.copy(base, 0, ref.at[4:8], recv.at[0:4], core),
            lambda: wires.copy(base, 1, ref.at[2:4], recv.at[4:6], across),
            lambda: wires.copy(base, 2, ref.at[0:2], recv.at[6:8], side),
        )
        self.spans = ((4, 0), (2, 4), (2, 6))

    def start(self, hop):
        self.hops[hop]().start()

    def finish(self, hop):
        self.hops[hop]().wait()
        size, at = self.spans[hop]
        self.ref[0:size] = self.ref[0:size] + self.recv[at : at + size]

    def step(self, hop):
        self.finish(hop)
        self.start(hop + 1)


def pull_columns(stats_ref, scale_ref, column_ref, width):
    for part in range(scale_ref.shape[0] // 128):
        at = slice(part * 128, (part + 1) * 128)
        scale = scale_ref[at, :]
        column_ref[at, :] = (
            stand(stats_ref[part // 2, part % 2 : part % 2 + 1, :]) * scale * scale / (2 * width)
        )


def pulled(reduce, chunk, refs, column_ref):
    scale_ref, value_ref, gain_ref, base_ref = refs
    at = lanes(chunk, 0, value_ref.shape[1])
    upstream = reduce.total(chunk)
    value = value_ref[:, at].astype(F32)
    scale = scale_ref[:, 0:1]
    back = scale * gain_ref[:, at] * upstream - value * column_ref[:, 0:1]
    return at, base_ref[:, at].astype(F32) + back, upstream * value * scale


def tile_columns(tile):
    return pl.ds(pl.multiple_of(tile * BLOCK, BLOCK), BLOCK)


SPLIT = 512


def middle_kernel(
    rows_in_ref,
    gates_in_ref,
    uppers_in_ref,
    value_in_ref,
    base_in_ref,
    hidden_in_ref,
    scale_in_ref,
    stats_in_ref,
    gain_ref,
    grad_ref,
    second_ref,
    result_ref,
    gain_grad_ref,
    whole_ref,
    rest_ref,
    *refs,
):
    ends, scratch = refs[:4], refs[4:]
    bufs = scratch[:7]
    stats_ref, stats_recv, column_ref, send_sems, recv_sems, own, gather_sem = scratch[7:14]
    stream, stream_sem, stage, stage_sem = scratch[14:18]
    down_tiles, down_recv, made_tiles, made_recv = scratch[18:22]
    weight_ref, hidden_ref, rows_ref, value_ref, base_ref, scale_ref = scratch[22:28]
    load_sem = scratch[28]
    rows, width = value_ref.shape
    columns = rows_ref.shape[2]
    units = gates_in_ref.shape[1]
    loads = Loads(
        (
            hidden_in_ref,
            rows_in_ref,
            gates_in_ref,
            uppers_in_ref,
            scale_in_ref.at[pl.ds(0, rows)],
            value_in_ref,
            base_in_ref,
        ),
        (
            hidden_ref,
            rows_ref,
            weight_ref.at[:, :units],
            weight_ref.at[:, units:],
            scale_ref,
            value_ref,
            base_ref,
        ),
        load_sem,
    )

    def fetch(ref, step, tile):
        slot = lax.rem(step, 2)
        return pltpu.make_async_copy(
            ref.at[:, :, tile_columns(tile)], stream.at[slot], stream_sem.at[slot]
        )

    fetch(grad_ref, 0, turn_tile(0)).start()
    loads.start()
    stats_ref[...] = stats_in_ref[...]
    greet(neighbours() + planes())
    wires = Wires(send_sems, recv_sems)
    base = REDUCE_KINDS + 1 + GATHER_KINDS
    down = Fold(wires, base, down_tiles, (down_recv,), ends[0], ends[1])
    made = Fold(wires, base + FOLD_KINDS, made_tiles, (made_recv,), ends[2], ends[3])
    stats = Stats(wires, REDUCE_KINDS, stats_ref, stats_recv)
    def make_down(step):
        @pl.when(step < 7)
        def _():
            fetch(grad_ref, step + 1, turn_tile(step + 1)).start()

        fetch(grad_ref, step, turn_tile(step)).wait()
        left = stream[lax.rem(step, 2)].reshape(4 * rows, BLOCK)
        down_tiles[turn_tile(step)] = weight_grad(
            left, hidden_ref[...].reshape(4 * rows, units)
        ).astype(B16)

    stats.start(0)
    loads.wait(0, 1)
    make_tiles(down, make_down, 0, 2)
    reduce = Reduce(wires, rows_ref, weight_ref, True, bufs)
    loads.wait(1, 4)

    def first_part():
        stats.step(0)
        make_tiles(down, make_down, 2, 4)

    def second_part():
        down.step()
        stats.step(1)
        make_tiles(down, make_down, 4, 6)

    reduce.start((first_part, second_part))
    reduce.middle()

    def store(step):
        slot = lax.rem(step, 2)
        return pltpu.make_async_copy(
            stage.at[slot], rest_ref.at[turn_tile(step)], stage_sem.at[slot]
        )

    def make(step):
        slot = lax.rem(step, 2)

        @pl.when(step < 7)
        def _():
            fetch(second_ref, step + 1, turn_tile(step + 1)).start()

        fetch(second_ref, step, turn_tile(step)).wait()

        @pl.when(step >= 2)
        def _():
            store(step - 2).wait()

        left = stream[slot].reshape(4 * rows, BLOCK)
        flat = rows_ref[...].reshape(4 * rows, columns)
        made.tiles[turn_tile(step)] = weight_grad(left, flat[:, :SPLIT]).astype(B16)
        stage[slot] = weight_grad(left, flat[:, SPLIT:]).astype(B16)
        store(step).start()

    loads.wait(4, 7)
    stats.finish(2)
    pull_columns(stats_ref, scale_ref, column_ref, width)
    gather = Gather(wires, REDUCE_KINDS + 1, whole_ref, own, gather_sem, 2)

    def finish_chunks(low, high):
        @pl.loop(low, high)
        def _(chunk):
            at, result, share = pulled(
                reduce, chunk, (scale_ref, value_ref, gain_ref, base_ref), column_ref
            )
            result_ref[:, at] = result
            own[chunk] = result.astype(B16)
            gather.send(chunk)
            gain_grad_ref[:, at] = jnp.sum(share, axis=0, keepdims=True)

    finish_chunks(0, 2)
    make_tiles(down, make_down, 6, 8)
    fetch(second_ref, 0, turn_tile(0)).start()
    make_tiles(made, make, 0, 4)
    finish_chunks(2, width // CHUNK)
    down.middle()
    make_tiles(made, make, 4, 8)
    for step in (6, 7):
        store(step).wait()
    gather.relay(0, 3)
    down.late()
    made.step()
    gather.relay(3)
    made.middle()
    gather.close()
    made.late()
    down.close()
    made.close()
    reduce.close()


def middle_call(
    rows, w_gates, w_uppers, stats, scale, value, gain, base, hidden, grad, second, number
):
    height, width = value.shape
    count = width // CHUNK
    columns = rows.shape[2]
    quarter, units = width // 4, hidden.shape[2]
    sizes = (units, SPLIT)
    ends, tiles = [], []
    for size in sizes:
        ends += [shape((quarter, size), F32), shape((quarter, size))]
        tiles += [pltpu.VMEM((8, quarter, size), B16)] + fold_scratch(quarter, size)
    loaded = (rows, w_gates, w_uppers, value, base, hidden, scale)
    return pl.pallas_call(
        middle_kernel,
        out_shape=[
            shape((height, width), F32),
            shape((1, width), F32),
            shape((4, height, 2 * width)),
            shape((8, quarter, columns - SPLIT)),
        ]
        + ends,
        in_specs=[IN_ANY] * 7 + [IN_VMEM] * 2 + [IN_ANY] * 2,
        out_specs=[IN_VMEM] * 2 + [IN_ANY] * 2 + [IN_VMEM, IN_ANY] * 2,
        scratch_shapes=reduce_scratch(height, width)
        + [
            pltpu.VMEM((8, 8, 128), F32),
            pltpu.VMEM((8, 8, 128), F32),
            pltpu.VMEM((height, 128), F32),
        ]
        + wire_scratch(REDUCE_KINDS + 1 + GATHER_KINDS + 2 * FOLD_KINDS, count)
        + gather_scratch(height, width)
        + [
            pltpu.VMEM((2, 4, height, BLOCK), B16),
            pltpu.SemaphoreType.DMA((2,)),
            pltpu.VMEM((2, quarter, columns - SPLIT), B16),
            pltpu.SemaphoreType.DMA((2,)),
        ]
        + tiles
        + [pltpu.VMEM((2 * width, columns), B16)]
        + load_scratch((hidden, rows, value, base))[:-1]
        + [pltpu.VMEM((height, 128), F32)]
        + [pltpu.SemaphoreType.DMA((len(loaded),))],
        compiler_params=remote_params(number),
        cost_estimate=cost(48 * height * units * width, 64 * height * width),
    )(*loaded, stats, gain, grad, second)


def last_kernel(
    rows_in_ref,
    weight_in_ref,
    value_in_ref,
    base_in_ref,
    stats_in_ref,
    scale_ref,
    gain_ref,
    mlp_ref,
    heads_ref,
    out_in_ref,
    project_in_ref,
    result_ref,
    totals_ref,
    out_mine_ref,
    out_theirs_ref,
    project_mine_ref,
    project_theirs_ref,
    *scratch,
):
    bufs = scratch[:7]
    stats_ref, stats_recv, column_ref, send_sems, recv_sems = scratch[7:12]
    out_ref, project_ref, sums_ref, sums_recv, load_sem = scratch[12:17]
    out_bufs, project_bufs = scratch[17:18], scratch[18:19]
    rows_ref, weight_ref, value_ref, base_ref = scratch[19:23]
    rows, width = value_ref.shape
    loads = Loads(
        (project_in_ref, weight_in_ref, rows_in_ref, value_in_ref, base_in_ref, out_in_ref),
        (project_ref, weight_ref, rows_ref, value_ref, base_ref, out_ref),
        load_sem,
    )
    loads.start()
    stats_ref[...] = stats_in_ref[...]
    sums_ref[...] = jnp.zeros_like(sums_ref)
    for row in range(8):
        sums_ref[8, row : row + 1, :] = mlp_ref[:, row * 128 : (row + 1) * 128]
    sums_ref[9, 0:2, :] = heads_ref[0, 0:2, :] + heads_ref[1, 0:2, :]
    greet(neighbours() + planes())
    wires = Wires(send_sems, recv_sems)
    base = REDUCE_KINDS + 1
    out = Fold(wires, base, out_ref, out_bufs, out_mine_ref, out_theirs_ref, out_in_ref)
    project = Fold(
        wires,
        base + FOLD_KINDS,
        project_ref,
        project_bufs,
        project_mine_ref,
        project_theirs_ref,
        project_in_ref,
    )
    stats = Stats(wires, REDUCE_KINDS, stats_ref, stats_recv)
    stats.start(0)
    out.start()
    loads.wait(0, 2)

    @pl.loop(0, 8)
    def _(tile):
        share = jnp.sum(
            project_ref[tile].astype(F32) * weight_ref[tile_columns(tile), :].astype(F32),
            axis=1,
            keepdims=True,
        )
        sums_ref[tile, 0:1, :] = lie(share[:128])
        sums_ref[tile, 1:2, :] = lie(share[128:])

    side_device, across, core = neighbours()
    near, mirror = planes()

    def hop(index):
        slot, device = ((0, core), (1, across), (2, near), (3, mirror), (2, near))[index]
        kind, chunk = divmod(index, 4)
        return wires.copy(
            base + 2 * FOLD_KINDS + kind, chunk, sums_ref, sums_recv.at[slot], device
        )

    def add(slot):
        sums_ref[...] = sums_ref[...] + sums_recv[slot]

    reduce = Reduce(wires, rows_ref, weight_ref, True, bufs)
    loads.wait(2, 3)
    hop(0).start()
    reduce.give(0)
    hop(0).wait()
    add(0)
    hop(1).start()
    stats.step(0)

    def after_two():
        hop(1).wait()
        add(1)

        @pl.when(jnp.logical_not(inner()))
        def _():
            hop(2).start()

        project.start()
        stats.step(1)

    reduce.rest((after_two, lambda: None))
    loads.wait(3, 6)
    out.step()
    ends_line = jnp.logical_not(inner())

    @pl.when(inner())
    def _():
        hop(2).wait_recv()
        add(2)
        hop(3).start()

    out.middle()
    reduce.middle()
    stats.finish(2)
    pull_columns(stats_ref, scale_ref, column_ref, width)

    project.step()

    @pl.when(inner())
    def _():
        hop(3).wait()
        add(3)
        hop(4).start()

    project.middle()

    @pl.loop(0, width // CHUNK)
    def _(chunk):
        at, result, _ = pulled(
            reduce, chunk, (scale_ref, value_ref, gain_ref, base_ref), column_ref
        )
        result_ref[:, at] = result.astype(B16)

    @pl.when(inner())
    def _():
        hop(4).wait_send()

    @pl.when(ends_line)
    def _():
        hop(2).wait_send()
        hop(4).wait_recv()
        sums_ref[...] = sums_recv[2]

    move = wires.copy(base + 2 * FOLD_KINDS + 1, 1, sums_ref, sums_recv.at[4], side_device)
    move.start()
    out.late()
    project.late()
    move.wait()
    totals_ref[0:4] = sums_ref[0:4] + sums_recv[4, 4:8]
    totals_ref[4:8] = sums_ref[4:8] + sums_recv[4, 0:4]
    totals_ref[8] = sums_ref[8]
    totals_ref[9] = sums_recv[4, 8]
    totals_ref[10] = sums_ref[9] + sums_recv[4, 9]
    project.close()
    out.close()
    reduce.close()


def last_call(
    rows, weight, stats, scale, value, gain, base, mlp_part, head_parts, out, project, number
):
    height, width = value.shape
    count = width // CHUNK
    quarter, branch = out.shape[1:]
    columns = rows.shape[2]
    return pl.pallas_call(
        last_kernel,
        out_shape=(
            shape((height, width)),
            shape((11, 8, 128), F32),
            shape((quarter, branch), F32),
            shape((quarter, branch)),
            shape((quarter, columns), F32),
            shape((quarter, columns)),
        ),
        in_specs=[IN_ANY] * 4 + [IN_VMEM] * 5 + [IN_ANY] * 2,
        out_specs=(IN_VMEM, IN_VMEM) + (IN_VMEM, IN_ANY) * 2,
        scratch_shapes=reduce_scratch(height, width)
        + [
            pltpu.VMEM((8, 8, 128), F32),
            pltpu.VMEM((8, 8, 128), F32),
            pltpu.VMEM((height, 128), F32),
        ]
        + wire_scratch(REDUCE_KINDS + 1 + 2 * FOLD_KINDS + 2, count)
        + [
            pltpu.VMEM((8, quarter, branch), B16),
            pltpu.VMEM((8, quarter, columns), B16),
            pltpu.VMEM((10, 8, 128), F32),
            pltpu.VMEM((5, 10, 8, 128), F32),
            pltpu.SemaphoreType.DMA((6,)),
        ]
        + fold_scratch(quarter, branch)
        + fold_scratch(quarter, columns)
        + load_scratch((rows, weight, value, base))[:4],
        compiler_params=remote_params(number),
        cost_estimate=cost(32 * height * columns * width, 64 * height * width),
    )(rows, weight, value, base, stats, scale, gain, mlp_part, head_parts, out, project)


def back_kernel(
    most,
    query_gain_ref,
    key_gain_ref,
    *refs,
):
    operands, refs = refs[:13], refs[13:]
    rest_ref, whole_ref, first_ref = refs[:3]
    output_ref, result_ref, stats_ref, gains_ref, out_ref, project_ref = refs[3:9]
    ends, scratch = refs[9:11], refs[11:]
    bufs = scratch[:7]
    key_acc, value_acc, send_sems, recv_sems, rest_sem = scratch[7:12]
    tiles, fold_recv = scratch[12:14]
    held, load_sem = scratch[14:27], scratch[27]
    upstream, acc, stream, stream_sem, stage, stage_sem = scratch[28:]
    hidden_ref, down_ref, branch_ref, mixed_ref, starts_ref, cosine_ref, sine_ref = held[:7]
    projected_ref, query_ref, key_ref, value_ref, log_ref, residual_ref = held[7:]
    attend_loads = Loads(operands, held, load_sem)
    attend_loads.start()
    width = residual_ref.shape[1]
    rows = residual_ref.shape[0]

    def fetch(ref, tile):
        slot = lax.rem(tile, 2)
        return pltpu.make_async_copy(
            ref.at[:, :, tile_columns(tile)], stream.at[slot], stream_sem.at[slot]
        )

    def each_tile(ref, target, right, work):
        columns = target.shape[2]

        def store(tile):
            slot = lax.rem(tile, 2)
            return pltpu.make_async_copy(
                stage.at[slot, :, :columns], target.at[tile], stage_sem.at[slot]
            )

        @pl.loop(0, 8)
        def _(tile):
            @pl.when(tile < 7)
            def _():
                fetch(ref, tile + 1).start()

            fetch(ref, tile).wait()

            @pl.when(tile >= 2)
            def _():
                store(tile - 2).wait()

            left = stream[lax.rem(tile, 2)].reshape(4 * rows, BLOCK)
            work(tile, left)
            stage[lax.rem(tile, 2), :, :columns] = weight_grad(
                left, right[...].reshape(4 * rows, columns)
            ).astype(B16)
            store(tile).start()

        for tile in (6, 7):
            store(tile).wait()

    fetch(whole_ref, 0).start()
    core = lax.rem(lax.axis_index("tx"), 2)
    load = pltpu.make_async_copy(rest_ref, tiles, rest_sem)
    load.start()
    greet(neighbours() + planes())
    wires = Wires(send_sems, recv_sems)
    fold = Fold(wires, REDUCE_KINDS, tiles, (fold_recv,), ends[0], ends[1], rest_ref)
    fold.start()
    reduce = Reduce(wires, hidden_ref, down_ref, False, bufs)
    attend_loads.wait(0, 2)
    reduce.start()
    attend_loads.wait(2, 13)
    load.wait()
    acc[...] = jnp.zeros_like(acc)

    def branch_work(tile, left):
        acc[...] += rows_dot(left, branch_ref[:, tile_columns(tile)])

    each_tile(whole_ref, out_ref, mixed_ref, branch_work)
    fetch(first_ref, 0).start()
    upstream[...] = acc[...].astype(B16).reshape(upstream.shape)
    fold.step()
    stats_ref[...] = jnp.zeros_like(stats_ref)
    fixed_refs = (starts_ref, cosine_ref, sine_ref, query_gain_ref, key_gain_ref)
    saved_refs = (query_ref, key_ref, value_ref, log_ref)

    @pl.loop(0, 2)
    def _(seq):
        attend_sequence_back(
            core,
            seq,
            most,
            projected_ref,
            upstream,
            fixed_refs,
            saved_refs,
            result_ref,
            stats_ref,
            gains_ref,
            (acc, key_acc, value_acc),
        )

        @pl.when(seq == 0)
        def _():
            reduce.middle()

    fold.middle()

    each_tile(first_ref, project_ref, result_ref, lambda tile, left: None)


    @pl.loop(0, width // CHUNK)
    def _(chunk):
        at = lanes(chunk, 0, width)
        output_ref[:, at] = (residual_ref[:, at] + reduce.total(chunk)).astype(B16)

    fold.late()
    fold.close()
    reduce.close()


def back_call(
    whole, first, w_branch, mixed, hidden, w_back, residual, fixed_args, projected, saved, rest, most, number
):
    height, width = residual.shape
    _, cosine, _, query_gain, _ = fixed_args
    depth = query_gain.shape[1]
    length = cosine.shape[1]
    columns = projected.shape[2]
    heads = columns // depth - 2
    quarter, columns_left = rest.shape[1:]
    loaded = (hidden, w_back, w_branch, mixed) + fixed_args[:3] + (projected,) + saved + (residual,)
    return pl.pallas_call(
        lambda *refs: back_kernel(most, *refs),
        out_shape=(
            shape((height, width)),
            shape((4, height, columns)),
            shape((8, 8, 128), F32),
            shape((2, 8, depth), F32),
            shape((8, quarter, heads * depth)),
            shape((8, quarter, columns)),
        )
        + (shape((quarter, columns_left), F32), shape((quarter, columns_left))),
        in_specs=[IN_VMEM] * 2 + [IN_ANY] * 16,
        out_specs=[IN_VMEM] * 4 + [IN_ANY] * 2 + [IN_VMEM, IN_ANY],
        scratch_shapes=reduce_scratch(height, width)
        + [
            pltpu.VMEM((length, depth), F32),
            pltpu.VMEM((length, depth), F32),
        ]
        + wire_scratch(REDUCE_KINDS + FOLD_KINDS, width // CHUNK)
        + [pltpu.SemaphoreType.DMA, pltpu.VMEM(rest.shape, B16)]
        + fold_scratch(quarter, columns_left)
        + load_scratch(loaded)
        + [
            pltpu.VMEM((4, height, heads * depth), B16),
            pltpu.VMEM((4 * height, heads * depth), F32),
            pltpu.VMEM((2, 4, height, BLOCK), B16),
            pltpu.SemaphoreType.DMA((2,)),
            pltpu.VMEM((2, quarter, columns), B16),
            pltpu.SemaphoreType.DMA((2,)),
        ],
        compiler_params=remote_params(number),
        cost_estimate=cost(16 * height * hidden.shape[2] * width, 64 * height * width),
    )(*fixed_args[3:], *loaded, rest, whole, first)


def finish_kernel(place_ref, *refs):
    downs, both, out, project = refs[0:2], refs[2:6], refs[6:8], refs[8:10]
    totals_ref, gain_ref = refs[10:12]
    moved, refs = refs[12:14], refs[14:]
    query_ref, key_ref, value_ref, out_ref, gate_ref, up_ref, down_ref = refs[:7]
    attn_ref, mlp_ref, query_gain_ref, key_gain_ref = refs[7:11]
    for source, target in zip(moved, refs[11:]):
        target[...] = source[...]
    query_gain_ref[...] = totals_ref[10, 0:1]
    key_gain_ref[...] = totals_ref[10, 1:2]
    first = place_ref[0] == 0

    def ordered(mine, theirs):
        theirs = theirs.astype(F32)
        return jnp.where(first, mine, theirs), jnp.where(first, theirs, mine)

    def put(target, at, mine, theirs):
        half = target.shape[1] // 2
        low, high = ordered(mine, theirs)
        target[:, at : at + mine.shape[1]] = low
        target[:, half + at : half + at + mine.shape[1]] = high

    def put_turned(target, at, mine, theirs):
        half = target.shape[0] // 2
        low, high = ordered(mine, theirs)
        target[at : at + mine.shape[1], :] = low.T
        target[half + at : half + at + mine.shape[1], :] = high.T

    put_turned(down_ref, 0, downs[0][...], downs[1][...])
    put_turned(out_ref, 0, out[0][...], out[1][...])
    at = 0
    for target in (query_ref, key_ref, value_ref):
        size = target.shape[1] // 2
        put(target, 0, project[0][:, at : at + size], project[1][:, at : at + size])
        at += size
    units = gate_ref.shape[1] // 2
    at = 0
    for index in (0, 2):
        low = 0
        while low < both[index].shape[1]:
            size = min(both[index].shape[1] - low, units - at % units)
            put(
                gate_ref if at < units else up_ref,
                at % units,
                both[index][:, low : low + size],
                both[index + 1][:, low : low + size],
            )
            low += size
            at += size
    mine = jnp.concatenate([totals_ref[tile, 0:2] for tile in range(4)], axis=0)
    theirs = jnp.concatenate([totals_ref[tile, 0:2] for tile in range(4, 8)], axis=0)
    low, high = ordered(mine / gain_ref[0:8], theirs / gain_ref[8:16])
    attn_ref[0:8], attn_ref[8:16] = low, high
    low, high = ordered(totals_ref[8], totals_ref[9])
    mlp_ref[0:8], mlp_ref[8:16] = low, high


def finish_call(place, parts, totals, gain, moved, sizes):
    quarter = parts[0].shape[0]
    queries, keys, branch, units = sizes
    return pl.pallas_call(
        finish_kernel,
        out_shape=(
            shape((quarter, queries), F32),
            shape((quarter, keys), F32),
            shape((quarter, keys), F32),
            shape((branch, quarter), F32),
            shape((quarter, units), F32),
            shape((quarter, units), F32),
            shape((units, quarter), F32),
            shape((16, 128), F32),
            shape((16, 128), F32),
            shape((1, 128), F32),
            shape((1, 128), F32),
        )
        + tuple(shape(item.shape, item.dtype) for item in moved),
        in_specs=[pl.BlockSpec(memory_space=pltpu.SMEM)] + [IN_VMEM] * (len(parts) + 4),
        out_specs=[IN_VMEM] * 13,
        compiler_params=pltpu.CompilerParams(vmem_limit_bytes=VMEM_MOST),
        cost_estimate=cost(0, 16 * 1024 * 1024),
    )(place, *parts, totals, gain, *moved)


def plane_device(
    tokens,
    seg_ids,
    w_query,
    w_key,
    w_value,
    w_out,
    w_gate,
    w_up,
    w_down,
    attn_gain,
    mlp_gain,
    query_gain,
    key_gain,
    cotangent,
):
    depth = query_gain.shape[0]
    most = seg_ids.shape[1] // 2
    rows, width = tokens.shape
    head_width = w_query.shape[1] // 2
    kv_width = w_key.shape[1] // 2
    units = w_gate.shape[1] // 2

    rate = np.float64(THETA) ** (-np.arange(depth // 2) * 2.0 / depth)
    rate = jnp.asarray(np.concatenate([rate, rate])[None].astype(np.float32))
    attn_row, mlp_row, starts, cosine, sine, token_whole, w_project, w_branch = open_call(
        tokens, w_query, w_key, w_value, w_out, attn_gain[None], mlp_gain[None], seg_ids, rate, 0
    )
    fixed_args = (starts, cosine, sine, query_gain[None], key_gain[None])
    (
        first,
        projected,
        first_scale,
        mixed,
        query,
        keys,
        values,
        logs,
        grad_whole,
        w_back,
        gate_quarter,
    ) = front_call(
        token_whole, w_project, attn_row, fixed_args, most, cotangent, w_down, w_gate, 1
    )
    residual, residual_whole, w_uppers, w_gates = branch_call(
        mixed, w_branch, tokens, w_up, w_gate, gate_quarter, 2
    )
    flat = (4 * rows, 2 * width)
    grad_flat = grad_whole.reshape(flat)
    second, hidden, unit_grads, second_scale, unit_stats = units_call(
        residual_whole.reshape(flat), grad_flat, w_gates, w_uppers, w_back, mlp_row
    )
    (
        residual_grad,
        mlp_gain_part,
        branch_whole,
        rest_tiles,
        *ends,
    ) = middle_call(
        unit_grads.reshape(4, rows, 2 * units),
        w_gates,
        w_uppers,
        unit_stats,
        second_scale,
        residual,
        mlp_gain[None],
        cotangent,
        hidden.reshape(4, rows, units),
        grad_whole,
        second.reshape(4, rows, 2 * width),
        3,
    )
    output, proj_grads, proj_stats, gain_parts, out_tiles, project_tiles, *rest_ends = back_call(
        branch_whole,
        first,
        w_branch,
        mixed,
        hidden.reshape(4, rows, units),
        w_back,
        residual,
        fixed_args,
        projected,
        (query, keys, values, logs),
        rest_tiles,
        most,
        4,
    )
    input_grad, totals, out_mine, out_theirs, project_mine, project_theirs = last_call(
        proj_grads,
        w_project,
        proj_stats,
        first_scale,
        tokens,
        attn_gain[None],
        residual_grad,
        mlp_gain_part,
        gain_parts,
        out_tiles,
        project_tiles,
        5,
    )
    place = lax.axis_index("ty").reshape(1).astype(jnp.int32)
    (
        query_share,
        key_share,
        value_share,
        out_share,
        gate_share,
        up_share,
        down_share,
        attn_total,
        mlp_total,
        query_total,
        key_total,
        output,
        input_grad,
    ) = finish_call(
        place,
        (*ends, *rest_ends, out_mine, out_theirs, project_mine, project_theirs),
        totals,
        attn_row.reshape(16, 128),
        (output, input_grad),
        (2 * head_width, 2 * kv_width, 2 * head_width, 2 * units),
    )
    attn_total, mlp_total = attn_total.reshape(-1), mlp_total.reshape(-1)
    query_total, key_total = query_total.reshape(-1), key_total.reshape(-1)
    return (
        output,
        input_grad,
        query_share,
        key_share,
        value_share,
        out_share,
        gate_share,
        up_share,
        down_share,
        attn_total,
        mlp_total,
        query_total,
        key_total,
    )


def solution(mesh):
    placed = (
        P(("dp", "tx"), "ty"),
        P(("dp", "ty"), None),
        P("ty", "tx"),
        P("ty", "tx"),
        P("ty", "tx"),
        P("tx", "ty"),
        P("ty", "tx"),
        P("ty", "tx"),
        P("tx", "ty"),
        P("ty"),
        P("ty"),
        P(),
        P(),
        P(("dp", "tx"), "ty"),
    )
    return jax.shard_map(
        plane_device if fits(mesh) else general_device,
        mesh=mesh,
        in_specs=placed,
        out_specs=(
            P(("dp", "tx"), "ty"),
            P(("dp", "tx"), "ty"),
            P(("ty", "dp"), "tx"),
            P(("ty", "dp"), "tx"),
            P(("ty", "dp"), "tx"),
            P("tx", ("ty", "dp")),
            P(("ty", "dp"), "tx"),
            P(("ty", "dp"), "tx"),
            P("tx", ("ty", "dp")),
            P(),
            P(),
            P(),
            P(),
        ),
        check_vma=False,
    )
```
